32 devices in a mesh: dp: 8 (over z, x), mod: 4 (over y, core).
Axes of the slice: x: 2, y: 2, z: 4, core: 2. Of those that a mesh axis runs over, the one named last changes fastest.
Arguments:
- tokens: bfloat16 [64, 256, 1152], P(('dp', 'mod')), may hold values from -6 to 6
- condition: bfloat16 [64, 1152], P(('dp', 'mod')), may hold values from -6 to 6
- timestep: int32 [64], P(('dp', 'mod')), may hold values from 0 to 999
- qkv_weight: bfloat16 [1152, 3456], P('dp'), may hold values from -0.1875 to 0.1875
- out_weight: bfloat16 [1152, 1152], P('dp'), may hold values from -1.5 to 1.5
- gate_weight: bfloat16 [1152, 3072], P('dp'), may hold values from -0.1875 to 0.1875
- up_weight: bfloat16 [1152, 3072], P('dp'), may hold values from -0.1875 to 0.1875
- down_weight: bfloat16 [3072, 1152], P('dp'), may hold values from -0.109375 to 0.109375
- mod_weight: bfloat16 [1152, 6912], P(None, 'mod'), may hold values from -0.1875 to 0.1875
- mod_bias: bfloat16 [6912], P('mod'), may hold values from -3 to 3
- cotangent: bfloat16 [64, 256, 1152], P(('dp', 'mod')), may hold values from -6 to 6
Outputs:
- output_tokens: bfloat16 [64, 256, 1152], P(('dp', 'mod'))
- grad_tokens: float32 [64, 256, 1152], P(('dp', 'mod'))
- grad_condition: float32 [64, 1152], P(('dp', 'mod'))
- grad_qkv: float32 [1152, 3456], P('dp')
- grad_proj: float32 [1152, 1152], P('dp')
- grad_gate: float32 [1152, 3072], P('dp')
- grad_up: float32 [1152, 3072], P('dp')
- grad_down: float32 [3072, 1152], P('dp')
- grad_mod: float32 [1152, 6912], P('dp', 'mod')
- grad_bias: float32 [6912], P('mod')
The draws below stay inside these ranges and needn't reach their ends.
All inputs are finite; a program needn't handle non-finite values.
Results may differ from the reference program's by a relative error of at most 0.015.
Values may be sent and summed in bfloat16 or wider, within the bound.
A program may use at most 384 MiB of HBM per device.

```python
import math
import jax
import jax.numpy as jnp
from jax import lax

D = 1152
H = 16
HD = 72
FF = 3072
GRID = 16
SEQ = 256
STEPS = 1000
IMG_DEV = 1
MICRO = 2
IMAGES = 64
N_MOD = 4


def plant(drawn, rng, low, largest):
    longest = drawn.shape.index(max(drawn.shape))
    spots = []
    for shift in (0, 1):
        where = [jax.random.randint(jax.random.fold_in(rng, axis), (), 0, length) for axis, length in enumerate(drawn.shape)]
        where[longest] = (where[longest] + shift) % drawn.shape[longest]
        spots.append(tuple(where))
    return drawn.at[spots[0]].set(low).at[spots[1]].set(largest)


def level_of(own_key, dims, shards, least, largest):
    level, own = 1.0, jax.random.fold_in(own_key, 6)
    for axis_at, blocks in shards:
        heights = jnp.exp(jax.random.uniform(jax.random.fold_in(own, axis_at), (blocks,), jnp.float32, least / len(shards), largest / len(shards)))
        level = level * jnp.repeat(heights, dims[axis_at] // blocks).reshape([-1 if axis == axis_at else 1 for axis in range(len(dims))])
    return level


def gaussian(key, dims, deviation, most, shards=(), kind=jnp.bfloat16):
    values = jax.random.normal(key, dims, jnp.float32) * deviation
    if len(shards) > 0:
        values = level_of(key, dims, shards, -0.22, 0.18) * values
    return jnp.clip(values, min=-most, max=most).astype(kind)


def setup_inputs(seed: int = 0) -> dict:
    seeds = jax.random.split(jax.random.key(seed), 12)
    return {
        "tokens": gaussian(seeds[0], (IMAGES, SEQ, D), 1.0, 6.0, ((0, 32),)),
        "condition": gaussian(seeds[1], (IMAGES, D), 1.0, 6.0, ((0, 32),)),
        "timestep": plant(jax.random.randint(seeds[2], (IMAGES,), 0, STEPS), jax.random.fold_in(seeds[2], 1), 0, STEPS - 1).astype(jnp.int32),
        "qkv_weight": gaussian(seeds[3], (D, 3 * D), D ** -0.5, 0.1875, ((0, 8),)),
        "out_weight": gaussian(seeds[4], (D, D), (D * 4 // SEQ) ** -0.5, 1.5, ((0, 8),)),
        "gate_weight": gaussian(seeds[5], (D, FF), D ** -0.5, 0.1875, ((0, 8),)),
        "up_weight": gaussian(seeds[6], (D, FF), D ** -0.5, 0.1875, ((0, 8),)),
        "down_weight": gaussian(seeds[7], (FF, D), FF ** -0.5, 0.109375, ((0, 8),)),
        "mod_weight": gaussian(seeds[8], (D, 6 * D), D ** -0.5, 0.1875, ((1, 4),)),
        "mod_bias": gaussian(seeds[9], (6 * D,), 0.5, 3.0, ((0, 4),)),
        "cotangent": gaussian(seeds[10], (IMAGES, SEQ, D), 1.0, 6.0, ((0, 32),)),
    }


PRECISE = lax.Precision.HIGHEST
EPSILON = 1e-06

@jax.custom_vjp
def low(v):
    return lax.optimization_barrier(v.astype(jnp.bfloat16)).astype(jnp.float32)

@jax.custom_vjp
def low_back(v):
    return v

def low_keep(v):
    return (low(v), None)

def low_pass(kept, grad):
    return (grad,)

def back_keep(v):
    return (v, None)

def back_low(kept, grad):
    return (low(grad),)
low.defvjp(low_keep, low_pass)
low_back.defvjp(back_keep, back_low)

def norm_rows(field):
    return field * lax.rsqrt(lax.optimization_barrier(jnp.mean(field * field, axis=-1, keepdims=True)) + EPSILON)

def embed_steps(timestep):
    half_width = D // 2
    frequency = jnp.exp(-math.log(10000.0) * jnp.arange(half_width, dtype=jnp.float32) / half_width)
    angles = timestep.astype(jnp.float32)[:, None] * frequency[None, :]
    return jnp.concatenate([jnp.cos(angles), jnp.sin(angles)], axis=1)

def rope_tables():
    quarter = HD // 4
    frequency = jnp.exp(-math.log(10000.0) * jnp.arange(quarter, dtype=jnp.float32) / quarter)
    position = jnp.arange(SEQ)
    row_index = (position // GRID).astype(jnp.float32)
    col_index = (position % GRID).astype(jnp.float32)
    angles = jnp.stack([row_index[:, None] * frequency[None, :], col_index[:, None] * frequency[None, :]], axis=1)
    return (jnp.cos(angles), jnp.sin(angles))

def rotate(field, cosine_table, sine_table):
    leading = field.shape[:-1]
    quarters = field.reshape(leading + (2, 2, HD // 4))
    first_half = quarters[..., 0, :]
    second_half = quarters[..., 1, :]
    cosine_rows = cosine_table[:, None]
    sine_rows = sine_table[:, None]
    turned_first = first_half * cosine_rows - second_half * sine_rows
    turned_second = first_half * sine_rows + second_half * cosine_rows
    return jnp.stack([turned_first, turned_second], axis=-2).reshape(field.shape)

def layer(block_in, mod_rows, qkv_full, proj_full, gate_full, up_full, down_full, cosine_table, sine_table):
    images = block_in.shape[0]
    shift_first, scale_first, gate_first, shift_second, scale_second, gate_second = [mod_rows[:, None, number * D:(number + 1) * D] for number in range(6)]
    heads_shape = (images, SEQ, H, HD)
    entry_first = low(norm_rows(block_in) * (1.0 + scale_first) + shift_first)
    projected = low_back(jnp.einsum('bsd,de->bse', entry_first, qkv_full, precision=PRECISE))
    queries = low_back(low(rotate(norm_rows(projected[..., :D].reshape(heads_shape)), cosine_table, sine_table)))
    keys_rot = low_back(low(rotate(norm_rows(projected[..., D:2 * D].reshape(heads_shape)), cosine_table, sine_table)))
    values = low_back(low(projected[..., 2 * D:].reshape(heads_shape)))
    scores = low_back(jnp.einsum('bqhd,bkhd->bhqk', queries, keys_rot, precision=PRECISE) / math.sqrt(HD))
    attention = low(jax.nn.softmax(scores, axis=-1))
    combined = low_back(low(jnp.einsum('bhqk,bkhd->bqhd', attention, values, precision=PRECISE).reshape(images, SEQ, D)))
    attended = low_back(jnp.einsum('bsd,de->bse', combined, proj_full, precision=PRECISE))
    residual = block_in + gate_first * attended
    entry_second = low(norm_rows(residual) * (1.0 + scale_second) + shift_second)
    gate_proj = low_back(jnp.einsum('bsd,df->bsf', entry_second, gate_full, precision=PRECISE))
    up_proj = low_back(jnp.einsum('bsd,df->bsf', entry_second, up_full, precision=PRECISE))
    hidden = low(jax.nn.silu(gate_proj) * up_proj)
    branch = low_back(jnp.einsum('bsf,fd->bsd', hidden, down_full, precision=PRECISE))
    return residual + gate_second * branch

def reference(tokens, condition, timestep, qkv_weight, out_weight, gate_weight, up_weight, down_weight, mod_weight, mod_bias, cotangent):
    floats = [array.astype(jnp.float32) for array in (tokens, condition, qkv_weight, out_weight, gate_weight, up_weight, down_weight, mod_weight, mod_bias)]
    cosine_table, sine_table = rope_tables()
    stepped = embed_steps(timestep)
    group_size = IMG_DEV * MICRO * N_MOD

    def forward(tokens_f, condition_f, qkv_f, proj_f, gate_f, up_f, down_f, mod_f, bias_f):
        acted_cond = low(jax.nn.silu(condition_f + stepped))
        modulation = low_back(low(jnp.dot(acted_cond, mod_f, precision=PRECISE) + bias_f))
        blocked = tokens_f.reshape(-1, group_size, SEQ, D)
        mod_blocked = modulation.reshape(-1, group_size, 6 * D)
        checked = jax.checkpoint(layer)

        def one_group(pieces):
            return checked(pieces[0], pieces[1], qkv_f, proj_f, gate_f, up_f, down_f, cosine_table, sine_table)
        results = lax.map(one_group, (blocked, mod_blocked))
        return results.reshape(tokens_f.shape)
    result, pullback = jax.vjp(forward, *floats)
    grads = pullback(cotangent.astype(jnp.float32))
    return (result.astype(jnp.bfloat16), grads[0], grads[1], grads[2], grads[3], grads[4], grads[5], grads[6], grads[7], grads[8])
```

```python
import math

import jax
import jax.numpy as jnp
from jax import lax
from jax.experimental import pallas as pl
from jax.experimental.pallas import tpu as pltpu
from jax.sharding import PartitionSpec as P

D = 1152
H = 16
HD = 72
GRID = 16
SEQ = 256
MICRO = 2


EPSILON = 1e-06


def norm_rows(field):
    scale_inv = lax.rsqrt(jnp.mean(field * field, axis=-1, keepdims=True) + EPSILON)
    return (field * scale_inv, scale_inv)


def norm_back(normed, scale_inv, gradient):
    return scale_inv * (gradient - normed * jnp.mean(gradient * normed, axis=-1, keepdims=True))


def embed_steps(timestep):
    half_width = D // 2
    frequency = jnp.exp(-math.log(10000.0) * jnp.arange(half_width, dtype=jnp.float32) / half_width)
    angles = timestep.astype(jnp.float32)[:, None] * frequency[None, :]
    return jnp.concatenate([jnp.cos(angles), jnp.sin(angles)], axis=1)


def rope_tables():
    quarter = HD // 4
    frequency = jnp.exp(-math.log(10000.0) * jnp.arange(quarter, dtype=jnp.float32) / quarter)
    position = jnp.arange(SEQ)
    row_index = (position // GRID).astype(jnp.float32)
    col_index = (position % GRID).astype(jnp.float32)
    angles = jnp.stack(
        [row_index[:, None] * frequency[None, :], col_index[:, None] * frequency[None, :]], axis=1
    )
    return (jnp.cos(angles), jnp.sin(angles))


def rotate(field, cosine_table, sine_table):
    leading = field.shape[:-1]
    quarters = field.reshape(leading + (2, 2, HD // 4))
    first_half = quarters[..., 0, :]
    second_half = quarters[..., 1, :]
    cosine_rows = cosine_table[:, None]
    sine_rows = sine_table[:, None]
    turned_first = first_half * cosine_rows - second_half * sine_rows
    turned_second = first_half * sine_rows + second_half * cosine_rows
    return jnp.stack([turned_first, turned_second], axis=-2).reshape(field.shape)


def pack_rows(arrays, count):
    return jnp.concatenate([array.reshape(count, -1) for array in arrays], axis=1).reshape(-1)


def unpack_rows(flat, shapes, count):
    pieces = []
    offset = 0
    for rows_all, columns in shapes:
        rows = rows_all // count
        pieces.append(flat[offset : offset + rows * columns].reshape(rows, columns))
        offset = offset + rows * columns
    return pieces


def layer_pass(block_in, mod_rows, cotangent, weights, tables):
    qkv_full, proj_full, gate_full, up_full, down_full = weights
    cosine_table, sine_table = tables
    images = block_in.shape[0]
    shift_first, scale_first, gate_first, shift_second, scale_second, gate_second = [
        mod_rows[:, None, number * D : (number + 1) * D] for number in range(6)
    ]
    heads_shape = (images, SEQ, H, HD)
    factor = 1.0 / math.sqrt(HD)
    inputs = block_in.astype(jnp.float32)
    normed_first, inv_first = norm_rows(inputs)
    entry_first = (normed_first * (1.0 + scale_first) + shift_first).astype(jnp.bfloat16)
    projected = jnp.einsum("bsd,de->bse", entry_first, qkv_full, preferred_element_type=jnp.float32)
    q_normed, q_inv = norm_rows(projected[..., :D].reshape(heads_shape))
    k_normed, k_inv = norm_rows(projected[..., D : 2 * D].reshape(heads_shape))
    queries = rotate(q_normed, cosine_table, sine_table).astype(jnp.bfloat16)
    keys_rot = rotate(k_normed, cosine_table, sine_table).astype(jnp.bfloat16)
    values = projected[..., 2 * D :].reshape(heads_shape).astype(jnp.bfloat16)
    scores = (
        jnp.einsum("bqhd,bkhd->bhqk", queries, keys_rot, preferred_element_type=jnp.float32)
        * factor
    )
    highest = jnp.max(scores, axis=-1, keepdims=True)
    log_total = highest + jnp.log(jnp.sum(jnp.exp(scores - highest), axis=-1, keepdims=True))
    weights_soft = jnp.exp(scores - log_total).astype(jnp.bfloat16)
    combined = (
        jnp.einsum("bhqk,bkhd->bqhd", weights_soft, values, preferred_element_type=jnp.float32)
        .reshape(images, SEQ, D)
        .astype(jnp.bfloat16)
    )
    attended = jnp.einsum("bsd,de->bse", combined, proj_full, preferred_element_type=jnp.float32)
    residual = inputs + gate_first * attended
    normed_second, inv_second = norm_rows(residual)
    entry_second = (normed_second * (1.0 + scale_second) + shift_second).astype(jnp.bfloat16)
    gate_proj = jnp.einsum(
        "bsd,df->bsf", entry_second, gate_full, preferred_element_type=jnp.float32
    )
    up_proj = jnp.einsum("bsd,df->bsf", entry_second, up_full, preferred_element_type=jnp.float32)
    sigma_gate = jax.nn.sigmoid(gate_proj)
    activated = gate_proj * sigma_gate
    hidden = (activated * up_proj).astype(jnp.bfloat16)
    branch = jnp.einsum("bsf,fd->bsd", hidden, down_full, preferred_element_type=jnp.float32)
    output = (residual + gate_second * branch).astype(jnp.bfloat16)
    grad_out = cotangent.astype(jnp.float32)
    d_gate_second = jnp.sum(grad_out * branch, axis=1)
    d_branch = (gate_second * grad_out).astype(jnp.bfloat16)
    d_hidden = jnp.einsum("bsd,fd->bsf", d_branch, down_full, preferred_element_type=jnp.float32)
    d_gate_proj = (d_hidden * up_proj * sigma_gate * (1.0 + gate_proj * (1.0 - sigma_gate))).astype(
        jnp.bfloat16
    )
    d_up_proj = (d_hidden * activated).astype(jnp.bfloat16)
    d_entry_second = jnp.einsum(
        "bsf,df->bsd", d_gate_proj, gate_full, preferred_element_type=jnp.float32
    )
    d_entry_second = d_entry_second + jnp.einsum(
        "bsf,df->bsd", d_up_proj, up_full, preferred_element_type=jnp.float32
    )
    d_shift_second = jnp.sum(d_entry_second, axis=1)
    d_scale_second = jnp.sum(d_entry_second * normed_second, axis=1)
    d_residual = grad_out + norm_back(
        normed_second, inv_second, d_entry_second * (1.0 + scale_second)
    )
    d_gate_first = jnp.sum(d_residual * attended, axis=1)
    d_attended = (gate_first * d_residual).astype(jnp.bfloat16)
    d_combined = (
        jnp.einsum("bse,de->bsd", d_attended, proj_full, preferred_element_type=jnp.float32)
        .astype(jnp.bfloat16)
        .reshape(heads_shape)
    )
    scores_again = (
        jnp.einsum("bqhd,bkhd->bhqk", queries, keys_rot, preferred_element_type=jnp.float32)
        * factor
    )
    recomputed = jnp.exp(scores_again - log_total)
    d_weights = jnp.einsum(
        "bqhd,bkhd->bhqk", d_combined, values, preferred_element_type=jnp.float32
    )
    d_scores = (
        recomputed * (d_weights - jnp.sum(recomputed * d_weights, axis=-1, keepdims=True))
    ).astype(jnp.bfloat16)
    d_values = jnp.einsum(
        "bhqk,bqhd->bkhd", weights_soft, d_combined, preferred_element_type=jnp.float32
    ).astype(jnp.bfloat16)
    d_queries = (
        (
            jnp.einsum("bhqk,bkhd->bqhd", d_scores, keys_rot, preferred_element_type=jnp.float32)
            * factor
        )
        .astype(jnp.bfloat16)
        .astype(jnp.float32)
    )
    d_keys = (
        (
            jnp.einsum("bhqk,bqhd->bkhd", d_scores, queries, preferred_element_type=jnp.float32)
            * factor
        )
        .astype(jnp.bfloat16)
        .astype(jnp.float32)
    )
    d_q_raw = norm_back(q_normed, q_inv, rotate(d_queries, cosine_table, -sine_table))
    d_k_raw = norm_back(k_normed, k_inv, rotate(d_keys, cosine_table, -sine_table))
    flat_shape = (images, SEQ, D)
    d_projected = jnp.concatenate(
        [
            d_q_raw.reshape(flat_shape),
            d_k_raw.reshape(flat_shape),
            d_values.astype(jnp.float32).reshape(flat_shape),
        ],
        axis=-1,
    ).astype(jnp.bfloat16)
    d_entry_first = jnp.einsum(
        "bse,de->bsd", d_projected, qkv_full, preferred_element_type=jnp.float32
    )
    d_shift_first = jnp.sum(d_entry_first, axis=1)
    d_scale_first = jnp.sum(d_entry_first * normed_first, axis=1)
    d_tokens = d_residual + norm_back(normed_first, inv_first, d_entry_first * (1.0 + scale_first))
    d_modulation = jnp.concatenate(
        [d_shift_first, d_scale_first, d_gate_first, d_shift_second, d_scale_second, d_gate_second],
        axis=1,
    ).astype(jnp.bfloat16)
    factors = (
        entry_first,
        d_projected,
        combined,
        d_attended,
        entry_second,
        d_gate_proj,
        d_up_proj,
        hidden,
        d_branch,
    )
    return (output, d_tokens, d_modulation, factors)


MESH = pl.DeviceIdType.MESH
WIDTH = 384
LANE_HALF = 2304
FF_HALF = 1536
BF16 = jnp.bfloat16
F32 = jnp.float32


def place():
    dp = lax.axis_index("dp")
    mod = lax.axis_index("mod")
    return dp // 2, dp % 2, mod // 2, mod % 2


def device(z, x, y, c):
    return (z * 2 + x, y * 2 + c)


def greet(peers):
    barrier = pltpu.get_barrier_semaphore()
    for peer in peers:
        pl.semaphore_signal(barrier, inc=1, device_id=peer, device_id_type=MESH)
    pl.semaphore_wait(barrier, len(peers))


def neighbours(z, x, y, c):
    around = [device((z + step) % 4, x, y, c) for step in (1, 2, 3)]
    return around + [device(z, 1 - x, y, c), device(z, x, 1 - y, c), device(z, x, y, 1 - c)]


def send(source, target, send_sem, recv_sem, peer):
    pltpu.make_async_remote_copy(
        src_ref=source,
        dst_ref=target,
        send_sem=send_sem,
        recv_sem=recv_sem,
        device_id=peer,
        device_id_type=MESH,
    ).start()


def drain(window, sem):
    pltpu.make_async_copy(window, window, sem).wait()


class Piece:
    def __init__(self, source, target, row, rows, column, edge):
        self.source, self.target = source, target
        self.row, self.rows, self.column, self.edge = row, rows, column, edge


def gather_pieces(refs, c, edge_of):
    packed, gate, up, down, packed_all, gate_all, up_all, down_all = refs
    pieces = []
    for j in range(6):
        pieces.append(Piece(packed, packed_all, 0, 144, c * LANE_HALF + j * WIDTH, edge_of(144, j)))
    for j in range(4):
        pieces.append(Piece(gate, gate_all, 0, 144, c * FF_HALF + j * WIDTH, edge_of(144, j)))
        pieces.append(Piece(up, up_all, 0, 144, c * FF_HALF + j * WIDTH, edge_of(144, j)))
    for j in range(3):
        pieces.append(Piece(down, down_all, c * 192, 192, j * WIDTH, edge_of(192, j)))
    return pieces


class Gather:
    def __init__(self, refs, sems, spot):
        self.z, self.x, self.y, self.c = spot
        self.pieces = gather_pieces(refs, self.c, lambda rows, j: rows // 3)
        self.send_sems, self.recv_sems, self.own_sems = sems
        self.refs = refs

    def columns(self, piece):
        return pl.ds(pl.multiple_of(piece.column, 128), WIDTH)

    def part(self, piece):
        keep = piece.rows - piece.edge
        return pl.ds(pl.multiple_of(piece.row + self.y * piece.edge, 16), keep), keep

    def mine(self, piece):
        return pl.ds(pl.multiple_of(piece.row + self.y * (piece.rows - piece.edge), 16), piece.edge)

    def own_copies(self):
        for k in range(4):
            pltpu.make_async_copy(
                self.refs[k], self.refs[4 + k].at[self.z, self.x], self.own_sems.at[k]
            ).start()

    def own_done(self):
        for k in range(4):
            drain(self.refs[k], self.own_sems.at[k])

    def start_z(self, t):
        p = self.pieces[t]
        rows, _ = self.part(p)
        here = p.source.at[rows, self.columns(p)]
        there = p.target.at[self.z, self.x, rows, self.columns(p)]
        for step in (1, 3, 2):
            peer = device((self.z + step) % 4, self.x, self.y, self.c)
            send(here, there, self.send_sems.at[0, t], self.recv_sems.at[0, t], peer)
        peer = device(self.z, 1 - self.x, self.y, self.c)
        send(here, there, self.send_sems.at[1, t], self.recv_sems.at[1, t], peer)

    def start_x(self, t):
        p = self.pieces[t]
        rows, keep = self.part(p)
        columns = self.columns(p)
        drain(p.target.at[pl.ds(0, 3), 0, pl.ds(0, keep), pl.ds(0, WIDTH)], self.recv_sems.at[0, t])
        x_peer = device(self.z, 1 - self.x, self.y, self.c)
        y_peer = device(self.z, self.x, 1 - self.y, self.c)
        for step in (1, 3, 2):
            other = (self.z + step) % 4
            block = p.target.at[other, self.x, rows, columns]
            send(block, block, self.send_sems.at[1, t], self.recv_sems.at[1, t], x_peer)
        for step in (1, 3, 2):
            other = (self.z + step) % 4
            block = p.target.at[other, self.x, self.mine(p), columns]
            send(block, block, self.send_sems.at[2, t], self.recv_sems.at[2, t], y_peer)

    def start_y(self, t):
        p = self.pieces[t]
        _, keep = self.part(p)
        columns = self.columns(p)
        drain(p.target.at[:, 0, pl.ds(0, keep), pl.ds(0, WIDTH)], self.recv_sems.at[1, t])
        y_peer = device(self.z, self.x, 1 - self.y, self.c)
        block = p.target.at[:, 1 - self.x, self.mine(p), columns]
        send(block, block, self.send_sems.at[2, t], self.recv_sems.at[2, t], y_peer)

    def start_c(self, t):
        p = self.pieces[t]
        columns = self.columns(p)
        half = pl.ds(pl.multiple_of(p.row, 16), p.rows)
        self.drain_seven(p.edge, self.recv_sems.at[2, t])
        peer = device(self.z, self.x, self.y, 1 - self.c)
        block = p.target.at[:, 1 - self.x, half, columns]
        send(block, block, self.send_sems.at[3, t], self.recv_sems.at[3, t], peer)
        for step in (1, 2, 3):
            block = p.target.at[(self.z + step) % 4, self.x, half, columns]
            send(block, block, self.send_sems.at[3, t], self.recv_sems.at[3, t], peer)

    def arrived(self, t):
        self.drain_seven(self.pieces[t].rows, self.recv_sems.at[3, t])

    def drain_seven(self, rows, sem):
        high = 96 if rows > 144 else rows
        drain(self.refs[4].at[pl.ds(0, rows // high), 0, pl.ds(0, high), pl.ds(0, 7 * WIDTH)], sem)

    def sent_z(self, t):
        p = self.pieces[t]
        _, keep = self.part(p)
        drain(p.target.at[pl.ds(0, 3), 0, pl.ds(0, keep), pl.ds(0, WIDTH)], self.send_sems.at[0, t])

    def sent_rest(self, t):
        p = self.pieces[t]
        _, keep = self.part(p)
        drain(p.target.at[:, 0, pl.ds(0, keep), pl.ds(0, WIDTH)], self.send_sems.at[1, t])
        for stage, rows in ((2, p.edge), (3, p.rows)):
            self.drain_seven(rows, self.send_sems.at[stage, t])


N_PIECES = 17


def gather_kernel(*refs):
    arrays, sems = refs[:8], refs[8:]
    spot = place()
    greet(neighbours(*spot))
    gather = Gather(arrays, sems, spot)
    gather.own_copies()
    ahead = 2
    for t in range(N_PIECES + 4 + ahead):
        if t < N_PIECES:
            if t >= ahead:
                gather.sent_z(t - ahead)
            gather.start_z(t)
        if 0 <= t - ahead < N_PIECES:
            gather.start_x(t - ahead)
        if 0 <= t - ahead - 1 < N_PIECES:
            gather.start_y(t - ahead - 1)
        if 0 <= t - ahead - 2 < N_PIECES:
            gather.start_c(t - ahead - 2)
        if 0 <= t - ahead - 3 < N_PIECES:
            gather.arrived(t - ahead - 3)
    for t in range(N_PIECES - ahead, N_PIECES):
        gather.sent_z(t)
    for t in range(N_PIECES):
        gather.sent_rest(t)
    gather.own_done()


def gather_weights(packed, gate, up, down):
    hbm = pl.BlockSpec(memory_space=pl.ANY)
    shapes = [
        jax.ShapeDtypeStruct((4, 2) + array.shape, BF16) for array in (packed, gate, up, down)
    ]
    return pl.pallas_call(
        gather_kernel,
        out_shape=shapes,
        in_specs=[hbm] * 4,
        out_specs=[hbm] * 4,
        scratch_shapes=[
            pltpu.SemaphoreType.DMA((4, N_PIECES)),
            pltpu.SemaphoreType.DMA((4, N_PIECES)),
            pltpu.SemaphoreType.DMA((4,)),
        ],
        name="gather_weights",
        compiler_params=pltpu.CompilerParams(
            collective_id=0, has_side_effects=True, vmem_limit_bytes=16 << 20
        ),
    )(packed, gate, up, down)


SCATTER_ROWS = (144,) * 14 + (192,) * 3
SCATTER_EDGE = tuple((32, 48)[j % 2] for j in range(14)) + (48,) * 3


class Scatter:
    def __init__(self, bufs, sems, outs, spot):
        self.z, self.x, self.y, self.c = spot
        self.held, self.got_y, self.got_x, self.got_z, self.mid, self.got_f, self.fin, self.got_c = bufs
        self.send_sems, self.recv_sems = sems
        self.outs = outs

    def shape(self, t):
        return SCATTER_ROWS[t], SCATTER_EDGE[t]

    def part(self, t):
        rows, edge = self.shape(t)
        return pl.ds(pl.multiple_of(self.y * edge, 16), rows - edge)

    def buf(self, group, t, rows=None):
        big, small = group
        return small.at[t] if t < 14 else big.at[t - 14]

    def start_y(self, t):
        rows, edge = self.shape(t)
        theirs = pl.ds(pl.multiple_of((1 - self.y) * (rows - edge), 16), edge)
        peer = device(self.z, self.x, 1 - self.y, self.c)
        send(
            self.buf(self.held, t).at[:, :, theirs, :],
            self.buf(self.got_y, t).at[:, :, pl.ds(0, edge), :],
            self.send_sems.at[0, t],
            self.recv_sems.at[0, t],
            peer,
        )

    def start_x(self, t):
        rows, edge = self.shape(t)
        held = self.buf(self.held, t)
        got = self.buf(self.got_y, t)
        drain(got.at[:, :, pl.ds(0, edge), :], self.recv_sems.at[0, t])
        mine = pl.ds(pl.multiple_of(self.y * (rows - edge), 16), edge)

        for k in range(4):
            for x in range(2):
                total = held[k, x, mine, :].astype(F32) + got[k, x, :edge, :].astype(F32)
                held[k, x, mine, :] = total.astype(BF16)
        peer = device(self.z, 1 - self.x, self.y, self.c)
        send(
            held.at[:, 1 - self.x, self.part(t), :],
            self.buf(self.got_x, t).at[:, pl.ds(0, rows - edge), :],
            self.send_sems.at[1, t],
            self.recv_sems.at[1, t],
            peer,
        )

    def start_z(self, t):
        rows, edge = self.shape(t)
        held = self.buf(self.held, t)
        got = self.buf(self.got_x, t)
        drain(got.at[:, pl.ds(0, rows - edge), :], self.recv_sems.at[1, t])
        part = self.part(t)
        for k in range(4):
            total = held[k, self.x, part, :].astype(F32) + got[k, : rows - edge, :].astype(F32)
            held[k, self.x, part, :] = total.astype(BF16)
        for step in (1, 3, 2):
            other = (self.z + step) % 4
            send(
                held.at[other, self.x, part, :],
                self.buf(self.got_z, t).at[step - 1, pl.ds(0, rows - edge), :],
                self.send_sems.at[2, t],
                self.recv_sems.at[2, t],
                device(other, self.x, self.y, self.c),
            )

    def start_f(self, t):
        rows, edge = self.shape(t)
        held = self.buf(self.held, t)
        got = self.buf(self.got_z, t)
        drain(got.at[:, pl.ds(0, rows - edge), :], self.recv_sems.at[2, t])
        total = held[self.z, self.x, self.part(t), :].astype(F32)
        for k in range(3):
            total = total + got[k, : rows - edge, :].astype(F32)
        mid = self.buf(self.mid, t)
        mid[: rows - edge, :] = total.astype(BF16)
        send(
            mid.at[pl.ds(0, rows - edge), :],
            self.buf(self.got_f, t).at[pl.ds(0, rows - edge), :],
            self.send_sems.at[3, t],
            self.recv_sems.at[3, t],
            device(self.z, self.x, 1 - self.y, self.c),
        )

    def start_c(self, t):
        rows, edge = self.shape(t)
        mid, got, fin = self.buf(self.mid, t), self.buf(self.got_f, t), self.buf(self.fin, t)
        y = self.y
        drain(got.at[pl.ds(0, rows - edge), :], self.recv_sems.at[3, t])
        both = rows - 2 * edge

        def at(offset, count):
            return pl.ds(pl.multiple_of(offset, 16), count)

        fin[at(y * (rows - edge), edge), :] = mid[at(y * both, edge), :]
        fin[at((1 - y) * (rows - edge), edge), :] = got[at((1 - y) * both, edge), :]
        total = mid[at((1 - y) * edge, both), :].astype(F32) + got[at(y * edge, both), :].astype(F32)
        fin[edge : edge + both, :] = total.astype(BF16)
        send(
            fin,
            self.buf(self.got_c, t),
            self.send_sems.at[4, t],
            self.recv_sems.at[4, t],
            device(self.z, self.x, self.y, 1 - self.c),
        )
        self.store(t, fin, self.c)

    def finish(self, t):
        got = self.buf(self.got_c, t)
        drain(got, self.recv_sems.at[4, t])
        self.store(t, got, 1 - self.c)

    def store(self, t, block, core):
        packed, gate, up, down = self.outs
        if t < 6:
            columns = pl.ds(pl.multiple_of(core * LANE_HALF + t * WIDTH, 128), WIDTH)
            packed[:, columns] = block[...].astype(F32)
        elif t < 14:
            target = (gate, up)[(t - 6) % 2]
            columns = pl.ds(pl.multiple_of(core * FF_HALF + (t - 6) // 2 * WIDTH, 128), WIDTH)
            target[:, columns] = block[...].astype(F32)
        else:
            rows = pl.ds(pl.multiple_of(core * 192, 16), 192)
            down[rows, (t - 14) * WIDTH : (t - 13) * WIDTH] = block[...].astype(F32)

    def sent(self, t):
        rows, edge = self.shape(t)
        drain(self.buf(self.got_y, t).at[:, :, pl.ds(0, edge), :], self.send_sems.at[0, t])
        drain(self.buf(self.got_x, t).at[:, pl.ds(0, rows - edge), :], self.send_sems.at[1, t])
        drain(self.buf(self.got_z, t).at[:, pl.ds(0, rows - edge), :], self.send_sems.at[2, t])
        drain(self.buf(self.got_f, t).at[pl.ds(0, rows - edge), :], self.send_sems.at[3, t])
        drain(self.buf(self.got_c, t), self.send_sems.at[4, t])


def scatter_scratch():
    shapes = []
    for lead, share in (((4, 2), 1), ((4, 2), 3), ((4,), 2), ((3,), 2), ((), 2), ((), 2), ((), 1), ((), 1)):
        for count, rows, edges in ((3, 192, (48, 48)), (14, 144, (32, 48))):
            height = {1: rows, 3: max(edges), 2: rows - min(edges)}[share]
            shapes.append(pltpu.VMEM((count,) + lead + (height, WIDTH), BF16))
    return shapes


def scatter_kernel(half_packed, half_gate, half_up, half_down, *rest):
    outs = rest[:4]
    scratch = rest[4:20]
    send_sems, recv_sems, load_sems = rest[20:]
    bufs = [(scratch[2 * k], scratch[2 * k + 1]) for k in range(8)]
    spot = place()
    greet(neighbours(*spot))
    scatter = Scatter(bufs, (send_sems, recv_sems), outs, spot)
    order = list(range(14, 17)) + list(range(6, 14)) + list(range(6))
    loads = []
    for t in range(N_PIECES):
        if t < 6:
            source = half_packed.at[:, :, :, pl.ds(t * WIDTH, WIDTH)]
        elif t < 14:
            source = (half_gate, half_up)[(t - 6) % 2].at[:, :, :, pl.ds((t - 6) // 2 * WIDTH, WIDTH)]
        else:
            source = half_down.at[:, :, :, pl.ds((t - 14) * WIDTH, WIDTH)]
        loads.append(pltpu.make_async_copy(source, scatter.buf(scatter.held, t), load_sems.at[t]))
    for t in order:
        loads[t].start()
    ahead = 2
    for k in range(N_PIECES + 6 + ahead):
        if k < N_PIECES:
            loads[order[k]].wait()
            scatter.start_y(order[k])
        for lag, stage in enumerate(
            (scatter.start_x, scatter.start_z, scatter.start_f, scatter.start_c, scatter.finish)
        ):
            if 0 <= k - ahead - lag < N_PIECES:
                stage(order[k - ahead - lag])
    for t in range(N_PIECES):
        scatter.sent(t)


def scatter_grads(half_packed, half_gate, half_up, half_down):
    hbm = pl.BlockSpec(memory_space=pl.ANY)
    vmem = pl.BlockSpec(memory_space=pltpu.VMEM)
    return pl.pallas_call(
        scatter_kernel,
        out_shape=[
            jax.ShapeDtypeStruct((144, 4608), F32),
            jax.ShapeDtypeStruct((144, 3072), F32),
            jax.ShapeDtypeStruct((144, 3072), F32),
            jax.ShapeDtypeStruct((384, 1152), F32),
        ],
        in_specs=[hbm] * 4,
        out_specs=[vmem] * 4,
        scratch_shapes=scatter_scratch()
        + [
            pltpu.SemaphoreType.DMA((5, N_PIECES)),
            pltpu.SemaphoreType.DMA((5, N_PIECES)),
            pltpu.SemaphoreType.DMA((N_PIECES,)),
        ],
        name="scatter_grads",
        compiler_params=pltpu.CompilerParams(
            collective_id=1, has_side_effects=True, vmem_limit_bytes=60 << 20
        ),
    )(half_packed, half_gate, half_up, half_down)


def body_general(
    tokens,
    condition,
    timestep,
    qkv_weight,
    out_weight,
    gate_weight,
    up_weight,
    down_weight,
    mod_weight,
    mod_bias,
    cotangent,
):
    gathered = (
        lax.all_gather(qkv_weight, "dp", axis=0, tiled=True),
        lax.all_gather(out_weight, "dp", axis=0, tiled=True),
        lax.all_gather(gate_weight, "dp", axis=0, tiled=True),
        lax.all_gather(up_weight, "dp", axis=0, tiled=True),
        lax.all_gather(down_weight, "dp", axis=0, tiled=True),
    )
    cond_total = condition.astype(jnp.float32) + embed_steps(timestep)
    acted_cond = jax.nn.silu(cond_total).astype(jnp.bfloat16)
    acted_group = lax.all_gather(acted_cond, "mod", axis=0, tiled=True)
    mod_part = (
        jnp.dot(acted_group, mod_weight, preferred_element_type=jnp.float32)
        + mod_bias.astype(jnp.float32)
    ).astype(jnp.bfloat16)
    modulation = lax.all_to_all(mod_part, "mod", split_axis=0, concat_axis=1, tiled=True).astype(
        jnp.float32
    )
    tables = rope_tables()
    per_micro = tokens.shape[0] // MICRO
    outputs = []
    token_grads = []
    mod_grads = []
    kept = []
    for micro_step in range(MICRO):
        start_row = micro_step * per_micro
        output, d_tokens, d_modulation, factors = layer_pass(
            tokens[start_row : start_row + per_micro],
            modulation[start_row : start_row + per_micro],
            cotangent[start_row : start_row + per_micro],
            gathered,
            tables,
        )
        outputs.append(output)
        token_grads.append(d_tokens)
        mod_grads.append(d_modulation)
        kept.append(factors)
    joined = [jnp.concatenate([factors[number] for factors in kept], axis=0) for number in range(9)]
    (
        entry_first,
        d_projected,
        combined,
        d_attended,
        entry_second,
        d_gate_proj,
        d_up_proj,
        hidden,
        d_branch,
    ) = joined
    grad_qkv = jnp.einsum(
        "bsd,bse->de", entry_first, d_projected, preferred_element_type=jnp.float32
    )
    grad_proj = jnp.einsum("bsd,bse->de", combined, d_attended, preferred_element_type=jnp.float32)
    grad_gate = jnp.einsum(
        "bsd,bsf->df", entry_second, d_gate_proj, preferred_element_type=jnp.float32
    )
    grad_up = jnp.einsum("bsd,bsf->df", entry_second, d_up_proj, preferred_element_type=jnp.float32)
    grad_down = jnp.einsum("bsf,bsd->fd", hidden, d_branch, preferred_element_type=jnp.float32)
    totals = (grad_qkv, grad_proj, grad_gate, grad_up, grad_down)
    output_tokens = jnp.concatenate(outputs, axis=0)
    grad_tokens = jnp.concatenate(token_grads, axis=0)
    mod_grad = jnp.concatenate(mod_grads, axis=0)
    mod_back = lax.all_to_all(mod_grad, "mod", split_axis=1, concat_axis=0, tiled=True)
    grad_mod_part = jnp.einsum(
        "id,ic->dc", acted_group, mod_back, preferred_element_type=jnp.float32
    )
    bias_part = jnp.sum(mod_back.astype(jnp.float32), axis=0)
    acted_grad_part = jnp.einsum(
        "ic,dc->id", mod_back, mod_weight, preferred_element_type=jnp.float32
    )
    acted_grad = lax.psum_scatter(
        acted_grad_part.astype(jnp.bfloat16), "mod", scatter_dimension=0, tiled=True
    ).astype(jnp.float32)
    sigma_cond = jax.nn.sigmoid(cond_total)
    grad_condition = acted_grad * sigma_cond * (1.0 + cond_total * (1.0 - sigma_cond))
    grad_bias = lax.psum(bias_part, "dp")
    count = lax.axis_size("dp")
    arrays = totals + (grad_mod_part,)
    shapes = [array.shape for array in arrays]
    flat = lax.psum_scatter(pack_rows(arrays, count), "dp", scatter_dimension=0, tiled=True)
    summed = unpack_rows(flat, shapes, count)
    finished = (
        lax.psum(summed[0].astype(jnp.bfloat16), "mod").astype(jnp.float32),
        lax.psum(summed[1].astype(jnp.bfloat16), "mod").astype(jnp.float32),
        lax.psum(summed[2].astype(jnp.bfloat16), "mod").astype(jnp.float32),
        lax.psum(summed[3].astype(jnp.bfloat16), "mod").astype(jnp.float32),
        lax.psum(summed[4].astype(jnp.bfloat16), "mod").astype(jnp.float32),
    )
    grad_mod = summed[5]
    return (
        output_tokens,
        grad_tokens,
        grad_condition,
        finished[0],
        finished[1],
        finished[2],
        finished[3],
        finished[4],
        grad_mod,
        grad_bias,
    )


def pair_exchange(array):
    return lax.ppermute(array, "mod", [(0, 1), (1, 0), (2, 3), (3, 2)])


def body_fast(
    tokens,
    condition,
    timestep,
    qkv_weight,
    out_weight,
    gate_weight,
    up_weight,
    down_weight,
    mod_weight,
    mod_bias,
    cotangent,
):
    core = lax.axis_index("mod") % 2
    packed = jnp.concatenate([qkv_weight, out_weight], axis=1)
    packed_all, gate_all, up_all, down_all = gather_weights(
        packed, gate_weight, up_weight, down_weight
    )
    packed_all = packed_all.reshape(D, 4 * D)
    gathered = (
        packed_all[:, : 3 * D],
        packed_all[:, 3 * D :],
        gate_all.reshape(D, -1),
        up_all.reshape(D, -1),
        down_all.reshape(-1, D),
    )
    cond_total = condition.astype(jnp.float32) + embed_steps(timestep)
    acted_cond = jax.nn.silu(cond_total).astype(jnp.bfloat16)
    acted_group = lax.all_gather(acted_cond, "mod", axis=0, tiled=True)
    mod_part = (
        jnp.dot(acted_group, mod_weight, preferred_element_type=jnp.float32)
        + mod_bias.astype(jnp.float32)
    ).astype(jnp.bfloat16)
    modulation = lax.all_to_all(mod_part, "mod", split_axis=0, concat_axis=1, tiled=True).astype(
        jnp.float32
    )
    tables = rope_tables()
    output_tokens, grad_tokens, mod_grad, factors = layer_pass(
        tokens, modulation, cotangent, gathered, tables
    )
    (
        entry_first,
        d_projected,
        combined,
        d_attended,
        entry_second,
        d_gate_proj,
        d_up_proj,
        hidden,
        d_branch,
    ) = [factor.reshape(-1, factor.shape[-1]) for factor in factors]

    def pair(factor):
        return jnp.concatenate([factor, pair_exchange(factor)], axis=0)

    def half(factor, width):
        return lax.dynamic_slice_in_dim(factor, core * width, width, 1)

    def other(factor, width):
        return lax.dynamic_slice_in_dim(factor, (1 - core) * width, width, 1)

    def pair_half(factor, width):
        return jnp.concatenate(
            [half(factor, width), pair_exchange(other(factor, width))], axis=0
        )

    def outer(left, right):
        return lax.dot_general(
            left, right, (((0,), (0,)), ((), ())), preferred_element_type=jnp.float32
        ).astype(BF16)

    entry_pair = pair(entry_first)
    second_pair = jnp.where(core == 0, entry_pair, pair(combined))
    packed_pair = pair_half(jnp.concatenate([d_projected, d_attended], axis=1), LANE_HALF)
    half_packed = jnp.concatenate(
        [outer(entry_pair, packed_pair[:, :D]), outer(second_pair, packed_pair[:, D:])], axis=1
    )
    entry_pair_b = pair(entry_second)
    half_gate = outer(entry_pair_b, pair_half(d_gate_proj, FF_HALF))
    half_up = outer(entry_pair_b, pair_half(d_up_proj, FF_HALF))
    by_core = hidden.reshape(-1, 8, 2, 192).transpose(0, 2, 1, 3).reshape(-1, 2 * FF_HALF)
    half_down = outer(pair_half(by_core, FF_HALF), pair(d_branch))
    grads = scatter_grads(
        half_packed.reshape(4, 2, 144, -1),
        half_gate.reshape(4, 2, 144, -1),
        half_up.reshape(4, 2, 144, -1),
        half_down.reshape(4, 2, 192, -1),
    )
    mod_back = lax.all_to_all(mod_grad, "mod", split_axis=1, concat_axis=0, tiled=True)
    acted_all = lax.all_gather(acted_group, "dp", axis=0, tiled=True)
    back_all = lax.all_gather(mod_back, "dp", axis=0, tiled=True)
    rows = D // 8
    acted_rows = lax.dynamic_slice_in_dim(acted_all, lax.axis_index("dp") * rows, rows, 1)
    grad_mod = jnp.einsum("id,ic->dc", acted_rows, back_all, preferred_element_type=jnp.float32)
    grad_bias = jnp.sum(back_all.astype(jnp.float32), axis=0)
    acted_grad_part = jnp.einsum(
        "ic,dc->id", mod_back, mod_weight, preferred_element_type=jnp.float32
    )
    acted_grad = lax.psum_scatter(
        acted_grad_part.astype(jnp.bfloat16), "mod", scatter_dimension=0, tiled=True
    ).astype(jnp.float32)
    sigma_cond = jax.nn.sigmoid(cond_total)
    grad_condition = acted_grad * sigma_cond * (1.0 + cond_total * (1.0 - sigma_cond))
    return (
        output_tokens,
        grad_tokens,
        grad_condition,
        grads[0][:, : 3 * D],
        grads[0][:, 3 * D :],
        grads[1],
        grads[2],
        grads[3],
        grad_mod,
        grad_bias,
    )


def pick_body(mesh):
    if dict(mesh.shape) == {"dp": 8, "mod": 4}:
        return body_fast
    return body_general


def solution(mesh):
    in_specs = (
        P(("dp", "mod"), None, None),
        P(("dp", "mod"), None),
        P(("dp", "mod")),
        P("dp", None),
        P("dp", None),
        P("dp", None),
        P("dp", None),
        P("dp", None),
        P(None, "mod"),
        P("mod"),
        P(("dp", "mod"), None, None),
    )
    out_specs = (
        P(("dp", "mod"), None, None),
        P(("dp", "mod"), None, None),
        P(("dp", "mod"), None),
        P("dp", None),
        P("dp", None),
        P("dp", None),
        P("dp", None),
        P("dp", None),
        P("dp", "mod"),
        P("mod"),
    )
    return jax.shard_map(pick_body(mesh), mesh=mesh, in_specs=in_specs, out_specs=out_specs, check_vma=False)
```

```python
import math
from types import SimpleNamespace
from typing import NamedTuple

import jax
import jax.numpy as jnp
from jax import lax
from jax.experimental import pallas as pl
from jax.experimental.pallas import tpu as pltpu
from jax.sharding import PartitionSpec as P

D = 1152
H = 16
HD = 72
GRID = 16
SEQ = 256
MICRO = 2


EPSILON = 1e-06


def norm_rows(field):
    scale_inv = lax.rsqrt(jnp.mean(field * field, axis=-1, keepdims=True) + EPSILON)
    return (field * scale_inv, scale_inv)


def norm_back(normed, scale_inv, gradient):
    return scale_inv * (gradient - normed * jnp.mean(gradient * normed, axis=-1, keepdims=True))


def embed_steps(timestep):
    half_width = D // 2
    frequency = jnp.exp(-math.log(10000.0) * jnp.arange(half_width, dtype=jnp.float32) / half_width)
    angles = timestep.astype(jnp.float32)[:, None] * frequency[None, :]
    return jnp.concatenate([jnp.cos(angles), jnp.sin(angles)], axis=1)


def rope_tables():
    quarter = HD // 4
    frequency = jnp.exp(-math.log(10000.0) * jnp.arange(quarter, dtype=jnp.float32) / quarter)
    position = jnp.arange(SEQ)
    row_index = (position // GRID).astype(jnp.float32)
    col_index = (position % GRID).astype(jnp.float32)
    angles = jnp.stack(
        [row_index[:, None] * frequency[None, :], col_index[:, None] * frequency[None, :]], axis=1
    )
    return (jnp.cos(angles), jnp.sin(angles))


def rotate(field, cosine_table, sine_table):
    leading = field.shape[:-1]
    quarters = field.reshape(leading + (2, 2, HD // 4))
    first_half = quarters[..., 0, :]
    second_half = quarters[..., 1, :]
    cosine_rows = cosine_table[:, None]
    sine_rows = sine_table[:, None]
    turned_first = first_half * cosine_rows - second_half * sine_rows
    turned_second = first_half * sine_rows + second_half * cosine_rows
    return jnp.stack([turned_first, turned_second], axis=-2).reshape(field.shape)


def pack_rows(arrays, count):
    return jnp.concatenate([array.reshape(count, -1) for array in arrays], axis=1).reshape(-1)


def unpack_rows(flat, shapes, count):
    pieces = []
    offset = 0
    for rows_all, columns in shapes:
        rows = rows_all // count
        pieces.append(flat[offset : offset + rows * columns].reshape(rows, columns))
        offset = offset + rows * columns
    return pieces


def layer_pass(block_in, mod_rows, cotangent, weights, tables):
    qkv_full, proj_full, gate_full, up_full, down_full = weights
    cosine_table, sine_table = tables
    images = block_in.shape[0]
    shift_first, scale_first, gate_first, shift_second, scale_second, gate_second = [
        mod_rows[:, None, number * D : (number + 1) * D] for number in range(6)
    ]
    heads_shape = (images, SEQ, H, HD)
    factor = 1.0 / math.sqrt(HD)
    inputs = block_in.astype(jnp.float32)
    normed_first, inv_first = norm_rows(inputs)
    entry_first = (normed_first * (1.0 + scale_first) + shift_first).astype(jnp.bfloat16)
    projected = jnp.einsum("bsd,de->bse", entry_first, qkv_full, preferred_element_type=jnp.float32)
    q_normed, q_inv = norm_rows(projected[..., :D].reshape(heads_shape))
    k_normed, k_inv = norm_rows(projected[..., D : 2 * D].reshape(heads_shape))
    queries = rotate(q_normed, cosine_table, sine_table).astype(jnp.bfloat16)
    keys_rot = rotate(k_normed, cosine_table, sine_table).astype(jnp.bfloat16)
    values = projected[..., 2 * D :].reshape(heads_shape).astype(jnp.bfloat16)
    scores = (
        jnp.einsum("bqhd,bkhd->bhqk", queries, keys_rot, preferred_element_type=jnp.float32)
        * factor
    )
    highest = jnp.max(scores, axis=-1, keepdims=True)
    log_total = highest + jnp.log(jnp.sum(jnp.exp(scores - highest), axis=-1, keepdims=True))
    weights_soft = jnp.exp(scores - log_total).astype(jnp.bfloat16)
    combined = (
        jnp.einsum("bhqk,bkhd->bqhd", weights_soft, values, preferred_element_type=jnp.float32)
        .reshape(images, SEQ, D)
        .astype(jnp.bfloat16)
    )
    attended = jnp.einsum("bsd,de->bse", combined, proj_full, preferred_element_type=jnp.float32)
    residual = inputs + gate_first * attended
    normed_second, inv_second = norm_rows(residual)
    entry_second = (normed_second * (1.0 + scale_second) + shift_second).astype(jnp.bfloat16)
    gate_proj = jnp.einsum(
        "bsd,df->bsf", entry_second, gate_full, preferred_element_type=jnp.float32
    )
    up_proj = jnp.einsum("bsd,df->bsf", entry_second, up_full, preferred_element_type=jnp.float32)
    sigma_gate = jax.nn.sigmoid(gate_proj)
    activated = gate_proj * sigma_gate
    hidden = (activated * up_proj).astype(jnp.bfloat16)
    branch = jnp.einsum("bsf,fd->bsd", hidden, down_full, preferred_element_type=jnp.float32)
    output = (residual + gate_second * branch).astype(jnp.bfloat16)
    grad_out = cotangent.astype(jnp.float32)
    d_gate_second = jnp.sum(grad_out * branch, axis=1)
    d_branch = (gate_second * grad_out).astype(jnp.bfloat16)
    d_hidden = jnp.einsum("bsd,fd->bsf", d_branch, down_full, preferred_element_type=jnp.float32)
    d_gate_proj = (d_hidden * up_proj * sigma_gate * (1.0 + gate_proj * (1.0 - sigma_gate))).astype(
        jnp.bfloat16
    )
    d_up_proj = (d_hidden * activated).astype(jnp.bfloat16)
    d_entry_second = jnp.einsum(
        "bsf,df->bsd", d_gate_proj, gate_full, preferred_element_type=jnp.float32
    )
    d_entry_second = d_entry_second + jnp.einsum(
        "bsf,df->bsd", d_up_proj, up_full, preferred_element_type=jnp.float32
    )
    d_shift_second = jnp.sum(d_entry_second, axis=1)
    d_scale_second = jnp.sum(d_entry_second * normed_second, axis=1)
    d_residual = grad_out + norm_back(
        normed_second, inv_second, d_entry_second * (1.0 + scale_second)
    )
    d_gate_first = jnp.sum(d_residual * attended, axis=1)
    d_attended = (gate_first * d_residual).astype(jnp.bfloat16)
    d_combined = (
        jnp.einsum("bse,de->bsd", d_attended, proj_full, preferred_element_type=jnp.float32)
        .astype(jnp.bfloat16)
        .reshape(heads_shape)
    )
    scores_again = (
        jnp.einsum("bqhd,bkhd->bhqk", queries, keys_rot, preferred_element_type=jnp.float32)
        * factor
    )
    recomputed = jnp.exp(scores_again - log_total)
    d_weights = jnp.einsum(
        "bqhd,bkhd->bhqk", d_combined, values, preferred_element_type=jnp.float32
    )
    d_scores = (
        recomputed * (d_weights - jnp.sum(recomputed * d_weights, axis=-1, keepdims=True))
    ).astype(jnp.bfloat16)
    d_values = jnp.einsum(
        "bhqk,bqhd->bkhd", weights_soft, d_combined, preferred_element_type=jnp.float32
    ).astype(jnp.bfloat16)
    d_queries = (
        (
            jnp.einsum("bhqk,bkhd->bqhd", d_scores, keys_rot, preferred_element_type=jnp.float32)
            * factor
        )
        .astype(jnp.bfloat16)
        .astype(jnp.float32)
    )
    d_keys = (
        (
            jnp.einsum("bhqk,bqhd->bkhd", d_scores, queries, preferred_element_type=jnp.float32)
            * factor
        )
        .astype(jnp.bfloat16)
        .astype(jnp.float32)
    )
    d_q_raw = norm_back(q_normed, q_inv, rotate(d_queries, cosine_table, -sine_table))
    d_k_raw = norm_back(k_normed, k_inv, rotate(d_keys, cosine_table, -sine_table))
    flat_shape = (images, SEQ, D)
    d_projected = jnp.concatenate(
        [
            d_q_raw.reshape(flat_shape),
            d_k_raw.reshape(flat_shape),
            d_values.astype(jnp.float32).reshape(flat_shape),
        ],
        axis=-1,
    ).astype(jnp.bfloat16)
    d_entry_first = jnp.einsum(
        "bse,de->bsd", d_projected, qkv_full, preferred_element_type=jnp.float32
    )
    d_shift_first = jnp.sum(d_entry_first, axis=1)
    d_scale_first = jnp.sum(d_entry_first * normed_first, axis=1)
    d_tokens = d_residual + norm_back(normed_first, inv_first, d_entry_first * (1.0 + scale_first))
    d_modulation = jnp.concatenate(
        [d_shift_first, d_scale_first, d_gate_first, d_shift_second, d_scale_second, d_gate_second],
        axis=1,
    ).astype(jnp.bfloat16)
    factors = (
        entry_first,
        d_projected,
        combined,
        d_attended,
        entry_second,
        d_gate_proj,
        d_up_proj,
        hidden,
        d_branch,
    )
    return (output, d_tokens, d_modulation, factors)


MESH = pl.DeviceIdType.MESH
WIDTH = 384
LANE_HALF = 2304
FF_HALF = 1536
BF16 = jnp.bfloat16
F32 = jnp.float32


def place():
    dp = lax.axis_index("dp")
    mod = lax.axis_index("mod")
    return dp // 2, dp % 2, mod // 2, mod % 2


def device(z, x, y, c):
    return (z * 2 + x, y * 2 + c)


def greet(peers):
    barrier = pltpu.get_barrier_semaphore()
    for peer in peers:
        pl.semaphore_signal(barrier, inc=1, device_id=peer, device_id_type=MESH)
    pl.semaphore_wait(barrier, len(peers))


def neighbours(z, x, y, c):
    around = [device((z + step) % 4, x, y, c) for step in (1, 2, 3)]
    return around + [device(z, 1 - x, y, c), device(z, x, 1 - y, c), device(z, x, y, 1 - c)]


def send(source, target, send_sem, recv_sem, peer):
    pltpu.make_async_remote_copy(
        src_ref=source,
        dst_ref=target,
        send_sem=send_sem,
        recv_sem=recv_sem,
        device_id=peer,
        device_id_type=MESH,
    ).start()


def drain(window, sem):
    pltpu.make_async_copy(window, window, sem).wait()


class Piece:
    def __init__(self, source, target, row, rows, column, edge):
        self.source, self.target = source, target
        self.row, self.rows, self.column, self.edge = row, rows, column, edge


def gather_pieces(refs, c, edge_of):
    packed, gate, up, down, packed_all, gate_all, up_all, down_all = refs
    pieces = []
    for j in range(6):
        pieces.append(Piece(packed, packed_all, 0, 144, c * LANE_HALF + j * WIDTH, edge_of(144, j)))
    for j in range(4):
        pieces.append(Piece(gate, gate_all, 0, 144, c * FF_HALF + j * WIDTH, edge_of(144, j)))
        pieces.append(Piece(up, up_all, 0, 144, c * FF_HALF + j * WIDTH, edge_of(144, j)))
    for j in range(3):
        pieces.append(Piece(down, down_all, c * 192, 192, j * WIDTH, edge_of(192, j)))
    return pieces


class Gather:
    def __init__(self, refs, sems, spot, stages):
        self.z, self.x, self.y, self.c = spot
        self.stages = stages
        self.pieces = gather_pieces(refs, self.c, lambda rows, j: rows // 3)
        self.send_sems, self.recv_sems, self.own_sems = sems
        self.refs = refs

    def columns(self, piece):
        return pl.ds(pl.multiple_of(piece.column, 128), WIDTH)

    def part(self, piece):
        keep = piece.rows - piece.edge
        return pl.ds(pl.multiple_of(piece.row + self.y * piece.edge, 16), keep), keep

    def mine(self, piece):
        return pl.ds(pl.multiple_of(piece.row + self.y * (piece.rows - piece.edge), 16), piece.edge)

    def own_copies(self):
        for k in range(4):
            pltpu.make_async_copy(self.refs[k], self.stages[k], self.own_sems.at[k]).start()

    def own_stores(self):
        for k in range(4):
            drain(self.stages[k], self.own_sems.at[k])
            pltpu.make_async_copy(
                self.stages[k], self.refs[4 + k].at[self.z, self.x], self.own_sems.at[k]
            ).start()

    def own_done(self):
        for k in range(4):
            drain(self.stages[k], self.own_sems.at[k])

    def start_z(self, t):
        p = self.pieces[t]
        rows, _ = self.part(p)
        here = p.source.at[rows, self.columns(p)]
        there = p.target.at[self.z, self.x, rows, self.columns(p)]
        for step in (1, 3, 2):
            peer = device((self.z + step) % 4, self.x, self.y, self.c)
            send(here, there, self.send_sems.at[0, t], self.recv_sems.at[0, t], peer)
        peer = device(self.z, 1 - self.x, self.y, self.c)
        send(here, there, self.send_sems.at[1, t], self.recv_sems.at[1, t], peer)

    def start_x(self, t):
        p = self.pieces[t]
        rows, keep = self.part(p)
        columns = self.columns(p)
        drain(p.target.at[pl.ds(0, 3), 0, pl.ds(0, keep), pl.ds(0, WIDTH)], self.recv_sems.at[0, t])
        x_peer = device(self.z, 1 - self.x, self.y, self.c)
        y_peer = device(self.z, self.x, 1 - self.y, self.c)
        for step in (1, 3, 2):
            other = (self.z + step) % 4
            block = p.target.at[other, self.x, rows, columns]
            send(block, block, self.send_sems.at[1, t], self.recv_sems.at[1, t], x_peer)
        for step in (1, 3, 2):
            other = (self.z + step) % 4
            block = p.target.at[other, self.x, self.mine(p), columns]
            send(block, block, self.send_sems.at[2, t], self.recv_sems.at[2, t], y_peer)

    def start_y(self, t):
        p = self.pieces[t]
        _, keep = self.part(p)
        columns = self.columns(p)
        drain(p.target.at[:, 0, pl.ds(0, keep), pl.ds(0, WIDTH)], self.recv_sems.at[1, t])
        y_peer = device(self.z, self.x, 1 - self.y, self.c)
        block = p.target.at[:, 1 - self.x, self.mine(p), columns]
        send(block, block, self.send_sems.at[2, t], self.recv_sems.at[2, t], y_peer)

    def start_c(self, t):
        p = self.pieces[t]
        columns = self.columns(p)
        half = pl.ds(pl.multiple_of(p.row, 16), p.rows)
        self.drain_seven(p.edge, self.recv_sems.at[2, t])
        peer = device(self.z, self.x, self.y, 1 - self.c)
        block = p.target.at[:, 1 - self.x, half, columns]
        send(block, block, self.send_sems.at[3, t], self.recv_sems.at[3, t], peer)
        for step in (1, 2, 3):
            block = p.target.at[(self.z + step) % 4, self.x, half, columns]
            send(block, block, self.send_sems.at[3, t], self.recv_sems.at[3, t], peer)

    def arrived(self, t):
        self.drain_seven(self.pieces[t].rows, self.recv_sems.at[3, t])

    def drain_seven(self, rows, sem):
        high = 96 if rows > 144 else rows
        drain(self.refs[4].at[pl.ds(0, rows // high), 0, pl.ds(0, high), pl.ds(0, 7 * WIDTH)], sem)

    def sent_z(self, t):
        p = self.pieces[t]
        _, keep = self.part(p)
        drain(p.target.at[pl.ds(0, 3), 0, pl.ds(0, keep), pl.ds(0, WIDTH)], self.send_sems.at[0, t])

    def sent_rest(self, t):
        p = self.pieces[t]
        _, keep = self.part(p)
        drain(p.target.at[:, 0, pl.ds(0, keep), pl.ds(0, WIDTH)], self.send_sems.at[1, t])
        for stage, rows in ((2, p.edge), (3, p.rows)):
            self.drain_seven(rows, self.send_sems.at[stage, t])


N_PIECES = 17


TOK = 512
TILE = 64
ATTN_STEPS = 8


def mm(left, right):
    return lax.dot_general(left, right, (((1,), (0,)), ((), ())), preferred_element_type=F32)


def mm_nt(left, right):
    return lax.dot_general(left, right, (((1,), (1,)), ((), ())), preferred_element_type=F32)


def mm_tn(left, right):
    return lax.dot_general(left, right, (((0,), (0,)), ((), ())), preferred_element_type=F32)


def split(value):
    high = value.astype(BF16)
    return high, (value - high.astype(F32)).astype(BF16)


def mm_split(value, right):
    high, low = split(value)
    return mm(high, right) + mm(low, right)


def partner(value, first):
    width = value.shape[1]
    return jnp.where(first, pltpu.roll(value, width - 18, 1), pltpu.roll(value, 18, 1))


def first_lanes(rows):
    return lax.broadcasted_iota(jnp.int32, (rows, D), 1) % 36 < 18


def rows_of(block, count):
    return pl.ds(pl.multiple_of(block * count, count), count)


def head_window(head):
    base = jnp.minimum(head * HD // 128 * 128, D - 256)
    offset = head * HD - base
    lane = lax.broadcasted_iota(jnp.int32, (SEQ, 256), 1)
    mask = (lane >= offset) & (lane < offset + HD)
    return pl.ds(pl.multiple_of(base, 128), 256), mask


def flat(ref_value):
    return ref_value.reshape(-1, ref_value.shape[-1])


class Saves:
    def __init__(self, sems):
        self.sems, self.count, self.open = sems, 0, []

    def local(self, source, target):
        copy = pltpu.make_async_copy(source, target, self.sems.at[self.count])
        self.count += 1
        copy.start()
        self.open.append(copy)
        return copy

    def done(self, copy):
        copy.wait()
        self.open = [other for other in self.open if other is not copy]

    def finish(self):
        for copy in self.open:
            copy.wait()


class Forward:
    def __init__(self, s, spot, gather):
        self.s, self.gather = s, gather
        self.z, self.x, self.y, self.c = spot
        self.saves = Saves(s.save_sems)
        self.pending = {}
        self.remote = []
        self.slots = {}


    def to_sibling(self, source, target):
        k = len(self.remote)
        peer = device(self.z, self.x, self.y, 1 - self.c)
        copy = pltpu.make_async_remote_copy(
            src_ref=source,
            dst_ref=target,
            send_sem=self.s.pair_send.at[k],
            recv_sem=self.s.pair_recv.at[k],
            device_id=peer,
            device_id_type=MESH,
        )
        copy.start()
        self.remote.append(copy)


    def load(self, key, part, source, target):
        if (key, part) not in self.pending:
            copy = pltpu.make_async_copy(source, target, self.s.load_sems.at[len(self.pending)])
            copy.start()
            self.pending[key, part] = copy

    def window(self, ref, column):
        return ref.at[:, :, :, pl.ds(column, WIDTH)]

    def load_qv(self, j):
        packed = self.gather.refs[4]
        self.load(j, 0, self.window(packed, j * WIDTH), self.s.w.at[j % 2, 0])
        self.load(j, 1, self.window(packed, LANE_HALF + j * WIDTH), self.s.w.at[j % 2, 1])

    def load_ko(self, j):
        packed = self.gather.refs[4]
        self.load(j, 0, self.window(packed, j * WIDTH), self.s.w.at[j % 2, 0])
        target = self.window(self.s.w_out, (j - 3) * WIDTH)
        self.load(j, 1, self.window(packed, LANE_HALF + j * WIDTH), target)

    def load_ff(self, j):
        at = (j // 2 + 4 * (j % 2)) * WIDTH
        self.load(6 + j, 0, self.window(self.gather.refs[5], at), self.s.w.at[j % 2, 0])
        self.load(6 + j, 1, self.window(self.gather.refs[6], at), self.s.w.at[j % 2, 1])

    def load_down(self, j):
        self.load(14 + j, 0, self.window(self.gather.refs[7], j * WIDTH), self.s.w_down.at[j % 2])

    def loaded(self, load, j, key):
        load(j)
        for part in range(2):
            if (key, part) in self.pending:
                self.pending[key, part].wait()


    def enter(self):
        s = self.s

        @pl.loop(0, TOK // TILE)
        def _(i):
            rows = rows_of(i, TILE)
            image = i // (SEQ // TILE)
            mod = s.mod
            normed, _ = norm_rows(s.tokens[rows, :].astype(F32))
            entry = normed * (1.0 + mod[image, 1:2, :]) + mod[image, 0:1, :]
            s.entry_a[rows, :] = entry.astype(BF16)
            branch = mod[image, 5:6, :] * s.cot[rows, :].astype(F32)
            s.d_branch[rows, :] = branch.astype(BF16)

        self.saves.local(s.d_branch, s.o_branch.at[pl.ds(0, TOK)])
        self.to_sibling(s.d_branch, s.o_branch.at[pl.ds(TOK, TOK)])
        self.turn(s.entry_a, s.t_a)
        self.share(s.t_a, s.o_lhs.at[0])

    def turn(self, source, target):
        @pl.loop(0, source.shape[1] // 128)
        def _(i):
            columns = rows_of(i, 128)
            target[columns, :] = source[:, columns].T

    def share(self, source, target):
        self.saves.local(source, target.at[:, pl.ds(0, TOK)])
        self.to_sibling(source, target.at[:, pl.ds(TOK, TOK)])

    def qv(self, j):
        s = self.s
        self.loaded(self.load_qv, j, j)
        columns = pl.ds(j * WIDTH, WIDTH)
        s.proj[:, columns] = mm(s.entry_a[...], flat(s.w[j % 2, 0]))
        s.v[:, columns] = mm(s.entry_a[...], flat(s.w[j % 2, 1])).astype(BF16)
        if j == 2:
            self.saves.local(s.v, s.o_qkv.at[2])

    def ko(self, j):
        s = self.s
        self.loaded(self.load_ko, j, j)
        columns = pl.ds((j - 3) * WIDTH, WIDTH)
        s.proj[:, columns] = mm(s.entry_a[...], flat(s.w[j % 2, 0]))

    def head_norm(self, which):
        s = self.s
        target, normed = (s.q, s.q_normed) if which == 0 else (s.k, s.k_normed)
        scale = s.scale_q if which == 0 else s.scale_k

        @pl.loop(0, TOK // TILE)
        def _(i):
            rows = rows_of(i, TILE)
            spots = rows_of(i % (SEQ // TILE), TILE)
            field = s.proj[rows, :]
            inverse = lax.rsqrt(mm_split(field * field, s.spread[...]) * (1.0 / HD) + EPSILON)
            scale[rows, :] = inverse
            field = field * mm_split(inverse, s.widen[...])
            normed[rows, :] = field.astype(BF16)
            turned = field * s.cos[spots, :] + partner(field, first_lanes(TILE)) * s.sin[spots, :]
            target[rows, :] = turned.astype(BF16)

        self.saves.local(target, s.o_qkv.at[which])
        self.saves.local(normed, s.o_normed.at[which])
        self.saves.local(scale, s.o_scale.at[which])

    def attend(self, k):
        s = self.s
        heads = H // ATTN_STEPS
        if k >= 2:
            self.saves.done(self.slots[k - 2])

        @pl.loop(0, heads)
        def _(i):
            window, mask = head_window(k * heads + i)
            for image in range(2):
                rows = pl.ds(image * SEQ, SEQ)
                query = jnp.where(mask, s.q[rows, window].astype(F32), 0.0).astype(BF16)
                scores = mm_nt(query, s.k[rows, window]) * (1.0 / math.sqrt(HD))
                powers = jnp.exp(scores - jnp.max(scores, axis=1, keepdims=True))
                total = jnp.sum(powers, axis=1, keepdims=True)
                soft = (powers * (1.0 / total)).astype(BF16)
                s.soft[k % 2, i, image] = soft
                mixed = mm(soft, s.v[rows, window])
                old = s.combined[rows, window].astype(F32)
                s.combined[rows, window] = jnp.where(mask, mixed, old).astype(BF16)

        self.slots[k] = self.saves.local(s.soft.at[k % 2], s.o_soft.at[pl.ds(k * heads, heads)])

    def leave(self):
        s = self.s
        self.saves.done(self.slots[ATTN_STEPS - 2])
        self.saves.done(self.slots[ATTN_STEPS - 1])
        self.turn(s.combined, s.t_c)
        self.share(s.t_c, s.o_lhs.at[1])
        for j in range(3):
            columns = pl.ds(j * WIDTH, WIDTH)
            s.proj[:, columns] = mm(s.combined[...], flat(s.w_out[:, :, :, columns]))

        @pl.loop(0, TOK // TILE)
        def _(i):
            rows = rows_of(i, TILE)
            image = i // (SEQ // TILE)
            mod = s.mod
            attended = s.proj[rows, :]
            s.attended[rows, :] = attended.astype(BF16)
            residual = s.tokens[rows, :].astype(F32) + mod[image, 2:3, :] * attended
            s.residual[rows, :] = residual
            normed, _ = norm_rows(residual)
            entry = normed * (1.0 + mod[image, 4:5, :]) + mod[image, 3:4, :]
            s.entry_b[rows, :] = entry.astype(BF16)

        self.saves.local(s.attended, s.o_attended)
        self.saves.local(s.residual, s.o_residual)
        self.turn(s.entry_b, s.t_b)
        self.share(s.t_b, s.o_lhs.at[2])

    def ff(self, j):
        s = self.s
        self.loaded(self.load_ff, j, 6 + j)
        shard = j // 2 + 4 * (j % 2)
        at = shard * WIDTH
        columns = pl.ds(at, WIDTH)
        s.wide[0] = mm(s.entry_b[...], flat(s.w[j % 2, 0]))
        s.wide[1] = mm(s.entry_b[...], flat(s.w[j % 2, 1]))
        if (6, j - 2) in self.slots:
            for copy in self.slots[(6, j - 2)]:
                self.saves.done(copy)
        slot = j % 2

        @pl.loop(0, TOK // TILE)
        def _(i):
            rows = rows_of(i, TILE)
            gate = s.wide[0, rows, :]
            up = s.wide[1, rows, :]
            sigma = 1.0 / (1.0 + jnp.exp(-gate))
            active = gate * sigma
            s.active[slot, 0, rows, :] = active.astype(BF16)
            slope = up * sigma * (1.0 + gate * (1.0 - sigma))
            s.active[slot, 1, rows, :] = slope.astype(BF16)
            s.hidden[rows, columns] = (active * up).astype(BF16)

        self.slots[(6, j)] = [
            self.saves.local(s.active.at[slot], s.o_active.at[shard]),
        ]
        for i in range(3):
            s.t_h[shard, 128 * i : 128 * i + 128, :] = s.hidden[:, at + 128 * i : at + 128 * i + 128].T
        mine = pl.ds(pl.multiple_of(self.c * 192, 16), 192)
        theirs = pl.ds(pl.multiple_of((1 - self.c) * 192, 16), 192)
        self.saves.local(s.t_h.at[shard, mine], s.o_hidden.at[shard, :, pl.ds(0, TOK)])
        self.to_sibling(s.t_h.at[shard, theirs], s.o_hidden.at[shard, :, pl.ds(TOK, TOK)])

    def down(self, j):
        s = self.s
        self.loaded(self.load_down, j, 14 + j)
        columns = pl.ds(j * WIDTH, WIDTH)
        s.wide[0] = mm(s.hidden[...], flat(s.w_down[j % 2]))
        for image in range(2):
            gate = s.mod[image, 5:6, columns]
            total = jnp.zeros((1, WIDTH), F32)
            for i in range(SEQ // TILE):
                rows = pl.ds(image * SEQ + i * TILE, TILE)
                branch = s.wide[0, rows, :]
                result = s.residual[rows, columns] + gate * branch
                s.result[rows, columns] = result.astype(BF16)
                total = total + jnp.sum(
                    s.cot[rows, columns].astype(F32) * branch, axis=0, keepdims=True
                )
            s.o_gate_b[image, 0:1, columns] = total
        if j == 2:
            self.saves.local(s.result, s.o_result)

    def plan(self):
        steps = [(None, self.enter, None, 0, 4)]
        steps += [(self.load_qv, self.qv, j, j + 1, 2.5) for j in range(3)]
        steps += [(None, self.head_norm, 0, 3, 8)]
        steps += [(self.load_ko, self.ko, j, j + 1, 1.5) for j in range(3, 6)]
        steps += [(None, self.head_norm, 1, 6, 8)]
        steps += [(None, self.attend, k, 6, 3) for k in range(ATTN_STEPS)]
        steps += [(None, self.leave, None, 6, 8)]
        steps += [(self.load_ff, self.ff, j, 8 + 2 * (j // 2), 4.5) for j in range(8)]
        steps += [(self.load_down, self.down, j, 15 + j, 4) for j in range(3)]
        return steps

    def finish(self):
        self.saves.finish()
        for copy in self.remote:
            copy.wait_send()
            copy.wait_recv()


class ForwardInputs(NamedTuple):
    packed: object
    gate: object
    up: object
    down: object
    tokens: object
    cot: object
    mod: object
    cos: object
    sin: object
    spread: object
    widen: object


FORWARD_OUTPUTS = dict(
    packed_all=((4, 2, 144, 4608), BF16),
    gate_all=((4, 2, 144, 3072), BF16),
    up_all=((4, 2, 144, 3072), BF16),
    down_all=((4, 2, 384, 1152), BF16),
    o_branch=((2 * TOK, D), BF16),
    o_lhs=((3, D, 2 * TOK), BF16),
    o_hidden=((8, 192, 2 * TOK), BF16),
    o_qkv=((3, TOK, D), BF16),
    o_normed=((2, TOK, D), BF16),
    o_scale=((2, TOK, 128), F32),
    o_soft=((H, 2, SEQ, SEQ), BF16),
    o_attended=((TOK, D), BF16),
    o_residual=((TOK, D), F32),
    o_active=((8, 2, TOK, WIDTH), BF16),
    o_result=((TOK, D), BF16),
    o_gate_b=((2, 8, D), F32),
)


def forward_scratch():
    def vmem(*shape, kind=BF16):
        return pltpu.VMEM(shape, kind)

    return dict(
        entry_a=vmem(TOK, D),
        d_branch=vmem(TOK, D),
        t_a=vmem(D, TOK),
        proj=vmem(TOK, D, kind=F32),
        q=vmem(TOK, D),
        k=vmem(TOK, D),
        v=vmem(TOK, D),
        q_normed=vmem(TOK, D),
        k_normed=vmem(TOK, D),
        scale_q=vmem(TOK, 128, kind=F32),
        scale_k=vmem(TOK, 128, kind=F32),
        soft=vmem(2, H // ATTN_STEPS, 2, SEQ, SEQ),
        combined=vmem(TOK, D),
        t_c=vmem(D, TOK),
        attended=vmem(TOK, D),
        residual=vmem(TOK, D, kind=F32),
        entry_b=vmem(TOK, D),
        t_b=vmem(D, TOK),
        wide=vmem(2, TOK, WIDTH, kind=F32),
        active=vmem(2, 2, TOK, WIDTH),
        hidden=vmem(TOK, 8 * WIDTH),
        t_h=vmem(8, WIDTH, TOK),
        result=vmem(TOK, D),
        w=vmem(2, 2, 4, 2, 144, WIDTH),
        w_out=vmem(4, 2, 144, D),
        w_down=vmem(2, 4, 2, 384, WIDTH),
        gather_send=pltpu.SemaphoreType.DMA((4, N_PIECES)),
        gather_recv=pltpu.SemaphoreType.DMA((4, N_PIECES)),
        own_packed=vmem(144, 4 * D),
        own_gate=vmem(144, 8 * WIDTH),
        own_up=vmem(144, 8 * WIDTH),
        own_down=vmem(384, D),
        own_sems=pltpu.SemaphoreType.DMA((4,)),
        save_sems=pltpu.SemaphoreType.DMA((48,)),
        load_sems=pltpu.SemaphoreType.DMA((48,)),
        pair_send=pltpu.SemaphoreType.DMA((16,)),
        pair_recv=pltpu.SemaphoreType.DMA((16,)),
    )


def run_step(steps, arrived):
    _, act, j, _, cost = steps.pop(0)
    if steps and steps[0][0] is not None and steps[0][3] <= arrived:
        steps[0][0](steps[0][2])
    act() if j is None else act(j)
    return cost


def forward_kernel(*refs):
    names = ForwardInputs._fields + tuple(FORWARD_OUTPUTS) + tuple(forward_scratch())
    s = SimpleNamespace(**dict(zip(names, refs, strict=True)))
    spot = place()
    greet(neighbours(*spot))
    arrays = [s.packed, s.gate, s.up, s.down, s.packed_all, s.gate_all, s.up_all, s.down_all]
    stages = [s.own_packed, s.own_gate, s.own_up, s.own_down]
    gather = Gather(arrays, (s.gather_send, s.gather_recv, s.own_sems), spot, stages)
    work = Forward(s, spot, gather)
    steps = work.plan()
    gather.own_copies()
    ahead = 2
    arrived = 0
    for t in range(N_PIECES + 4 + ahead):
        if t == 1:
            gather.own_stores()
        if t < N_PIECES:
            if t >= ahead:
                gather.sent_z(t - ahead)
            gather.start_z(t)
        if 0 <= t - ahead < N_PIECES:
            gather.start_x(t - ahead)
        if 0 <= t - ahead - 1 < N_PIECES:
            gather.start_y(t - ahead - 1)
        if 0 <= t - ahead - 2 < N_PIECES:
            gather.start_c(t - ahead - 2)
        if 0 <= t - ahead - 3 < N_PIECES:
            if arrived == 0:
                gather.own_done()
            gather.arrived(t - ahead - 3)
            arrived += 1
        spent = 0.0
        while steps and steps[0][3] <= arrived and spent < 6.0:
            spent += run_step(steps, arrived)
    while steps:
        run_step(steps, arrived)
    for t in range(N_PIECES - ahead, N_PIECES):
        gather.sent_z(t)
    for t in range(N_PIECES):
        gather.sent_rest(t)
    work.finish()


def forward_pass(packed, gate, up, down, tokens, cotangent, mod, tables):
    hbm = pl.BlockSpec(memory_space=pl.ANY)
    vmem = pl.BlockSpec(memory_space=pltpu.VMEM)
    out = pl.pallas_call(
        forward_kernel,
        out_shape=[jax.ShapeDtypeStruct(*spec) for spec in FORWARD_OUTPUTS.values()],
        in_specs=[hbm] * 4 + [vmem] * 7,
        out_specs=[hbm] * 15 + [vmem],
        scratch_shapes=list(forward_scratch().values()),
        name="forward_pass",
        compiler_params=pltpu.CompilerParams(
            collective_id=0, has_side_effects=True, vmem_limit_bytes=60 << 20
        ),
    )(packed, gate, up, down, tokens, cotangent, mod, *tables)
    return SimpleNamespace(**dict(zip(FORWARD_OUTPUTS, out)))


def head_tables():
    cosine, sine = rope_tables()

    def lanes(table, signed):
        first = -table if signed else table
        return jnp.tile(jnp.stack([first, table], axis=2).reshape(SEQ, HD), (1, H))

    head = jnp.arange(D) // HD
    spread = (head[:, None] == jnp.arange(128)[None, :]).astype(BF16)
    return lanes(cosine, False), lanes(sine, True), spread, spread.T


SCATTER_ROWS = (144,) * 14 + (192,) * 3
SCATTER_EDGE = tuple((32, 48)[j % 2] for j in range(14)) + (48,) * 3
ORDER = (14, 15, 16) + tuple(range(6, 14)) + tuple(range(6))


class Reduce:
    def __init__(self, s, spot):
        self.s = s
        self.z, self.x, self.y, self.c = spot
        self.stage = {}
        self.open = []

    def shape(self, t):
        return SCATTER_ROWS[t], SCATTER_EDGE[t]

    def part(self, t):
        rows, edge = self.shape(t)
        return pl.ds(pl.multiple_of(self.y * edge, 16), rows - edge)

    def held(self, t):
        s = self.s
        return s.held_big.at[t - 14] if t >= 14 else s.held.at[t if t < 6 else t - 6]

    def pick(self, small, big, t):
        return big.at[t - 14] if t >= 14 else small.at[t]

    def got_y(self, t):
        return self.pick(self.s.got_y, self.s.got_y_big, t)

    def got_x(self, t):
        return self.pick(self.s.got_x, self.s.got_x_big, t)

    def got_z(self, t):
        return self.pick(self.s.got_z, self.s.got_z_big, t)

    def got_f(self, t):
        return self.pick(self.s.got_f, self.s.got_f_big, t)

    def sems(self, stage, t):
        return self.s.scatter_send.at[stage, t], self.s.scatter_recv.at[stage, t]

    def produced(self, t):
        self.stage[t] = -1
        self.ask()

    def ask(self):
        entered = sum(stage > 0 for stage in self.stage.values())
        for t in ORDER[: entered + 3]:
            if self.stage.get(t) == -1:
                self.stage[t] = 0
                self.start_y(t)

    def advance(self):
        stages = (self.start_x, self.start_z, self.start_f, self.start_c)
        under_way = [t for t in ORDER if 0 < self.stage.get(t, 4) < 4]
        waiting = [t for t in ORDER if self.stage.get(t) == 0]
        for t in under_way + waiting[:1]:
            stages[self.stage[t]](t)
            self.stage[t] += 1
        self.ask()

    def free(self, t):
        while self.stage[t] < 4:
            self.advance()
        if t in self.open:
            self.sent(t)

    def start_y(self, t):
        rows, edge = self.shape(t)
        theirs = pl.ds(pl.multiple_of((1 - self.y) * (rows - edge), 16), edge)
        send(
            self.held(t).at[:, :, theirs, :],
            self.got_y(t).at[:, :, pl.ds(0, edge), :],
            *self.sems(0, t),
            device(self.z, self.x, 1 - self.y, self.c),
        )

    def start_x(self, t):
        rows, edge = self.shape(t)
        held, got = self.held(t), self.got_y(t)
        drain(got.at[:, :, pl.ds(0, edge), :], self.s.scatter_recv.at[0, t])
        mine = pl.ds(pl.multiple_of(self.y * (rows - edge), 16), edge)

        @pl.loop(0, 4)
        def _(k):
            for x in range(2):
                total = held[k, x, mine, :].astype(F32) + got[k, x, pl.ds(0, edge), :].astype(F32)
                held[k, x, mine, :] = total.astype(BF16)

        send(
            held.at[:, 1 - self.x, self.part(t), :],
            self.got_x(t).at[:, pl.ds(0, rows - edge), :],
            *self.sems(1, t),
            device(self.z, 1 - self.x, self.y, self.c),
        )

    def start_z(self, t):
        rows, edge = self.shape(t)
        held, got = self.held(t), self.got_x(t)
        keep = rows - edge
        drain(got.at[:, pl.ds(0, keep), :], self.s.scatter_recv.at[1, t])
        part = self.part(t)

        @pl.loop(0, 4)
        def _(k):
            total = held[k, self.x, part, :].astype(F32) + got[k, pl.ds(0, keep), :].astype(F32)
            held[k, self.x, part, :] = total.astype(BF16)

        for step in (1, 3, 2):
            other = (self.z + step) % 4
            send(
                held.at[other, self.x, part, :],
                self.got_z(t).at[step - 1, pl.ds(0, keep), :],
                *self.sems(2, t),
                device(other, self.x, self.y, self.c),
            )

    def start_f(self, t):
        rows, edge = self.shape(t)
        held, got = self.held(t), self.got_z(t)
        keep = rows - edge
        drain(got.at[:, pl.ds(0, keep), :], self.s.scatter_recv.at[2, t])
        part = self.part(t)
        total = held[self.z, self.x, part, :].astype(F32)
        for k in range(3):
            total = total + got[k, pl.ds(0, keep), :].astype(F32)
        held[self.z, self.x, part, :] = total.astype(BF16)
        send(
            held.at[self.z, self.x, part, :],
            self.got_f(t).at[pl.ds(0, keep), :],
            *self.sems(3, t),
            device(self.z, self.x, 1 - self.y, self.c),
        )

    def target(self, t):
        s = self.s
        if t < 6:
            columns = pl.ds(pl.multiple_of(self.c * LANE_HALF + t * WIDTH, 128), WIDTH)
            return s.g_packed.at[:, columns]
        if t < 14:
            columns = pl.ds(pl.multiple_of(self.c * FF_HALF + (t - 6) // 2 * WIDTH, 128), WIDTH)
            return (s.g_gate, s.g_up)[(t - 6) % 2].at[:, columns]
        rows = pl.ds(pl.multiple_of(self.c * 192, 16), 192)
        return s.g_down.at[rows, pl.ds((t - 14) * WIDTH, WIDTH)]

    def start_c(self, t):
        rows, edge = self.shape(t)
        held, got = self.held(t), self.got_f(t)
        y, keep, both = self.y, rows - edge, rows - 2 * edge
        drain(got.at[pl.ds(0, keep), :], self.s.scatter_recv.at[3, t])
        drain(self.got_y(t).at[:, :, pl.ds(0, edge), :], self.s.scatter_send.at[0, t])
        drain(self.got_x(t).at[:, pl.ds(0, keep), :], self.s.scatter_send.at[1, t])
        mid, fin = held.at[self.z, self.x], held.at[self.z, 1 - self.x]

        def at(offset, count):
            return pl.ds(pl.multiple_of(offset, 16), count)

        own, other = at(y * keep, edge), at((1 - y) * keep, edge)
        fin[own, :] = mid[own, :]
        fin[other, :] = got[at((1 - y) * both, edge), :]
        total = mid[pl.ds(edge, both), :].astype(F32) + got[at(y * edge, both), :].astype(F32)
        fin[pl.ds(edge, both), :] = total.astype(BF16)
        target = self.target(t)
        send(fin, target, *self.sems(4, t), device(self.z, self.x, y, 1 - self.c))
        pltpu.make_async_copy(fin, target, self.s.store_sems.at[t]).start()
        self.open.append(t)

    def sent(self, t):
        self.open.remove(t)
        rows, edge = self.shape(t)
        sems = self.s.scatter_send
        drain(self.got_z(t).at[:, pl.ds(0, rows - edge), :], sems.at[2, t])
        drain(self.got_f(t).at[pl.ds(0, rows - edge), :], sems.at[3, t])
        drain(self.target(t), sems.at[4, t])
        drain(self.target(t), self.s.store_sems.at[t])

    def finish(self):
        for t in ORDER:
            self.free(t)
        for t in range(N_PIECES):
            drain(self.target(t), self.s.scatter_recv.at[4, t])


class Backward:
    def __init__(self, s, spot, reduce):
        self.s, self.reduce = s, reduce
        self.z, self.x, self.y, self.c = spot
        self.pending = {}
        self.remote = {}
        self.copies = 0

    def load(self, key, source, target):
        if key not in self.pending:
            copy = pltpu.make_async_copy(source, target, self.s.load_sems.at[self.copies])
            self.copies += 1
            copy.start()
            self.pending[key] = copy

    def wait(self, *keys):
        for key in keys:
            self.pending.pop(key).wait()

    def to_sibling(self, key, source, target):
        k = len(self.remote)
        copy = pltpu.make_async_remote_copy(
            src_ref=source,
            dst_ref=target,
            send_sem=self.s.pair_send.at[k],
            recv_sem=self.s.pair_recv.at[k],
            device_id=device(self.z, self.x, self.y, 1 - self.c),
            device_id_type=MESH,
        )
        copy.start()
        self.remote[key] = copy


    def grad_down(self, hidden, branch):
        s, reduce = self.s, self.reduce

        @pl.loop(0, 4)
        def _(k):
            left = hidden[pl.ds(2 * k, 2)].reshape(384, 2 * TOK)
            total = mm(left, branch[...]).astype(BF16)
            for j in range(3):
                block = total[:, j * WIDTH : (j + 1) * WIDTH]
                s.held_big[j, k] = block.reshape(2, 192, WIDTH)

        for t in (14, 15, 16):
            reduce.produced(t)

    def column(self, w):
        half = (1 - self.c) if w % 2 == 0 else self.c
        return half * 4 + w // 2

    def load_ff(self, f, w):
        s = self.s
        window = self.column(w)
        columns = pl.ds(pl.multiple_of(window * WIDTH, 128), WIDTH)
        slot = w % 2
        self.load((1, w), s.down_all.at[window // 2, window % 2], f.w_down.at[slot])
        self.load((2, w), s.gate_all.at[:, :, :, columns], s.w.at[slot, :, :, :, pl.ds(0, WIDTH)])
        self.load((3, w), s.up_all.at[:, :, :, columns], s.w.at[slot, :, :, :, pl.ds(WIDTH, WIDTH)])
        self.load((4, w), s.o_active.at[window], f.active.at[slot])

    def ff(self, f, w):
        s = self.s
        slot = w % 2
        self.load_ff(f, w)
        self.wait((1, w), (2, w), (3, w), (4, w))
        if w < 7:
            self.load_ff(f, w + 1)
        f.wide[...] = mm_nt(f.branch[pl.ds(0, TOK), :], f.w_down[slot])
        if w >= 2:
            if slot == 0:
                self.remote[5, w - 2].wait_send()
            else:
                self.wait((5, w - 2))
        steep = f.steep.at[slot]

        @pl.loop(0, TOK // TILE)
        def _(i):
            rows = rows_of(i, TILE)
            back = f.wide[rows, :]
            steep[rows, 0:WIDTH] = (back * f.active[slot, 1, rows, :].astype(F32)).astype(BF16)
            steep[rows, WIDTH : 2 * WIDTH] = (
                back * f.active[slot, 0, rows, :].astype(F32)
            ).astype(BF16)

        j = w // 2
        if slot == 0:
            self.to_sibling((5, w), steep, s.r_ff.at[j, pl.ds(TOK, TOK)])
        else:
            self.load((5, w), steep, s.r_ff.at[j, pl.ds(0, TOK)])
        product = mm_nt(steep[...], flat(s.w[slot]))
        if w == 0:
            s.acc[...] = product
        else:
            s.acc[...] += product

    def load_grad_ff(self, j):
        s = self.s
        self.remote[5, 2 * j].wait_recv()
        if (5, 2 * j + 1) in self.pending:
            self.wait((5, 2 * j + 1))
        self.load((6, j), s.r_ff.at[j], s.right.at[j % 2])

    def grad_ff(self, j):
        s = self.s
        self.wait((6, j))
        right = s.right.at[j % 2]

        @pl.loop(0, 4)
        def _(k):
            left = s.left[pl.ds(pl.multiple_of(k * 288, 32), 288), :]
            total = mm(left, right[...]).astype(BF16)
            for half in range(2):
                block = total[:, half * WIDTH : (half + 1) * WIDTH]
                s.held[2 * j + half, k] = block.reshape(2, 144, WIDTH)

        self.reduce.produced(6 + 2 * j)
        self.reduce.produced(7 + 2 * j)

    def feed_forward(self, f):
        s, reduce = self.s, self.reduce
        self.wait(11, 12)
        self.load((7, 0), s.o_lhs.at[2], s.left)
        self.grad_down(f.hidden, f.branch)
        for w in range(8):
            self.ff(f, w)
            if w == 0:
                self.wait((7, 0))
            if w % 2 == 1:
                reduce.advance()
                if w >= 3:
                    self.load_grad_ff(w // 2 - 1)
            elif w >= 4:
                self.grad_ff(w // 2 - 2)
        self.load_grad_ff(3)
        self.grad_ff(2)
        reduce.advance()
        self.grad_ff(3)
        self.remote[5, 6].wait_send()


    def middle(self, f):
        s = self.s
        self.load(21, s.cot, f.cot)
        self.load(22, s.o_residual, s.d_residual)
        self.load(23, s.o_attended, f.attended)
        self.wait(21, 22, 23)
        s.d_mod[...] = jnp.zeros_like(s.d_mod)

        @pl.loop(0, TOK // TILE)
        def _(i):
            rows = rows_of(i, TILE)
            image = i // (SEQ // TILE)
            mod, d_mod = s.mod, s.d_mod
            normed, inverse = norm_rows(s.d_residual[rows, :])
            d_entry = s.acc[rows, :]
            d_mod[image, 3:4, :] += jnp.sum(d_entry, axis=0, keepdims=True)
            d_mod[image, 4:5, :] += jnp.sum(d_entry * normed, axis=0, keepdims=True)
            back = norm_back(normed, inverse, d_entry * (1.0 + mod[image, 4:5, :]))
            d_residual = f.cot[rows, :].astype(F32) + back
            s.d_residual[rows, :] = d_residual
            attended = f.attended[rows, :].astype(F32)
            d_mod[image, 2:3, :] += jnp.sum(d_residual * attended, axis=0, keepdims=True)
            s.joined[rows, 3 * D : 4 * D] = (mod[image, 2:3, :] * d_residual).astype(BF16)


    def load_soft(self, f, k):
        heads = H // ATTN_STEPS
        self.load((31, k), self.s.o_soft.at[pl.ds(k * heads, heads)], f.soft.at[k % 2])

    def attend(self, f, k):
        s = self.s
        heads = H // ATTN_STEPS
        self.load_soft(f, k)
        self.wait((31, k))
        if k + 1 < ATTN_STEPS:
            self.load_soft(f, k + 1)
        factor = 1.0 / math.sqrt(HD)

        @pl.loop(0, heads)
        def _(i):
            head = k * heads + i
            window, mask = head_window(head)
            base = jnp.minimum(head * HD // 128 * 128, D - 256)
            for image in range(2):
                rows = pl.ds(image * SEQ, SEQ)
                back = jnp.where(mask, f.back[rows, window].astype(F32), 0.0).astype(BF16)
                soft = f.soft[k % 2, i, image]
                d_soft = mm_nt(back, f.qkv[2, rows, window])
                wide = soft.astype(F32)
                d_scores = (
                    wide * (d_soft - jnp.sum(wide * d_soft, axis=1, keepdims=True))
                ).astype(BF16)
                results = (
                    mm(d_scores, f.qkv[1, rows, window]) * factor,
                    mm_tn(d_scores, f.qkv[0, rows, window]) * factor,
                    mm_tn(soft, back),
                )
                for part, result in enumerate(results):
                    place_at = pl.ds(pl.multiple_of(part * D + base, 128), 256)
                    old = s.joined[rows, place_at].astype(F32)
                    s.joined[rows, place_at] = jnp.where(mask, result, old).astype(BF16)

    def head_back(self, f, which):
        s = self.s

        @pl.loop(0, TOK // TILE)
        def _(i):
            rows = rows_of(i, TILE)
            spots = rows_of(i % (SEQ // TILE), TILE)
            columns = pl.ds(which * D, D)
            grad = s.joined[rows, columns].astype(F32)
            grad = grad * f.cos[spots, :] - partner(grad, first_lanes(TILE)) * f.sin[spots, :]
            normed = f.normed[which, rows, :].astype(F32)
            mean = mm_split(grad * normed, s.spread[...]) * (1.0 / HD)
            scale = mm_split(f.scale[which, rows, :], s.widen[...])
            result = scale * (grad - normed * mm_split(mean, s.widen[...]))
            s.joined[rows, columns] = result.astype(BF16)

    def attention(self, f):
        s, reduce = self.s, self.reduce
        self.load(24, s.packed_all.at[:, :, :, pl.ds(3 * D, 768)], s.w.at[0])
        self.load(25, s.packed_all.at[:, :, :, pl.ds(3 * D + 768, WIDTH)], s.w.at[1, :, :, :, pl.ds(0, WIDTH)])
        for k in range(3):
            self.load((41, k), s.o_qkv.at[k], f.qkv.at[k])
        self.load_soft(f, 0)
        self.load(42, s.o_normed, f.normed)
        self.load(43, s.o_scale, f.scale)
        self.load(44, s.cos, f.cos)
        self.load(45, s.sin, f.sin)
        self.wait(24, 25)
        joined = s.joined
        s.acc[...] = mm_nt(joined[:, 3 * D : 3 * D + 768], flat(s.w[0]))
        s.acc[...] += mm_nt(joined[:, 3 * D + 768 :], flat(s.w[1, :, :, :, 0:WIDTH]))
        f.back[...] = s.acc[...].astype(BF16)
        self.wait((41, 0), (41, 1), (41, 2))
        for k in range(ATTN_STEPS):
            self.attend(f, k)
            reduce.advance()
        self.wait(42, 43, 44, 45)
        self.head_back(f, 0)
        reduce.advance()
        self.head_back(f, 1)


    def load_entry(self, k):
        s = self.s
        width = 768 if k < 4 else WIDTH
        self.load(
            (51, k),
            s.packed_all.at[:, :, :, pl.ds(k * 768, width)],
            s.w.at[k % 2, :, :, :, pl.ds(0, width)],
        )

    def entry(self, k):
        s = self.s
        width = 768 if k < 4 else WIDTH
        self.load_entry(k)
        self.wait((51, k))
        if k < 4:
            self.load_entry(k + 1)
        product = mm_nt(s.joined[:, k * 768 : k * 768 + width], flat(s.w[k % 2, :, :, :, 0:width]))
        if k == 0:
            s.acc[...] = product
        else:
            s.acc[...] += product

    def grad_packed(self, f, jj):
        s = self.s
        self.wait((61, jj))
        right = s.right.at[jj % 2]

        @pl.loop(0, 4)
        def _(k):
            rows = pl.ds(pl.multiple_of(k * 288, 32), 288)
            for half in range(2):
                j = 2 * jj + half
                left = s.left if j < 3 else f.left
                total = mm(left[rows, :], right[:, half * WIDTH : (half + 1) * WIDTH])
                s.held[j, k] = total.astype(BF16).reshape(2, 144, WIDTH)

        self.reduce.produced(2 * jj)
        self.reduce.produced(2 * jj + 1)

    def load_right(self, jj):
        self.load((61, jj), self.s.r_packed.at[:, pl.ds(768 * jj, 768)], self.s.right.at[jj % 2])

    def last(self, f):
        s, reduce = self.s, self.reduce
        mine = pl.ds(pl.multiple_of(self.c * LANE_HALF, 128), LANE_HALF)
        theirs = pl.ds(pl.multiple_of((1 - self.c) * LANE_HALF, 128), LANE_HALF)
        self.to_sibling((71, 0), s.joined.at[:, theirs], s.r_packed.at[pl.ds(TOK, TOK)])
        self.load(71, s.joined.at[:, mine], s.r_packed.at[pl.ds(0, TOK)])
        self.load(72, s.o_lhs.at[0], s.left)
        self.load(73, s.o_lhs.at[self.c], f.left)
        self.load(74, s.tokens, f.tokens)
        reduce.advance()
        self.entry(0)
        self.remote[71, 0].wait_recv()
        self.wait(71, 72, 73)
        self.load_right(0)
        self.load_right(1)
        for jj in range(3):
            reduce.free(6 + 2 * jj)
            reduce.free(7 + 2 * jj)
            self.grad_packed(f, jj)
            if jj == 0:
                self.load_right(2)
            self.entry(1 + jj)
            reduce.advance()
        self.entry(4)
        reduce.advance()
        self.wait(74)

        @pl.loop(0, TOK // TILE)
        def _(i):
            rows = rows_of(i, TILE)
            image = i // (SEQ // TILE)
            mod, d_mod = s.mod, s.d_mod
            normed, inverse = norm_rows(f.tokens[rows, :].astype(F32))
            d_entry = s.acc[rows, :]
            d_mod[image, 0:1, :] += jnp.sum(d_entry, axis=0, keepdims=True)
            d_mod[image, 1:2, :] += jnp.sum(d_entry * normed, axis=0, keepdims=True)
            back = norm_back(normed, inverse, d_entry * (1.0 + mod[image, 1:2, :]))
            s.d_residual[rows, :] += back

        self.load(75, s.d_residual, s.g_tokens)
        reduce.finish()
        self.wait(75)
        self.remote[71, 0].wait_send()


class BackwardInputs(NamedTuple):
    packed_all: object
    gate_all: object
    up_all: object
    down_all: object
    o_branch: object
    o_lhs: object
    o_hidden: object
    o_qkv: object
    o_normed: object
    o_scale: object
    o_soft: object
    o_attended: object
    o_residual: object
    o_active: object
    tokens: object
    cot: object
    cos: object
    sin: object
    mod: object
    spread: object
    widen: object


BACKWARD_OUTPUTS = dict(
    g_packed=((144, 4 * D), BF16),
    g_gate=((144, 8 * WIDTH), BF16),
    g_up=((144, 8 * WIDTH), BF16),
    g_down=((384, D), BF16),
    g_tokens=((TOK, D), F32),
    r_ff=((4, 2 * TOK, 2 * WIDTH), BF16),
    r_packed=((2 * TOK, LANE_HALF), BF16),
    d_mod=((2, 8, D), F32),
)


def vmem(*shape, kind=BF16):
    return pltpu.VMEM(shape, kind)


def backward_scratch():
    return dict(
        held=vmem(8, 4, 2, 144, WIDTH),
        held_big=vmem(3, 4, 2, 192, WIDTH),
        got_y=vmem(14, 4, 2, 48, WIDTH),
        got_y_big=vmem(3, 4, 2, 48, WIDTH),
        got_x=vmem(14, 4, 112, WIDTH),
        got_x_big=vmem(3, 4, 144, WIDTH),
        got_z=vmem(14, 3, 112, WIDTH),
        got_z_big=vmem(3, 3, 144, WIDTH),
        got_f=vmem(14, 112, WIDTH),
        got_f_big=vmem(3, 144, WIDTH),
        w=vmem(2, 4, 2, 144, 2 * WIDTH),
        acc=vmem(TOK, D, kind=F32),
        d_residual=vmem(TOK, D, kind=F32),
        joined=vmem(TOK, 4 * D),
        left=vmem(D, 2 * TOK),
        right=vmem(2, 2 * TOK, 2 * WIDTH),
        scatter_send=pltpu.SemaphoreType.DMA((5, N_PIECES)),
        scatter_recv=pltpu.SemaphoreType.DMA((5, N_PIECES)),
        store_sems=pltpu.SemaphoreType.DMA((N_PIECES,)),
        load_sems=pltpu.SemaphoreType.DMA((96,)),
        pair_send=pltpu.SemaphoreType.DMA((8,)),
        pair_recv=pltpu.SemaphoreType.DMA((8,)),
    )


def backward_kernel(*refs):
    names = BackwardInputs._fields + tuple(BACKWARD_OUTPUTS) + tuple(backward_scratch())
    s = SimpleNamespace(**dict(zip(names, refs, strict=True)))
    spot = place()
    greet(neighbours(*spot))
    reduce = Reduce(s, spot)
    work = Backward(s, spot, reduce)

    def scoped(act, before=None, **shapes):
        def run(*held):
            f = SimpleNamespace(**dict(zip(shapes, held, strict=True)))
            if before is not None:
                before(f)
            act(f)

        pl.run_scoped(run, *shapes.values())

    def first_loads(f):
        work.load(11, s.o_hidden, f.hidden)
        work.load(12, s.o_branch, f.branch)
        work.load_ff(f, 0)

    scoped(
        work.feed_forward,
        first_loads,
        hidden=vmem(8, 192, 2 * TOK),
        branch=vmem(2 * TOK, D),
        w_down=vmem(2, 384, D),
        active=vmem(2, 2, TOK, WIDTH),
        wide=vmem(TOK, WIDTH, kind=F32),
        steep=vmem(2, TOK, 2 * WIDTH),
    )
    scoped(work.middle, cot=vmem(TOK, D), attended=vmem(TOK, D))
    reduce.advance()
    scoped(
        work.attention,
        qkv=vmem(3, TOK, D),
        normed=vmem(2, TOK, D),
        scale=vmem(2, TOK, 128, kind=F32),
        soft=vmem(2, H // ATTN_STEPS, 2, SEQ, SEQ),
        back=vmem(TOK, D),
        cos=vmem(SEQ, D, kind=F32),
        sin=vmem(SEQ, D, kind=F32),
    )
    scoped(work.last, left=vmem(D, 2 * TOK), tokens=vmem(TOK, D))


def backward_pass(f, tokens, cotangent, mod, tables):
    hbm = pl.BlockSpec(memory_space=pl.ANY)
    inside = pl.BlockSpec(memory_space=pltpu.VMEM)
    cosine, sine, spread, widen = tables
    given = BackwardInputs(
        f.packed_all,
        f.gate_all,
        f.up_all,
        f.down_all,
        f.o_branch,
        f.o_lhs,
        f.o_hidden,
        f.o_qkv,
        f.o_normed,
        f.o_scale,
        f.o_soft,
        f.o_attended,
        f.o_residual,
        f.o_active,
        tokens,
        cotangent,
        cosine,
        sine,
        mod,
        spread,
        widen,
    )
    out = pl.pallas_call(
        backward_kernel,
        out_shape=[jax.ShapeDtypeStruct(*spec) for spec in BACKWARD_OUTPUTS.values()],
        in_specs=[hbm] * 18 + [inside] * 3,
        out_specs=[hbm] * 7 + [inside],
        scratch_shapes=list(backward_scratch().values()),
        name="backward_pass",
        compiler_params=pltpu.CompilerParams(
            collective_id=1, has_side_effects=True, vmem_limit_bytes=60 << 20
        ),
    )(*given)
    return SimpleNamespace(**dict(zip(BACKWARD_OUTPUTS, out)))


def body_general(
    tokens,
    condition,
    timestep,
    qkv_weight,
    out_weight,
    gate_weight,
    up_weight,
    down_weight,
    mod_weight,
    mod_bias,
    cotangent,
):
    gathered = (
        lax.all_gather(qkv_weight, "dp", axis=0, tiled=True),
        lax.all_gather(out_weight, "dp", axis=0, tiled=True),
        lax.all_gather(gate_weight, "dp", axis=0, tiled=True),
        lax.all_gather(up_weight, "dp", axis=0, tiled=True),
        lax.all_gather(down_weight, "dp", axis=0, tiled=True),
    )
    cond_total = condition.astype(jnp.float32) + embed_steps(timestep)
    acted_cond = jax.nn.silu(cond_total).astype(jnp.bfloat16)
    acted_group = lax.all_gather(acted_cond, "mod", axis=0, tiled=True)
    mod_part = (
        jnp.dot(acted_group, mod_weight, preferred_element_type=jnp.float32)
        + mod_bias.astype(jnp.float32)
    ).astype(jnp.bfloat16)
    modulation = lax.all_to_all(mod_part, "mod", split_axis=0, concat_axis=1, tiled=True).astype(
        jnp.float32
    )
    tables = rope_tables()
    per_micro = tokens.shape[0] // MICRO
    outputs = []
    token_grads = []
    mod_grads = []
    kept = []
    for micro_step in range(MICRO):
        start_row = micro_step * per_micro
        output, d_tokens, d_modulation, factors = layer_pass(
            tokens[start_row : start_row + per_micro],
            modulation[start_row : start_row + per_micro],
            cotangent[start_row : start_row + per_micro],
            gathered,
            tables,
        )
        outputs.append(output)
        token_grads.append(d_tokens)
        mod_grads.append(d_modulation)
        kept.append(factors)
    joined = [jnp.concatenate([factors[number] for factors in kept], axis=0) for number in range(9)]
    (
        entry_first,
        d_projected,
        combined,
        d_attended,
        entry_second,
        d_gate_proj,
        d_up_proj,
        hidden,
        d_branch,
    ) = joined
    grad_qkv = jnp.einsum(
        "bsd,bse->de", entry_first, d_projected, preferred_element_type=jnp.float32
    )
    grad_proj = jnp.einsum("bsd,bse->de", combined, d_attended, preferred_element_type=jnp.float32)
    grad_gate = jnp.einsum(
        "bsd,bsf->df", entry_second, d_gate_proj, preferred_element_type=jnp.float32
    )
    grad_up = jnp.einsum("bsd,bsf->df", entry_second, d_up_proj, preferred_element_type=jnp.float32)
    grad_down = jnp.einsum("bsf,bsd->fd", hidden, d_branch, preferred_element_type=jnp.float32)
    totals = (grad_qkv, grad_proj, grad_gate, grad_up, grad_down)
    output_tokens = jnp.concatenate(outputs, axis=0)
    grad_tokens = jnp.concatenate(token_grads, axis=0)
    mod_grad = jnp.concatenate(mod_grads, axis=0)
    mod_back = lax.all_to_all(mod_grad, "mod", split_axis=1, concat_axis=0, tiled=True)
    grad_mod_part = jnp.einsum(
        "id,ic->dc", acted_group, mod_back, preferred_element_type=jnp.float32
    )
    bias_part = jnp.sum(mod_back.astype(jnp.float32), axis=0)
    acted_grad_part = jnp.einsum(
        "ic,dc->id", mod_back, mod_weight, preferred_element_type=jnp.float32
    )
    acted_grad = lax.psum_scatter(
        acted_grad_part.astype(jnp.bfloat16), "mod", scatter_dimension=0, tiled=True
    ).astype(jnp.float32)
    sigma_cond = jax.nn.sigmoid(cond_total)
    grad_condition = acted_grad * sigma_cond * (1.0 + cond_total * (1.0 - sigma_cond))
    grad_bias = lax.psum(bias_part, "dp")
    count = lax.axis_size("dp")
    arrays = totals + (grad_mod_part,)
    shapes = [array.shape for array in arrays]
    flat = lax.psum_scatter(pack_rows(arrays, count), "dp", scatter_dimension=0, tiled=True)
    summed = unpack_rows(flat, shapes, count)
    finished = (
        lax.psum(summed[0].astype(jnp.bfloat16), "mod").astype(jnp.float32),
        lax.psum(summed[1].astype(jnp.bfloat16), "mod").astype(jnp.float32),
        lax.psum(summed[2].astype(jnp.bfloat16), "mod").astype(jnp.float32),
        lax.psum(summed[3].astype(jnp.bfloat16), "mod").astype(jnp.float32),
        lax.psum(summed[4].astype(jnp.bfloat16), "mod").astype(jnp.float32),
    )
    grad_mod = summed[5]
    return (
        output_tokens,
        grad_tokens,
        grad_condition,
        finished[0],
        finished[1],
        finished[2],
        finished[3],
        finished[4],
        grad_mod,
        grad_bias,
    )


def body_fast(
    tokens,
    condition,
    timestep,
    qkv_weight,
    out_weight,
    gate_weight,
    up_weight,
    down_weight,
    mod_weight,
    mod_bias,
    cotangent,
):
    packed = jnp.concatenate([qkv_weight, out_weight], axis=1)
    cond_total = condition.astype(jnp.float32) + embed_steps(timestep)
    acted_cond = jax.nn.silu(cond_total).astype(jnp.bfloat16)
    acted_group = lax.all_gather(acted_cond, "mod", axis=0, tiled=True)
    mod_part = (
        jnp.dot(acted_group, mod_weight, preferred_element_type=jnp.float32)
        + mod_bias.astype(jnp.float32)
    ).astype(jnp.bfloat16)
    modulation = lax.all_to_all(mod_part, "mod", split_axis=0, concat_axis=1, tiled=True).astype(
        jnp.float32
    )
    mod_rows = jnp.pad(modulation.reshape(2, 6, D), ((0, 0), (0, 2), (0, 0)))
    flat_tokens, flat_cotangent = tokens.reshape(TOK, D), cotangent.reshape(TOK, D)
    tables = head_tables()
    f = forward_pass(
        packed,
        gate_weight,
        up_weight,
        down_weight,
        flat_tokens,
        flat_cotangent,
        mod_rows,
        tables,
    )
    b = backward_pass(f, flat_tokens, flat_cotangent, mod_rows, tables)
    mod_grad = b.d_mod[:, :6, :].at[:, 5, :].set(f.o_gate_b[:, 0, :]).reshape(2, 6 * D).astype(BF16)
    mod_back = lax.all_to_all(mod_grad, "mod", split_axis=1, concat_axis=0, tiled=True)
    acted_all = lax.all_gather(acted_group, "dp", axis=0, tiled=True)
    back_all = lax.all_gather(mod_back, "dp", axis=0, tiled=True)
    rows = D // 8
    acted_rows = lax.dynamic_slice_in_dim(acted_all, lax.axis_index("dp") * rows, rows, 1)
    grad_mod = jnp.einsum("id,ic->dc", acted_rows, back_all, preferred_element_type=jnp.float32)
    grad_bias = jnp.sum(back_all.astype(jnp.float32), axis=0)
    acted_grad_part = jnp.einsum(
        "ic,dc->id", mod_back, mod_weight, preferred_element_type=jnp.float32
    )
    acted_grad = lax.psum_scatter(
        acted_grad_part.astype(jnp.bfloat16), "mod", scatter_dimension=0, tiled=True
    ).astype(jnp.float32)
    sigma_cond = jax.nn.sigmoid(cond_total)
    grad_condition = acted_grad * sigma_cond * (1.0 + cond_total * (1.0 - sigma_cond))
    return (
        f.o_result.reshape(tokens.shape),
        b.g_tokens.reshape(tokens.shape),
        grad_condition,
        b.g_packed[:, : 3 * D].astype(F32),
        b.g_packed[:, 3 * D :].astype(F32),
        b.g_gate.astype(F32),
        b.g_up.astype(F32),
        b.g_down.astype(F32),
        grad_mod,
        grad_bias,
    )


def pick_body(mesh):
    if dict(mesh.shape) == {"dp": 8, "mod": 4}:
        return body_fast
    return body_general


def solution(mesh):
    in_specs = (
        P(("dp", "mod"), None, None),
        P(("dp", "mod"), None),
        P(("dp", "mod")),
        P("dp", None),
        P("dp", None),
        P("dp", None),
        P("dp", None),
        P("dp", None),
        P(None, "mod"),
        P("mod"),
        P(("dp", "mod"), None, None),
    )
    out_specs = (
        P(("dp", "mod"), None, None),
        P(("dp", "mod"), None, None),
        P(("dp", "mod"), None),
        P("dp", None),
        P("dp", None),
        P("dp", None),
        P("dp", None),
        P("dp", None),
        P("dp", "mod"),
        P("mod"),
    )
    return jax.shard_map(pick_body(mesh), mesh=mesh, in_specs=in_specs, out_specs=out_specs, check_vma=False)
```

```python
import math
from types import SimpleNamespace
from typing import NamedTuple

import jax
import jax.numpy as jnp
from jax import lax
import numpy as np
from jax.experimental import pallas as pl
from jax.experimental.pallas import tpu as pltpu
from jax.sharding import PartitionSpec as P

D = 1152
H = 16
HD = 72
GRID = 16
SEQ = 256
MICRO = 2


EPSILON = 1e-06


def norm_rows(field):
    scale_inv = lax.rsqrt(jnp.mean(field * field, axis=-1, keepdims=True) + EPSILON)
    return (field * scale_inv, scale_inv)


def norm_back(normed, scale_inv, gradient):
    return scale_inv * (gradient - normed * jnp.mean(gradient * normed, axis=-1, keepdims=True))


def embed_steps(timestep):
    half_width = D // 2
    frequency = jnp.exp(-math.log(10000.0) * jnp.arange(half_width, dtype=jnp.float32) / half_width)
    angles = timestep.astype(jnp.float32)[:, None] * frequency[None, :]
    return jnp.concatenate([jnp.cos(angles), jnp.sin(angles)], axis=1)


def rope_tables():
    quarter = HD // 4
    frequency = jnp.exp(-math.log(10000.0) * jnp.arange(quarter, dtype=jnp.float32) / quarter)
    position = jnp.arange(SEQ)
    row_index = (position // GRID).astype(jnp.float32)
    col_index = (position % GRID).astype(jnp.float32)
    angles = jnp.stack(
        [row_index[:, None] * frequency[None, :], col_index[:, None] * frequency[None, :]], axis=1
    )
    return (jnp.cos(angles), jnp.sin(angles))


def rotate(field, cosine_table, sine_table):
    leading = field.shape[:-1]
    quarters = field.reshape(leading + (2, 2, HD // 4))
    first_half = quarters[..., 0, :]
    second_half = quarters[..., 1, :]
    cosine_rows = cosine_table[:, None]
    sine_rows = sine_table[:, None]
    turned_first = first_half * cosine_rows - second_half * sine_rows
    turned_second = first_half * sine_rows + second_half * cosine_rows
    return jnp.stack([turned_first, turned_second], axis=-2).reshape(field.shape)


def pack_rows(arrays, count):
    return jnp.concatenate([array.reshape(count, -1) for array in arrays], axis=1).reshape(-1)


def unpack_rows(flat, shapes, count):
    pieces = []
    offset = 0
    for rows_all, columns in shapes:
        rows = rows_all // count
        pieces.append(flat[offset : offset + rows * columns].reshape(rows, columns))
        offset = offset + rows * columns
    return pieces


def layer_pass(block_in, mod_rows, cotangent, weights, tables):
    qkv_full, proj_full, gate_full, up_full, down_full = weights
    cosine_table, sine_table = tables
    images = block_in.shape[0]
    shift_first, scale_first, gate_first, shift_second, scale_second, gate_second = [
        mod_rows[:, None, number * D : (number + 1) * D] for number in range(6)
    ]
    heads_shape = (images, SEQ, H, HD)
    factor = 1.0 / math.sqrt(HD)
    inputs = block_in.astype(jnp.float32)
    normed_first, inv_first = norm_rows(inputs)
    entry_first = (normed_first * (1.0 + scale_first) + shift_first).astype(jnp.bfloat16)
    projected = jnp.einsum("bsd,de->bse", entry_first, qkv_full, preferred_element_type=jnp.float32)
    q_normed, q_inv = norm_rows(projected[..., :D].reshape(heads_shape))
    k_normed, k_inv = norm_rows(projected[..., D : 2 * D].reshape(heads_shape))
    queries = rotate(q_normed, cosine_table, sine_table).astype(jnp.bfloat16)
    keys_rot = rotate(k_normed, cosine_table, sine_table).astype(jnp.bfloat16)
    values = projected[..., 2 * D :].reshape(heads_shape).astype(jnp.bfloat16)
    scores = (
        jnp.einsum("bqhd,bkhd->bhqk", queries, keys_rot, preferred_element_type=jnp.float32)
        * factor
    )
    highest = jnp.max(scores, axis=-1, keepdims=True)
    log_total = highest + jnp.log(jnp.sum(jnp.exp(scores - highest), axis=-1, keepdims=True))
    weights_soft = jnp.exp(scores - log_total).astype(jnp.bfloat16)
    combined = (
        jnp.einsum("bhqk,bkhd->bqhd", weights_soft, values, preferred_element_type=jnp.float32)
        .reshape(images, SEQ, D)
        .astype(jnp.bfloat16)
    )
    attended = jnp.einsum("bsd,de->bse", combined, proj_full, preferred_element_type=jnp.float32)
    residual = inputs + gate_first * attended
    normed_second, inv_second = norm_rows(residual)
    entry_second = (normed_second * (1.0 + scale_second) + shift_second).astype(jnp.bfloat16)
    gate_proj = jnp.einsum(
        "bsd,df->bsf", entry_second, gate_full, preferred_element_type=jnp.float32
    )
    up_proj = jnp.einsum("bsd,df->bsf", entry_second, up_full, preferred_element_type=jnp.float32)
    sigma_gate = jax.nn.sigmoid(gate_proj)
    activated = gate_proj * sigma_gate
    hidden = (activated * up_proj).astype(jnp.bfloat16)
    branch = jnp.einsum("bsf,fd->bsd", hidden, down_full, preferred_element_type=jnp.float32)
    output = (residual + gate_second * branch).astype(jnp.bfloat16)
    grad_out = cotangent.astype(jnp.float32)
    d_gate_second = jnp.sum(grad_out * branch, axis=1)
    d_branch = (gate_second * grad_out).astype(jnp.bfloat16)
    d_hidden = jnp.einsum("bsd,fd->bsf", d_branch, down_full, preferred_element_type=jnp.float32)
    d_gate_proj = (d_hidden * up_proj * sigma_gate * (1.0 + gate_proj * (1.0 - sigma_gate))).astype(
        jnp.bfloat16
    )
    d_up_proj = (d_hidden * activated).astype(jnp.bfloat16)
    d_entry_second = jnp.einsum(
        "bsf,df->bsd", d_gate_proj, gate_full, preferred_element_type=jnp.float32
    )
    d_entry_second = d_entry_second + jnp.einsum(
        "bsf,df->bsd", d_up_proj, up_full, preferred_element_type=jnp.float32
    )
    d_shift_second = jnp.sum(d_entry_second, axis=1)
    d_scale_second = jnp.sum(d_entry_second * normed_second, axis=1)
    d_residual = grad_out + norm_back(
        normed_second, inv_second, d_entry_second * (1.0 + scale_second)
    )
    d_gate_first = jnp.sum(d_residual * attended, axis=1)
    d_attended = (gate_first * d_residual).astype(jnp.bfloat16)
    d_combined = (
        jnp.einsum("bse,de->bsd", d_attended, proj_full, preferred_element_type=jnp.float32)
        .astype(jnp.bfloat16)
        .reshape(heads_shape)
    )
    scores_again = (
        jnp.einsum("bqhd,bkhd->bhqk", queries, keys_rot, preferred_element_type=jnp.float32)
        * factor
    )
    recomputed = jnp.exp(scores_again - log_total)
    d_weights = jnp.einsum(
        "bqhd,bkhd->bhqk", d_combined, values, preferred_element_type=jnp.float32
    )
    d_scores = (
        recomputed * (d_weights - jnp.sum(recomputed * d_weights, axis=-1, keepdims=True))
    ).astype(jnp.bfloat16)
    d_values = jnp.einsum(
        "bhqk,bqhd->bkhd", weights_soft, d_combined, preferred_element_type=jnp.float32
    ).astype(jnp.bfloat16)
    d_queries = (
        (
            jnp.einsum("bhqk,bkhd->bqhd", d_scores, keys_rot, preferred_element_type=jnp.float32)
            * factor
        )
        .astype(jnp.bfloat16)
        .astype(jnp.float32)
    )
    d_keys = (
        (
            jnp.einsum("bhqk,bqhd->bkhd", d_scores, queries, preferred_element_type=jnp.float32)
            * factor
        )
        .astype(jnp.bfloat16)
        .astype(jnp.float32)
    )
    d_q_raw = norm_back(q_normed, q_inv, rotate(d_queries, cosine_table, -sine_table))
    d_k_raw = norm_back(k_normed, k_inv, rotate(d_keys, cosine_table, -sine_table))
    flat_shape = (images, SEQ, D)
    d_projected = jnp.concatenate(
        [
            d_q_raw.reshape(flat_shape),
            d_k_raw.reshape(flat_shape),
            d_values.astype(jnp.float32).reshape(flat_shape),
        ],
        axis=-1,
    ).astype(jnp.bfloat16)
    d_entry_first = jnp.einsum(
        "bse,de->bsd", d_projected, qkv_full, preferred_element_type=jnp.float32
    )
    d_shift_first = jnp.sum(d_entry_first, axis=1)
    d_scale_first = jnp.sum(d_entry_first * normed_first, axis=1)
    d_tokens = d_residual + norm_back(normed_first, inv_first, d_entry_first * (1.0 + scale_first))
    d_modulation = jnp.concatenate(
        [d_shift_first, d_scale_first, d_gate_first, d_shift_second, d_scale_second, d_gate_second],
        axis=1,
    ).astype(jnp.bfloat16)
    factors = (
        entry_first,
        d_projected,
        combined,
        d_attended,
        entry_second,
        d_gate_proj,
        d_up_proj,
        hidden,
        d_branch,
    )
    return (output, d_tokens, d_modulation, factors)


MESH = pl.DeviceIdType.MESH
WIDTH = 384
LANE_HALF = 2304
FF_HALF = 1536
BF16 = jnp.bfloat16
F32 = jnp.float32


def place():
    dp = lax.axis_index("dp")
    mod = lax.axis_index("mod")
    return dp // 2, dp % 2, mod // 2, mod % 2


def device(z, x, y, c):
    return (z * 2 + x, y * 2 + c)


def greet(peers):
    barrier = pltpu.get_barrier_semaphore()
    for peer in peers:
        pl.semaphore_signal(barrier, inc=1, device_id=peer, device_id_type=MESH)
    pl.semaphore_wait(barrier, len(peers))


def neighbours(z, x, y, c):
    around = [device((z + step) % 4, x, y, c) for step in (1, 2, 3)]
    return around + [device(z, 1 - x, y, c), device(z, x, 1 - y, c), device(z, x, y, 1 - c)]


def send(source, target, send_sem, recv_sem, peer):
    pltpu.make_async_remote_copy(
        src_ref=source,
        dst_ref=target,
        send_sem=send_sem,
        recv_sem=recv_sem,
        device_id=peer,
        device_id_type=MESH,
    ).start()


def drain(window, sem):
    pltpu.make_async_copy(window, window, sem).wait()


class Piece:
    def __init__(self, source, target, row, rows, column, edge):
        self.source, self.target = source, target
        self.row, self.rows, self.column, self.edge = row, rows, column, edge


def gather_pieces(refs, c, edge_of):
    packed, gate, up, down, packed_all, gate_all, up_all, down_all = refs
    pieces = []
    for j in range(6):
        pieces.append(Piece(packed, packed_all, 0, 144, c * LANE_HALF + j * WIDTH, edge_of(144, j)))
    for j in range(4):
        pieces.append(Piece(gate, gate_all, 0, 144, c * FF_HALF + j * WIDTH, edge_of(144, j)))
        pieces.append(Piece(up, up_all, 0, 144, c * FF_HALF + j * WIDTH, edge_of(144, j)))
    for j in range(3):
        pieces.append(Piece(down, down_all, c * 192, 192, j * WIDTH, edge_of(192, j)))
    return pieces


class Gather:
    def __init__(self, refs, sems, spot, stages):
        self.z, self.x, self.y, self.c = spot
        self.stages = stages
        self.pieces = gather_pieces(refs, self.c, lambda rows, j: rows // 3)
        self.send_sems, self.recv_sems, self.own_sems = sems
        self.refs = refs

    def columns(self, piece):
        return pl.ds(pl.multiple_of(piece.column, 128), WIDTH)

    def part(self, piece):
        keep = piece.rows - piece.edge
        return pl.ds(pl.multiple_of(piece.row + self.y * piece.edge, 16), keep), keep

    def mine(self, piece):
        return pl.ds(pl.multiple_of(piece.row + self.y * (piece.rows - piece.edge), 16), piece.edge)

    def own_copies(self):
        for k in range(4):
            pltpu.make_async_copy(self.refs[k], self.stages[k], self.own_sems.at[k]).start()

    def own_stores(self):
        for k in range(4):
            drain(self.stages[k], self.own_sems.at[k])
            pltpu.make_async_copy(
                self.stages[k], self.refs[4 + k].at[self.z, self.x], self.own_sems.at[k]
            ).start()

    def own_done(self):
        for k in range(4):
            drain(self.stages[k], self.own_sems.at[k])

    def start_z(self, t):
        p = self.pieces[t]
        rows, _ = self.part(p)
        here = p.source.at[rows, self.columns(p)]
        there = p.target.at[self.z, self.x, rows, self.columns(p)]
        for step in (1, 3, 2):
            peer = device((self.z + step) % 4, self.x, self.y, self.c)
            send(here, there, self.send_sems.at[0, t], self.recv_sems.at[0, t], peer)
        peer = device(self.z, 1 - self.x, self.y, self.c)
        send(here, there, self.send_sems.at[1, t], self.recv_sems.at[1, t], peer)

    def start_x(self, t):
        p = self.pieces[t]
        rows, keep = self.part(p)
        columns = self.columns(p)
        drain(p.target.at[pl.ds(0, 3), 0, pl.ds(0, keep), pl.ds(0, WIDTH)], self.recv_sems.at[0, t])
        x_peer = device(self.z, 1 - self.x, self.y, self.c)
        y_peer = device(self.z, self.x, 1 - self.y, self.c)
        for step in (1, 3, 2):
            other = (self.z + step) % 4
            block = p.target.at[other, self.x, rows, columns]
            send(block, block, self.send_sems.at[1, t], self.recv_sems.at[1, t], x_peer)
        for step in (1, 3, 2):
            other = (self.z + step) % 4
            block = p.target.at[other, self.x, self.mine(p), columns]
            send(block, block, self.send_sems.at[2, t], self.recv_sems.at[2, t], y_peer)

    def start_y(self, t):
        p = self.pieces[t]
        _, keep = self.part(p)
        columns = self.columns(p)
        drain(p.target.at[:, 0, pl.ds(0, keep), pl.ds(0, WIDTH)], self.recv_sems.at[1, t])
        y_peer = device(self.z, self.x, 1 - self.y, self.c)
        block = p.target.at[:, 1 - self.x, self.mine(p), columns]
        send(block, block, self.send_sems.at[2, t], self.recv_sems.at[2, t], y_peer)

    def start_c(self, t):
        p = self.pieces[t]
        columns = self.columns(p)
        half = pl.ds(pl.multiple_of(p.row, 16), p.rows)
        self.drain_seven(p.edge, self.recv_sems.at[2, t])
        peer = device(self.z, self.x, self.y, 1 - self.c)
        block = p.target.at[:, 1 - self.x, half, columns]
        send(block, block, self.send_sems.at[3, t], self.recv_sems.at[3, t], peer)
        for step in (1, 2, 3):
            block = p.target.at[(self.z + step) % 4, self.x, half, columns]
            send(block, block, self.send_sems.at[3, t], self.recv_sems.at[3, t], peer)

    def arrived(self, t):
        self.drain_seven(self.pieces[t].rows, self.recv_sems.at[3, t])

    def drain_seven(self, rows, sem):
        high = 96 if rows > 144 else rows
        drain(self.refs[4].at[pl.ds(0, rows // high), 0, pl.ds(0, high), pl.ds(0, 7 * WIDTH)], sem)

    def sent_z(self, t):
        p = self.pieces[t]
        _, keep = self.part(p)
        drain(p.target.at[pl.ds(0, 3), 0, pl.ds(0, keep), pl.ds(0, WIDTH)], self.send_sems.at[0, t])

    def sent_rest(self, t):
        p = self.pieces[t]
        _, keep = self.part(p)
        drain(p.target.at[:, 0, pl.ds(0, keep), pl.ds(0, WIDTH)], self.send_sems.at[1, t])
        for stage, rows in ((2, p.edge), (3, p.rows)):
            self.drain_seven(rows, self.send_sems.at[stage, t])


N_PIECES = 17


class Group:
    def __init__(self, spot, parts, got_c, got_y, blocks, send_sems, recv_sems):
        _, _, self.y, self.c = spot
        z, x, y, c = spot
        self.sibling, self.across = device(z, x, y, 1 - c), device(z, x, 1 - y, c)
        self.parts, self.got_c, self.got_y, self.blocks = parts, got_c, got_y, blocks
        self.send_sems, self.recv_sems = send_sems, recv_sems

    def sems(self, k):
        return self.send_sems.at[k], self.recv_sems.at[k]

    def start(self):
        for y in range(2):
            source = self.parts.at[2 * y + 1 - self.c]
            send(source, self.got_c.at[y], *self.sems(y), self.sibling)

    def across_y(self):
        for y in range(2):
            drain(self.got_c.at[y], self.recv_sems.at[y])
        own = self.parts.at[2 * (1 - self.y) + self.c]
        send(own, self.got_y.at[self.c], *self.sems(2), self.across)
        send(self.got_c.at[1 - self.y], self.got_y.at[1 - self.c], *self.sems(3), self.across)

    def finish(self):
        for k in (2, 3):
            drain(self.got_y.at[k - 2], self.recv_sems.at[k])
        y, c, blocks = self.y, self.c, self.blocks
        blocks[2 * y + c] = self.parts[2 * y + c]
        blocks[2 * y + 1 - c] = self.got_c[y]
        for k in range(2):
            blocks[2 * (1 - y) + k] = self.got_y[k]
        for k in range(4):
            drain(self.got_y.at[k % 2], self.send_sems.at[k])


def group_scratch(columns):
    return [
        pltpu.VMEM((4, 8, columns), F32),
        pltpu.VMEM((2, 8, columns), F32),
        pltpu.VMEM((2, 8, columns), F32),
        pltpu.VMEM((4, 8, columns), F32),
        pltpu.SemaphoreType.DMA((4,)),
        pltpu.SemaphoreType.DMA((4,)),
    ]


MOD_PART = 1728
SLIM = (24, 128)


class Acted:
    def __init__(self, s, spot):
        self.s = s
        self.z, self.x, self.y, self.c = spot

    def hop(self, k, where, peers):
        block = self.s.acted_all.at[where]
        for peer in peers:
            send(block, block, self.s.acted_send.at[k], self.s.acted_recv.at[k], peer)

    def step(self, k):
        z, x, y, c = self.z, self.x, self.y, self.c
        s = self.s
        if k == 0:
            pltpu.make_async_copy(s.acted_slim, s.acted_all.at[z, x, y, c], s.acted_own).start()
            drain(s.acted_slim, s.acted_own)
            self.hop(0, (z, x, y, c), [device(z, x, y, 1 - c)])
        elif k == 1:
            drain(s.acted_slim, s.acted_recv.at[0])
            self.hop(1, (z, x, y), [device(z, x, 1 - y, c)])
        elif k == 2:
            drain(s.acted_all.at[0, 0, 0], s.acted_recv.at[1])
            self.hop(2, (z, x), [device(z, 1 - x, y, c)])
        elif k == 3:
            drain(s.acted_all.at[0, 0], s.acted_recv.at[2])
            self.hop(3, (z,), [device((z + step) % 4, x, y, c) for step in (1, 3, 2)])
        else:
            drain(s.acted_all.at[pl.ds(0, 3)], s.acted_recv.at[3])
            drain(s.acted_slim, s.acted_send.at[0])
            drain(s.acted_all.at[0, 0, 0], s.acted_send.at[1])
            drain(s.acted_all.at[0, 0], s.acted_send.at[2])
            drain(s.acted_all.at[pl.ds(0, 3)], s.acted_send.at[3])


TOK = 512
TILE = 64
ATTN_STEPS = 8


def mm(left, right):
    return lax.dot_general(left, right, (((1,), (0,)), ((), ())), preferred_element_type=F32)


def mm_nt(left, right):
    return lax.dot_general(left, right, (((1,), (1,)), ((), ())), preferred_element_type=F32)


def mm_tn(left, right):
    return lax.dot_general(left, right, (((0,), (0,)), ((), ())), preferred_element_type=F32)


def split(value):
    high = value.astype(BF16)
    return high, (value - high.astype(F32)).astype(BF16)


def mm_split(value, right):
    high, low = split(value)
    return mm(high, right) + mm(low, right)


def partner(value, first):
    width = value.shape[1]
    return jnp.where(first, pltpu.roll(value, width - 18, 1), pltpu.roll(value, 18, 1))


def first_lanes(rows):
    return lax.broadcasted_iota(jnp.int32, (rows, D), 1) % 36 < 18


def rows_of(block, count):
    return pl.ds(pl.multiple_of(block * count, count), count)


def head_window(head):
    base = jnp.minimum(head * HD // 128 * 128, D - 256)
    offset = head * HD - base
    lane = lax.broadcasted_iota(jnp.int32, (SEQ, 256), 1)
    mask = (lane >= offset) & (lane < offset + HD)
    return pl.ds(pl.multiple_of(base, 128), 256), mask


def flat(ref_value):
    return ref_value.reshape(-1, ref_value.shape[-1])


class Saves:
    def __init__(self, sems):
        self.sems, self.count, self.open = sems, 0, []

    def local(self, source, target):
        copy = pltpu.make_async_copy(source, target, self.sems.at[self.count])
        self.count += 1
        copy.start()
        self.open.append(copy)
        return copy

    def done(self, copy):
        copy.wait()
        self.open = [other for other in self.open if other is not copy]

    def finish(self):
        for copy in self.open:
            copy.wait()


class Forward:
    def __init__(self, s, spot, gather):
        self.s, self.gather = s, gather
        self.z, self.x, self.y, self.c = spot
        self.saves = Saves(s.save_sems)
        self.pending = {}
        self.remote = []
        self.slots = {}


    def to_sibling(self, source, target):
        k = len(self.remote)
        peer = device(self.z, self.x, self.y, 1 - self.c)
        copy = pltpu.make_async_remote_copy(
            src_ref=source,
            dst_ref=target,
            send_sem=self.s.pair_send.at[k],
            recv_sem=self.s.pair_recv.at[k],
            device_id=peer,
            device_id_type=MESH,
        )
        copy.start()
        self.remote.append(copy)


    def load(self, key, part, source, target):
        if (key, part) not in self.pending:
            copy = pltpu.make_async_copy(source, target, self.s.load_sems.at[len(self.pending)])
            copy.start()
            self.pending[key, part] = copy

    def window(self, ref, column):
        return ref.at[:, :, :, pl.ds(column, WIDTH)]

    def load_qv(self, j):
        packed = self.gather.refs[4]
        self.load(j, 0, self.window(packed, j * WIDTH), self.s.w.at[j % 2, 0])
        self.load(j, 1, self.window(packed, LANE_HALF + j * WIDTH), self.s.w.at[j % 2, 1])

    def load_ko(self, j):
        packed = self.gather.refs[4]
        self.load(j, 0, self.window(packed, j * WIDTH), self.s.w.at[j % 2, 0])
        target = self.window(self.s.w_out, (j - 3) * WIDTH)
        self.load(j, 1, self.window(packed, LANE_HALF + j * WIDTH), target)

    def load_ff(self, j):
        at = (j // 2 + 4 * (j % 2)) * WIDTH
        self.load(6 + j, 0, self.window(self.gather.refs[5], at), self.s.w.at[j % 2, 0])
        self.load(6 + j, 1, self.window(self.gather.refs[6], at), self.s.w.at[j % 2, 1])

    def load_down(self, j):
        self.load(14 + j, 0, self.window(self.gather.refs[7], j * WIDTH), self.s.w_down.at[j % 2])

    def loaded(self, load, j, key):
        load(j)
        for part in range(2):
            if (key, part) in self.pending:
                self.pending[key, part].wait()


    def modulate(self):
        s, y, c = self.s, self.y, self.c
        spot = (self.z, self.x, y, c)
        load = pltpu.make_async_copy(s.mod_weight, s.mod_w, s.acted_own)
        load.start()
        s.acted_group[2 * y + c] = s.acted[...]
        own = s.acted_group.at[2 * y + c]
        sibling, across = device(self.z, self.x, y, 1 - c), device(self.z, self.x, 1 - y, c)
        send(own, own, s.first_send.at[0], s.first_recv.at[0], sibling)
        drain(own, s.first_recv.at[0])
        pair = s.acted_group.at[pl.ds(2 * y, 2)]
        send(pair, pair, s.first_send.at[1], s.first_recv.at[1], across)
        load.wait()
        drain(pair, s.first_recv.at[1])
        parts = mm_nt(s.acted_group[...].reshape(32, D).astype(BF16), s.mod_w[...]) + s.bias[...]
        s.mod_parts[...] = parts.astype(BF16).astype(F32).reshape(4, 8, MOD_PART)
        group = Group(
            spot, s.mod_parts, s.mod_got_c, s.mod_got_y, s.mod_blocks, s.mod_send, s.mod_recv
        )
        group.start()
        group.across_y()
        group.finish()
        for m in range(4):
            s.mod_flat[:, m * MOD_PART : (m + 1) * MOD_PART] = s.mod_blocks[m]
        for image in range(2):
            for k in range(6):
                s.o_mod[image, k : k + 1, :] = s.mod_flat[image : image + 1, k * D : (k + 1) * D]
        drain(own, s.first_send.at[0])
        drain(pair, s.first_send.at[1])

    def enter(self):
        s = self.s

        @pl.loop(0, TOK // TILE)
        def _(i):
            rows = rows_of(i, TILE)
            image = i // (SEQ // TILE)
            mod = s.o_mod
            normed, _ = norm_rows(s.tokens[rows, :].astype(F32))
            entry = normed * (1.0 + mod[image, 1:2, :]) + mod[image, 0:1, :]
            s.entry_a[rows, :] = entry.astype(BF16)
            branch = mod[image, 5:6, :] * s.cot[rows, :].astype(F32)
            s.d_branch[rows, :] = branch.astype(BF16)

        self.saves.local(s.d_branch, s.o_branch.at[pl.ds(0, TOK)])
        self.to_sibling(s.d_branch, s.o_branch.at[pl.ds(TOK, TOK)])
        self.turn(s.entry_a, s.t_a)
        self.share(s.t_a, s.o_lhs.at[0])

    def turn(self, source, target):
        @pl.loop(0, source.shape[1] // 128)
        def _(i):
            columns = rows_of(i, 128)
            target[columns, :] = source[:, columns].T

    def share(self, source, target):
        self.saves.local(source, target.at[:, pl.ds(0, TOK)])
        self.to_sibling(source, target.at[:, pl.ds(TOK, TOK)])

    def qv(self, j):
        s = self.s
        self.loaded(self.load_qv, j, j)
        columns = pl.ds(j * WIDTH, WIDTH)
        s.proj[:, columns] = mm(s.entry_a[...], flat(s.w[j % 2, 0]))
        s.v[:, columns] = mm(s.entry_a[...], flat(s.w[j % 2, 1])).astype(BF16)
        if j == 2:
            self.saves.local(s.v, s.o_qkv.at[2])

    def ko(self, j):
        s = self.s
        self.loaded(self.load_ko, j, j)
        columns = pl.ds((j - 3) * WIDTH, WIDTH)
        s.proj[:, columns] = mm(s.entry_a[...], flat(s.w[j % 2, 0]))

    def head_norm(self, which):
        s = self.s
        target, normed = (s.q, s.q_normed) if which == 0 else (s.k, s.k_normed)
        scale = s.scale_q if which == 0 else s.scale_k

        @pl.loop(0, TOK // TILE)
        def _(i):
            rows = rows_of(i, TILE)
            spots = rows_of(i % (SEQ // TILE), TILE)
            field = s.proj[rows, :]
            inverse = lax.rsqrt(mm_split(field * field, s.spread[...]) * (1.0 / HD) + EPSILON)
            scale[rows, :] = inverse
            field = field * mm_split(inverse, s.widen[...])
            normed[rows, :] = field.astype(BF16)
            turned = field * s.cos[spots, :] + partner(field, first_lanes(TILE)) * s.sin[spots, :]
            target[rows, :] = turned.astype(BF16)

        self.saves.local(target, s.o_qkv.at[which])
        self.saves.local(normed, s.o_normed.at[which])
        self.saves.local(scale, s.o_scale.at[which])

    def attend(self, k):
        s = self.s
        heads = H // ATTN_STEPS
        if k >= 2:
            self.saves.done(self.slots[k - 2])

        @pl.loop(0, heads)
        def _(i):
            window, mask = head_window(k * heads + i)
            for image in range(2):
                rows = pl.ds(image * SEQ, SEQ)
                query = jnp.where(mask, s.q[rows, window].astype(F32), 0.0).astype(BF16)
                scores = mm_nt(query, s.k[rows, window]) * (1.0 / math.sqrt(HD))
                powers = jnp.exp(scores - jnp.max(scores, axis=1, keepdims=True))
                total = jnp.sum(powers, axis=1, keepdims=True)
                soft = (powers * (1.0 / total)).astype(BF16)
                s.soft[k % 2, i, image] = soft
                mixed = mm(soft, s.v[rows, window])
                old = s.combined[rows, window].astype(F32)
                s.combined[rows, window] = jnp.where(mask, mixed, old).astype(BF16)

        self.slots[k] = self.saves.local(s.soft.at[k % 2], s.o_soft.at[pl.ds(k * heads, heads)])

    def leave(self):
        s = self.s
        self.saves.done(self.slots[ATTN_STEPS - 2])
        self.saves.done(self.slots[ATTN_STEPS - 1])
        self.turn(s.combined, s.t_c)
        self.share(s.t_c, s.o_lhs.at[1])
        for j in range(3):
            columns = pl.ds(j * WIDTH, WIDTH)
            s.proj[:, columns] = mm(s.combined[...], flat(s.w_out[:, :, :, columns]))

        @pl.loop(0, TOK // TILE)
        def _(i):
            rows = rows_of(i, TILE)
            image = i // (SEQ // TILE)
            mod = s.o_mod
            attended = s.proj[rows, :]
            s.attended[rows, :] = attended.astype(BF16)
            residual = s.tokens[rows, :].astype(F32) + mod[image, 2:3, :] * attended
            s.residual[rows, :] = residual
            normed, _ = norm_rows(residual)
            entry = normed * (1.0 + mod[image, 4:5, :]) + mod[image, 3:4, :]
            s.entry_b[rows, :] = entry.astype(BF16)

        self.saves.local(s.attended, s.o_attended)
        self.saves.local(s.residual, s.o_residual)
        self.turn(s.entry_b, s.t_b)
        self.share(s.t_b, s.o_lhs.at[2])

    def ff(self, j):
        s = self.s
        self.loaded(self.load_ff, j, 6 + j)
        shard = j // 2 + 4 * (j % 2)
        at = shard * WIDTH
        columns = pl.ds(at, WIDTH)
        s.wide[0] = mm(s.entry_b[...], flat(s.w[j % 2, 0]))
        s.wide[1] = mm(s.entry_b[...], flat(s.w[j % 2, 1]))
        if (6, j - 2) in self.slots:
            for copy in self.slots[(6, j - 2)]:
                self.saves.done(copy)
        slot = j % 2

        @pl.loop(0, TOK // TILE)
        def _(i):
            rows = rows_of(i, TILE)
            gate = s.wide[0, rows, :]
            up = s.wide[1, rows, :]
            sigma = 1.0 / (1.0 + jnp.exp(-gate))
            active = gate * sigma
            s.active[slot, 0, rows, :] = active.astype(BF16)
            slope = up * sigma * (1.0 + gate * (1.0 - sigma))
            s.active[slot, 1, rows, :] = slope.astype(BF16)
            s.hidden[rows, columns] = (active * up).astype(BF16)

        self.slots[(6, j)] = [
            self.saves.local(s.active.at[slot], s.o_active.at[shard]),
        ]
        for i in range(3):
            s.t_h[shard, 128 * i : 128 * i + 128, :] = s.hidden[:, at + 128 * i : at + 128 * i + 128].T
        mine = pl.ds(pl.multiple_of(self.c * 192, 16), 192)
        theirs = pl.ds(pl.multiple_of((1 - self.c) * 192, 16), 192)
        self.saves.local(s.t_h.at[shard, mine], s.o_hidden.at[shard, :, pl.ds(0, TOK)])
        self.to_sibling(s.t_h.at[shard, theirs], s.o_hidden.at[shard, :, pl.ds(TOK, TOK)])

    def down(self, j):
        s = self.s
        self.loaded(self.load_down, j, 14 + j)
        columns = pl.ds(j * WIDTH, WIDTH)
        s.wide[0] = mm(s.hidden[...], flat(s.w_down[j % 2]))
        for image in range(2):
            gate = s.o_mod[image, 5:6, columns]
            total = jnp.zeros((1, WIDTH), F32)
            for i in range(SEQ // TILE):
                rows = pl.ds(image * SEQ + i * TILE, TILE)
                branch = s.wide[0, rows, :]
                result = s.residual[rows, columns] + gate * branch
                s.result[rows, columns] = result.astype(BF16)
                total = total + jnp.sum(
                    s.cot[rows, columns].astype(F32) * branch, axis=0, keepdims=True
                )
            s.o_gate_b[image, 0:1, columns] = total
        if j == 2:
            self.saves.local(s.result, s.o_result)

    def plan(self):
        steps = [(None, self.modulate, None, 0, 7), (None, self.enter, None, 0, 4)]
        steps += [(self.load_qv, self.qv, j, j + 1, 2.5) for j in range(3)]
        steps += [(None, self.head_norm, 0, 3, 8)]
        steps += [(self.load_ko, self.ko, j, j + 1, 1.5) for j in range(3, 6)]
        steps += [(None, self.head_norm, 1, 6, 8)]
        steps += [(None, self.attend, k, 6, 3) for k in range(ATTN_STEPS)]
        steps += [(None, self.leave, None, 6, 8)]
        steps += [(self.load_ff, self.ff, j, 8 + 2 * (j // 2), 4.5) for j in range(8)]
        steps += [(self.load_down, self.down, j, 15 + j, 4) for j in range(3)]
        return steps

    def finish(self):
        self.saves.finish()
        for copy in self.remote:
            copy.wait_send()
            copy.wait_recv()


class ForwardInputs(NamedTuple):
    packed: object
    gate: object
    up: object
    down: object
    tokens: object
    cot: object
    acted: object
    bias: object
    mod_weight: object
    acted_slim: object
    cos: object
    sin: object
    spread: object
    widen: object


FORWARD_OUTPUTS = dict(
    packed_all=((4, 2, 144, 4608), BF16),
    gate_all=((4, 2, 144, 3072), BF16),
    up_all=((4, 2, 144, 3072), BF16),
    down_all=((4, 2, 384, 1152), BF16),
    o_branch=((2 * TOK, D), BF16),
    o_lhs=((3, D, 2 * TOK), BF16),
    o_hidden=((8, 192, 2 * TOK), BF16),
    o_qkv=((3, TOK, D), BF16),
    o_normed=((2, TOK, D), BF16),
    o_scale=((2, TOK, 128), F32),
    o_soft=((H, 2, SEQ, SEQ), BF16),
    o_attended=((TOK, D), BF16),
    o_residual=((TOK, D), F32),
    o_active=((8, 2, TOK, WIDTH), BF16),
    o_result=((TOK, D), BF16),
    acted_all=((4, 2, 2, 2) + SLIM, F32),
    o_mod=((2, 8, D), F32),
    o_gate_b=((2, 8, D), F32),
)


def forward_scratch():
    def vmem(*shape, kind=BF16):
        return pltpu.VMEM(shape, kind)

    return dict(
        entry_a=vmem(TOK, D),
        d_branch=vmem(TOK, D),
        t_a=vmem(D, TOK),
        proj=vmem(TOK, D, kind=F32),
        q=vmem(TOK, D),
        k=vmem(TOK, D),
        v=vmem(TOK, D),
        q_normed=vmem(TOK, D),
        k_normed=vmem(TOK, D),
        scale_q=vmem(TOK, 128, kind=F32),
        scale_k=vmem(TOK, 128, kind=F32),
        soft=vmem(2, H // ATTN_STEPS, 2, SEQ, SEQ),
        combined=vmem(TOK, D),
        t_c=vmem(D, TOK),
        attended=vmem(TOK, D),
        residual=vmem(TOK, D, kind=F32),
        entry_b=vmem(TOK, D),
        t_b=vmem(D, TOK),
        wide=vmem(2, TOK, WIDTH, kind=F32),
        active=vmem(2, 2, TOK, WIDTH),
        hidden=vmem(TOK, 8 * WIDTH),
        t_h=vmem(8, WIDTH, TOK),
        result=vmem(TOK, D),
        w=vmem(2, 2, 4, 2, 144, WIDTH),
        w_out=vmem(4, 2, 144, D),
        w_down=vmem(2, 4, 2, 384, WIDTH),
        gather_send=pltpu.SemaphoreType.DMA((4, N_PIECES)),
        gather_recv=pltpu.SemaphoreType.DMA((4, N_PIECES)),
        mod_w=vmem(MOD_PART, D),
        acted_group=vmem(4, 8, D, kind=F32),
        mod_flat=vmem(8, 4 * MOD_PART, kind=F32),
        mod_parts=group_scratch(MOD_PART)[0],
        mod_got_c=group_scratch(MOD_PART)[1],
        mod_got_y=group_scratch(MOD_PART)[2],
        mod_blocks=group_scratch(MOD_PART)[3],
        mod_send=group_scratch(MOD_PART)[4],
        mod_recv=group_scratch(MOD_PART)[5],
        acted_send=pltpu.SemaphoreType.DMA((4,)),
        acted_recv=pltpu.SemaphoreType.DMA((4,)),
        acted_own=pltpu.SemaphoreType.DMA,
        first_send=pltpu.SemaphoreType.DMA((2,)),
        first_recv=pltpu.SemaphoreType.DMA((2,)),
        own_packed=vmem(144, 4 * D),
        own_gate=vmem(144, 8 * WIDTH),
        own_up=vmem(144, 8 * WIDTH),
        own_down=vmem(384, D),
        own_sems=pltpu.SemaphoreType.DMA((4,)),
        save_sems=pltpu.SemaphoreType.DMA((48,)),
        load_sems=pltpu.SemaphoreType.DMA((48,)),
        pair_send=pltpu.SemaphoreType.DMA((16,)),
        pair_recv=pltpu.SemaphoreType.DMA((16,)),
    )


def run_step(steps, arrived):
    _, act, j, _, cost = steps.pop(0)
    if steps and steps[0][0] is not None and steps[0][3] <= arrived:
        steps[0][0](steps[0][2])
    act() if j is None else act(j)
    return cost


def forward_kernel(*refs):
    names = ForwardInputs._fields + tuple(FORWARD_OUTPUTS) + tuple(forward_scratch())
    s = SimpleNamespace(**dict(zip(names, refs, strict=True)))
    spot = place()
    greet(neighbours(*spot))
    arrays = [s.packed, s.gate, s.up, s.down, s.packed_all, s.gate_all, s.up_all, s.down_all]
    stages = [s.own_packed, s.own_gate, s.own_up, s.own_down]
    gather = Gather(arrays, (s.gather_send, s.gather_recv, s.own_sems), spot, stages)
    work = Forward(s, spot, gather)
    steps = work.plan()
    gather.own_copies()
    acted = Acted(s, spot)
    ahead = 2
    arrived = 0
    for t in range(N_PIECES + 4 + ahead):
        if t == 1:
            gather.own_stores()
        if t < N_PIECES:
            if t >= ahead:
                gather.sent_z(t - ahead)
            gather.start_z(t)
        if 0 <= t - ahead < N_PIECES:
            gather.start_x(t - ahead)
        if 0 <= t - ahead - 1 < N_PIECES:
            gather.start_y(t - ahead - 1)
        if 0 <= t - ahead - 2 < N_PIECES:
            gather.start_c(t - ahead - 2)
        if 0 <= t - ahead - 3 < N_PIECES:
            if arrived == 0:
                gather.own_done()
            gather.arrived(t - ahead - 3)
            arrived += 1
        if 5 <= t < 10:
            acted.step(t - 5)
        spent = 0.0
        while steps and steps[0][3] <= arrived and spent < 6.0:
            spent += run_step(steps, arrived)
    while steps:
        run_step(steps, arrived)
    for t in range(N_PIECES - ahead, N_PIECES):
        gather.sent_z(t)
    for t in range(N_PIECES):
        gather.sent_rest(t)
    work.finish()


def forward_pass(*given):
    hbm = pl.BlockSpec(memory_space=pl.ANY)
    inside = pl.BlockSpec(memory_space=pltpu.VMEM)
    out = pl.pallas_call(
        forward_kernel,
        out_shape=[jax.ShapeDtypeStruct(*spec) for spec in FORWARD_OUTPUTS.values()],
        in_specs=[hbm] * 4 + [inside] * 4 + [hbm] * 2 + [inside] * 4,
        out_specs=[hbm] * 16 + [inside] * 2,
        scratch_shapes=list(forward_scratch().values()),
        name="forward_pass",
        compiler_params=pltpu.CompilerParams(
            collective_id=0, has_side_effects=True, vmem_limit_bytes=60 << 20
        ),
    )(*ForwardInputs(*given))
    return SimpleNamespace(**dict(zip(FORWARD_OUTPUTS, out)))


def head_tables():
    lane = np.arange(D) % HD
    frequency = np.exp(-math.log(10000.0) * (lane % 18) / 18)
    token = np.arange(SEQ)[:, None]
    angle = np.where(lane < 36, token // GRID, token % GRID) * frequency
    sign = np.where(lane % 36 < 18, -1.0, 1.0)
    spread = (np.arange(D)[:, None] // HD == np.arange(128)).astype(np.float32)
    return (
        jnp.asarray(np.cos(angle), F32),
        jnp.asarray(np.sin(angle) * sign, F32),
        jnp.asarray(spread, BF16),
        jnp.asarray(spread.T, BF16),
    )


SCATTER_ROWS = (144,) * 14 + (192,) * 3
SCATTER_EDGE = tuple((32, 48)[j % 2] for j in range(14)) + (48,) * 3
ORDER = (14, 15, 16) + tuple(range(6, 14)) + tuple(range(6))


class Reduce:
    def __init__(self, s, spot):
        self.s = s
        self.z, self.x, self.y, self.c = spot
        self.stage = {}
        self.open = []

    def shape(self, t):
        return SCATTER_ROWS[t], SCATTER_EDGE[t]

    def part(self, t):
        rows, edge = self.shape(t)
        return pl.ds(pl.multiple_of(self.y * edge, 16), rows - edge)

    def held(self, t):
        s = self.s
        return s.held_big.at[t - 14] if t >= 14 else s.held.at[t if t < 6 else t - 6]

    def pick(self, small, big, t):
        return big.at[t - 14] if t >= 14 else small.at[t]

    def got_y(self, t):
        return self.pick(self.s.got_y, self.s.got_y_big, t)

    def got_x(self, t):
        return self.pick(self.s.got_x, self.s.got_x_big, t)

    def got_z(self, t):
        return self.pick(self.s.got_z, self.s.got_z_big, t)

    def got_f(self, t):
        return self.pick(self.s.got_f, self.s.got_f_big, t)

    def sems(self, stage, t):
        return self.s.scatter_send.at[stage, t], self.s.scatter_recv.at[stage, t]

    def produced(self, t):
        self.stage[t] = -1
        self.ask()

    def ask(self):
        entered = sum(stage > 0 for stage in self.stage.values())
        for t in ORDER[: entered + 3]:
            if self.stage.get(t) == -1:
                self.stage[t] = 0
                self.start_y(t)

    def advance(self):
        stages = (self.start_x, self.start_z, self.start_f, self.start_c)
        under_way = [t for t in ORDER if 0 < self.stage.get(t, 4) < 4]
        waiting = [t for t in ORDER if self.stage.get(t) == 0]
        for t in under_way + waiting[:1]:
            stages[self.stage[t]](t)
            self.stage[t] += 1
        self.ask()

    def free(self, t):
        while self.stage[t] < 4:
            self.advance()
        if t in self.open:
            self.sent(t)

    def start_y(self, t):
        rows, edge = self.shape(t)
        theirs = pl.ds(pl.multiple_of((1 - self.y) * (rows - edge), 16), edge)
        send(
            self.held(t).at[:, :, theirs, :],
            self.got_y(t).at[:, :, pl.ds(0, edge), :],
            *self.sems(0, t),
            device(self.z, self.x, 1 - self.y, self.c),
        )

    def start_x(self, t):
        rows, edge = self.shape(t)
        held, got = self.held(t), self.got_y(t)
        drain(got.at[:, :, pl.ds(0, edge), :], self.s.scatter_recv.at[0, t])
        mine = pl.ds(pl.multiple_of(self.y * (rows - edge), 16), edge)

        @pl.loop(0, 4)
        def _(k):
            for x in range(2):
                total = held[k, x, mine, :].astype(F32) + got[k, x, pl.ds(0, edge), :].astype(F32)
                held[k, x, mine, :] = total.astype(BF16)

        send(
            held.at[:, 1 - self.x, self.part(t), :],
            self.got_x(t).at[:, pl.ds(0, rows - edge), :],
            *self.sems(1, t),
            device(self.z, 1 - self.x, self.y, self.c),
        )

    def start_z(self, t):
        rows, edge = self.shape(t)
        held, got = self.held(t), self.got_x(t)
        keep = rows - edge
        drain(got.at[:, pl.ds(0, keep), :], self.s.scatter_recv.at[1, t])
        part = self.part(t)

        @pl.loop(0, 4)
        def _(k):
            total = held[k, self.x, part, :].astype(F32) + got[k, pl.ds(0, keep), :].astype(F32)
            held[k, self.x, part, :] = total.astype(BF16)

        for step in (1, 3, 2):
            other = (self.z + step) % 4
            send(
                held.at[other, self.x, part, :],
                self.got_z(t).at[step - 1, pl.ds(0, keep), :],
                *self.sems(2, t),
                device(other, self.x, self.y, self.c),
            )

    def start_f(self, t):
        rows, edge = self.shape(t)
        held, got = self.held(t), self.got_z(t)
        keep = rows - edge
        drain(got.at[:, pl.ds(0, keep), :], self.s.scatter_recv.at[2, t])
        part = self.part(t)
        total = held[self.z, self.x, part, :].astype(F32)
        for k in range(3):
            total = total + got[k, pl.ds(0, keep), :].astype(F32)
        held[self.z, self.x, part, :] = total.astype(BF16)
        send(
            held.at[self.z, self.x, part, :],
            self.got_f(t).at[pl.ds(0, keep), :],
            *self.sems(3, t),
            device(self.z, self.x, 1 - self.y, self.c),
        )

    def target(self, t):
        s = self.s
        if t < 6:
            columns = pl.ds(pl.multiple_of(self.c * LANE_HALF + t * WIDTH, 128), WIDTH)
            return s.g_packed.at[:, columns]
        if t < 14:
            columns = pl.ds(pl.multiple_of(self.c * FF_HALF + (t - 6) // 2 * WIDTH, 128), WIDTH)
            return (s.g_gate, s.g_up)[(t - 6) % 2].at[:, columns]
        rows = pl.ds(pl.multiple_of(self.c * 192, 16), 192)
        return s.g_down.at[rows, pl.ds((t - 14) * WIDTH, WIDTH)]

    def start_c(self, t):
        rows, edge = self.shape(t)
        held, got = self.held(t), self.got_f(t)
        y, keep, both = self.y, rows - edge, rows - 2 * edge
        drain(got.at[pl.ds(0, keep), :], self.s.scatter_recv.at[3, t])
        drain(self.got_y(t).at[:, :, pl.ds(0, edge), :], self.s.scatter_send.at[0, t])
        drain(self.got_x(t).at[:, pl.ds(0, keep), :], self.s.scatter_send.at[1, t])
        mid, fin = held.at[self.z, self.x], held.at[self.z, 1 - self.x]

        def at(offset, count):
            return pl.ds(pl.multiple_of(offset, 16), count)

        own, other = at(y * keep, edge), at((1 - y) * keep, edge)
        fin[own, :] = mid[own, :]
        fin[other, :] = got[at((1 - y) * both, edge), :]
        total = mid[pl.ds(edge, both), :].astype(F32) + got[at(y * edge, both), :].astype(F32)
        fin[pl.ds(edge, both), :] = total.astype(BF16)
        target = self.target(t)
        send(fin, target, *self.sems(4, t), device(self.z, self.x, y, 1 - self.c))
        pltpu.make_async_copy(fin, target, self.s.store_sems.at[t]).start()
        self.open.append(t)

    def sent(self, t):
        self.open.remove(t)
        rows, edge = self.shape(t)
        sems = self.s.scatter_send
        drain(self.got_z(t).at[:, pl.ds(0, rows - edge), :], sems.at[2, t])
        drain(self.got_f(t).at[pl.ds(0, rows - edge), :], sems.at[3, t])
        drain(self.target(t), sems.at[4, t])
        drain(self.target(t), self.s.store_sems.at[t])

    def finish(self):
        for t in ORDER:
            self.free(t)
        for t in range(N_PIECES):
            drain(self.target(t), self.s.scatter_recv.at[4, t])


class Backward:
    def __init__(self, s, spot, reduce):
        self.s, self.reduce = s, reduce
        self.z, self.x, self.y, self.c = spot
        self.pending = {}
        self.remote = {}
        self.copies = 0

    def load(self, key, source, target):
        if key not in self.pending:
            copy = pltpu.make_async_copy(source, target, self.s.load_sems.at[self.copies])
            self.copies += 1
            copy.start()
            self.pending[key] = copy

    def wait(self, *keys):
        for key in keys:
            self.pending.pop(key).wait()

    def to_sibling(self, key, source, target):
        k = len(self.remote)
        copy = pltpu.make_async_remote_copy(
            src_ref=source,
            dst_ref=target,
            send_sem=self.s.pair_send.at[k],
            recv_sem=self.s.pair_recv.at[k],
            device_id=device(self.z, self.x, self.y, 1 - self.c),
            device_id_type=MESH,
        )
        copy.start()
        self.remote[key] = copy


    def grad_down(self, hidden, branch):
        s, reduce = self.s, self.reduce

        @pl.loop(0, 4)
        def _(k):
            left = hidden[pl.ds(2 * k, 2)].reshape(384, 2 * TOK)
            total = mm(left, branch[...]).astype(BF16)
            for j in range(3):
                block = total[:, j * WIDTH : (j + 1) * WIDTH]
                s.held_big[j, k] = block.reshape(2, 192, WIDTH)

        for t in (14, 15, 16):
            reduce.produced(t)

    def column(self, w):
        half = (1 - self.c) if w % 2 == 0 else self.c
        return half * 4 + w // 2

    def load_ff(self, f, w):
        s = self.s
        window = self.column(w)
        columns = pl.ds(pl.multiple_of(window * WIDTH, 128), WIDTH)
        slot = w % 2
        self.load((1, w), s.down_all.at[window // 2, window % 2], f.w_down.at[slot])
        self.load((2, w), s.gate_all.at[:, :, :, columns], s.w.at[slot, :, :, :, pl.ds(0, WIDTH)])
        self.load((3, w), s.up_all.at[:, :, :, columns], s.w.at[slot, :, :, :, pl.ds(WIDTH, WIDTH)])
        self.load((4, w), s.o_active.at[window], f.active.at[slot])

    def ff(self, f, w):
        s = self.s
        slot = w % 2
        self.load_ff(f, w)
        self.wait((1, w), (2, w), (3, w), (4, w))
        if w < 7:
            self.load_ff(f, w + 1)
        f.wide[...] = mm_nt(f.branch[pl.ds(0, TOK), :], f.w_down[slot])
        if w >= 2:
            if slot == 0:
                self.remote[5, w - 2].wait_send()
            else:
                self.wait((5, w - 2))
        steep = f.steep.at[slot]

        @pl.loop(0, TOK // TILE)
        def _(i):
            rows = rows_of(i, TILE)
            back = f.wide[rows, :]
            steep[rows, 0:WIDTH] = (back * f.active[slot, 1, rows, :].astype(F32)).astype(BF16)
            steep[rows, WIDTH : 2 * WIDTH] = (
                back * f.active[slot, 0, rows, :].astype(F32)
            ).astype(BF16)

        j = w // 2
        if slot == 0:
            self.to_sibling((5, w), steep, s.r_ff.at[j, pl.ds(TOK, TOK)])
        else:
            self.load((5, w), steep, s.r_ff.at[j, pl.ds(0, TOK)])
        product = mm_nt(steep[...], flat(s.w[slot]))
        if w == 0:
            s.acc[...] = product
        else:
            s.acc[...] += product

    def load_grad_ff(self, j):
        s = self.s
        self.remote[5, 2 * j].wait_recv()
        if (5, 2 * j + 1) in self.pending:
            self.wait((5, 2 * j + 1))
        self.load((6, j), s.r_ff.at[j], s.right.at[j % 2])

    def grad_ff(self, j):
        s = self.s
        self.wait((6, j))
        right = s.right.at[j % 2]

        @pl.loop(0, 4)
        def _(k):
            left = s.left[pl.ds(pl.multiple_of(k * 288, 32), 288), :]
            total = mm(left, right[...]).astype(BF16)
            for half in range(2):
                block = total[:, half * WIDTH : (half + 1) * WIDTH]
                s.held[2 * j + half, k] = block.reshape(2, 144, WIDTH)

        self.reduce.produced(6 + 2 * j)
        self.reduce.produced(7 + 2 * j)

    def feed_forward(self, f):
        s, reduce = self.s, self.reduce
        self.wait(11, 12)
        self.load((7, 0), s.o_lhs.at[2], s.left)
        self.grad_down(f.hidden, f.branch)
        for w in range(8):
            self.ff(f, w)
            if w == 0:
                self.wait((7, 0))
            if w % 2 == 1:
                reduce.advance()
                if w >= 3:
                    self.load_grad_ff(w // 2 - 1)
            elif w >= 4:
                self.grad_ff(w // 2 - 2)
        self.load_grad_ff(3)
        self.grad_ff(2)
        reduce.advance()
        self.grad_ff(3)
        self.remote[5, 6].wait_send()


    def middle(self, f):
        s = self.s
        self.load(21, s.cot, f.cot)
        self.load(22, s.o_residual, s.d_residual)
        self.load(23, s.o_attended, f.attended)
        self.wait(21, 22, 23)
        s.d_mod[...] = jnp.zeros_like(s.d_mod)

        @pl.loop(0, TOK // TILE)
        def _(i):
            rows = rows_of(i, TILE)
            image = i // (SEQ // TILE)
            mod, d_mod = s.mod, s.d_mod
            normed, inverse = norm_rows(s.d_residual[rows, :])
            d_entry = s.acc[rows, :]
            d_mod[image, 3:4, :] += jnp.sum(d_entry, axis=0, keepdims=True)
            d_mod[image, 4:5, :] += jnp.sum(d_entry * normed, axis=0, keepdims=True)
            back = norm_back(normed, inverse, d_entry * (1.0 + mod[image, 4:5, :]))
            d_residual = f.cot[rows, :].astype(F32) + back
            s.d_residual[rows, :] = d_residual
            attended = f.attended[rows, :].astype(F32)
            d_mod[image, 2:3, :] += jnp.sum(d_residual * attended, axis=0, keepdims=True)
            s.joined[rows, 3 * D : 4 * D] = (mod[image, 2:3, :] * d_residual).astype(BF16)


    def load_soft(self, f, k):
        heads = H // ATTN_STEPS
        self.load((31, k), self.s.o_soft.at[pl.ds(k * heads, heads)], f.soft.at[k % 2])

    def attend(self, f, k):
        s = self.s
        heads = H // ATTN_STEPS
        self.load_soft(f, k)
        self.wait((31, k))
        if k + 1 < ATTN_STEPS:
            self.load_soft(f, k + 1)
        factor = 1.0 / math.sqrt(HD)

        @pl.loop(0, heads)
        def _(i):
            head = k * heads + i
            window, mask = head_window(head)
            base = jnp.minimum(head * HD // 128 * 128, D - 256)
            for image in range(2):
                rows = pl.ds(image * SEQ, SEQ)
                back = jnp.where(mask, f.back[rows, window].astype(F32), 0.0).astype(BF16)
                soft = f.soft[k % 2, i, image]
                d_soft = mm_nt(back, f.qkv[2, rows, window])
                wide = soft.astype(F32)
                d_scores = (
                    wide * (d_soft - jnp.sum(wide * d_soft, axis=1, keepdims=True))
                ).astype(BF16)
                results = (
                    mm(d_scores, f.qkv[1, rows, window]) * factor,
                    mm_tn(d_scores, f.qkv[0, rows, window]) * factor,
                    mm_tn(soft, back),
                )
                for part, result in enumerate(results):
                    place_at = pl.ds(pl.multiple_of(part * D + base, 128), 256)
                    old = s.joined[rows, place_at].astype(F32)
                    s.joined[rows, place_at] = jnp.where(mask, result, old).astype(BF16)

    def head_back(self, f, which):
        s = self.s

        @pl.loop(0, TOK // TILE)
        def _(i):
            rows = rows_of(i, TILE)
            spots = rows_of(i % (SEQ // TILE), TILE)
            columns = pl.ds(which * D, D)
            grad = s.joined[rows, columns].astype(F32)
            grad = grad * f.cos[spots, :] - partner(grad, first_lanes(TILE)) * f.sin[spots, :]
            normed = f.normed[which, rows, :].astype(F32)
            mean = mm_split(grad * normed, s.spread[...]) * (1.0 / HD)
            scale = mm_split(f.scale[which, rows, :], s.widen[...])
            result = scale * (grad - normed * mm_split(mean, s.widen[...]))
            s.joined[rows, columns] = result.astype(BF16)

    def attention(self, f):
        s, reduce = self.s, self.reduce
        self.load(24, s.packed_all.at[:, :, :, pl.ds(3 * D, 768)], s.w.at[0])
        self.load(25, s.packed_all.at[:, :, :, pl.ds(3 * D + 768, WIDTH)], s.w.at[1, :, :, :, pl.ds(0, WIDTH)])
        for k in range(3):
            self.load((41, k), s.o_qkv.at[k], f.qkv.at[k])
        self.load_soft(f, 0)
        self.load(42, s.o_normed, f.normed)
        self.load(43, s.o_scale, f.scale)
        self.load(44, s.cos, f.cos)
        self.load(45, s.sin, f.sin)
        self.wait(24, 25)
        joined = s.joined
        s.acc[...] = mm_nt(joined[:, 3 * D : 3 * D + 768], flat(s.w[0]))
        s.acc[...] += mm_nt(joined[:, 3 * D + 768 :], flat(s.w[1, :, :, :, 0:WIDTH]))
        f.back[...] = s.acc[...].astype(BF16)
        self.wait((41, 0), (41, 1), (41, 2))
        for k in range(ATTN_STEPS):
            self.attend(f, k)
            reduce.advance()
        self.wait(42, 43, 44, 45)
        self.head_back(f, 0)
        reduce.advance()
        self.head_back(f, 1)


    def load_entry(self, k):
        s = self.s
        width = 768 if k < 4 else WIDTH
        self.load(
            (51, k),
            s.packed_all.at[:, :, :, pl.ds(k * 768, width)],
            s.w.at[k % 2, :, :, :, pl.ds(0, width)],
        )

    def entry(self, k):
        s = self.s
        width = 768 if k < 4 else WIDTH
        self.load_entry(k)
        self.wait((51, k))
        if k < 4:
            self.load_entry(k + 1)
        product = mm_nt(s.joined[:, k * 768 : k * 768 + width], flat(s.w[k % 2, :, :, :, 0:width]))
        if k == 0:
            s.acc[...] = product
        else:
            s.acc[...] += product

    def grad_packed(self, f, jj):
        s = self.s
        self.wait((61, jj))
        right = s.right.at[jj % 2]

        @pl.loop(0, 4)
        def _(k):
            rows = pl.ds(pl.multiple_of(k * 288, 32), 288)
            for half in range(2):
                j = 2 * jj + half
                left = s.left if j < 3 else f.left
                total = mm(left[rows, :], right[:, half * WIDTH : (half + 1) * WIDTH])
                s.held[j, k] = total.astype(BF16).reshape(2, 144, WIDTH)

        self.reduce.produced(2 * jj)
        self.reduce.produced(2 * jj + 1)

    def load_right(self, jj):
        self.load((61, jj), self.s.r_packed.at[:, pl.ds(768 * jj, 768)], self.s.right.at[jj % 2])

    def last(self, f):
        s, reduce = self.s, self.reduce
        mine = pl.ds(pl.multiple_of(self.c * LANE_HALF, 128), LANE_HALF)
        theirs = pl.ds(pl.multiple_of((1 - self.c) * LANE_HALF, 128), LANE_HALF)
        self.to_sibling((71, 0), s.joined.at[:, theirs], s.r_packed.at[pl.ds(TOK, TOK)])
        self.load(71, s.joined.at[:, mine], s.r_packed.at[pl.ds(0, TOK)])
        self.load(72, s.o_lhs.at[0], s.left)
        self.load(73, s.o_lhs.at[self.c], f.left)
        self.load(74, s.tokens, f.tokens)
        self.load(76, s.mod_weight, f.mod_w)
        reduce.advance()
        self.entry(0)
        self.remote[71, 0].wait_recv()
        self.wait(71, 72, 73)
        self.load_right(0)
        self.load_right(1)
        for jj in range(3):
            reduce.free(6 + 2 * jj)
            reduce.free(7 + 2 * jj)
            self.grad_packed(f, jj)
            if jj == 0:
                self.load_right(2)
            self.entry(1 + jj)
            reduce.advance()
        self.entry(4)
        reduce.advance()
        self.wait(74)

        @pl.loop(0, TOK // TILE)
        def _(i):
            rows = rows_of(i, TILE)
            image = i // (SEQ // TILE)
            mod, d_mod = s.mod, s.d_mod
            normed, inverse = norm_rows(f.tokens[rows, :].astype(F32))
            d_entry = s.acc[rows, :]
            d_mod[image, 0:1, :] += jnp.sum(d_entry, axis=0, keepdims=True)
            d_mod[image, 1:2, :] += jnp.sum(d_entry * normed, axis=0, keepdims=True)
            back = norm_back(normed, inverse, d_entry * (1.0 + mod[image, 1:2, :]))
            s.d_residual[rows, :] += back

        self.load(75, s.d_residual, s.g_tokens)
        self.modulation(f)
        reduce.finish()
        self.wait(75)
        self.remote[71, 0].wait_send()

    def modulation(self, f):
        s, reduce = self.s, self.reduce
        z, x, y, c = spot = (self.z, self.x, self.y, self.c)
        s.back_flat[...] = jnp.zeros_like(s.back_flat)
        for image in range(2):
            for k in range(6):
                row = s.gate_b[image, 0:1, :] if k == 5 else s.d_mod[image, k : k + 1, :]
                rounded = row.astype(BF16).astype(F32)
                s.back_flat[image : image + 1, k * D : (k + 1) * D] = rounded
        for m in range(4):
            s.back_parts[m] = s.back_flat[:, m * MOD_PART : (m + 1) * MOD_PART]
        group = Group(
            spot, s.back_parts, s.back_got_c, s.back_got_y, s.back_blocks, s.back_send, s.back_recv
        )
        group.start()
        reduce.advance()
        group.across_y()
        reduce.advance()
        group.finish()
        for m in range(4):
            s.back[2 * m : 2 * m + 2, :] = s.back_blocks[m, 0:2, :]
        x_peer = device(z, 1 - x, y, c)
        send(s.back, s.back_got_x, s.wide_send.at[0], s.wide_recv.at[0], x_peer)
        self.wait(76)
        partial = mm(s.back[...].astype(BF16), f.mod_w[...])
        s.cond_parts[...] = jnp.zeros_like(s.cond_parts)
        for m in range(4):
            s.cond_parts[m, 0:2, :] = partial[2 * m : 2 * m + 2, :]
        cond = Group(
            spot, s.cond_parts, s.cond_got_c, s.cond_got_y, s.cond_blocks, s.cond_send, s.cond_recv
        )
        cond.start()
        drain(s.back, s.wide_recv.at[0])
        own, other = s.back[...], s.back_got_x[...]
        low = jnp.where(x == 0, own, other)
        high = jnp.where(x == 0, other, own)
        s.back_all[z] = jnp.concatenate([low, high], axis=0).astype(BF16)
        block = s.back_all.at[z]
        for step in (1, 3, 2):
            peer = device((z + step) % 4, x, y, c)
            send(block, block, s.wide_send.at[1], s.wide_recv.at[1], peer)
        cond.across_y()
        reduce.advance()
        cond.finish()
        total = s.cond_blocks[0] + s.cond_blocks[1] + s.cond_blocks[2] + s.cond_blocks[3]
        s.o_cond[...] = total
        reduce.advance()
        drain(s.back_all.at[pl.ds(0, 3)], s.wide_recv.at[1])
        self.load(77, s.back_all, s.o_back)
        drain(s.back, s.wide_send.at[0])
        drain(s.back_all.at[pl.ds(0, 3)], s.wide_send.at[1])
        self.wait(77)


class BackwardInputs(NamedTuple):
    packed_all: object
    gate_all: object
    up_all: object
    down_all: object
    o_branch: object
    o_lhs: object
    o_hidden: object
    o_qkv: object
    o_normed: object
    o_scale: object
    o_soft: object
    o_attended: object
    o_residual: object
    o_active: object
    tokens: object
    cot: object
    cos: object
    sin: object
    mod: object
    spread: object
    widen: object
    gate_b: object
    mod_weight: object


BACKWARD_OUTPUTS = dict(
    g_packed=((144, 4 * D), BF16),
    g_gate=((144, 8 * WIDTH), BF16),
    g_up=((144, 8 * WIDTH), BF16),
    g_down=((384, D), BF16),
    g_tokens=((TOK, D), F32),
    r_ff=((4, 2 * TOK, 2 * WIDTH), BF16),
    r_packed=((2 * TOK, LANE_HALF), BF16),
    o_back=((4, 16, MOD_PART), BF16),
    o_cond=((8, D), F32),
)


def vmem(*shape, kind=BF16):
    return pltpu.VMEM(shape, kind)


def backward_scratch():
    return dict(
        held=vmem(8, 4, 2, 144, WIDTH),
        held_big=vmem(3, 4, 2, 192, WIDTH),
        got_y=vmem(14, 4, 2, 48, WIDTH),
        got_y_big=vmem(3, 4, 2, 48, WIDTH),
        got_x=vmem(14, 4, 112, WIDTH),
        got_x_big=vmem(3, 4, 144, WIDTH),
        got_z=vmem(14, 3, 112, WIDTH),
        got_z_big=vmem(3, 3, 144, WIDTH),
        got_f=vmem(14, 112, WIDTH),
        got_f_big=vmem(3, 144, WIDTH),
        w=vmem(2, 4, 2, 144, 2 * WIDTH),
        acc=vmem(TOK, D, kind=F32),
        d_residual=vmem(TOK, D, kind=F32),
        joined=vmem(TOK, 4 * D),
        left=vmem(D, 2 * TOK),
        right=vmem(2, 2 * TOK, 2 * WIDTH),
        d_mod=vmem(2, 8, D, kind=F32),
        back_flat=vmem(8, 4 * MOD_PART, kind=F32),
        back_parts=group_scratch(MOD_PART)[0],
        back_got_c=group_scratch(MOD_PART)[1],
        back_got_y=group_scratch(MOD_PART)[2],
        back_blocks=group_scratch(MOD_PART)[3],
        back_send=group_scratch(MOD_PART)[4],
        back_recv=group_scratch(MOD_PART)[5],
        cond_parts=group_scratch(D)[0],
        cond_got_c=group_scratch(D)[1],
        cond_got_y=group_scratch(D)[2],
        cond_blocks=group_scratch(D)[3],
        cond_send=group_scratch(D)[4],
        cond_recv=group_scratch(D)[5],
        back=vmem(8, MOD_PART, kind=F32),
        back_got_x=vmem(8, MOD_PART, kind=F32),
        back_all=vmem(4, 16, MOD_PART),
        wide_send=pltpu.SemaphoreType.DMA((2,)),
        wide_recv=pltpu.SemaphoreType.DMA((2,)),
        scatter_send=pltpu.SemaphoreType.DMA((5, N_PIECES)),
        scatter_recv=pltpu.SemaphoreType.DMA((5, N_PIECES)),
        store_sems=pltpu.SemaphoreType.DMA((N_PIECES,)),
        load_sems=pltpu.SemaphoreType.DMA((96,)),
        pair_send=pltpu.SemaphoreType.DMA((8,)),
        pair_recv=pltpu.SemaphoreType.DMA((8,)),
    )


def backward_kernel(*refs):
    names = BackwardInputs._fields + tuple(BACKWARD_OUTPUTS) + tuple(backward_scratch())
    s = SimpleNamespace(**dict(zip(names, refs, strict=True)))
    spot = place()
    greet(neighbours(*spot))
    reduce = Reduce(s, spot)
    work = Backward(s, spot, reduce)

    def scoped(act, before=None, **shapes):
        def run(*held):
            f = SimpleNamespace(**dict(zip(shapes, held, strict=True)))
            if before is not None:
                before(f)
            act(f)

        pl.run_scoped(run, *shapes.values())

    def first_loads(f):
        work.load(11, s.o_hidden, f.hidden)
        work.load(12, s.o_branch, f.branch)
        work.load_ff(f, 0)

    scoped(
        work.feed_forward,
        first_loads,
        hidden=vmem(8, 192, 2 * TOK),
        branch=vmem(2 * TOK, D),
        w_down=vmem(2, 384, D),
        active=vmem(2, 2, TOK, WIDTH),
        wide=vmem(TOK, WIDTH, kind=F32),
        steep=vmem(2, TOK, 2 * WIDTH),
    )
    scoped(work.middle, cot=vmem(TOK, D), attended=vmem(TOK, D))
    reduce.advance()
    scoped(
        work.attention,
        qkv=vmem(3, TOK, D),
        normed=vmem(2, TOK, D),
        scale=vmem(2, TOK, 128, kind=F32),
        soft=vmem(2, H // ATTN_STEPS, 2, SEQ, SEQ),
        back=vmem(TOK, D),
        cos=vmem(SEQ, D, kind=F32),
        sin=vmem(SEQ, D, kind=F32),
    )
    scoped(work.last, left=vmem(D, 2 * TOK), tokens=vmem(TOK, D), mod_w=vmem(MOD_PART, D))


def backward_pass(f, tokens, cotangent, mod_weight, tables):
    hbm = pl.BlockSpec(memory_space=pl.ANY)
    inside = pl.BlockSpec(memory_space=pltpu.VMEM)
    cosine, sine, spread, widen = tables
    given = BackwardInputs(
        f.packed_all,
        f.gate_all,
        f.up_all,
        f.down_all,
        f.o_branch,
        f.o_lhs,
        f.o_hidden,
        f.o_qkv,
        f.o_normed,
        f.o_scale,
        f.o_soft,
        f.o_attended,
        f.o_residual,
        f.o_active,
        tokens,
        cotangent,
        cosine,
        sine,
        f.o_mod,
        spread,
        widen,
        f.o_gate_b,
        mod_weight,
    )
    out = pl.pallas_call(
        backward_kernel,
        out_shape=[jax.ShapeDtypeStruct(*spec) for spec in BACKWARD_OUTPUTS.values()],
        in_specs=[hbm] * 18 + [inside] * 4 + [hbm],
        out_specs=[hbm] * 8 + [inside],
        scratch_shapes=list(backward_scratch().values()),
        name="backward_pass",
        compiler_params=pltpu.CompilerParams(
            collective_id=1, has_side_effects=True, vmem_limit_bytes=60 << 20
        ),
    )(*given)
    return SimpleNamespace(**dict(zip(BACKWARD_OUTPUTS, out)))


def body_general(
    tokens,
    condition,
    timestep,
    qkv_weight,
    out_weight,
    gate_weight,
    up_weight,
    down_weight,
    mod_weight,
    mod_bias,
    cotangent,
):
    gathered = (
        lax.all_gather(qkv_weight, "dp", axis=0, tiled=True),
        lax.all_gather(out_weight, "dp", axis=0, tiled=True),
        lax.all_gather(gate_weight, "dp", axis=0, tiled=True),
        lax.all_gather(up_weight, "dp", axis=0, tiled=True),
        lax.all_gather(down_weight, "dp", axis=0, tiled=True),
    )
    cond_total = condition.astype(jnp.float32) + embed_steps(timestep)
    acted_cond = jax.nn.silu(cond_total).astype(jnp.bfloat16)
    acted_group = lax.all_gather(acted_cond, "mod", axis=0, tiled=True)
    mod_part = (
        jnp.dot(acted_group, mod_weight, preferred_element_type=jnp.float32)
        + mod_bias.astype(jnp.float32)
    ).astype(jnp.bfloat16)
    modulation = lax.all_to_all(mod_part, "mod", split_axis=0, concat_axis=1, tiled=True).astype(
        jnp.float32
    )
    tables = rope_tables()
    per_micro = tokens.shape[0] // MICRO
    outputs = []
    token_grads = []
    mod_grads = []
    kept = []
    for micro_step in range(MICRO):
        start_row = micro_step * per_micro
        output, d_tokens, d_modulation, factors = layer_pass(
            tokens[start_row : start_row + per_micro],
            modulation[start_row : start_row + per_micro],
            cotangent[start_row : start_row + per_micro],
            gathered,
            tables,
        )
        outputs.append(output)
        token_grads.append(d_tokens)
        mod_grads.append(d_modulation)
        kept.append(factors)
    joined = [jnp.concatenate([factors[number] for factors in kept], axis=0) for number in range(9)]
    (
        entry_first,
        d_projected,
        combined,
        d_attended,
        entry_second,
        d_gate_proj,
        d_up_proj,
        hidden,
        d_branch,
    ) = joined
    grad_qkv = jnp.einsum(
        "bsd,bse->de", entry_first, d_projected, preferred_element_type=jnp.float32
    )
    grad_proj = jnp.einsum("bsd,bse->de", combined, d_attended, preferred_element_type=jnp.float32)
    grad_gate = jnp.einsum(
        "bsd,bsf->df", entry_second, d_gate_proj, preferred_element_type=jnp.float32
    )
    grad_up = jnp.einsum("bsd,bsf->df", entry_second, d_up_proj, preferred_element_type=jnp.float32)
    grad_down = jnp.einsum("bsf,bsd->fd", hidden, d_branch, preferred_element_type=jnp.float32)
    totals = (grad_qkv, grad_proj, grad_gate, grad_up, grad_down)
    output_tokens = jnp.concatenate(outputs, axis=0)
    grad_tokens = jnp.concatenate(token_grads, axis=0)
    mod_grad = jnp.concatenate(mod_grads, axis=0)
    mod_back = lax.all_to_all(mod_grad, "mod", split_axis=1, concat_axis=0, tiled=True)
    grad_mod_part = jnp.einsum(
        "id,ic->dc", acted_group, mod_back, preferred_element_type=jnp.float32
    )
    bias_part = jnp.sum(mod_back.astype(jnp.float32), axis=0)
    acted_grad_part = jnp.einsum(
        "ic,dc->id", mod_back, mod_weight, preferred_element_type=jnp.float32
    )
    acted_grad = lax.psum_scatter(
        acted_grad_part.astype(jnp.bfloat16), "mod", scatter_dimension=0, tiled=True
    ).astype(jnp.float32)
    sigma_cond = jax.nn.sigmoid(cond_total)
    grad_condition = acted_grad * sigma_cond * (1.0 + cond_total * (1.0 - sigma_cond))
    grad_bias = lax.psum(bias_part, "dp")
    count = lax.axis_size("dp")
    arrays = totals + (grad_mod_part,)
    shapes = [array.shape for array in arrays]
    flat = lax.psum_scatter(pack_rows(arrays, count), "dp", scatter_dimension=0, tiled=True)
    summed = unpack_rows(flat, shapes, count)
    finished = (
        lax.psum(summed[0].astype(jnp.bfloat16), "mod").astype(jnp.float32),
        lax.psum(summed[1].astype(jnp.bfloat16), "mod").astype(jnp.float32),
        lax.psum(summed[2].astype(jnp.bfloat16), "mod").astype(jnp.float32),
        lax.psum(summed[3].astype(jnp.bfloat16), "mod").astype(jnp.float32),
        lax.psum(summed[4].astype(jnp.bfloat16), "mod").astype(jnp.float32),
    )
    grad_mod = summed[5]
    return (
        output_tokens,
        grad_tokens,
        grad_condition,
        finished[0],
        finished[1],
        finished[2],
        finished[3],
        finished[4],
        grad_mod,
        grad_bias,
    )


def body_fast(
    tokens,
    condition,
    timestep,
    qkv_weight,
    out_weight,
    gate_weight,
    up_weight,
    down_weight,
    mod_weight,
    mod_bias,
    cotangent,
):
    packed = jnp.concatenate([qkv_weight, out_weight], axis=1)
    cond_total = condition.astype(jnp.float32) + embed_steps(timestep)
    acted_cond = jax.nn.silu(cond_total).astype(jnp.bfloat16)
    acted_rows = acted_cond.astype(F32)
    acted_slim = jnp.pad(acted_rows.reshape(-1, 128), ((0, 6), (0, 0)))
    flat_tokens, flat_cotangent = tokens.reshape(TOK, D), cotangent.reshape(TOK, D)
    tables = head_tables()
    f = forward_pass(
        packed,
        gate_weight,
        up_weight,
        down_weight,
        flat_tokens,
        flat_cotangent,
        jnp.pad(acted_rows, ((0, 6), (0, 0))),
        mod_bias.astype(F32).reshape(1, -1),
        mod_weight.T,
        acted_slim,
        *tables,
    )
    b = backward_pass(f, flat_tokens, flat_cotangent, mod_weight.T, tables)
    acted_all = f.acted_all.reshape(32, -1)[:, : 2 * D].reshape(64, D).astype(BF16)
    back_all = b.o_back.reshape(64, -1)
    rows = D // 8
    acted_part = lax.dynamic_slice_in_dim(acted_all, lax.axis_index("dp") * rows, rows, 1)
    grad_mod = jnp.einsum("id,ic->dc", acted_part, back_all, preferred_element_type=jnp.float32)
    grad_bias = jnp.sum(back_all.astype(jnp.float32), axis=0)
    sigma_cond = jax.nn.sigmoid(cond_total)
    grad_condition = b.o_cond[:2] * sigma_cond * (1.0 + cond_total * (1.0 - sigma_cond))
    return (
        f.o_result.reshape(tokens.shape),
        b.g_tokens.reshape(tokens.shape),
        grad_condition,
        b.g_packed[:, : 3 * D].astype(F32),
        b.g_packed[:, 3 * D :].astype(F32),
        b.g_gate.astype(F32),
        b.g_up.astype(F32),
        b.g_down.astype(F32),
        grad_mod,
        grad_bias,
    )


def pick_body(mesh):
    if dict(mesh.shape) == {"dp": 8, "mod": 4}:
        return body_fast
    return body_general


def solution(mesh):
    in_specs = (
        P(("dp", "mod"), None, None),
        P(("dp", "mod"), None),
        P(("dp", "mod")),
        P("dp", None),
        P("dp", None),
        P("dp", None),
        P("dp", None),
        P("dp", None),
        P(None, "mod"),
        P("mod"),
        P(("dp", "mod"), None, None),
    )
    out_specs = (
        P(("dp", "mod"), None, None),
        P(("dp", "mod"), None, None),
        P(("dp", "mod"), None),
        P("dp", None),
        P("dp", None),
        P("dp", None),
        P("dp", None),
        P("dp", None),
        P("dp", "mod"),
        P("mod"),
    )
    return jax.shard_map(pick_body(mesh), mesh=mesh, in_specs=in_specs, out_specs=out_specs, check_vma=False)
```

```python
import math
from types import SimpleNamespace
from typing import NamedTuple

import jax
import jax.numpy as jnp
from jax import lax
import numpy as np
from jax.experimental import pallas as pl
from jax.experimental.pallas import tpu as pltpu
from jax.sharding import PartitionSpec as P

D = 1152
H = 16
HD = 72
GRID = 16
SEQ = 256
MICRO = 2


EPSILON = 1e-06


def norm_rows(field):
    scale_inv = lax.rsqrt(jnp.mean(field * field, axis=-1, keepdims=True) + EPSILON)
    return (field * scale_inv, scale_inv)


def norm_back(normed, scale_inv, gradient):
    return scale_inv * (gradient - normed * jnp.mean(gradient * normed, axis=-1, keepdims=True))


def embed_steps(timestep):
    half_width = D // 2
    frequency = jnp.exp(-math.log(10000.0) * jnp.arange(half_width, dtype=jnp.float32) / half_width)
    angles = timestep.astype(jnp.float32)[:, None] * frequency[None, :]
    return jnp.concatenate([jnp.cos(angles), jnp.sin(angles)], axis=1)


def rope_tables():
    quarter = HD // 4
    frequency = jnp.exp(-math.log(10000.0) * jnp.arange(quarter, dtype=jnp.float32) / quarter)
    position = jnp.arange(SEQ)
    row_index = (position // GRID).astype(jnp.float32)
    col_index = (position % GRID).astype(jnp.float32)
    angles = jnp.stack(
        [row_index[:, None] * frequency[None, :], col_index[:, None] * frequency[None, :]], axis=1
    )
    return (jnp.cos(angles), jnp.sin(angles))


def rotate(field, cosine_table, sine_table):
    leading = field.shape[:-1]
    quarters = field.reshape(leading + (2, 2, HD // 4))
    first_half = quarters[..., 0, :]
    second_half = quarters[..., 1, :]
    cosine_rows = cosine_table[:, None]
    sine_rows = sine_table[:, None]
    turned_first = first_half * cosine_rows - second_half * sine_rows
    turned_second = first_half * sine_rows + second_half * cosine_rows
    return jnp.stack([turned_first, turned_second], axis=-2).reshape(field.shape)


def pack_rows(arrays, count):
    return jnp.concatenate([array.reshape(count, -1) for array in arrays], axis=1).reshape(-1)


def unpack_rows(flat, shapes, count):
    pieces = []
    offset = 0
    for rows_all, columns in shapes:
        rows = rows_all // count
        pieces.append(flat[offset : offset + rows * columns].reshape(rows, columns))
        offset = offset + rows * columns
    return pieces


def layer_pass(block_in, mod_rows, cotangent, weights, tables):
    qkv_full, proj_full, gate_full, up_full, down_full = weights
    cosine_table, sine_table = tables
    images = block_in.shape[0]
    shift_first, scale_first, gate_first, shift_second, scale_second, gate_second = [
        mod_rows[:, None, number * D : (number + 1) * D] for number in range(6)
    ]
    heads_shape = (images, SEQ, H, HD)
    factor = 1.0 / math.sqrt(HD)
    inputs = block_in.astype(jnp.float32)
    normed_first, inv_first = norm_rows(inputs)
    entry_first = (normed_first * (1.0 + scale_first) + shift_first).astype(jnp.bfloat16)
    projected = jnp.einsum("bsd,de->bse", entry_first, qkv_full, preferred_element_type=jnp.float32)
    q_normed, q_inv = norm_rows(projected[..., :D].reshape(heads_shape))
    k_normed, k_inv = norm_rows(projected[..., D : 2 * D].reshape(heads_shape))
    queries = rotate(q_normed, cosine_table, sine_table).astype(jnp.bfloat16)
    keys_rot = rotate(k_normed, cosine_table, sine_table).astype(jnp.bfloat16)
    values = projected[..., 2 * D :].reshape(heads_shape).astype(jnp.bfloat16)
    scores = (
        jnp.einsum("bqhd,bkhd->bhqk", queries, keys_rot, preferred_element_type=jnp.float32)
        * factor
    )
    highest = jnp.max(scores, axis=-1, keepdims=True)
    log_total = highest + jnp.log(jnp.sum(jnp.exp(scores - highest), axis=-1, keepdims=True))
    weights_soft = jnp.exp(scores - log_total).astype(jnp.bfloat16)
    combined = (
        jnp.einsum("bhqk,bkhd->bqhd", weights_soft, values, preferred_element_type=jnp.float32)
        .reshape(images, SEQ, D)
        .astype(jnp.bfloat16)
    )
    attended = jnp.einsum("bsd,de->bse", combined, proj_full, preferred_element_type=jnp.float32)
    residual = inputs + gate_first * attended
    normed_second, inv_second = norm_rows(residual)
    entry_second = (normed_second * (1.0 + scale_second) + shift_second).astype(jnp.bfloat16)
    gate_proj = jnp.einsum(
        "bsd,df->bsf", entry_second, gate_full, preferred_element_type=jnp.float32
    )
    up_proj = jnp.einsum("bsd,df->bsf", entry_second, up_full, preferred_element_type=jnp.float32)
    sigma_gate = jax.nn.sigmoid(gate_proj)
    activated = gate_proj * sigma_gate
    hidden = (activated * up_proj).astype(jnp.bfloat16)
    branch = jnp.einsum("bsf,fd->bsd", hidden, down_full, preferred_element_type=jnp.float32)
    output = (residual + gate_second * branch).astype(jnp.bfloat16)
    grad_out = cotangent.astype(jnp.float32)
    d_gate_second = jnp.sum(grad_out * branch, axis=1)
    d_branch = (gate_second * grad_out).astype(jnp.bfloat16)
    d_hidden = jnp.einsum("bsd,fd->bsf", d_branch, down_full, preferred_element_type=jnp.float32)
    d_gate_proj = (d_hidden * up_proj * sigma_gate * (1.0 + gate_proj * (1.0 - sigma_gate))).astype(
        jnp.bfloat16
    )
    d_up_proj = (d_hidden * activated).astype(jnp.bfloat16)
    d_entry_second = jnp.einsum(
        "bsf,df->bsd", d_gate_proj, gate_full, preferred_element_type=jnp.float32
    )
    d_entry_second = d_entry_second + jnp.einsum(
        "bsf,df->bsd", d_up_proj, up_full, preferred_element_type=jnp.float32
    )
    d_shift_second = jnp.sum(d_entry_second, axis=1)
    d_scale_second = jnp.sum(d_entry_second * normed_second, axis=1)
    d_residual = grad_out + norm_back(
        normed_second, inv_second, d_entry_second * (1.0 + scale_second)
    )
    d_gate_first = jnp.sum(d_residual * attended, axis=1)
    d_attended = (gate_first * d_residual).astype(jnp.bfloat16)
    d_combined = (
        jnp.einsum("bse,de->bsd", d_attended, proj_full, preferred_element_type=jnp.float32)
        .astype(jnp.bfloat16)
        .reshape(heads_shape)
    )
    scores_again = (
        jnp.einsum("bqhd,bkhd->bhqk", queries, keys_rot, preferred_element_type=jnp.float32)
        * factor
    )
    recomputed = jnp.exp(scores_again - log_total)
    d_weights = jnp.einsum(
        "bqhd,bkhd->bhqk", d_combined, values, preferred_element_type=jnp.float32
    )
    d_scores = (
        recomputed * (d_weights - jnp.sum(recomputed * d_weights, axis=-1, keepdims=True))
    ).astype(jnp.bfloat16)
    d_values = jnp.einsum(
        "bhqk,bqhd->bkhd", weights_soft, d_combined, preferred_element_type=jnp.float32
    ).astype(jnp.bfloat16)
    d_queries = (
        (
            jnp.einsum("bhqk,bkhd->bqhd", d_scores, keys_rot, preferred_element_type=jnp.float32)
            * factor
        )
        .astype(jnp.bfloat16)
        .astype(jnp.float32)
    )
    d_keys = (
        (
            jnp.einsum("bhqk,bqhd->bkhd", d_scores, queries, preferred_element_type=jnp.float32)
            * factor
        )
        .astype(jnp.bfloat16)
        .astype(jnp.float32)
    )
    d_q_raw = norm_back(q_normed, q_inv, rotate(d_queries, cosine_table, -sine_table))
    d_k_raw = norm_back(k_normed, k_inv, rotate(d_keys, cosine_table, -sine_table))
    flat_shape = (images, SEQ, D)
    d_projected = jnp.concatenate(
        [
            d_q_raw.reshape(flat_shape),
            d_k_raw.reshape(flat_shape),
            d_values.astype(jnp.float32).reshape(flat_shape),
        ],
        axis=-1,
    ).astype(jnp.bfloat16)
    d_entry_first = jnp.einsum(
        "bse,de->bsd", d_projected, qkv_full, preferred_element_type=jnp.float32
    )
    d_shift_first = jnp.sum(d_entry_first, axis=1)
    d_scale_first = jnp.sum(d_entry_first * normed_first, axis=1)
    d_tokens = d_residual + norm_back(normed_first, inv_first, d_entry_first * (1.0 + scale_first))
    d_modulation = jnp.concatenate(
        [d_shift_first, d_scale_first, d_gate_first, d_shift_second, d_scale_second, d_gate_second],
        axis=1,
    ).astype(jnp.bfloat16)
    factors = (
        entry_first,
        d_projected,
        combined,
        d_attended,
        entry_second,
        d_gate_proj,
        d_up_proj,
        hidden,
        d_branch,
    )
    return (output, d_tokens, d_modulation, factors)


MESH = pl.DeviceIdType.MESH
WIDTH = 384
LANE_HALF = 2304
FF_HALF = 1536
BF16 = jnp.bfloat16
F32 = jnp.float32


def place():
    dp = lax.axis_index("dp")
    mod = lax.axis_index("mod")
    return dp // 2, dp % 2, mod // 2, mod % 2


def device(z, x, y, c):
    return (z * 2 + x, y * 2 + c)


def greet(peers):
    barrier = pltpu.get_barrier_semaphore()
    for peer in peers:
        pl.semaphore_signal(barrier, inc=1, device_id=peer, device_id_type=MESH)
    pl.semaphore_wait(barrier, len(peers))


def neighbours(z, x, y, c):
    around = [device((z + step) % 4, x, y, c) for step in (1, 2, 3)]
    return around + [device(z, 1 - x, y, c), device(z, x, 1 - y, c), device(z, x, y, 1 - c)]


def send(source, target, send_sem, recv_sem, peer):
    pltpu.make_async_remote_copy(
        src_ref=source,
        dst_ref=target,
        send_sem=send_sem,
        recv_sem=recv_sem,
        device_id=peer,
        device_id_type=MESH,
    ).start()


def drain(window, sem):
    pltpu.make_async_copy(window, window, sem).wait()


class Piece:
    def __init__(self, source, target, row, rows, column, edge):
        self.source, self.target = source, target
        self.row, self.rows, self.column, self.edge = row, rows, column, edge


def gather_pieces(refs, c, edge_of):
    packed, gate, up, down, packed_all, gate_all, up_all, down_all = refs
    pieces = []
    for j in range(6):
        pieces.append(Piece(packed, packed_all, 0, 144, c * LANE_HALF + j * WIDTH, edge_of(144, j)))
    for j in range(4):
        pieces.append(Piece(gate, gate_all, 0, 144, c * FF_HALF + j * WIDTH, edge_of(144, j)))
        pieces.append(Piece(up, up_all, 0, 144, c * FF_HALF + j * WIDTH, edge_of(144, j)))
    for j in range(3):
        pieces.append(Piece(down, down_all, c * 192, 192, j * WIDTH, edge_of(192, j)))
    return pieces


class Gather:
    def __init__(self, refs, sems, spot, stages):
        self.z, self.x, self.y, self.c = spot
        self.stages = stages
        self.pieces = gather_pieces(refs, self.c, lambda rows, j: 64 if rows == 144 and j % 3 == 2 else rows // 3)
        self.send_sems, self.recv_sems, self.own_sems = sems
        self.refs = refs

    def columns(self, piece):
        return pl.ds(pl.multiple_of(piece.column, 128), WIDTH)

    def part(self, piece):
        keep = piece.rows - piece.edge
        return pl.ds(pl.multiple_of(piece.row + self.y * piece.edge, 16), keep), keep

    def mine(self, piece):
        return pl.ds(pl.multiple_of(piece.row + self.y * (piece.rows - piece.edge), 16), piece.edge)

    def own_copies(self):
        for k in range(4):
            pltpu.make_async_copy(self.refs[k], self.stages[k], self.own_sems.at[k]).start()

    def own_stores(self):
        for k in range(4):
            drain(self.stages[k], self.own_sems.at[k])
            pltpu.make_async_copy(
                self.stages[k], self.refs[4 + k].at[self.z, self.x], self.own_sems.at[k]
            ).start()

    def own_done(self):
        for k in range(4):
            drain(self.stages[k], self.own_sems.at[k])

    def start_z(self, t):
        p = self.pieces[t]
        rows, _ = self.part(p)
        here = p.source.at[rows, self.columns(p)]
        there = p.target.at[self.z, self.x, rows, self.columns(p)]
        for step in (1, 3, 2):
            peer = device((self.z + step) % 4, self.x, self.y, self.c)
            send(here, there, self.send_sems.at[0, t], self.recv_sems.at[0, t], peer)
        peer = device(self.z, 1 - self.x, self.y, self.c)
        send(here, there, self.send_sems.at[1, t], self.recv_sems.at[1, t], peer)

    def start_x(self, t):
        p = self.pieces[t]
        rows, keep = self.part(p)
        columns = self.columns(p)
        drain(p.target.at[pl.ds(0, 3), 0, pl.ds(0, keep), pl.ds(0, WIDTH)], self.recv_sems.at[0, t])
        x_peer = device(self.z, 1 - self.x, self.y, self.c)
        y_peer = device(self.z, self.x, 1 - self.y, self.c)
        for step in (1, 3, 2):
            other = (self.z + step) % 4
            block = p.target.at[other, self.x, rows, columns]
            send(block, block, self.send_sems.at[1, t], self.recv_sems.at[1, t], x_peer)
        for step in (1, 3, 2):
            other = (self.z + step) % 4
            block = p.target.at[other, self.x, self.mine(p), columns]
            send(block, block, self.send_sems.at[2, t], self.recv_sems.at[2, t], y_peer)

    def start_y(self, t):
        p = self.pieces[t]
        _, keep = self.part(p)
        columns = self.columns(p)
        drain(p.target.at[:, 0, pl.ds(0, keep), pl.ds(0, WIDTH)], self.recv_sems.at[1, t])
        y_peer = device(self.z, self.x, 1 - self.y, self.c)
        block = p.target.at[:, 1 - self.x, self.mine(p), columns]
        send(block, block, self.send_sems.at[2, t], self.recv_sems.at[2, t], y_peer)

    def start_c(self, t):
        p = self.pieces[t]
        columns = self.columns(p)
        half = pl.ds(pl.multiple_of(p.row, 16), p.rows)
        self.drain_seven(p.edge, self.recv_sems.at[2, t])
        peer = device(self.z, self.x, self.y, 1 - self.c)
        block = p.target.at[:, 1 - self.x, half, columns]
        send(block, block, self.send_sems.at[3, t], self.recv_sems.at[3, t], peer)
        for step in (1, 2, 3):
            block = p.target.at[(self.z + step) % 4, self.x, half, columns]
            send(block, block, self.send_sems.at[3, t], self.recv_sems.at[3, t], peer)

    def arrived(self, t):
        self.drain_seven(self.pieces[t].rows, self.recv_sems.at[3, t])

    def drain_seven(self, rows, sem):
        high = 96 if rows > 144 else rows
        drain(self.refs[4].at[pl.ds(0, rows // high), 0, pl.ds(0, high), pl.ds(0, 7 * WIDTH)], sem)

    def sent_z(self, t):
        p = self.pieces[t]
        _, keep = self.part(p)
        drain(p.target.at[pl.ds(0, 3), 0, pl.ds(0, keep), pl.ds(0, WIDTH)], self.send_sems.at[0, t])

    def sent_rest(self, t):
        p = self.pieces[t]
        _, keep = self.part(p)
        drain(p.target.at[:, 0, pl.ds(0, keep), pl.ds(0, WIDTH)], self.send_sems.at[1, t])
        for stage, rows in ((2, p.edge), (3, p.rows)):
            self.drain_seven(rows, self.send_sems.at[stage, t])


N_PIECES = 17


class Group:
    def __init__(self, spot, parts, got_c, got_y, blocks, send_sems, recv_sems):
        _, _, self.y, self.c = spot
        z, x, y, c = spot
        self.sibling, self.across = device(z, x, y, 1 - c), device(z, x, 1 - y, c)
        self.parts, self.got_c, self.got_y, self.blocks = parts, got_c, got_y, blocks
        self.send_sems, self.recv_sems = send_sems, recv_sems

    def sems(self, k):
        return self.send_sems.at[k], self.recv_sems.at[k]

    def start(self):
        for y in range(2):
            source = self.parts.at[2 * y + 1 - self.c]
            send(source, self.got_c.at[y], *self.sems(y), self.sibling)

    def across_y(self):
        for y in range(2):
            drain(self.got_c.at[y], self.recv_sems.at[y])
        own = self.parts.at[2 * (1 - self.y) + self.c]
        send(own, self.got_y.at[self.c], *self.sems(2), self.across)
        send(self.got_c.at[1 - self.y], self.got_y.at[1 - self.c], *self.sems(3), self.across)

    def finish(self):
        for k in (2, 3):
            drain(self.got_y.at[k - 2], self.recv_sems.at[k])
        y, c, blocks = self.y, self.c, self.blocks
        blocks[2 * y + c] = self.parts[2 * y + c]
        blocks[2 * y + 1 - c] = self.got_c[y]
        for k in range(2):
            blocks[2 * (1 - y) + k] = self.got_y[k]
        for k in range(4):
            drain(self.got_y.at[k % 2], self.send_sems.at[k])


def group_scratch(columns):
    return [
        pltpu.VMEM((4, 8, columns), F32),
        pltpu.VMEM((2, 8, columns), F32),
        pltpu.VMEM((2, 8, columns), F32),
        pltpu.VMEM((4, 8, columns), F32),
        pltpu.SemaphoreType.DMA((4,)),
        pltpu.SemaphoreType.DMA((4,)),
    ]


MOD_PART = 1728
SLIM = (24, 128)


class Acted:
    def __init__(self, s, spot):
        self.s = s
        self.z, self.x, self.y, self.c = spot

    def hop(self, k, where, peers):
        block = self.s.acted_all.at[where]
        for peer in peers:
            send(block, block, self.s.acted_send.at[k], self.s.acted_recv.at[k], peer)

    def step(self, k):
        z, x, y, c = self.z, self.x, self.y, self.c
        s = self.s
        if k == 0:
            pltpu.make_async_copy(s.acted_slim, s.acted_all.at[z, x, y, c], s.acted_own).start()
            drain(s.acted_slim, s.acted_own)
            self.hop(0, (z, x, y, c), [device(z, x, y, 1 - c)])
        elif k == 1:
            drain(s.acted_slim, s.acted_recv.at[0])
            self.hop(1, (z, x, y), [device(z, x, 1 - y, c)])
        elif k == 2:
            drain(s.acted_all.at[0, 0, 0], s.acted_recv.at[1])
            self.hop(2, (z, x), [device(z, 1 - x, y, c)])
        elif k == 3:
            drain(s.acted_all.at[0, 0], s.acted_recv.at[2])
            self.hop(3, (z,), [device((z + step) % 4, x, y, c) for step in (1, 3, 2)])
        else:
            drain(s.acted_all.at[pl.ds(0, 3)], s.acted_recv.at[3])
            drain(s.acted_slim, s.acted_send.at[0])
            drain(s.acted_all.at[0, 0, 0], s.acted_send.at[1])
            drain(s.acted_all.at[0, 0], s.acted_send.at[2])
            drain(s.acted_all.at[pl.ds(0, 3)], s.acted_send.at[3])


TOK = 512
TILE = 128
HEAD_TILE = 256
ATTN_STEPS = 4


def mm(left, right):
    return lax.dot_general(left, right, (((1,), (0,)), ((), ())), preferred_element_type=F32)


def mm_nt(left, right):
    return lax.dot_general(left, right, (((1,), (1,)), ((), ())), preferred_element_type=F32)


def mm_tn(left, right):
    return lax.dot_general(left, right, (((0,), (0,)), ((), ())), preferred_element_type=F32)


def split(value):
    high = value.astype(BF16)
    return high, (value - high.astype(F32)).astype(BF16)


def mm_split(value, right):
    high, low = split(value)
    return mm(high, right) + mm(low, right)


def partner(value, first):
    width = value.shape[1]
    return jnp.where(first, pltpu.roll(value, width - 18, 1), pltpu.roll(value, 18, 1))


def first_lanes(rows):
    return lax.broadcasted_iota(jnp.int32, (rows, D), 1) % 36 < 18


def rows_of(block, count):
    return pl.ds(pl.multiple_of(block * count, count), count)


def head_window(head):
    base = min(head * HD // 128 * 128, D - 256)
    offset = head * HD - base
    lane = lax.broadcasted_iota(jnp.int32, (SEQ, 256), 1)
    return base, (lane >= offset) & (lane < offset + HD)


def flat(ref_value):
    return ref_value.reshape(-1, ref_value.shape[-1])


class Saves:
    def __init__(self, sems):
        self.sems, self.count, self.open = sems, 0, []

    def local(self, source, target):
        copy = pltpu.make_async_copy(source, target, self.sems.at[self.count])
        self.count += 1
        copy.start()
        self.open.append(copy)
        return copy

    def done(self, copy):
        copy.wait()
        self.open = [other for other in self.open if other is not copy]

    def finish(self):
        for copy in self.open:
            copy.wait()


class Forward:
    def __init__(self, s, spot, gather):
        self.s, self.gather = s, gather
        self.z, self.x, self.y, self.c = spot
        self.saves = Saves(s.save_sems)
        self.pending = {}
        self.remote = []
        self.slots = {}


    def to_sibling(self, source, target):
        k = len(self.remote)
        peer = device(self.z, self.x, self.y, 1 - self.c)
        copy = pltpu.make_async_remote_copy(
            src_ref=source,
            dst_ref=target,
            send_sem=self.s.pair_send.at[k],
            recv_sem=self.s.pair_recv.at[k],
            device_id=peer,
            device_id_type=MESH,
        )
        copy.start()
        self.remote.append(copy)


    def load(self, key, part, source, target):
        if (key, part) not in self.pending:
            copy = pltpu.make_async_copy(source, target, self.s.load_sems.at[len(self.pending)])
            copy.start()
            self.pending[key, part] = copy

    def window(self, ref, column):
        return ref.at[:, :, :, pl.ds(column, WIDTH)]

    def load_qv(self, j):
        packed, target = self.gather.refs[4], self.s.w.at[j % 2, 0]
        self.load(j, 0, self.window(packed, j * WIDTH), self.window(target, 0))
        self.load(j, 1, self.window(packed, LANE_HALF + j * WIDTH), self.window(target, WIDTH))

    def load_ko(self, j):
        packed = self.gather.refs[4]
        self.load(j, 0, self.window(packed, j * WIDTH), self.window(self.s.w.at[j % 2, 0], 0))
        target = self.window(self.s.w_out, (j - 3) * WIDTH)
        self.load(j, 1, self.window(packed, LANE_HALF + j * WIDTH), target)

    def load_ff(self, j):
        for part in range(4):
            which, half = part // 2, part % 2
            target = self.window(self.s.w.at[j % 2, which], half * WIDTH)
            self.load(6 + j, part, self.window(self.gather.refs[5 + which], (j + 4 * half) * WIDTH), target)

    def load_down(self, j):
        self.load(14 + j, 0, self.window(self.gather.refs[7], j * WIDTH), self.s.w_down.at[j % 2])

    def loaded(self, load, j, key):
        load(j)
        for part in range(4):
            if (key, part) in self.pending:
                self.pending[key, part].wait()


    def modulate(self, k):
        s, y, c = self.s, self.y, self.c
        spot = (self.z, self.x, y, c)
        own = s.acted_group.at[2 * y + c]
        pair = s.acted_group.at[pl.ds(2 * y, 2)]
        load = pltpu.make_async_copy(s.mod_weight, s.mod_w, s.acted_own)
        group = Group(
            spot, s.mod_parts, s.mod_got_c, s.mod_got_y, s.mod_blocks, s.mod_send, s.mod_recv
        )
        if k == 0:
            load.start()
            s.acted_group[2 * y + c] = s.acted[...]
            send(own, own, *self.first(0), device(self.z, self.x, y, 1 - c))
        elif k == 1:
            drain(own, s.first_recv.at[0])
            send(pair, pair, *self.first(1), device(self.z, self.x, 1 - y, c))
        elif k == 2:
            load.wait()
            drain(pair, s.first_recv.at[1])
            total = mm_nt(s.acted_group[...].reshape(32, D).astype(BF16), s.mod_w[...]) + s.bias[...]
            s.mod_parts[...] = total.astype(BF16).astype(F32).reshape(4, 8, MOD_PART)
            group.start()
        elif k == 3:
            group.across_y()
        else:
            group.finish()
            for m in range(4):
                s.mod_flat[:, m * MOD_PART : (m + 1) * MOD_PART] = s.mod_blocks[m]
            for image in range(2):
                for m in range(6):
                    row = s.mod_flat[image : image + 1, m * D : (m + 1) * D]
                    s.o_mod[image, m : m + 1, :] = row
            drain(own, s.first_send.at[0])
            drain(pair, s.first_send.at[1])

    def first(self, k):
        return self.s.first_send.at[k], self.s.first_recv.at[k]

    def enter(self):
        s = self.s

        @pl.loop(0, TOK // TILE)
        def _(i):
            rows = rows_of(i, TILE)
            image = i // (SEQ // TILE)
            mod = s.o_mod
            normed, _ = norm_rows(s.tokens[rows, :].astype(F32))
            entry = normed * (1.0 + mod[image, 1:2, :]) + mod[image, 0:1, :]
            s.entry_a[rows, :] = entry.astype(BF16)
            branch = mod[image, 5:6, :] * s.cot[rows, :].astype(F32)
            s.d_branch[rows, :] = branch.astype(BF16)

        self.saves.local(s.d_branch, s.o_branch.at[pl.ds(0, TOK)])
        self.to_sibling(s.d_branch, s.o_branch.at[pl.ds(TOK, TOK)])
        self.turn(s.entry_a, s.t_a)
        self.share(s.t_a, s.o_lhs.at[0])

    def turn(self, source, target):
        @pl.loop(0, source.shape[1] // 128)
        def _(i):
            columns = rows_of(i, 128)
            target[columns, :] = source[:, columns].T

    def share(self, source, target):
        self.shared = [self.saves.local(source, target.at[:, pl.ds(0, TOK)])]
        self.to_sibling(source, target.at[:, pl.ds(TOK, TOK)])

    def qv(self, j):
        s = self.s
        self.loaded(self.load_qv, j, j)
        columns = pl.ds(j * WIDTH, WIDTH)
        both = mm(s.entry_a[...], flat(s.w[j % 2, 0]))
        s.proj[:, columns] = both[:, :WIDTH]
        s.v[:, columns] = both[:, WIDTH:].astype(BF16)
        if j == 2:
            self.saves.local(s.v, s.o_qkv.at[2])

    def ko(self, j):
        s = self.s
        self.loaded(self.load_ko, j, j)
        columns = pl.ds((j - 3) * WIDTH, WIDTH)
        s.proj[:, columns] = mm(s.entry_a[...], flat(s.w[j % 2, 0, :, :, :, 0:WIDTH]))

    def head_norm(self, which):
        s = self.s
        target, normed = (s.q, s.q_normed) if which == 0 else (s.k, s.k_normed)
        scale = s.scale_q if which == 0 else s.scale_k

        @pl.loop(0, TOK // HEAD_TILE)
        def _(i):
            rows = rows_of(i, HEAD_TILE)
            spots = rows_of(i % (SEQ // HEAD_TILE), HEAD_TILE)
            field = s.proj[rows, :]
            inverse = lax.rsqrt(mm_split(field * field, s.spread[...]) * (1.0 / HD) + EPSILON)
            scale[rows, :] = inverse
            field = field * mm_split(inverse, s.widen[...])
            normed[rows, :] = field.astype(BF16)
            turned = field * s.cos[spots, :] + partner(field, first_lanes(HEAD_TILE)) * s.sin[spots, :]
            target[rows, :] = turned.astype(BF16)

        self.saves.local(target, s.o_qkv.at[which])
        self.saves.local(normed, s.o_normed.at[which])
        self.saves.local(scale, s.o_scale.at[which])

    def attend(self, k):
        s = self.s
        heads = H // ATTN_STEPS
        if k >= 1:
            self.saves.done(self.slots[k - 1])
        for i in range(heads):
            base, mask = head_window(k * heads + i)
            window = pl.ds(base, 256)
            for image in range(2):
                rows = pl.ds(image * SEQ, SEQ)
                query = jnp.where(mask, s.q[rows, window].astype(F32), 0.0).astype(BF16)
                scores = mm_nt(query, s.k[rows, window]) * (1.0 / math.sqrt(HD))
                powers = jnp.exp(scores - jnp.max(scores, axis=1, keepdims=True))
                total = jnp.sum(powers, axis=1, keepdims=True)
                soft = (powers * (1.0 / total)).astype(BF16)
                s.soft[i, image] = soft
                mixed = mm(soft, s.v[rows, window])
                old = s.combined[rows, window].astype(F32)
                s.combined[rows, window] = jnp.where(mask, mixed, old).astype(BF16)

        self.slots[k] = self.saves.local(s.soft, s.o_soft.at[pl.ds(k * heads, heads)])

    def leave(self):
        s = self.s
        self.saves.done(self.slots[ATTN_STEPS - 1])
        for copy in self.shared:
            self.saves.done(copy)
        self.remote[1].wait_send()
        self.turn(s.combined, s.t_a)
        self.share(s.t_a, s.o_lhs.at[1])
        for j in range(3):
            columns = pl.ds(j * WIDTH, WIDTH)
            s.proj[:, columns] = mm(s.combined[...], flat(s.w_out[:, :, :, columns]))

        @pl.loop(0, TOK // TILE)
        def _(i):
            rows = rows_of(i, TILE)
            image = i // (SEQ // TILE)
            mod = s.o_mod
            attended = s.proj[rows, :]
            s.attended[rows, :] = attended.astype(BF16)
            residual = s.tokens[rows, :].astype(F32) + mod[image, 2:3, :] * attended
            s.residual[rows, :] = residual
            normed, _ = norm_rows(residual)
            entry = normed * (1.0 + mod[image, 4:5, :]) + mod[image, 3:4, :]
            s.entry_b[rows, :] = entry.astype(BF16)

        self.attended = self.saves.local(s.attended, s.o_attended)
        self.saves.local(s.residual, s.o_residual)
        self.turn(s.entry_b, s.t_b)
        self.share(s.t_b, s.o_lhs.at[2])

    def ff(self, j):
        s = self.s
        self.loaded(self.load_ff, j, 6 + j)
        s.wide[0] = mm(s.entry_b[...], flat(s.w[j % 2, 0]))
        s.wide[1] = mm(s.entry_b[...], flat(s.w[j % 2, 1]))
        mine = pl.ds(pl.multiple_of(self.c * 192, 16), 192)
        theirs = pl.ds(pl.multiple_of((1 - self.c) * 192, 16), 192)
        for half in range(2):
            shard = j + 4 * half
            at = shard * WIDTH
            if (6, j - 1, half) in self.slots:
                self.saves.done(self.slots[6, j - 1, half])

            @pl.loop(0, TOK // TILE)
            def _(i, half=half, at=at):
                rows = rows_of(i, TILE)
                gate = s.wide[0, rows, half * WIDTH : (half + 1) * WIDTH]
                up = s.wide[1, rows, half * WIDTH : (half + 1) * WIDTH]
                sigma = 1.0 / (1.0 + jnp.exp(-gate))
                active = gate * sigma
                s.active[half, 0, rows, :] = active.astype(BF16)
                slope = up * sigma * (1.0 + gate * (1.0 - sigma))
                s.active[half, 1, rows, :] = slope.astype(BF16)
                s.hidden[rows, at : at + WIDTH] = (active * up).astype(BF16)

            self.slots[6, j, half] = self.saves.local(s.active.at[half], s.o_active.at[shard])
            for i in range(3):
                turned = s.hidden[:, at + 128 * i : at + 128 * i + 128].T
                s.t_h[shard, 128 * i : 128 * i + 128, :] = turned
            self.saves.local(s.t_h.at[shard, mine], s.o_hidden.at[shard, :, pl.ds(0, TOK)])
            self.to_sibling(s.t_h.at[shard, theirs], s.o_hidden.at[shard, :, pl.ds(TOK, TOK)])

    def down(self, j):
        s = self.s
        self.loaded(self.load_down, j, 14 + j)
        if j == 0:
            self.saves.done(self.attended)
        columns = pl.ds(j * WIDTH, WIDTH)
        s.wide[0, :, 0:WIDTH] = mm(s.hidden[...], flat(s.w_down[j % 2]))
        for image in range(2):
            gate = s.o_mod[image, 5:6, columns]
            total = jnp.zeros((1, WIDTH), F32)
            for i in range(SEQ // TILE):
                rows = pl.ds(image * SEQ + i * TILE, TILE)
                branch = s.wide[0, rows, 0:WIDTH]
                result = s.residual[rows, columns] + gate * branch
                s.attended[rows, columns] = result.astype(BF16)
                total = total + jnp.sum(
                    s.cot[rows, columns].astype(F32) * branch, axis=0, keepdims=True
                )
            s.o_gate_b[image, 0:1, columns] = total
        if j == 2:
            self.saves.local(s.attended, s.o_result)

    def plan(self):
        steps = [(None, self.modulate, k, 0, 7) for k in range(5)] + [(None, self.enter, None, 0, 4)]
        steps += [(self.load_qv, self.qv, j, j + 1, 2.5) for j in range(3)]
        steps += [(None, self.head_norm, 0, 3, 4)]
        steps += [(self.load_ko, self.ko, j, j + 1, 1.5) for j in range(3, 6)]
        steps += [(None, self.head_norm, 1, 6, 4)]
        steps += [(None, self.attend, k, 6, 3) for k in range(ATTN_STEPS)]
        steps += [(None, self.leave, None, 6, 6)]
        steps += [(self.load_ff, self.ff, j, 8 + 2 * j, 5.5) for j in range(4)]
        steps += [(self.load_down, self.down, j, 15 + j, 3) for j in range(3)]
        return steps

    def finish(self):
        self.saves.finish()
        for k, copy in enumerate(self.remote):
            if k != 1:
                copy.wait_send()
            copy.wait_recv()


class ForwardInputs(NamedTuple):
    packed: object
    gate: object
    up: object
    down: object
    tokens: object
    cot: object
    acted: object
    bias: object
    mod_weight: object
    acted_slim: object
    cos: object
    sin: object
    spread: object
    widen: object


FORWARD_OUTPUTS = dict(
    packed_all=((4, 2, 144, 4608), BF16),
    gate_all=((4, 2, 144, 3072), BF16),
    up_all=((4, 2, 144, 3072), BF16),
    down_all=((4, 2, 384, 1152), BF16),
    o_branch=((2 * TOK, D), BF16),
    o_lhs=((3, D, 2 * TOK), BF16),
    o_hidden=((8, 192, 2 * TOK), BF16),
    o_qkv=((3, TOK, D), BF16),
    o_normed=((2, TOK, D), BF16),
    o_scale=((2, TOK, 128), F32),
    o_soft=((H, 2, SEQ, SEQ), BF16),
    o_attended=((TOK, D), BF16),
    o_residual=((TOK, D), F32),
    o_active=((8, 2, TOK, WIDTH), BF16),
    o_result=((TOK, D), BF16),
    acted_all=((4, 2, 2, 2) + SLIM, F32),
    o_mod=((2, 8, D), F32),
    o_gate_b=((2, 8, D), F32),
)


def forward_scratch():
    def vmem(*shape, kind=BF16):
        return pltpu.VMEM(shape, kind)

    return dict(
        entry_a=vmem(TOK, D),
        d_branch=vmem(TOK, D),
        t_a=vmem(D, TOK),
        proj=vmem(TOK, D, kind=F32),
        q=vmem(TOK, D),
        k=vmem(TOK, D),
        v=vmem(TOK, D),
        q_normed=vmem(TOK, D),
        k_normed=vmem(TOK, D),
        scale_q=vmem(TOK, 128, kind=F32),
        scale_k=vmem(TOK, 128, kind=F32),
        soft=vmem(H // ATTN_STEPS, 2, SEQ, SEQ),
        combined=vmem(TOK, D),
        attended=vmem(TOK, D),
        residual=vmem(TOK, D, kind=F32),
        entry_b=vmem(TOK, D),
        t_b=vmem(D, TOK),
        wide=vmem(2, TOK, 2 * WIDTH, kind=F32),
        active=vmem(2, 2, TOK, WIDTH),
        hidden=vmem(TOK, 8 * WIDTH),
        t_h=vmem(8, WIDTH, TOK),
        w=vmem(2, 2, 4, 2, 144, 2 * WIDTH),
        w_out=vmem(4, 2, 144, D),
        w_down=vmem(2, 4, 2, 384, WIDTH),
        gather_send=pltpu.SemaphoreType.DMA((4, N_PIECES)),
        gather_recv=pltpu.SemaphoreType.DMA((4, N_PIECES)),
        mod_w=vmem(MOD_PART, D),
        acted_group=vmem(4, 8, D, kind=F32),
        mod_flat=vmem(8, 4 * MOD_PART, kind=F32),
        mod_parts=group_scratch(MOD_PART)[0],
        mod_got_c=group_scratch(MOD_PART)[1],
        mod_got_y=group_scratch(MOD_PART)[2],
        mod_blocks=group_scratch(MOD_PART)[3],
        mod_send=group_scratch(MOD_PART)[4],
        mod_recv=group_scratch(MOD_PART)[5],
        acted_send=pltpu.SemaphoreType.DMA((4,)),
        acted_recv=pltpu.SemaphoreType.DMA((4,)),
        acted_own=pltpu.SemaphoreType.DMA,
        first_send=pltpu.SemaphoreType.DMA((2,)),
        first_recv=pltpu.SemaphoreType.DMA((2,)),
        own_packed=vmem(144, 4 * D),
        own_down=vmem(384, D),
        own_sems=pltpu.SemaphoreType.DMA((4,)),
        save_sems=pltpu.SemaphoreType.DMA((56,)),
        load_sems=pltpu.SemaphoreType.DMA((48,)),
        pair_send=pltpu.SemaphoreType.DMA((16,)),
        pair_recv=pltpu.SemaphoreType.DMA((16,)),
    )


def run_step(steps, arrived):
    _, act, j, _, cost = steps.pop(0)
    if steps and steps[0][0] is not None and steps[0][3] <= arrived:
        steps[0][0](steps[0][2])
    act() if j is None else act(j)
    return cost


def forward_kernel(*refs):
    names = ForwardInputs._fields + tuple(FORWARD_OUTPUTS) + tuple(forward_scratch())
    s = SimpleNamespace(**dict(zip(names, refs, strict=True)))
    spot = place()
    greet(neighbours(*spot))
    arrays = [s.packed, s.gate, s.up, s.down, s.packed_all, s.gate_all, s.up_all, s.down_all]
    own_gate, own_up = s.hidden.at[pl.ds(0, 144)], s.hidden.at[pl.ds(144, 144)]
    stages = [s.own_packed, own_gate, own_up, s.own_down]
    gather = Gather(arrays, (s.gather_send, s.gather_recv, s.own_sems), spot, stages)
    work = Forward(s, spot, gather)
    steps = work.plan()
    gather.own_copies()
    acted = Acted(s, spot)
    ahead = 2
    arrived = 0
    for t in range(N_PIECES + 4 + ahead):
        if t == 1:
            gather.own_stores()
        if t < N_PIECES:
            if t >= ahead:
                gather.sent_z(t - ahead)
            gather.start_z(t)
        if 0 <= t - ahead < N_PIECES:
            gather.start_x(t - ahead)
        if 0 <= t - ahead - 1 < N_PIECES:
            gather.start_y(t - ahead - 1)
        if 0 <= t - ahead - 2 < N_PIECES:
            gather.start_c(t - ahead - 2)
        if 0 <= t - ahead - 3 < N_PIECES:
            if arrived == 0:
                gather.own_done()
            gather.arrived(t - ahead - 3)
            arrived += 1
        if t >= 6 and t % 3 == 0 and t // 3 - 2 < 5:
            acted.step(t // 3 - 2)
        spent = 0.0
        while steps and steps[0][3] <= arrived and spent < 6.0:
            spent += run_step(steps, arrived)
    while steps:
        run_step(steps, arrived)
    for t in range(N_PIECES - ahead, N_PIECES):
        gather.sent_z(t)
    for t in range(N_PIECES):
        gather.sent_rest(t)
    work.finish()


def forward_pass(*given):
    hbm = pl.BlockSpec(memory_space=pl.ANY)
    inside = pl.BlockSpec(memory_space=pltpu.VMEM)
    out = pl.pallas_call(
        forward_kernel,
        out_shape=[jax.ShapeDtypeStruct(*spec) for spec in FORWARD_OUTPUTS.values()],
        in_specs=[hbm] * 4 + [inside] * 4 + [hbm] * 2 + [inside] * 4,
        out_specs=[hbm] * 16 + [inside] * 2,
        scratch_shapes=list(forward_scratch().values()),
        name="forward_pass",
        compiler_params=pltpu.CompilerParams(
            collective_id=0, has_side_effects=True, vmem_limit_bytes=121 << 19
        ),
    )(*ForwardInputs(*given))
    return SimpleNamespace(**dict(zip(FORWARD_OUTPUTS, out)))


def head_tables():
    lane = np.arange(D) % HD
    frequency = np.exp(-math.log(10000.0) * (lane % 18) / 18)
    token = np.arange(SEQ)[:, None]
    angle = np.where(lane < 36, token // GRID, token % GRID) * frequency
    sign = np.where(lane % 36 < 18, -1.0, 1.0)
    spread = (np.arange(D)[:, None] // HD == np.arange(128)).astype(np.float32)
    return (
        jnp.asarray(np.cos(angle), F32),
        jnp.asarray(np.sin(angle) * sign, F32),
        jnp.asarray(spread, BF16),
        jnp.asarray(spread.T, BF16),
    )


SCATTER_ROWS = (144,) * 14 + (192,) * 3
SCATTER_EDGE = tuple((32, 48)[j % 2] for j in range(14)) + (48,) * 3
ORDER = (14, 15, 16) + tuple(range(6, 14)) + tuple(range(6))


class Reduce:
    def __init__(self, s, spot):
        self.s = s
        self.z, self.x, self.y, self.c = spot
        self.stage = {}
        self.open = []

    def shape(self, t):
        return SCATTER_ROWS[t], SCATTER_EDGE[t]

    def part(self, t):
        rows, edge = self.shape(t)
        return pl.ds(pl.multiple_of(self.y * edge, 16), rows - edge)

    def held(self, t):
        s = self.s
        return s.held_big.at[t - 14] if t >= 14 else s.held.at[t if t < 6 else t - 6]

    def pick(self, small, big, t):
        return big.at[t - 14] if t >= 14 else small.at[t]

    def got_y(self, t):
        return self.pick(self.s.got_y, self.s.got_y_big, t)

    def got_x(self, t):
        return self.pick(self.s.got_x, self.s.got_x_big, t)

    def got_z(self, t):
        return self.pick(self.s.got_z, self.s.got_z_big, t)

    def got_f(self, t):
        return self.pick(self.s.got_f, self.s.got_f_big, t)

    def sems(self, stage, t):
        return self.s.scatter_send.at[stage, t], self.s.scatter_recv.at[stage, t]

    def produced(self, t):
        self.stage[t] = -1
        self.ask()

    def ask(self):
        entered = sum(stage > 0 for stage in self.stage.values())
        for t in ORDER[: entered + 3]:
            if self.stage.get(t) == -1:
                self.stage[t] = 0
                self.start_y(t)

    def advance(self):
        stages = (self.start_x, self.start_z, self.start_f, self.start_c)
        under_way = [t for t in ORDER if 0 < self.stage.get(t, 4) < 4]
        waiting = [t for t in ORDER if self.stage.get(t) == 0]
        for t in waiting[:1] + under_way[::-1]:
            stages[self.stage[t]](t)
            self.stage[t] += 1
        self.ask()

    def free(self, t):
        while self.stage[t] < 4:
            self.advance()
        if t in self.open:
            self.sent(t)

    def start_y(self, t):
        rows, edge = self.shape(t)
        theirs = pl.ds(pl.multiple_of((1 - self.y) * (rows - edge), 16), edge)
        send(
            self.held(t).at[:, :, theirs, :],
            self.got_y(t).at[:, :, pl.ds(0, edge), :],
            *self.sems(0, t),
            device(self.z, self.x, 1 - self.y, self.c),
        )

    def start_x(self, t):
        rows, edge = self.shape(t)
        held, got = self.held(t), self.got_y(t)
        drain(got.at[:, :, pl.ds(0, edge), :], self.s.scatter_recv.at[0, t])
        mine = pl.ds(pl.multiple_of(self.y * (rows - edge), 16), edge)

        @pl.loop(0, 4)
        def _(k):
            for x in range(2):
                total = held[k, x, mine, :].astype(F32) + got[k, x, pl.ds(0, edge), :].astype(F32)
                held[k, x, mine, :] = total.astype(BF16)

        send(
            held.at[:, 1 - self.x, self.part(t), :],
            self.got_x(t).at[:, pl.ds(0, rows - edge), :],
            *self.sems(1, t),
            device(self.z, 1 - self.x, self.y, self.c),
        )

    def start_z(self, t):
        rows, edge = self.shape(t)
        held, got = self.held(t), self.got_x(t)
        keep = rows - edge
        drain(got.at[:, pl.ds(0, keep), :], self.s.scatter_recv.at[1, t])
        part = self.part(t)

        @pl.loop(0, 4)
        def _(k):
            total = held[k, self.x, part, :].astype(F32) + got[k, pl.ds(0, keep), :].astype(F32)
            held[k, self.x, part, :] = total.astype(BF16)

        for step in (1, 3, 2):
            other = (self.z + step) % 4
            send(
                held.at[other, self.x, part, :],
                self.got_z(t).at[step - 1, pl.ds(0, keep), :],
                *self.sems(2, t),
                device(other, self.x, self.y, self.c),
            )

    def start_f(self, t):
        rows, edge = self.shape(t)
        held, got = self.held(t), self.got_z(t)
        keep = rows - edge
        drain(got.at[:, pl.ds(0, keep), :], self.s.scatter_recv.at[2, t])
        part = self.part(t)
        total = held[self.z, self.x, part, :].astype(F32)
        for k in range(3):
            total = total + got[k, pl.ds(0, keep), :].astype(F32)
        held[self.z, self.x, part, :] = total.astype(BF16)
        send(
            held.at[self.z, self.x, part, :],
            self.got_f(t).at[pl.ds(0, keep), :],
            *self.sems(3, t),
            device(self.z, self.x, 1 - self.y, self.c),
        )

    def target(self, t):
        s = self.s
        if t < 6:
            columns = pl.ds(pl.multiple_of(self.c * LANE_HALF + t * WIDTH, 128), WIDTH)
            return s.g_packed.at[:, columns]
        if t < 14:
            columns = pl.ds(pl.multiple_of(self.c * FF_HALF + (t - 6) // 2 * WIDTH, 128), WIDTH)
            return (s.g_gate, s.g_up)[(t - 6) % 2].at[:, columns]
        rows = pl.ds(pl.multiple_of(self.c * 192, 16), 192)
        return s.g_down.at[rows, pl.ds((t - 14) * WIDTH, WIDTH)]

    def start_c(self, t):
        rows, edge = self.shape(t)
        held, got = self.held(t), self.got_f(t)
        y, keep, both = self.y, rows - edge, rows - 2 * edge
        drain(got.at[pl.ds(0, keep), :], self.s.scatter_recv.at[3, t])
        drain(self.got_y(t).at[:, :, pl.ds(0, edge), :], self.s.scatter_send.at[0, t])
        drain(self.got_x(t).at[:, pl.ds(0, keep), :], self.s.scatter_send.at[1, t])
        mid, fin = held.at[self.z, self.x], held.at[self.z, 1 - self.x]

        def at(offset, count):
            return pl.ds(pl.multiple_of(offset, 16), count)

        own, other = at(y * keep, edge), at((1 - y) * keep, edge)
        fin[own, :] = mid[own, :]
        fin[other, :] = got[at((1 - y) * both, edge), :]
        total = mid[pl.ds(edge, both), :].astype(F32) + got[at(y * edge, both), :].astype(F32)
        fin[pl.ds(edge, both), :] = total.astype(BF16)
        target = self.target(t)
        send(fin, target, *self.sems(4, t), device(self.z, self.x, y, 1 - self.c))
        pltpu.make_async_copy(fin, target, self.s.store_sems.at[t]).start()
        self.open.append(t)

    def sent(self, t):
        self.open.remove(t)
        rows, edge = self.shape(t)
        sems = self.s.scatter_send
        drain(self.got_z(t).at[:, pl.ds(0, rows - edge), :], sems.at[2, t])
        drain(self.got_f(t).at[pl.ds(0, rows - edge), :], sems.at[3, t])
        drain(self.target(t), sems.at[4, t])
        drain(self.target(t), self.s.store_sems.at[t])

    def finish(self):
        for t in ORDER:
            self.free(t)
        for t in range(N_PIECES):
            drain(self.target(t), self.s.scatter_recv.at[4, t])


class Backward:
    def __init__(self, s, spot, reduce):
        self.s, self.reduce = s, reduce
        self.z, self.x, self.y, self.c = spot
        self.pending = {}
        self.remote = {}
        self.copies = 0

    def load(self, key, source, target):
        if key not in self.pending:
            copy = pltpu.make_async_copy(source, target, self.s.load_sems.at[self.copies])
            self.copies += 1
            copy.start()
            self.pending[key] = copy

    def wait(self, *keys):
        for key in keys:
            self.pending.pop(key).wait()

    def to_sibling(self, key, source, target):
        k = len(self.remote)
        copy = pltpu.make_async_remote_copy(
            src_ref=source,
            dst_ref=target,
            send_sem=self.s.pair_send.at[k],
            recv_sem=self.s.pair_recv.at[k],
            device_id=device(self.z, self.x, self.y, 1 - self.c),
            device_id_type=MESH,
        )
        copy.start()
        self.remote[key] = copy


    def grad_down(self, hidden, branch):
        s, reduce = self.s, self.reduce

        @pl.loop(0, 4)
        def _(k):
            left = hidden[pl.ds(2 * k, 2)].reshape(384, 2 * TOK)
            total = mm(left, branch[...]).astype(BF16)
            for j in range(3):
                block = total[:, j * WIDTH : (j + 1) * WIDTH]
                s.held_big[j, k] = block.reshape(2, 192, WIDTH)

        for t in (14, 15, 16):
            reduce.produced(t)

    def column(self, w):
        half = (1 - self.c) if w % 2 == 0 else self.c
        return half * 4 + w // 2

    def load_ff(self, f, w):
        s = self.s
        window = self.column(w)
        columns = pl.ds(pl.multiple_of(window * WIDTH, 128), WIDTH)
        slot = w % 2
        self.load((1, w), s.down_all.at[window // 2, window % 2], f.w_down.at[slot])
        self.load((2, w), s.gate_all.at[:, :, :, columns], s.w.at[slot, :, :, :, pl.ds(0, WIDTH)])
        self.load((3, w), s.up_all.at[:, :, :, columns], s.w.at[slot, :, :, :, pl.ds(WIDTH, WIDTH)])
        self.load((4, w), s.o_active.at[window], f.active.at[slot])

    def ff(self, f, w):
        s = self.s
        slot = w % 2
        self.load_ff(f, w)
        self.wait((1, w), (2, w), (3, w), (4, w))
        if w < 7:
            self.load_ff(f, w + 1)
        s.d_residual[:, 0:WIDTH] = mm_nt(f.branch[pl.ds(0, TOK), :], f.w_down[slot])
        if w >= 2:
            if slot == 0:
                self.remote[5, w - 2].wait_send()
            else:
                self.wait((5, w - 2))
        steep = f.steep.at[slot]

        @pl.loop(0, TOK // TILE)
        def _(i):
            rows = rows_of(i, TILE)
            back = s.d_residual[rows, 0:WIDTH]
            steep[rows, 0:WIDTH] = (back * f.active[slot, 1, rows, :].astype(F32)).astype(BF16)
            steep[rows, WIDTH : 2 * WIDTH] = (
                back * f.active[slot, 0, rows, :].astype(F32)
            ).astype(BF16)

        j = w // 2
        if slot == 0:
            self.to_sibling((5, w), steep, s.r_ff.at[j, pl.ds(TOK, TOK)])
        else:
            self.load((5, w), steep, s.r_ff.at[j, pl.ds(0, TOK)])
        product = mm_nt(steep[...], flat(s.w[slot]))
        if w == 0:
            s.acc[...] = product
        else:
            s.acc[...] += product

    def load_grad_ff(self, j):
        s = self.s
        self.remote[5, 2 * j].wait_recv()
        if (5, 2 * j + 1) in self.pending:
            self.wait((5, 2 * j + 1))
        self.load((6, j), s.r_ff.at[j], s.right.at[j % 2])

    def grad_ff(self, j):
        s = self.s
        self.wait((6, j))
        right = s.right.at[j % 2]

        @pl.loop(0, 2)
        def _(k):
            left = s.left[pl.ds(pl.multiple_of(k * 576, 64), 576), :]
            total = mm(left, right[...]).astype(BF16)
            for half in range(2):
                block = total[:, half * WIDTH : (half + 1) * WIDTH]
                s.held[2 * j + half, pl.ds(2 * k, 2)] = block.reshape(2, 2, 144, WIDTH)

        self.reduce.produced(6 + 2 * j)
        self.reduce.produced(7 + 2 * j)

    def feed_forward(self, f):
        s, reduce = self.s, self.reduce
        self.wait(11, 12)
        self.load((7, 0), s.o_lhs.at[2], s.left)
        self.grad_down(f.hidden, f.branch)
        for w in range(8):
            self.ff(f, w)
            if w == 0:
                self.wait((7, 0))
            if w % 2 == 1:
                reduce.advance()
                if w >= 3:
                    self.load_grad_ff(w // 2 - 1)
            elif w >= 4:
                self.grad_ff(w // 2 - 2)
        self.load_grad_ff(3)
        self.grad_ff(2)
        self.grad_ff(3)
        self.remote[5, 6].wait_send()


    def middle(self, f):
        s = self.s
        self.load(21, s.cot, f.cot)
        self.load(22, s.o_residual, s.d_residual)
        self.load(23, s.o_attended, f.attended)
        self.wait(21, 22, 23)
        s.d_mod[...] = jnp.zeros_like(s.d_mod)

        @pl.loop(0, TOK // TILE)
        def _(i):
            rows = rows_of(i, TILE)
            image = i // (SEQ // TILE)
            mod, d_mod = s.mod, s.d_mod
            normed, inverse = norm_rows(s.d_residual[rows, :])
            d_entry = s.acc[rows, :]
            d_mod[image, 3:4, :] += jnp.sum(d_entry, axis=0, keepdims=True)
            d_mod[image, 4:5, :] += jnp.sum(d_entry * normed, axis=0, keepdims=True)
            back = norm_back(normed, inverse, d_entry * (1.0 + mod[image, 4:5, :]))
            d_residual = f.cot[rows, :].astype(F32) + back
            s.d_residual[rows, :] = d_residual
            attended = f.attended[rows, :].astype(F32)
            d_mod[image, 2:3, :] += jnp.sum(d_residual * attended, axis=0, keepdims=True)
            s.joined[rows, 3 * D : 4 * D] = (mod[image, 2:3, :] * d_residual).astype(BF16)


    def load_soft(self, f, k):
        heads = H // ATTN_STEPS
        self.load((31, k), self.s.o_soft.at[pl.ds(k * heads, heads)], f.soft)

    def attend(self, f, k):
        s = self.s
        heads = H // ATTN_STEPS
        self.wait((31, k))
        factor = 1.0 / math.sqrt(HD)
        for i in range(heads):
            base, mask = head_window(k * heads + i)
            window = pl.ds(base, 256)
            for image in range(2):
                rows = pl.ds(image * SEQ, SEQ)
                back = jnp.where(mask, f.back[rows, window].astype(F32), 0.0).astype(BF16)
                soft = f.soft[i, image]
                d_soft = mm_nt(back, f.qkv[2, rows, window])
                wide = soft.astype(F32)
                d_scores = (
                    wide * (d_soft - jnp.sum(wide * d_soft, axis=1, keepdims=True))
                ).astype(BF16)
                results = (
                    mm(d_scores, f.qkv[1, rows, window]) * factor,
                    mm_tn(d_scores, f.qkv[0, rows, window]) * factor,
                    mm_tn(soft, back),
                )
                for part, result in enumerate(results):
                    place_at = pl.ds(part * D + base, 256)
                    old = s.joined[rows, place_at].astype(F32)
                    s.joined[rows, place_at] = jnp.where(mask, result, old).astype(BF16)
        if k + 1 < ATTN_STEPS:
            self.load_soft(f, k + 1)

    def head_back(self, f, which):
        s = self.s

        @pl.loop(0, TOK // HEAD_TILE)
        def _(i):
            rows = rows_of(i, HEAD_TILE)
            spots = rows_of(i % (SEQ // HEAD_TILE), HEAD_TILE)
            columns = pl.ds(which * D, D)
            grad = s.joined[rows, columns].astype(F32)
            grad = grad * f.cos[spots, :] - partner(grad, first_lanes(HEAD_TILE)) * f.sin[spots, :]
            normed = f.normed[which, rows, :].astype(F32)
            mean = mm_split(grad * normed, s.spread[...]) * (1.0 / HD)
            scale = mm_split(s.acc[rows, which * 128 : which * 128 + 128], s.widen[...])
            result = scale * (grad - normed * mm(mean.astype(BF16), s.widen[...]))
            s.joined[rows, columns] = result.astype(BF16)

    def attention(self, f):
        s, reduce = self.s, self.reduce
        self.load(24, s.packed_all.at[:, :, :, pl.ds(3 * D, 768)], s.w.at[0])
        self.load(25, s.packed_all.at[:, :, :, pl.ds(3 * D + 768, WIDTH)], s.w.at[1, :, :, :, pl.ds(0, WIDTH)])
        for k in range(3):
            self.load((41, k), s.o_qkv.at[k], f.qkv.at[k])
        self.load_soft(f, 0)
        self.load(42, s.o_normed, f.normed)
        self.load(44, s.cos, f.cos)
        self.load(45, s.sin, f.sin)
        self.wait(24, 25)
        joined = s.joined
        s.acc[...] = mm_nt(joined[:, 3 * D : 3 * D + 768], flat(s.w[0]))
        s.acc[...] += mm_nt(joined[:, 3 * D + 768 :], flat(s.w[1, :, :, :, 0:WIDTH]))
        f.back[...] = s.acc[...].astype(BF16)
        for k in range(2):
            self.load((43, k), s.o_scale.at[k], s.acc.at[:, pl.ds(128 * k, 128)])
        reduce.advance()
        self.wait((41, 0), (41, 1), (41, 2))
        for k in range(ATTN_STEPS):
            self.attend(f, k)
            if k % 2 == 1:
                reduce.advance()
        self.wait(42, (43, 0), (43, 1), 44, 45)
        self.head_back(f, 0)
        reduce.advance()
        self.head_back(f, 1)


    def load_entry(self, k):
        s = self.s
        width = 768 if k < 4 else WIDTH
        self.load(
            (51, k),
            s.packed_all.at[:, :, :, pl.ds(k * 768, width)],
            s.w.at[k % 2, :, :, :, pl.ds(0, width)],
        )

    def entry(self, k):
        s = self.s
        width = 768 if k < 4 else WIDTH
        self.load_entry(k)
        self.wait((51, k))
        if k < 4:
            self.load_entry(k + 1)
        product = mm_nt(s.joined[:, k * 768 : k * 768 + width], flat(s.w[k % 2, :, :, :, 0:width]))
        if k == 0:
            s.acc[...] = product
        else:
            s.acc[...] += product

    def grad_packed(self, f, jj):
        s = self.s
        self.wait((61, jj))
        right = s.right.at[jj % 2]

        @pl.loop(0, 2)
        def _(k):
            rows = pl.ds(pl.multiple_of(k * 576, 64), 576)
            for half in range(2):
                j = 2 * jj + half
                left = s.left if j < 3 else f.left
                total = mm(left[rows, :], right[:, half * WIDTH : (half + 1) * WIDTH])
                s.held[j, pl.ds(2 * k, 2)] = total.astype(BF16).reshape(2, 2, 144, WIDTH)

        self.reduce.produced(2 * jj)
        self.reduce.produced(2 * jj + 1)

    def load_right(self, jj):
        self.load((61, jj), self.s.r_packed.at[:, pl.ds(768 * jj, 768)], self.s.right.at[jj % 2])

    def last(self, f):
        s, reduce = self.s, self.reduce
        mine = pl.ds(pl.multiple_of(self.c * LANE_HALF, 128), LANE_HALF)
        theirs = pl.ds(pl.multiple_of((1 - self.c) * LANE_HALF, 128), LANE_HALF)
        self.to_sibling((71, 0), s.joined.at[:, theirs], s.r_packed.at[pl.ds(TOK, TOK)])
        self.load(71, s.joined.at[:, mine], s.r_packed.at[pl.ds(0, TOK)])
        self.load(72, s.o_lhs.at[0], s.left)
        self.load(73, s.o_lhs.at[self.c], f.left)
        self.load(74, s.tokens, f.tokens)
        self.load(76, s.mod_weight, f.mod_w)
        reduce.advance()
        self.entry(0)
        self.remote[71, 0].wait_recv()
        self.wait(71, 72, 73)
        self.load_right(0)
        self.load_right(1)
        for jj in range(3):
            reduce.free(6 + 2 * jj)
            reduce.free(7 + 2 * jj)
            self.grad_packed(f, jj)
            if jj == 0:
                self.load_right(2)
            self.entry(1 + jj)
            reduce.advance()
        self.entry(4)
        reduce.advance()
        self.wait(74)

        @pl.loop(0, TOK // TILE)
        def _(i):
            rows = rows_of(i, TILE)
            image = i // (SEQ // TILE)
            mod, d_mod = s.mod, s.d_mod
            normed, inverse = norm_rows(f.tokens[rows, :].astype(F32))
            d_entry = s.acc[rows, :]
            d_mod[image, 0:1, :] += jnp.sum(d_entry, axis=0, keepdims=True)
            d_mod[image, 1:2, :] += jnp.sum(d_entry * normed, axis=0, keepdims=True)
            back = norm_back(normed, inverse, d_entry * (1.0 + mod[image, 1:2, :]))
            s.d_residual[rows, :] += back

        self.load(75, s.d_residual, s.g_tokens)
        self.modulation(f)
        reduce.finish()
        self.wait(75)
        self.remote[71, 0].wait_send()

    def modulation(self, f):
        s, reduce = self.s, self.reduce
        z, x, y, c = spot = (self.z, self.x, self.y, self.c)
        s.back_flat[...] = jnp.zeros_like(s.back_flat)
        for image in range(2):
            for k in range(6):
                row = s.gate_b[image, 0:1, :] if k == 5 else s.d_mod[image, k : k + 1, :]
                rounded = row.astype(BF16).astype(F32)
                s.back_flat[image : image + 1, k * D : (k + 1) * D] = rounded
        for m in range(4):
            s.back_parts[m] = s.back_flat[:, m * MOD_PART : (m + 1) * MOD_PART]
        group = Group(
            spot, s.back_parts, s.back_got_c, s.back_got_y, s.back_blocks, s.back_send, s.back_recv
        )
        group.start()
        reduce.advance()
        group.across_y()
        reduce.advance()
        group.finish()
        for m in range(4):
            s.back[2 * m : 2 * m + 2, :] = s.back_blocks[m, 0:2, :]
        x_peer = device(z, 1 - x, y, c)
        send(s.back, s.back_got_x, s.wide_send.at[0], s.wide_recv.at[0], x_peer)
        self.wait(76)
        partial = mm(s.back[...].astype(BF16), f.mod_w[...])
        s.cond_parts[...] = jnp.zeros_like(s.cond_parts)
        for m in range(4):
            s.cond_parts[m, 0:2, :] = partial[2 * m : 2 * m + 2, :]
        cond = Group(
            spot, s.cond_parts, s.cond_got_c, s.cond_got_y, s.cond_blocks, s.cond_send, s.cond_recv
        )
        cond.start()
        drain(s.back, s.wide_recv.at[0])
        own, other = s.back[...], s.back_got_x[...]
        low = jnp.where(x == 0, own, other)
        high = jnp.where(x == 0, other, own)
        s.back_all[z] = jnp.concatenate([low, high], axis=0).astype(BF16)
        block = s.back_all.at[z]
        for step in (1, 3, 2):
            peer = device((z + step) % 4, x, y, c)
            send(block, block, s.wide_send.at[1], s.wide_recv.at[1], peer)
        cond.across_y()
        reduce.advance()
        cond.finish()
        total = s.cond_blocks[0] + s.cond_blocks[1] + s.cond_blocks[2] + s.cond_blocks[3]
        s.o_cond[...] = total
        reduce.advance()
        drain(s.back_all.at[pl.ds(0, 3)], s.wide_recv.at[1])
        self.load(77, s.back_all, s.o_back)
        drain(s.back, s.wide_send.at[0])
        drain(s.back_all.at[pl.ds(0, 3)], s.wide_send.at[1])
        self.wait(77)


class BackwardInputs(NamedTuple):
    packed_all: object
    gate_all: object
    up_all: object
    down_all: object
    o_branch: object
    o_lhs: object
    o_hidden: object
    o_qkv: object
    o_normed: object
    o_scale: object
    o_soft: object
    o_attended: object
    o_residual: object
    o_active: object
    tokens: object
    cot: object
    cos: object
    sin: object
    mod: object
    spread: object
    widen: object
    gate_b: object
    mod_weight: object


BACKWARD_OUTPUTS = dict(
    g_packed=((144, 4 * D), BF16),
    g_gate=((144, 8 * WIDTH), BF16),
    g_up=((144, 8 * WIDTH), BF16),
    g_down=((384, D), BF16),
    g_tokens=((TOK, D), F32),
    r_ff=((4, 2 * TOK, 2 * WIDTH), BF16),
    r_packed=((2 * TOK, LANE_HALF), BF16),
    o_back=((4, 16, MOD_PART), BF16),
    o_cond=((8, D), F32),
)


def vmem(*shape, kind=BF16):
    return pltpu.VMEM(shape, kind)


def backward_scratch():
    return dict(
        held=vmem(8, 4, 2, 144, WIDTH),
        held_big=vmem(3, 4, 2, 192, WIDTH),
        got_y=vmem(14, 4, 2, 48, WIDTH),
        got_y_big=vmem(3, 4, 2, 48, WIDTH),
        got_x=vmem(14, 4, 112, WIDTH),
        got_x_big=vmem(3, 4, 144, WIDTH),
        got_z=vmem(14, 3, 112, WIDTH),
        got_z_big=vmem(3, 3, 144, WIDTH),
        got_f=vmem(14, 112, WIDTH),
        got_f_big=vmem(3, 144, WIDTH),
        w=vmem(2, 4, 2, 144, 2 * WIDTH),
        acc=vmem(TOK, D, kind=F32),
        d_residual=vmem(TOK, D, kind=F32),
        joined=vmem(TOK, 4 * D),
        left=vmem(D, 2 * TOK),
        right=vmem(2, 2 * TOK, 2 * WIDTH),
        d_mod=vmem(2, 8, D, kind=F32),
        back_flat=vmem(8, 4 * MOD_PART, kind=F32),
        back_parts=group_scratch(MOD_PART)[0],
        back_got_c=group_scratch(MOD_PART)[1],
        back_got_y=group_scratch(MOD_PART)[2],
        back_blocks=group_scratch(MOD_PART)[3],
        back_send=group_scratch(MOD_PART)[4],
        back_recv=group_scratch(MOD_PART)[5],
        cond_parts=group_scratch(D)[0],
        cond_got_c=group_scratch(D)[1],
        cond_got_y=group_scratch(D)[2],
        cond_blocks=group_scratch(D)[3],
        cond_send=group_scratch(D)[4],
        cond_recv=group_scratch(D)[5],
        back=vmem(8, MOD_PART, kind=F32),
        back_got_x=vmem(8, MOD_PART, kind=F32),
        back_all=vmem(4, 16, MOD_PART),
        wide_send=pltpu.SemaphoreType.DMA((2,)),
        wide_recv=pltpu.SemaphoreType.DMA((2,)),
        scatter_send=pltpu.SemaphoreType.DMA((5, N_PIECES)),
        scatter_recv=pltpu.SemaphoreType.DMA((5, N_PIECES)),
        store_sems=pltpu.SemaphoreType.DMA((N_PIECES,)),
        load_sems=pltpu.SemaphoreType.DMA((112,)),
        pair_send=pltpu.SemaphoreType.DMA((8,)),
        pair_recv=pltpu.SemaphoreType.DMA((8,)),
    )


def backward_kernel(*refs):
    names = BackwardInputs._fields + tuple(BACKWARD_OUTPUTS) + tuple(backward_scratch())
    s = SimpleNamespace(**dict(zip(names, refs, strict=True)))
    spot = place()
    greet(neighbours(*spot))
    reduce = Reduce(s, spot)
    work = Backward(s, spot, reduce)

    def scoped(act, before=None, **shapes):
        def run(*held):
            f = SimpleNamespace(**dict(zip(shapes, held, strict=True)))
            if before is not None:
                before(f)
            act(f)

        pl.run_scoped(run, *shapes.values())

    def first_loads(f):
        work.load(11, s.o_hidden, f.hidden)
        work.load(12, s.o_branch, f.branch)
        work.load_ff(f, 0)

    scoped(
        work.feed_forward,
        first_loads,
        hidden=vmem(8, 192, 2 * TOK),
        branch=vmem(2 * TOK, D),
        w_down=vmem(2, 384, D),
        active=vmem(2, 2, TOK, WIDTH),
        steep=vmem(2, TOK, 2 * WIDTH),
    )
    scoped(work.middle, cot=vmem(TOK, D), attended=vmem(TOK, D))
    reduce.advance()
    scoped(
        work.attention,
        qkv=vmem(3, TOK, D),
        normed=vmem(2, TOK, D),
        soft=vmem(H // ATTN_STEPS, 2, SEQ, SEQ),
        back=vmem(TOK, D),
        cos=vmem(SEQ, D, kind=F32),
        sin=vmem(SEQ, D, kind=F32),
    )
    scoped(work.last, left=vmem(D, 2 * TOK), tokens=vmem(TOK, D), mod_w=vmem(MOD_PART, D))


def backward_pass(f, tokens, cotangent, mod_weight, tables):
    hbm = pl.BlockSpec(memory_space=pl.ANY)
    inside = pl.BlockSpec(memory_space=pltpu.VMEM)
    cosine, sine, spread, widen = tables
    given = BackwardInputs(
        f.packed_all,
        f.gate_all,
        f.up_all,
        f.down_all,
        f.o_branch,
        f.o_lhs,
        f.o_hidden,
        f.o_qkv,
        f.o_normed,
        f.o_scale,
        f.o_soft,
        f.o_attended,
        f.o_residual,
        f.o_active,
        tokens,
        cotangent,
        cosine,
        sine,
        f.o_mod,
        spread,
        widen,
        f.o_gate_b,
        mod_weight,
    )
    out = pl.pallas_call(
        backward_kernel,
        out_shape=[jax.ShapeDtypeStruct(*spec) for spec in BACKWARD_OUTPUTS.values()],
        in_specs=[hbm] * 18 + [inside] * 4 + [hbm],
        out_specs=[hbm] * 8 + [inside],
        scratch_shapes=list(backward_scratch().values()),
        name="backward_pass",
        compiler_params=pltpu.CompilerParams(
            collective_id=1, has_side_effects=True, vmem_limit_bytes=121 << 19
        ),
    )(*given)
    return SimpleNamespace(**dict(zip(BACKWARD_OUTPUTS, out)))


class SettleInputs(NamedTuple):
    packed: object
    gate: object
    up: object
    down: object
    acted: object
    back: object
    cond: object
    total: object


SETTLE_OUTPUTS = dict(
    g_qkv=((144, 3 * D), F32),
    g_proj=((144, D), F32),
    g_gate=((144, 8 * WIDTH), F32),
    g_up=((144, 8 * WIDTH), F32),
    g_down=((384, D), F32),
    g_mod=((144, MOD_PART), F32),
    g_bias=((1, MOD_PART), F32),
    g_cond=((2, D), F32),
)


def settle_scratch():
    return dict(
        v_packed=vmem(144, 4 * D),
        v_gate=vmem(144, 8 * WIDTH),
        v_up=vmem(144, 8 * WIDTH),
        v_down=vmem(384, D),
        w_qkv=vmem(144, 3 * D, kind=F32),
        w_proj=vmem(144, D, kind=F32),
        w_gate=vmem(144, 8 * WIDTH, kind=F32),
        w_up=vmem(144, 8 * WIDTH, kind=F32),
        w_down=vmem(384, D, kind=F32),
        w_mod=vmem(144, MOD_PART, kind=F32),
        load_sems=pltpu.SemaphoreType.DMA((4,)),
        store_sems=pltpu.SemaphoreType.DMA((6,)),
    )


def settle_kernel(*refs):
    names = SettleInputs._fields + tuple(SETTLE_OUTPUTS) + tuple(settle_scratch())
    s = SimpleNamespace(**dict(zip(names, refs, strict=True)))
    pairs = ((s.packed, s.v_packed), (s.gate, s.v_gate), (s.up, s.v_up), (s.down, s.v_down))
    loads = [pltpu.make_async_copy(a, b, s.load_sems.at[k]) for k, (a, b) in enumerate(pairs)]
    for load in loads:
        load.start()
    stores = []

    def store(source, target):
        copy = pltpu.make_async_copy(source, target, s.store_sems.at[len(stores)])
        copy.start()
        stores.append(copy)

    def widen(source, target, offset=0):
        count = target.shape[0] // 16

        @pl.loop(0, count)
        def _(i):
            rows = rows_of(i, 16)
            columns = pl.ds(offset, target.shape[1])
            target[rows, :] = source[rows, columns].astype(F32)

    s.w_mod[...] = mm_tn(s.acted[...], s.back[...])
    store(s.w_mod, s.g_mod)
    loads[0].wait()
    widen(s.v_packed, s.w_qkv)
    store(s.w_qkv, s.g_qkv)
    widen(s.v_packed, s.w_proj, 3 * D)
    store(s.w_proj, s.g_proj)
    for k, (source, target, out) in enumerate(
        ((s.v_gate, s.w_gate, s.g_gate), (s.v_up, s.w_up, s.g_up), (s.v_down, s.w_down, s.g_down))
    ):
        loads[k + 1].wait()
        widen(source, target)
        store(target, out)
    s.g_bias[...] = jnp.sum(s.back[...].astype(F32), axis=0, keepdims=True)
    total = s.total[...]
    sigma = 1.0 / (1.0 + jnp.exp(-total))
    s.g_cond[...] = s.cond[0:2, :] * sigma * (1.0 + total * (1.0 - sigma))
    for copy in stores:
        copy.wait()


def settle(*given):
    hbm = pl.BlockSpec(memory_space=pl.ANY)
    inside = pl.BlockSpec(memory_space=pltpu.VMEM)
    out = pl.pallas_call(
        settle_kernel,
        out_shape=[jax.ShapeDtypeStruct(*spec) for spec in SETTLE_OUTPUTS.values()],
        in_specs=[hbm] * 4 + [inside] * 4,
        out_specs=[hbm] * 6 + [inside] * 2,
        scratch_shapes=list(settle_scratch().values()),
        name="settle",
        compiler_params=pltpu.CompilerParams(vmem_limit_bytes=60 << 20),
    )(*SettleInputs(*given))
    return SimpleNamespace(**dict(zip(SETTLE_OUTPUTS, out)))


def body_general(
    tokens,
    condition,
    timestep,
    qkv_weight,
    out_weight,
    gate_weight,
    up_weight,
    down_weight,
    mod_weight,
    mod_bias,
    cotangent,
):
    gathered = (
        lax.all_gather(qkv_weight, "dp", axis=0, tiled=True),
        lax.all_gather(out_weight, "dp", axis=0, tiled=True),
        lax.all_gather(gate_weight, "dp", axis=0, tiled=True),
        lax.all_gather(up_weight, "dp", axis=0, tiled=True),
        lax.all_gather(down_weight, "dp", axis=0, tiled=True),
    )
    cond_total = condition.astype(jnp.float32) + embed_steps(timestep)
    acted_cond = jax.nn.silu(cond_total).astype(jnp.bfloat16)
    acted_group = lax.all_gather(acted_cond, "mod", axis=0, tiled=True)
    mod_part = (
        jnp.dot(acted_group, mod_weight, preferred_element_type=jnp.float32)
        + mod_bias.astype(jnp.float32)
    ).astype(jnp.bfloat16)
    modulation = lax.all_to_all(mod_part, "mod", split_axis=0, concat_axis=1, tiled=True).astype(
        jnp.float32
    )
    tables = rope_tables()
    per_micro = tokens.shape[0] // MICRO
    outputs = []
    token_grads = []
    mod_grads = []
    kept = []
    for micro_step in range(MICRO):
        start_row = micro_step * per_micro
        output, d_tokens, d_modulation, factors = layer_pass(
            tokens[start_row : start_row + per_micro],
            modulation[start_row : start_row + per_micro],
            cotangent[start_row : start_row + per_micro],
            gathered,
            tables,
        )
        outputs.append(output)
        token_grads.append(d_tokens)
        mod_grads.append(d_modulation)
        kept.append(factors)
    joined = [jnp.concatenate([factors[number] for factors in kept], axis=0) for number in range(9)]
    (
        entry_first,
        d_projected,
        combined,
        d_attended,
        entry_second,
        d_gate_proj,
        d_up_proj,
        hidden,
        d_branch,
    ) = joined
    grad_qkv = jnp.einsum(
        "bsd,bse->de", entry_first, d_projected, preferred_element_type=jnp.float32
    )
    grad_proj = jnp.einsum("bsd,bse->de", combined, d_attended, preferred_element_type=jnp.float32)
    grad_gate = jnp.einsum(
        "bsd,bsf->df", entry_second, d_gate_proj, preferred_element_type=jnp.float32
    )
    grad_up = jnp.einsum("bsd,bsf->df", entry_second, d_up_proj, preferred_element_type=jnp.float32)
    grad_down = jnp.einsum("bsf,bsd->fd", hidden, d_branch, preferred_element_type=jnp.float32)
    totals = (grad_qkv, grad_proj, grad_gate, grad_up, grad_down)
    output_tokens = jnp.concatenate(outputs, axis=0)
    grad_tokens = jnp.concatenate(token_grads, axis=0)
    mod_grad = jnp.concatenate(mod_grads, axis=0)
    mod_back = lax.all_to_all(mod_grad, "mod", split_axis=1, concat_axis=0, tiled=True)
    grad_mod_part = jnp.einsum(
        "id,ic->dc", acted_group, mod_back, preferred_element_type=jnp.float32
    )
    bias_part = jnp.sum(mod_back.astype(jnp.float32), axis=0)
    acted_grad_part = jnp.einsum(
        "ic,dc->id", mod_back, mod_weight, preferred_element_type=jnp.float32
    )
    acted_grad = lax.psum_scatter(
        acted_grad_part.astype(jnp.bfloat16), "mod", scatter_dimension=0, tiled=True
    ).astype(jnp.float32)
    sigma_cond = jax.nn.sigmoid(cond_total)
    grad_condition = acted_grad * sigma_cond * (1.0 + cond_total * (1.0 - sigma_cond))
    grad_bias = lax.psum(bias_part, "dp")
    count = lax.axis_size("dp")
    arrays = totals + (grad_mod_part,)
    shapes = [array.shape for array in arrays]
    flat = lax.psum_scatter(pack_rows(arrays, count), "dp", scatter_dimension=0, tiled=True)
    summed = unpack_rows(flat, shapes, count)
    finished = (
        lax.psum(summed[0].astype(jnp.bfloat16), "mod").astype(jnp.float32),
        lax.psum(summed[1].astype(jnp.bfloat16), "mod").astype(jnp.float32),
        lax.psum(summed[2].astype(jnp.bfloat16), "mod").astype(jnp.float32),
        lax.psum(summed[3].astype(jnp.bfloat16), "mod").astype(jnp.float32),
        lax.psum(summed[4].astype(jnp.bfloat16), "mod").astype(jnp.float32),
    )
    grad_mod = summed[5]
    return (
        output_tokens,
        grad_tokens,
        grad_condition,
        finished[0],
        finished[1],
        finished[2],
        finished[3],
        finished[4],
        grad_mod,
        grad_bias,
    )


def body_fast(
    tokens,
    condition,
    timestep,
    qkv_weight,
    out_weight,
    gate_weight,
    up_weight,
    down_weight,
    mod_weight,
    mod_bias,
    cotangent,
):
    packed = jnp.concatenate([qkv_weight, out_weight], axis=1)
    cond_total = condition.astype(jnp.float32) + embed_steps(timestep)
    acted_cond = jax.nn.silu(cond_total).astype(jnp.bfloat16)
    acted_rows = acted_cond.astype(F32)
    acted_slim = jnp.pad(acted_rows.reshape(-1, 128), ((0, 6), (0, 0)))
    flat_tokens, flat_cotangent = tokens.reshape(TOK, D), cotangent.reshape(TOK, D)
    tables = head_tables()
    f = forward_pass(
        packed,
        gate_weight,
        up_weight,
        down_weight,
        flat_tokens,
        flat_cotangent,
        jnp.pad(acted_rows, ((0, 6), (0, 0))),
        mod_bias.astype(F32).reshape(1, -1),
        mod_weight.T,
        acted_slim,
        *tables,
    )
    b = backward_pass(f, flat_tokens, flat_cotangent, mod_weight.T, tables)
    acted_all = f.acted_all.reshape(32, -1)[:, : 2 * D].reshape(64, D).astype(BF16)
    back_all = b.o_back.reshape(64, -1)
    rows = D // 8
    acted_part = lax.dynamic_slice_in_dim(acted_all, lax.axis_index("dp") * rows, rows, 1)
    g = settle(b.g_packed, b.g_gate, b.g_up, b.g_down, acted_part, back_all, b.o_cond, cond_total)
    return (
        f.o_result.reshape(tokens.shape),
        b.g_tokens.reshape(tokens.shape),
        g.g_cond,
        g.g_qkv,
        g.g_proj,
        g.g_gate,
        g.g_up,
        g.g_down,
        g.g_mod,
        g.g_bias.reshape(-1),
    )


def pick_body(mesh):
    if dict(mesh.shape) == {"dp": 8, "mod": 4}:
        return body_fast
    return body_general


def solution(mesh):
    in_specs = (
        P(("dp", "mod"), None, None),
        P(("dp", "mod"), None),
        P(("dp", "mod")),
        P("dp", None),
        P("dp", None),
        P("dp", None),
        P("dp", None),
        P("dp", None),
        P(None, "mod"),
        P("mod"),
        P(("dp", "mod"), None, None),
    )
    out_specs = (
        P(("dp", "mod"), None, None),
        P(("dp", "mod"), None, None),
        P(("dp", "mod"), None),
        P("dp", None),
        P("dp", None),
        P("dp", None),
        P("dp", None),
        P("dp", None),
        P("dp", "mod"),
        P("mod"),
    )
    return jax.shard_map(pick_body(mesh), mesh=mesh, in_specs=in_specs, out_specs=out_specs, check_vma=False)
```

```python
import math
from types import SimpleNamespace
from typing import NamedTuple

import jax
import jax.numpy as jnp
from jax import lax
import numpy as np
from jax.experimental import pallas as pl
from jax.experimental.pallas import tpu as pltpu
from jax.sharding import PartitionSpec as P

D = 1152
H = 16
HD = 72
GRID = 16
SEQ = 256
MICRO = 2


EPSILON = 1e-06


def norm_rows(field):
    scale_inv = lax.rsqrt(jnp.mean(field * field, axis=-1, keepdims=True) + EPSILON)
    return (field * scale_inv, scale_inv)


def norm_back(normed, scale_inv, gradient):
    return scale_inv * (gradient - normed * jnp.mean(gradient * normed, axis=-1, keepdims=True))


def embed_steps(timestep):
    half_width = D // 2
    frequency = jnp.exp(-math.log(10000.0) * jnp.arange(half_width, dtype=jnp.float32) / half_width)
    angles = timestep.astype(jnp.float32)[:, None] * frequency[None, :]
    return jnp.concatenate([jnp.cos(angles), jnp.sin(angles)], axis=1)


def rope_tables():
    quarter = HD // 4
    frequency = jnp.exp(-math.log(10000.0) * jnp.arange(quarter, dtype=jnp.float32) / quarter)
    position = jnp.arange(SEQ)
    row_index = (position // GRID).astype(jnp.float32)
    col_index = (position % GRID).astype(jnp.float32)
    angles = jnp.stack(
        [row_index[:, None] * frequency[None, :], col_index[:, None] * frequency[None, :]], axis=1
    )
    return (jnp.cos(angles), jnp.sin(angles))


def rotate(field, cosine_table, sine_table):
    leading = field.shape[:-1]
    quarters = field.reshape(leading + (2, 2, HD // 4))
    first_half = quarters[..., 0, :]
    second_half = quarters[..., 1, :]
    cosine_rows = cosine_table[:, None]
    sine_rows = sine_table[:, None]
    turned_first = first_half * cosine_rows - second_half * sine_rows
    turned_second = first_half * sine_rows + second_half * cosine_rows
    return jnp.stack([turned_first, turned_second], axis=-2).reshape(field.shape)


def pack_rows(arrays, count):
    return jnp.concatenate([array.reshape(count, -1) for array in arrays], axis=1).reshape(-1)


def unpack_rows(flat, shapes, count):
    pieces = []
    offset = 0
    for rows_all, columns in shapes:
        rows = rows_all // count
        pieces.append(flat[offset : offset + rows * columns].reshape(rows, columns))
        offset = offset + rows * columns
    return pieces


def layer_pass(block_in, mod_rows, cotangent, weights, tables):
    qkv_full, proj_full, gate_full, up_full, down_full = weights
    cosine_table, sine_table = tables
    images = block_in.shape[0]
    shift_first, scale_first, gate_first, shift_second, scale_second, gate_second = [
        mod_rows[:, None, number * D : (number + 1) * D] for number in range(6)
    ]
    heads_shape = (images, SEQ, H, HD)
    factor = 1.0 / math.sqrt(HD)
    inputs = block_in.astype(jnp.float32)
    normed_first, inv_first = norm_rows(inputs)
    entry_first = (normed_first * (1.0 + scale_first) + shift_first).astype(jnp.bfloat16)
    projected = jnp.einsum("bsd,de->bse", entry_first, qkv_full, preferred_element_type=jnp.float32)
    q_normed, q_inv = norm_rows(projected[..., :D].reshape(heads_shape))
    k_normed, k_inv = norm_rows(projected[..., D : 2 * D].reshape(heads_shape))
    queries = rotate(q_normed, cosine_table, sine_table).astype(jnp.bfloat16)
    keys_rot = rotate(k_normed, cosine_table, sine_table).astype(jnp.bfloat16)
    values = projected[..., 2 * D :].reshape(heads_shape).astype(jnp.bfloat16)
    scores = (
        jnp.einsum("bqhd,bkhd->bhqk", queries, keys_rot, preferred_element_type=jnp.float32)
        * factor
    )
    highest = jnp.max(scores, axis=-1, keepdims=True)
    log_total = highest + jnp.log(jnp.sum(jnp.exp(scores - highest), axis=-1, keepdims=True))
    weights_soft = jnp.exp(scores - log_total).astype(jnp.bfloat16)
    combined = (
        jnp.einsum("bhqk,bkhd->bqhd", weights_soft, values, preferred_element_type=jnp.float32)
        .reshape(images, SEQ, D)
        .astype(jnp.bfloat16)
    )
    attended = jnp.einsum("bsd,de->bse", combined, proj_full, preferred_element_type=jnp.float32)
    residual = inputs + gate_first * attended
    normed_second, inv_second = norm_rows(residual)
    entry_second = (normed_second * (1.0 + scale_second) + shift_second).astype(jnp.bfloat16)
    gate_proj = jnp.einsum(
        "bsd,df->bsf", entry_second, gate_full, preferred_element_type=jnp.float32
    )
    up_proj = jnp.einsum("bsd,df->bsf", entry_second, up_full, preferred_element_type=jnp.float32)
    sigma_gate = jax.nn.sigmoid(gate_proj)
    activated = gate_proj * sigma_gate
    hidden = (activated * up_proj).astype(jnp.bfloat16)
    branch = jnp.einsum("bsf,fd->bsd", hidden, down_full, preferred_element_type=jnp.float32)
    output = (residual + gate_second * branch).astype(jnp.bfloat16)
    grad_out = cotangent.astype(jnp.float32)
    d_gate_second = jnp.sum(grad_out * branch, axis=1)
    d_branch = (gate_second * grad_out).astype(jnp.bfloat16)
    d_hidden = jnp.einsum("bsd,fd->bsf", d_branch, down_full, preferred_element_type=jnp.float32)
    d_gate_proj = (d_hidden * up_proj * sigma_gate * (1.0 + gate_proj * (1.0 - sigma_gate))).astype(
        jnp.bfloat16
    )
    d_up_proj = (d_hidden * activated).astype(jnp.bfloat16)
    d_entry_second = jnp.einsum(
        "bsf,df->bsd", d_gate_proj, gate_full, preferred_element_type=jnp.float32
    )
    d_entry_second = d_entry_second + jnp.einsum(
        "bsf,df->bsd", d_up_proj, up_full, preferred_element_type=jnp.float32
    )
    d_shift_second = jnp.sum(d_entry_second, axis=1)
    d_scale_second = jnp.sum(d_entry_second * normed_second, axis=1)
    d_residual = grad_out + norm_back(
        normed_second, inv_second, d_entry_second * (1.0 + scale_second)
    )
    d_gate_first = jnp.sum(d_residual * attended, axis=1)
    d_attended = (gate_first * d_residual).astype(jnp.bfloat16)
    d_combined = (
        jnp.einsum("bse,de->bsd", d_attended, proj_full, preferred_element_type=jnp.float32)
        .astype(jnp.bfloat16)
        .reshape(heads_shape)
    )
    scores_again = (
        jnp.einsum("bqhd,bkhd->bhqk", queries, keys_rot, preferred_element_type=jnp.float32)
        * factor
    )
    recomputed = jnp.exp(scores_again - log_total)
    d_weights = jnp.einsum(
        "bqhd,bkhd->bhqk", d_combined, values, preferred_element_type=jnp.float32
    )
    d_scores = (
        recomputed * (d_weights - jnp.sum(recomputed * d_weights, axis=-1, keepdims=True))
    ).astype(jnp.bfloat16)
    d_values = jnp.einsum(
        "bhqk,bqhd->bkhd", weights_soft, d_combined, preferred_element_type=jnp.float32
    ).astype(jnp.bfloat16)
    d_queries = (
        (
            jnp.einsum("bhqk,bkhd->bqhd", d_scores, keys_rot, preferred_element_type=jnp.float32)
            * factor
        )
        .astype(jnp.bfloat16)
        .astype(jnp.float32)
    )
    d_keys = (
        (
            jnp.einsum("bhqk,bqhd->bkhd", d_scores, queries, preferred_element_type=jnp.float32)
            * factor
        )
        .astype(jnp.bfloat16)
        .astype(jnp.float32)
    )
    d_q_raw = norm_back(q_normed, q_inv, rotate(d_queries, cosine_table, -sine_table))
    d_k_raw = norm_back(k_normed, k_inv, rotate(d_keys, cosine_table, -sine_table))
    flat_shape = (images, SEQ, D)
    d_projected = jnp.concatenate(
        [
            d_q_raw.reshape(flat_shape),
            d_k_raw.reshape(flat_shape),
            d_values.astype(jnp.float32).reshape(flat_shape),
        ],
        axis=-1,
    ).astype(jnp.bfloat16)
    d_entry_first = jnp.einsum(
        "bse,de->bsd", d_projected, qkv_full, preferred_element_type=jnp.float32
    )
    d_shift_first = jnp.sum(d_entry_first, axis=1)
    d_scale_first = jnp.sum(d_entry_first * normed_first, axis=1)
    d_tokens = d_residual + norm_back(normed_first, inv_first, d_entry_first * (1.0 + scale_first))
    d_modulation = jnp.concatenate(
        [d_shift_first, d_scale_first, d_gate_first, d_shift_second, d_scale_second, d_gate_second],
        axis=1,
    ).astype(jnp.bfloat16)
    factors = (
        entry_first,
        d_projected,
        combined,
        d_attended,
        entry_second,
        d_gate_proj,
        d_up_proj,
        hidden,
        d_branch,
    )
    return (output, d_tokens, d_modulation, factors)


MESH = pl.DeviceIdType.MESH
WIDTH = 384
LANE_HALF = 2304
FF_HALF = 1536
BF16 = jnp.bfloat16
F32 = jnp.float32


def place():
    dp = lax.axis_index("dp")
    mod = lax.axis_index("mod")
    return dp // 2, dp % 2, mod // 2, mod % 2


def device(z, x, y, c):
    return (z * 2 + x, y * 2 + c)


def greet(peers):
    barrier = pltpu.get_barrier_semaphore()
    for peer in peers:
        pl.semaphore_signal(barrier, inc=1, device_id=peer, device_id_type=MESH)
    pl.semaphore_wait(barrier, len(peers))


def neighbours(z, x, y, c):
    around = [device((z + step) % 4, x, y, c) for step in (1, 2, 3)]
    return around + [device(z, 1 - x, y, c), device(z, x, 1 - y, c), device(z, x, y, 1 - c)]


def send(source, target, send_sem, recv_sem, peer):
    pltpu.make_async_remote_copy(
        src_ref=source,
        dst_ref=target,
        send_sem=send_sem,
        recv_sem=recv_sem,
        device_id=peer,
        device_id_type=MESH,
    ).start()


def drain(window, sem):
    pltpu.make_async_copy(window, window, sem).wait()


class Piece:
    def __init__(self, source, target, row, rows, column, edge):
        self.source, self.target = source, target
        self.row, self.rows, self.column, self.edge = row, rows, column, edge


def gather_pieces(refs, c, edge_of):
    packed, gate, up, down, packed_all, gate_all, up_all, down_all = refs
    pieces = []
    for j in range(6):
        pieces.append(Piece(packed, packed_all, 0, 144, c * LANE_HALF + j * WIDTH, edge_of(144, j)))
    for j in range(4):
        pieces.append(Piece(gate, gate_all, 0, 144, c * FF_HALF + j * WIDTH, edge_of(144, j)))
        pieces.append(Piece(up, up_all, 0, 144, c * FF_HALF + j * WIDTH, edge_of(144, j)))
    for j in range(3):
        pieces.append(Piece(down, down_all, c * 192, 192, j * WIDTH, edge_of(192, j)))
    return pieces


class Gather:
    def __init__(self, refs, sems, spot, stages):
        self.z, self.x, self.y, self.c = spot
        self.stages = stages
        self.pieces = gather_pieces(refs, self.c, lambda rows, j: 64 if rows == 144 and j % 3 == 2 else rows // 3)
        self.send_sems, self.recv_sems, self.own_sems = sems
        self.refs = refs

    def columns(self, piece):
        return pl.ds(pl.multiple_of(piece.column, 128), WIDTH)

    def part(self, piece):
        keep = piece.rows - piece.edge
        return pl.ds(pl.multiple_of(piece.row + self.y * piece.edge, 16), keep), keep

    def mine(self, piece):
        return pl.ds(pl.multiple_of(piece.row + self.y * (piece.rows - piece.edge), 16), piece.edge)

    def own_copies(self):
        for k in range(4):
            pltpu.make_async_copy(self.refs[k], self.stages[k], self.own_sems.at[k]).start()

    def own_stores(self):
        for k in range(4):
            drain(self.stages[k], self.own_sems.at[k])
            pltpu.make_async_copy(
                self.stages[k], self.refs[4 + k].at[self.z, self.x], self.own_sems.at[k]
            ).start()

    def own_done(self):
        for k in range(4):
            drain(self.stages[k], self.own_sems.at[k])

    def start_z(self, t):
        p = self.pieces[t]
        rows, _ = self.part(p)
        here = p.source.at[rows, self.columns(p)]
        there = p.target.at[self.z, self.x, rows, self.columns(p)]
        for step in (1, 3, 2):
            peer = device((self.z + step) % 4, self.x, self.y, self.c)
            send(here, there, self.send_sems.at[0, t], self.recv_sems.at[0, t], peer)
        peer = device(self.z, 1 - self.x, self.y, self.c)
        send(here, there, self.send_sems.at[1, t], self.recv_sems.at[1, t], peer)

    def start_x(self, t):
        p = self.pieces[t]
        rows, keep = self.part(p)
        columns = self.columns(p)
        drain(p.target.at[pl.ds(0, 3), 0, pl.ds(0, keep), pl.ds(0, WIDTH)], self.recv_sems.at[0, t])
        x_peer = device(self.z, 1 - self.x, self.y, self.c)
        y_peer = device(self.z, self.x, 1 - self.y, self.c)
        for step in (1, 3, 2):
            other = (self.z + step) % 4
            block = p.target.at[other, self.x, rows, columns]
            send(block, block, self.send_sems.at[1, t], self.recv_sems.at[1, t], x_peer)
        for step in (1, 3, 2):
            other = (self.z + step) % 4
            block = p.target.at[other, self.x, self.mine(p), columns]
            send(block, block, self.send_sems.at[2, t], self.recv_sems.at[2, t], y_peer)

    def start_y(self, t):
        p = self.pieces[t]
        _, keep = self.part(p)
        columns = self.columns(p)
        drain(p.target.at[:, 0, pl.ds(0, keep), pl.ds(0, WIDTH)], self.recv_sems.at[1, t])
        y_peer = device(self.z, self.x, 1 - self.y, self.c)
        block = p.target.at[:, 1 - self.x, self.mine(p), columns]
        send(block, block, self.send_sems.at[2, t], self.recv_sems.at[2, t], y_peer)

    def start_c(self, t):
        p = self.pieces[t]
        columns = self.columns(p)
        half = pl.ds(pl.multiple_of(p.row, 16), p.rows)
        self.drain_seven(p.edge, self.recv_sems.at[2, t])
        peer = device(self.z, self.x, self.y, 1 - self.c)
        block = p.target.at[:, 1 - self.x, half, columns]
        send(block, block, self.send_sems.at[3, t], self.recv_sems.at[3, t], peer)
        for step in (1, 2, 3):
            block = p.target.at[(self.z + step) % 4, self.x, half, columns]
            send(block, block, self.send_sems.at[3, t], self.recv_sems.at[3, t], peer)

    def arrived(self, t):
        self.drain_seven(self.pieces[t].rows, self.recv_sems.at[3, t])

    def drain_seven(self, rows, sem):
        high = 96 if rows > 144 else rows
        drain(self.refs[4].at[pl.ds(0, rows // high), 0, pl.ds(0, high), pl.ds(0, 7 * WIDTH)], sem)

    def sent_z(self, t):
        p = self.pieces[t]
        _, keep = self.part(p)
        drain(p.target.at[pl.ds(0, 3), 0, pl.ds(0, keep), pl.ds(0, WIDTH)], self.send_sems.at[0, t])

    def sent_rest(self, t):
        p = self.pieces[t]
        _, keep = self.part(p)
        drain(p.target.at[:, 0, pl.ds(0, keep), pl.ds(0, WIDTH)], self.send_sems.at[1, t])
        for stage, rows in ((2, p.edge), (3, p.rows)):
            self.drain_seven(rows, self.send_sems.at[stage, t])


N_PIECES = 17


class Group:
    def __init__(self, spot, parts, got_c, got_y, blocks, send_sems, recv_sems):
        _, _, self.y, self.c = spot
        z, x, y, c = spot
        self.sibling, self.across = device(z, x, y, 1 - c), device(z, x, 1 - y, c)
        self.parts, self.got_c, self.got_y, self.blocks = parts, got_c, got_y, blocks
        self.send_sems, self.recv_sems = send_sems, recv_sems

    def sems(self, k):
        return self.send_sems.at[k], self.recv_sems.at[k]

    def start(self):
        for y in range(2):
            source = self.parts.at[2 * y + 1 - self.c]
            send(source, self.got_c.at[y], *self.sems(y), self.sibling)

    def across_y(self):
        for y in range(2):
            drain(self.got_c.at[y], self.recv_sems.at[y])
        own = self.parts.at[2 * (1 - self.y) + self.c]
        send(own, self.got_y.at[self.c], *self.sems(2), self.across)
        send(self.got_c.at[1 - self.y], self.got_y.at[1 - self.c], *self.sems(3), self.across)

    def finish(self):
        for k in (2, 3):
            drain(self.got_y.at[k - 2], self.recv_sems.at[k])
        y, c, blocks = self.y, self.c, self.blocks
        blocks[2 * y + c] = self.parts[2 * y + c]
        blocks[2 * y + 1 - c] = self.got_c[y]
        for k in range(2):
            blocks[2 * (1 - y) + k] = self.got_y[k]
        for k in range(4):
            drain(self.got_y.at[k % 2], self.send_sems.at[k])


def group_scratch(columns):
    return [
        pltpu.VMEM((4, 8, columns), F32),
        pltpu.VMEM((2, 8, columns), F32),
        pltpu.VMEM((2, 8, columns), F32),
        pltpu.VMEM((4, 8, columns), F32),
        pltpu.SemaphoreType.DMA((4,)),
        pltpu.SemaphoreType.DMA((4,)),
    ]


MOD_PART = 1728
SLIM = (24, 128)


class Acted:
    def __init__(self, s, spot):
        self.s = s
        self.z, self.x, self.y, self.c = spot

    def hop(self, k, where, peers):
        block = self.s.acted_all.at[where]
        for peer in peers:
            send(block, block, self.s.acted_send.at[k], self.s.acted_recv.at[k], peer)

    def step(self, k):
        z, x, y, c = self.z, self.x, self.y, self.c
        s = self.s
        if k == 0:
            pltpu.make_async_copy(s.acted_slim, s.acted_all.at[z, x, y, c], s.acted_own).start()
            drain(s.acted_slim, s.acted_own)
            self.hop(0, (z, x, y, c), [device(z, x, y, 1 - c)])
        elif k == 1:
            drain(s.acted_slim, s.acted_recv.at[0])
            self.hop(1, (z, x, y), [device(z, x, 1 - y, c)])
        elif k == 2:
            drain(s.acted_all.at[0, 0, 0], s.acted_recv.at[1])
            self.hop(2, (z, x), [device(z, 1 - x, y, c)])
        elif k == 3:
            drain(s.acted_all.at[0, 0], s.acted_recv.at[2])
            self.hop(3, (z,), [device((z + step) % 4, x, y, c) for step in (1, 3, 2)])
        else:
            drain(s.acted_all.at[pl.ds(0, 3)], s.acted_recv.at[3])
            drain(s.acted_slim, s.acted_send.at[0])
            drain(s.acted_all.at[0, 0, 0], s.acted_send.at[1])
            drain(s.acted_all.at[0, 0], s.acted_send.at[2])
            drain(s.acted_all.at[pl.ds(0, 3)], s.acted_send.at[3])


TOK = 512
TILE = 128
HEAD_TILE = 256
ATTN_STEPS = 4
STEP_BUDGET = 3.0
GATHER_AHEAD = 2


def mm(left, right):
    return lax.dot_general(left, right, (((1,), (0,)), ((), ())), preferred_element_type=F32)


def mm_nt(left, right):
    return lax.dot_general(left, right, (((1,), (1,)), ((), ())), preferred_element_type=F32)


def mm_tn(left, right):
    return lax.dot_general(left, right, (((0,), (0,)), ((), ())), preferred_element_type=F32)


def split(value):
    high = value.astype(BF16)
    return high, (value - high.astype(F32)).astype(BF16)


def mm_split(value, right):
    high, low = split(value)
    return mm(high, right) + mm(low, right)


def partner(value, first):
    width = value.shape[1]
    return jnp.where(first, pltpu.roll(value, width - 18, 1), pltpu.roll(value, 18, 1))


def first_lanes(rows):
    return lax.broadcasted_iota(jnp.int32, (rows, D), 1) % 36 < 18


def rows_of(block, count):
    return pl.ds(pl.multiple_of(block * count, count), count)


def head_window(head):
    base = min(head * HD // 128 * 128, D - 256)
    offset = head * HD - base
    lane = lax.broadcasted_iota(jnp.int32, (SEQ, 256), 1)
    return base, (lane >= offset) & (lane < offset + HD)


def flat(ref_value):
    return ref_value.reshape(-1, ref_value.shape[-1])


class Saves:
    def __init__(self, sems):
        self.sems, self.count, self.open = sems, 0, []

    def local(self, source, target):
        copy = pltpu.make_async_copy(source, target, self.sems.at[self.count])
        self.count += 1
        copy.start()
        self.open.append(copy)
        return copy

    def done(self, copy):
        copy.wait()
        self.open = [other for other in self.open if other is not copy]

    def finish(self):
        for copy in self.open:
            copy.wait()


class Forward:
    def __init__(self, s, spot, gather):
        self.s, self.gather = s, gather
        self.z, self.x, self.y, self.c = spot
        self.saves = Saves(s.save_sems)
        self.pending = {}
        self.remote = []
        self.slots = {}


    def to_sibling(self, source, target):
        k = len(self.remote)
        peer = device(self.z, self.x, self.y, 1 - self.c)
        copy = pltpu.make_async_remote_copy(
            src_ref=source,
            dst_ref=target,
            send_sem=self.s.pair_send.at[k],
            recv_sem=self.s.pair_recv.at[k],
            device_id=peer,
            device_id_type=MESH,
        )
        copy.start()
        self.remote.append(copy)


    def load(self, key, part, source, target):
        if (key, part) not in self.pending:
            copy = pltpu.make_async_copy(source, target, self.s.load_sems.at[len(self.pending)])
            copy.start()
            self.pending[key, part] = copy

    def window(self, ref, column):
        return ref.at[:, :, :, pl.ds(column, WIDTH)]

    def load_qv(self, j):
        packed, target = self.gather.refs[4], self.s.w.at[j % 2, 0]
        self.load(j, 0, self.window(packed, j * WIDTH), self.window(target, 0))
        self.load(j, 1, self.window(packed, LANE_HALF + j * WIDTH), self.window(target, WIDTH))

    def load_ko(self, j):
        packed = self.gather.refs[4]
        self.load(j, 0, self.window(packed, j * WIDTH), self.window(self.s.w.at[j % 2, 0], 0))
        target = self.window(self.s.w_out, (j - 3) * WIDTH)
        self.load(j, 1, self.window(packed, LANE_HALF + j * WIDTH), target)

    def load_ff(self, j):
        for part in range(4):
            which, half = part // 2, part % 2
            target = self.window(self.s.w.at[j % 2, which], half * WIDTH)
            self.load(6 + j, part, self.window(self.gather.refs[5 + which], (j + 4 * half) * WIDTH), target)

    def load_down(self, j):
        self.load(14 + j, 0, self.window(self.gather.refs[7], j * WIDTH), self.s.w_down.at[j % 2])

    def loaded(self, load, j, key):
        load(j)
        for part in range(4):
            if (key, part) in self.pending:
                self.pending[key, part].wait()


    def modulate(self, k):
        s, y, c = self.s, self.y, self.c
        spot = (self.z, self.x, y, c)
        own = s.acted_group.at[2 * y + c]
        pair = s.acted_group.at[pl.ds(2 * y, 2)]
        load = pltpu.make_async_copy(s.mod_weight, s.mod_w, s.acted_own)
        group = Group(
            spot, s.mod_parts, s.mod_got_c, s.mod_got_y, s.mod_blocks, s.mod_send, s.mod_recv
        )
        if k == 0:
            load.start()
            s.acted_group[2 * y + c] = s.acted[...]
            send(own, own, *self.first(0), device(self.z, self.x, y, 1 - c))
        elif k == 1:
            drain(own, s.first_recv.at[0])
            send(pair, pair, *self.first(1), device(self.z, self.x, 1 - y, c))
        elif k == 2:
            load.wait()
            drain(pair, s.first_recv.at[1])
            total = mm_nt(s.acted_group[...].reshape(32, D).astype(BF16), s.mod_w[...]) + s.bias[...]
            s.mod_parts[...] = total.astype(BF16).astype(F32).reshape(4, 8, MOD_PART)
            group.start()
        elif k == 3:
            group.across_y()
        else:
            group.finish()
            for m in range(4):
                s.mod_flat[:, m * MOD_PART : (m + 1) * MOD_PART] = s.mod_blocks[m]
            for image in range(2):
                for m in range(6):
                    row = s.mod_flat[image : image + 1, m * D : (m + 1) * D]
                    s.o_mod[image, m : m + 1, :] = row
            drain(own, s.first_send.at[0])
            drain(pair, s.first_send.at[1])

    def first(self, k):
        return self.s.first_send.at[k], self.s.first_recv.at[k]

    def enter(self):
        s = self.s

        @pl.loop(0, TOK // TILE)
        def _(i):
            rows = rows_of(i, TILE)
            image = i // (SEQ // TILE)
            mod = s.o_mod
            normed, _ = norm_rows(s.tokens[rows, :].astype(F32))
            entry = normed * (1.0 + mod[image, 1:2, :]) + mod[image, 0:1, :]
            s.entry_a[rows, :] = entry.astype(BF16)
            branch = mod[image, 5:6, :] * s.cot[rows, :].astype(F32)
            s.d_branch[rows, :] = branch.astype(BF16)

        self.saves.local(s.d_branch, s.o_branch.at[pl.ds(0, TOK)])
        self.to_sibling(s.d_branch, s.o_branch.at[pl.ds(TOK, TOK)])
        self.turn(s.entry_a, s.t_a)
        self.share(s.t_a, s.o_lhs.at[0])

    def turn(self, source, target):
        @pl.loop(0, source.shape[1] // 128)
        def _(i):
            columns = rows_of(i, 128)
            target[columns, :] = source[:, columns].T

    def share(self, source, target):
        self.shared = [self.saves.local(source, target.at[:, pl.ds(0, TOK)])]
        self.to_sibling(source, target.at[:, pl.ds(TOK, TOK)])

    def qv(self, j):
        s = self.s
        self.loaded(self.load_qv, j, j)
        columns = pl.ds(j * WIDTH, WIDTH)
        both = mm(s.entry_a[...], flat(s.w[j % 2, 0]))
        s.proj[:, columns] = both[:, :WIDTH]
        s.v[:, columns] = both[:, WIDTH:].astype(BF16)
        if j == 2:
            self.saves.local(s.v, s.o_qkv.at[2])

    def ko(self, j):
        s = self.s
        self.loaded(self.load_ko, j, j)
        columns = pl.ds((j - 3) * WIDTH, WIDTH)
        s.proj[:, columns] = mm(s.entry_a[...], flat(s.w[j % 2, 0, :, :, :, 0:WIDTH]))

    def head_norm(self, which):
        s = self.s
        target, normed = (s.q, s.q_normed) if which == 0 else (s.k, s.k_normed)
        scale = s.scale_q if which == 0 else s.scale_k

        @pl.loop(0, TOK // HEAD_TILE)
        def _(i):
            rows = rows_of(i, HEAD_TILE)
            spots = rows_of(i % (SEQ // HEAD_TILE), HEAD_TILE)
            field = s.proj[rows, :]
            inverse = lax.rsqrt(mm_split(field * field, s.spread[...]) * (1.0 / HD) + EPSILON)
            scale[rows, :] = inverse
            field = field * mm_split(inverse, s.widen[...])
            normed[rows, :] = field.astype(BF16)
            turned = field * s.cos[spots, :] + partner(field, first_lanes(HEAD_TILE)) * s.sin[spots, :]
            target[rows, :] = turned.astype(BF16)

        self.saves.local(target, s.o_qkv.at[which])
        self.saves.local(normed, s.o_normed.at[which])
        self.saves.local(scale, s.o_scale.at[which])

    def attend(self, k):
        s = self.s
        heads = H // ATTN_STEPS
        if k >= 1:
            self.saves.done(self.slots[k - 1])
        for i in range(heads):
            base, mask = head_window(k * heads + i)
            window = pl.ds(base, 256)
            for image in range(2):
                rows = pl.ds(image * SEQ, SEQ)
                query = jnp.where(mask, s.q[rows, window].astype(F32), 0.0).astype(BF16)
                scores = mm_nt(query, s.k[rows, window]) * (1.0 / math.sqrt(HD))
                powers = jnp.exp(scores - jnp.max(scores, axis=1, keepdims=True))
                total = jnp.sum(powers, axis=1, keepdims=True)
                soft = (powers * (1.0 / total)).astype(BF16)
                s.soft[i, image] = soft
                mixed = mm(soft, s.v[rows, window])
                old = s.combined[rows, window].astype(F32)
                s.combined[rows, window] = jnp.where(mask, mixed, old).astype(BF16)

        self.slots[k] = self.saves.local(s.soft, s.o_soft.at[pl.ds(k * heads, heads)])

    def leave(self):
        s = self.s
        self.saves.done(self.slots[ATTN_STEPS - 1])
        for copy in self.shared:
            self.saves.done(copy)
        self.remote[1].wait_send()
        self.turn(s.combined, s.t_a)
        self.share(s.t_a, s.o_lhs.at[1])
        for j in range(3):
            columns = pl.ds(j * WIDTH, WIDTH)
            s.proj[:, columns] = mm(s.combined[...], flat(s.w_out[:, :, :, columns]))

        @pl.loop(0, TOK // TILE)
        def _(i):
            rows = rows_of(i, TILE)
            image = i // (SEQ // TILE)
            mod = s.o_mod
            attended = s.proj[rows, :]
            s.attended[rows, :] = attended.astype(BF16)
            residual = s.tokens[rows, :].astype(F32) + mod[image, 2:3, :] * attended
            s.residual[rows, :] = residual
            normed, _ = norm_rows(residual)
            entry = normed * (1.0 + mod[image, 4:5, :]) + mod[image, 3:4, :]
            s.entry_b[rows, :] = entry.astype(BF16)

        self.attended = self.saves.local(s.attended, s.o_attended)
        self.saves.local(s.residual, s.o_residual)
        self.turn(s.entry_b, s.t_b)
        self.share(s.t_b, s.o_lhs.at[2])

    def ff(self, j):
        s = self.s
        self.loaded(self.load_ff, j, 6 + j)
        s.wide[0] = mm(s.entry_b[...], flat(s.w[j % 2, 0]))
        s.wide[1] = mm(s.entry_b[...], flat(s.w[j % 2, 1]))
        mine = pl.ds(pl.multiple_of(self.c * 192, 16), 192)
        theirs = pl.ds(pl.multiple_of((1 - self.c) * 192, 16), 192)
        for half in range(2):
            shard = j + 4 * half
            at = shard * WIDTH
            if (6, j - 1, half) in self.slots:
                self.saves.done(self.slots[6, j - 1, half])

            @pl.loop(0, TOK // TILE)
            def _(i, half=half, at=at):
                rows = rows_of(i, TILE)
                gate = s.wide[0, rows, half * WIDTH : (half + 1) * WIDTH]
                up = s.wide[1, rows, half * WIDTH : (half + 1) * WIDTH]
                sigma = 1.0 / (1.0 + jnp.exp(-gate))
                active = gate * sigma
                s.active[half, 0, rows, :] = active.astype(BF16)
                slope = up * sigma * (1.0 + gate * (1.0 - sigma))
                s.active[half, 1, rows, :] = slope.astype(BF16)
                s.hidden[rows, at : at + WIDTH] = (active * up).astype(BF16)

            self.slots[6, j, half] = self.saves.local(s.active.at[half], s.o_active.at[shard])
            for i in range(3):
                turned = s.hidden[:, at + 128 * i : at + 128 * i + 128].T
                s.t_h[shard, 128 * i : 128 * i + 128, :] = turned
            self.saves.local(s.t_h.at[shard, mine], s.o_hidden.at[shard, :, pl.ds(0, TOK)])
            self.to_sibling(s.t_h.at[shard, theirs], s.o_hidden.at[shard, :, pl.ds(TOK, TOK)])

    def down(self, j):
        s = self.s
        self.loaded(self.load_down, j, 14 + j)
        if j == 0:
            self.saves.done(self.attended)
        columns = pl.ds(j * WIDTH, WIDTH)
        s.wide[0, :, 0:WIDTH] = mm(s.hidden[...], flat(s.w_down[j % 2]))
        for image in range(2):
            gate = s.o_mod[image, 5:6, columns]
            total = jnp.zeros((1, WIDTH), F32)
            for i in range(SEQ // TILE):
                rows = pl.ds(image * SEQ + i * TILE, TILE)
                branch = s.wide[0, rows, 0:WIDTH]
                result = s.residual[rows, columns] + gate * branch
                s.attended[rows, columns] = result.astype(BF16)
                total = total + jnp.sum(
                    s.cot[rows, columns].astype(F32) * branch, axis=0, keepdims=True
                )
            s.o_gate_b[image, 0:1, columns] = total
        if j == 2:
            self.saves.local(s.attended, s.o_result)

    def plan(self):
        steps = [(None, self.modulate, k, 0, 7) for k in range(5)] + [(None, self.enter, None, 0, 4)]
        steps += [(self.load_qv, self.qv, j, j + 1, 2.5) for j in range(3)]
        steps += [(None, self.head_norm, 0, 3, 4)]
        steps += [(self.load_ko, self.ko, j, j + 1, 1.5) for j in range(3, 6)]
        steps += [(None, self.head_norm, 1, 6, 4)]
        steps += [(None, self.attend, k, 6, 3) for k in range(ATTN_STEPS)]
        steps += [(None, self.leave, None, 6, 6)]
        steps += [(self.load_ff, self.ff, j, 8 + 2 * j, 5.5) for j in range(4)]
        steps += [(self.load_down, self.down, j, 15 + j, 3) for j in range(3)]
        return steps

    def finish(self):
        self.saves.finish()
        for k, copy in enumerate(self.remote):
            if k != 1:
                copy.wait_send()
            copy.wait_recv()


class ForwardInputs(NamedTuple):
    packed: object
    gate: object
    up: object
    down: object
    tokens: object
    cot: object
    acted: object
    bias: object
    mod_weight: object
    acted_slim: object
    cos: object
    sin: object
    spread: object
    widen: object


FORWARD_OUTPUTS = dict(
    packed_all=((4, 2, 144, 4608), BF16),
    gate_all=((4, 2, 144, 3072), BF16),
    up_all=((4, 2, 144, 3072), BF16),
    down_all=((4, 2, 384, 1152), BF16),
    o_branch=((2 * TOK, D), BF16),
    o_lhs=((3, D, 2 * TOK), BF16),
    o_hidden=((8, 192, 2 * TOK), BF16),
    o_qkv=((3, TOK, D), BF16),
    o_normed=((2, TOK, D), BF16),
    o_scale=((2, TOK, 128), F32),
    o_soft=((H, 2, SEQ, SEQ), BF16),
    o_attended=((TOK, D), BF16),
    o_residual=((TOK, D), F32),
    o_active=((8, 2, TOK, WIDTH), BF16),
    o_result=((TOK, D), BF16),
    acted_all=((4, 2, 2, 2) + SLIM, F32),
    o_mod=((2, 8, D), F32),
    o_gate_b=((2, 8, D), F32),
)


def forward_scratch():
    def vmem(*shape, kind=BF16):
        return pltpu.VMEM(shape, kind)

    return dict(
        entry_a=vmem(TOK, D),
        d_branch=vmem(TOK, D),
        t_a=vmem(D, TOK),
        proj=vmem(TOK, D, kind=F32),
        q=vmem(TOK, D),
        k=vmem(TOK, D),
        v=vmem(TOK, D),
        q_normed=vmem(TOK, D),
        k_normed=vmem(TOK, D),
        scale_q=vmem(TOK, 128, kind=F32),
        scale_k=vmem(TOK, 128, kind=F32),
        soft=vmem(H // ATTN_STEPS, 2, SEQ, SEQ),
        combined=vmem(TOK, D),
        attended=vmem(TOK, D),
        residual=vmem(TOK, D, kind=F32),
        entry_b=vmem(TOK, D),
        t_b=vmem(D, TOK),
        wide=vmem(2, TOK, 2 * WIDTH, kind=F32),
        active=vmem(2, 2, TOK, WIDTH),
        hidden=vmem(TOK, 8 * WIDTH),
        t_h=vmem(8, WIDTH, TOK),
        w=vmem(2, 2, 4, 2, 144, 2 * WIDTH),
        w_out=vmem(4, 2, 144, D),
        w_down=vmem(2, 4, 2, 384, WIDTH),
        gather_send=pltpu.SemaphoreType.DMA((4, N_PIECES)),
        gather_recv=pltpu.SemaphoreType.DMA((4, N_PIECES)),
        mod_w=vmem(MOD_PART, D),
        acted_group=vmem(4, 8, D, kind=F32),
        mod_flat=vmem(8, 4 * MOD_PART, kind=F32),
        mod_parts=group_scratch(MOD_PART)[0],
        mod_got_c=group_scratch(MOD_PART)[1],
        mod_got_y=group_scratch(MOD_PART)[2],
        mod_blocks=group_scratch(MOD_PART)[3],
        mod_send=group_scratch(MOD_PART)[4],
        mod_recv=group_scratch(MOD_PART)[5],
        acted_send=pltpu.SemaphoreType.DMA((4,)),
        acted_recv=pltpu.SemaphoreType.DMA((4,)),
        acted_own=pltpu.SemaphoreType.DMA,
        first_send=pltpu.SemaphoreType.DMA((2,)),
        first_recv=pltpu.SemaphoreType.DMA((2,)),
        own_packed=vmem(144, 4 * D),
        own_down=vmem(384, D),
        own_sems=pltpu.SemaphoreType.DMA((4,)),
        save_sems=pltpu.SemaphoreType.DMA((56,)),
        load_sems=pltpu.SemaphoreType.DMA((48,)),
        pair_send=pltpu.SemaphoreType.DMA((16,)),
        pair_recv=pltpu.SemaphoreType.DMA((16,)),
    )


def run_step(steps, arrived):
    _, act, j, _, cost = steps.pop(0)
    if steps and steps[0][0] is not None and steps[0][3] <= arrived:
        steps[0][0](steps[0][2])
    act() if j is None else act(j)
    return cost


def forward_kernel(*refs):
    names = ForwardInputs._fields + tuple(FORWARD_OUTPUTS) + tuple(forward_scratch())
    s = SimpleNamespace(**dict(zip(names, refs, strict=True)))
    spot = place()
    greet(neighbours(*spot))
    arrays = [s.packed, s.gate, s.up, s.down, s.packed_all, s.gate_all, s.up_all, s.down_all]
    own_gate, own_up = s.hidden.at[pl.ds(0, 144)], s.hidden.at[pl.ds(144, 144)]
    stages = [s.own_packed, own_gate, own_up, s.own_down]
    gather = Gather(arrays, (s.gather_send, s.gather_recv, s.own_sems), spot, stages)
    work = Forward(s, spot, gather)
    steps = work.plan()
    gather.own_copies()
    acted = Acted(s, spot)
    ahead = GATHER_AHEAD
    arrived = 0
    for t in range(N_PIECES + 4 + ahead):
        if t == 1:
            gather.own_stores()
        if t < N_PIECES:
            if t >= ahead:
                gather.sent_z(t - ahead)
            gather.start_z(t)
        if 0 <= t - ahead < N_PIECES:
            gather.start_x(t - ahead)
        if 0 <= t - ahead - 1 < N_PIECES:
            gather.start_y(t - ahead - 1)
        if 0 <= t - ahead - 2 < N_PIECES:
            gather.start_c(t - ahead - 2)
        if 0 <= t - ahead - 3 < N_PIECES:
            if arrived == 0:
                gather.own_done()
            gather.arrived(t - ahead - 3)
            arrived += 1
        if t >= 6 and t % 3 == 0 and t // 3 - 2 < 5:
            acted.step(t // 3 - 2)
        spent = 0.0
        while steps and steps[0][3] <= arrived and spent < STEP_BUDGET:
            spent += run_step(steps, arrived)
    while steps:
        run_step(steps, arrived)
    for t in range(N_PIECES - ahead, N_PIECES):
        gather.sent_z(t)
    for t in range(N_PIECES):
        gather.sent_rest(t)
    work.finish()


def forward_pass(*given):
    hbm = pl.BlockSpec(memory_space=pl.ANY)
    inside = pl.BlockSpec(memory_space=pltpu.VMEM)
    out = pl.pallas_call(
        forward_kernel,
        out_shape=[jax.ShapeDtypeStruct(*spec) for spec in FORWARD_OUTPUTS.values()],
        in_specs=[hbm] * 4 + [inside] * 4 + [hbm] * 2 + [inside] * 4,
        out_specs=[hbm] * 16 + [inside] * 2,
        scratch_shapes=list(forward_scratch().values()),
        name="forward_pass",
        compiler_params=pltpu.CompilerParams(
            collective_id=0, has_side_effects=True, vmem_limit_bytes=121 << 19
        ),
    )(*ForwardInputs(*given))
    return SimpleNamespace(**dict(zip(FORWARD_OUTPUTS, out)))


def head_tables():
    lane = np.arange(D) % HD
    frequency = np.exp(-math.log(10000.0) * (lane % 18) / 18)
    token = np.arange(SEQ)[:, None]
    angle = np.where(lane < 36, token // GRID, token % GRID) * frequency
    sign = np.where(lane % 36 < 18, -1.0, 1.0)
    spread = (np.arange(D)[:, None] // HD == np.arange(128)).astype(np.float32)
    return (
        jnp.asarray(np.cos(angle), F32),
        jnp.asarray(np.sin(angle) * sign, F32),
        jnp.asarray(spread, BF16),
        jnp.asarray(spread.T, BF16),
    )


SCATTER_ROWS = (144,) * 14 + (192,) * 3
SCATTER_EDGE = tuple((32, 48)[j % 2] for j in range(14)) + (48,) * 3
ASKED = 3
ORDER = (14, 15, 16) + tuple(range(6, 14)) + tuple(range(6))


class Reduce:
    def __init__(self, s, spot):
        self.s = s
        self.z, self.x, self.y, self.c = spot
        self.stage = {}
        self.open = []

    def shape(self, t):
        return SCATTER_ROWS[t], SCATTER_EDGE[t]

    def part(self, t):
        rows, edge = self.shape(t)
        return pl.ds(pl.multiple_of(self.y * edge, 16), rows - edge)

    def held(self, t):
        s = self.s
        return s.held_big.at[t - 14] if t >= 14 else s.held.at[t if t < 6 else t - 6]

    def pick(self, small, big, t):
        return big.at[t - 14] if t >= 14 else small.at[t]

    def got_y(self, t):
        return self.pick(self.s.got_y, self.s.got_y_big, t)

    def got_x(self, t):
        return self.pick(self.s.got_x, self.s.got_x_big, t)

    def got_z(self, t):
        return self.pick(self.s.got_z, self.s.got_z_big, t)

    def got_f(self, t):
        return self.pick(self.s.got_f, self.s.got_f_big, t)

    def sems(self, stage, t):
        return self.s.scatter_send.at[stage, t], self.s.scatter_recv.at[stage, t]

    def produced(self, t):
        self.stage[t] = -1
        self.ask()

    def ask(self):
        entered = sum(stage > 0 for stage in self.stage.values())
        for t in ORDER[: entered + ASKED]:
            if self.stage.get(t) == -1:
                self.stage[t] = 0
                self.start_y(t)

    def advance(self):
        stages = (self.start_x, self.start_z, self.start_f, self.start_c)
        under_way = [t for t in ORDER if 0 < self.stage.get(t, 4) < 4]
        waiting = [t for t in ORDER if self.stage.get(t) == 0]
        for t in waiting[:1] + under_way[::-1]:
            stages[self.stage[t]](t)
            self.stage[t] += 1
        self.ask()

    def free(self, t):
        while self.stage[t] < 4:
            self.advance()
        if t in self.open:
            self.sent(t)

    def start_y(self, t):
        rows, edge = self.shape(t)
        theirs = pl.ds(pl.multiple_of((1 - self.y) * (rows - edge), 16), edge)
        send(
            self.held(t).at[:, :, theirs, :],
            self.got_y(t).at[:, :, pl.ds(0, edge), :],
            *self.sems(0, t),
            device(self.z, self.x, 1 - self.y, self.c),
        )

    def start_x(self, t):
        rows, edge = self.shape(t)
        held, got = self.held(t), self.got_y(t)
        drain(got.at[:, :, pl.ds(0, edge), :], self.s.scatter_recv.at[0, t])
        mine = pl.ds(pl.multiple_of(self.y * (rows - edge), 16), edge)

        @pl.loop(0, 4)
        def _(k):
            for x in range(2):
                total = held[k, x, mine, :].astype(F32) + got[k, x, pl.ds(0, edge), :].astype(F32)
                held[k, x, mine, :] = total.astype(BF16)

        send(
            held.at[:, 1 - self.x, self.part(t), :],
            self.got_x(t).at[:, pl.ds(0, rows - edge), :],
            *self.sems(1, t),
            device(self.z, 1 - self.x, self.y, self.c),
        )

    def start_z(self, t):
        rows, edge = self.shape(t)
        held, got = self.held(t), self.got_x(t)
        keep = rows - edge
        drain(got.at[:, pl.ds(0, keep), :], self.s.scatter_recv.at[1, t])
        part = self.part(t)

        @pl.loop(0, 4)
        def _(k):
            total = held[k, self.x, part, :].astype(F32) + got[k, pl.ds(0, keep), :].astype(F32)
            held[k, self.x, part, :] = total.astype(BF16)

        for step in (1, 3, 2):
            other = (self.z + step) % 4
            send(
                held.at[other, self.x, part, :],
                self.got_z(t).at[step - 1, pl.ds(0, keep), :],
                *self.sems(2, t),
                device(other, self.x, self.y, self.c),
            )

    def start_f(self, t):
        rows, edge = self.shape(t)
        held, got = self.held(t), self.got_z(t)
        keep = rows - edge
        drain(got.at[:, pl.ds(0, keep), :], self.s.scatter_recv.at[2, t])
        part = self.part(t)
        total = held[self.z, self.x, part, :].astype(F32)
        for k in range(3):
            total = total + got[k, pl.ds(0, keep), :].astype(F32)
        held[self.z, self.x, part, :] = total.astype(BF16)
        send(
            held.at[self.z, self.x, part, :],
            self.got_f(t).at[pl.ds(0, keep), :],
            *self.sems(3, t),
            device(self.z, self.x, 1 - self.y, self.c),
        )

    def target(self, t):
        s = self.s
        if t < 6:
            columns = pl.ds(pl.multiple_of(self.c * LANE_HALF + t * WIDTH, 128), WIDTH)
            return s.g_packed.at[:, columns]
        if t < 14:
            columns = pl.ds(pl.multiple_of(self.c * FF_HALF + (t - 6) // 2 * WIDTH, 128), WIDTH)
            return (s.g_gate, s.g_up)[(t - 6) % 2].at[:, columns]
        rows = pl.ds(pl.multiple_of(self.c * 192, 16), 192)
        return s.g_down.at[rows, pl.ds((t - 14) * WIDTH, WIDTH)]

    def start_c(self, t):
        rows, edge = self.shape(t)
        held, got = self.held(t), self.got_f(t)
        y, keep, both = self.y, rows - edge, rows - 2 * edge
        drain(got.at[pl.ds(0, keep), :], self.s.scatter_recv.at[3, t])
        drain(self.got_y(t).at[:, :, pl.ds(0, edge), :], self.s.scatter_send.at[0, t])
        drain(self.got_x(t).at[:, pl.ds(0, keep), :], self.s.scatter_send.at[1, t])
        mid, fin = held.at[self.z, self.x], held.at[self.z, 1 - self.x]

        def at(offset, count):
            return pl.ds(pl.multiple_of(offset, 16), count)

        own, other = at(y * keep, edge), at((1 - y) * keep, edge)
        fin[own, :] = mid[own, :]
        fin[other, :] = got[at((1 - y) * both, edge), :]
        total = mid[pl.ds(edge, both), :].astype(F32) + got[at(y * edge, both), :].astype(F32)
        fin[pl.ds(edge, both), :] = total.astype(BF16)
        target = self.target(t)
        send(fin, target, *self.sems(4, t), device(self.z, self.x, y, 1 - self.c))
        pltpu.make_async_copy(fin, target, self.s.store_sems.at[t]).start()
        self.open.append(t)

    def sent(self, t):
        self.open.remove(t)
        rows, edge = self.shape(t)
        sems = self.s.scatter_send
        drain(self.got_z(t).at[:, pl.ds(0, rows - edge), :], sems.at[2, t])
        drain(self.got_f(t).at[pl.ds(0, rows - edge), :], sems.at[3, t])
        drain(self.target(t), sems.at[4, t])
        drain(self.target(t), self.s.store_sems.at[t])

    def finish(self):
        for t in ORDER:
            self.free(t)
        for t in range(N_PIECES):
            drain(self.target(t), self.s.scatter_recv.at[4, t])


class Backward:
    def __init__(self, s, spot, reduce):
        self.s, self.reduce = s, reduce
        self.z, self.x, self.y, self.c = spot
        self.pending = {}
        self.remote = {}
        self.copies = 0

    def load(self, key, source, target):
        if key not in self.pending:
            copy = pltpu.make_async_copy(source, target, self.s.load_sems.at[self.copies])
            self.copies += 1
            copy.start()
            self.pending[key] = copy

    def wait(self, *keys):
        for key in keys:
            self.pending.pop(key).wait()

    def to_sibling(self, key, source, target):
        k = len(self.remote)
        copy = pltpu.make_async_remote_copy(
            src_ref=source,
            dst_ref=target,
            send_sem=self.s.pair_send.at[k],
            recv_sem=self.s.pair_recv.at[k],
            device_id=device(self.z, self.x, self.y, 1 - self.c),
            device_id_type=MESH,
        )
        copy.start()
        self.remote[key] = copy


    def grad_down(self, hidden, branch):
        s, reduce = self.s, self.reduce

        @pl.loop(0, 4)
        def _(k):
            left = hidden[pl.ds(2 * k, 2)].reshape(384, 2 * TOK)
            total = mm(left, branch[...]).astype(BF16)
            for j in range(3):
                block = total[:, j * WIDTH : (j + 1) * WIDTH]
                s.held_big[j, k] = block.reshape(2, 192, WIDTH)

        for t in (14, 15, 16):
            reduce.produced(t)

    def column(self, w):
        half = (1 - self.c) if w % 2 == 0 else self.c
        return half * 4 + w // 2

    def load_ff(self, f, w):
        s = self.s
        window = self.column(w)
        columns = pl.ds(pl.multiple_of(window * WIDTH, 128), WIDTH)
        slot = w % 2
        self.load((1, w), s.down_all.at[window // 2, window % 2], f.w_down.at[slot])
        self.load((2, w), s.gate_all.at[:, :, :, columns], s.w.at[slot, :, :, :, pl.ds(0, WIDTH)])
        self.load((3, w), s.up_all.at[:, :, :, columns], s.w.at[slot, :, :, :, pl.ds(WIDTH, WIDTH)])
        self.load((4, w), s.o_active.at[window], f.active.at[slot])

    def ff(self, f, w):
        s = self.s
        slot = w % 2
        self.load_ff(f, w)
        self.wait((1, w), (2, w), (3, w), (4, w))
        if w < 7:
            self.load_ff(f, w + 1)
        s.d_residual[:, 0:WIDTH] = mm_nt(f.branch[pl.ds(0, TOK), :], f.w_down[slot])
        if w >= 2:
            if slot == 0:
                self.remote[5, w - 2].wait_send()
            else:
                self.wait((5, w - 2))
        steep = f.steep.at[slot]

        @pl.loop(0, TOK // TILE)
        def _(i):
            rows = rows_of(i, TILE)
            back = s.d_residual[rows, 0:WIDTH]
            steep[rows, 0:WIDTH] = (back * f.active[slot, 1, rows, :].astype(F32)).astype(BF16)
            steep[rows, WIDTH : 2 * WIDTH] = (
                back * f.active[slot, 0, rows, :].astype(F32)
            ).astype(BF16)

        j = w // 2
        if slot == 0:
            self.to_sibling((5, w), steep, s.r_ff.at[j, pl.ds(TOK, TOK)])
        else:
            self.load((5, w), steep, s.r_ff.at[j, pl.ds(0, TOK)])
        product = mm_nt(steep[...], flat(s.w[slot]))
        if w == 0:
            s.acc[...] = product
        else:
            s.acc[...] += product

    def load_grad_ff(self, j):
        s = self.s
        self.remote[5, 2 * j].wait_recv()
        if (5, 2 * j + 1) in self.pending:
            self.wait((5, 2 * j + 1))
        self.load((6, j), s.r_ff.at[j], s.right.at[j % 2])

    def grad_ff(self, j):
        s = self.s
        self.wait((6, j))
        right = s.right.at[j % 2]

        @pl.loop(0, 2)
        def _(k):
            left = s.left[pl.ds(pl.multiple_of(k * 576, 64), 576), :]
            total = mm(left, right[...]).astype(BF16)
            for half in range(2):
                block = total[:, half * WIDTH : (half + 1) * WIDTH]
                s.held[2 * j + half, pl.ds(2 * k, 2)] = block.reshape(2, 2, 144, WIDTH)

        self.reduce.produced(6 + 2 * j)
        self.reduce.produced(7 + 2 * j)

    def feed_forward(self, f):
        s, reduce = self.s, self.reduce
        self.wait(11, 12)
        self.load((7, 0), s.o_lhs.at[2], s.left)
        self.grad_down(f.hidden, f.branch)
        for w in range(8):
            self.ff(f, w)
            if w == 0:
                self.wait((7, 0))
            if w % 2 == 1:
                reduce.advance()
                if w >= 3:
                    self.load_grad_ff(w // 2 - 1)
            elif w >= 4:
                self.grad_ff(w // 2 - 2)
        self.load_grad_ff(3)
        self.grad_ff(2)
        self.grad_ff(3)
        self.remote[5, 6].wait_send()


    def middle(self, f):
        s = self.s
        self.load(21, s.cot, f.cot)
        self.load(22, s.o_residual, s.d_residual)
        self.load(23, s.o_attended, f.attended)
        self.wait(21, 22, 23)
        s.d_mod[...] = jnp.zeros_like(s.d_mod)

        @pl.loop(0, TOK // TILE)
        def _(i):
            rows = rows_of(i, TILE)
            image = i // (SEQ // TILE)
            mod, d_mod = s.mod, s.d_mod
            normed, inverse = norm_rows(s.d_residual[rows, :])
            d_entry = s.acc[rows, :]
            d_mod[image, 3:4, :] += jnp.sum(d_entry, axis=0, keepdims=True)
            d_mod[image, 4:5, :] += jnp.sum(d_entry * normed, axis=0, keepdims=True)
            back = norm_back(normed, inverse, d_entry * (1.0 + mod[image, 4:5, :]))
            d_residual = f.cot[rows, :].astype(F32) + back
            s.d_residual[rows, :] = d_residual
            attended = f.attended[rows, :].astype(F32)
            d_mod[image, 2:3, :] += jnp.sum(d_residual * attended, axis=0, keepdims=True)
            s.joined[rows, 3 * D : 4 * D] = (mod[image, 2:3, :] * d_residual).astype(BF16)


    def load_soft(self, f, k):
        heads = H // ATTN_STEPS
        self.load((31, k), self.s.o_soft.at[pl.ds(k * heads, heads)], f.soft)

    def attend(self, f, k):
        s = self.s
        heads = H // ATTN_STEPS
        self.wait((31, k))
        factor = 1.0 / math.sqrt(HD)
        for i in range(heads):
            base, mask = head_window(k * heads + i)
            window = pl.ds(base, 256)
            for image in range(2):
                rows = pl.ds(image * SEQ, SEQ)
                back = jnp.where(mask, f.back[rows, window].astype(F32), 0.0).astype(BF16)
                soft = f.soft[i, image]
                d_soft = mm_nt(back, f.qkv[2, rows, window])
                wide = soft.astype(F32)
                d_scores = (
                    wide * (d_soft - jnp.sum(wide * d_soft, axis=1, keepdims=True))
                ).astype(BF16)
                results = (
                    mm(d_scores, f.qkv[1, rows, window]) * factor,
                    mm_tn(d_scores, f.qkv[0, rows, window]) * factor,
                    mm_tn(soft, back),
                )
                for part, result in enumerate(results):
                    place_at = pl.ds(part * D + base, 256)
                    old = s.joined[rows, place_at].astype(F32)
                    s.joined[rows, place_at] = jnp.where(mask, result, old).astype(BF16)
        if k + 1 < ATTN_STEPS:
            self.load_soft(f, k + 1)

    def head_back(self, f, which):
        s = self.s

        @pl.loop(0, TOK // HEAD_TILE)
        def _(i):
            rows = rows_of(i, HEAD_TILE)
            spots = rows_of(i % (SEQ // HEAD_TILE), HEAD_TILE)
            columns = pl.ds(which * D, D)
            grad = s.joined[rows, columns].astype(F32)
            grad = grad * f.cos[spots, :] - partner(grad, first_lanes(HEAD_TILE)) * f.sin[spots, :]
            normed = f.normed[which, rows, :].astype(F32)
            mean = mm_split(grad * normed, s.spread[...]) * (1.0 / HD)
            scale = mm_split(s.acc[rows, which * 128 : which * 128 + 128], s.widen[...])
            result = scale * (grad - normed * mm(mean.astype(BF16), s.widen[...]))
            s.joined[rows, columns] = result.astype(BF16)

    def attention(self, f):
        s, reduce = self.s, self.reduce
        self.load(24, s.packed_all.at[:, :, :, pl.ds(3 * D, 768)], s.w.at[0])
        self.load(25, s.packed_all.at[:, :, :, pl.ds(3 * D + 768, WIDTH)], s.w.at[1, :, :, :, pl.ds(0, WIDTH)])
        for k in range(3):
            self.load((41, k), s.o_qkv.at[k], f.qkv.at[k])
        self.load_soft(f, 0)
        self.load(42, s.o_normed, f.normed)
        self.load(44, s.cos, f.cos)
        self.load(45, s.sin, f.sin)
        self.wait(24, 25)
        joined = s.joined
        s.acc[...] = mm_nt(joined[:, 3 * D : 3 * D + 768], flat(s.w[0]))
        s.acc[...] += mm_nt(joined[:, 3 * D + 768 :], flat(s.w[1, :, :, :, 0:WIDTH]))
        f.back[...] = s.acc[...].astype(BF16)
        for k in range(2):
            self.load((43, k), s.o_scale.at[k], s.acc.at[:, pl.ds(128 * k, 128)])
        reduce.advance()
        self.wait((41, 0), (41, 1), (41, 2))
        for k in range(ATTN_STEPS):
            self.attend(f, k)
            if k % 2 == 1:
                reduce.advance()
        self.wait(42, (43, 0), (43, 1), 44, 45)
        self.head_back(f, 0)
        self.trade(0)
        reduce.advance()
        self.head_back(f, 1)
        self.trade(1)

    def trade(self, k):
        s = self.s
        columns = pl.ds(k * D, D)
        theirs = pl.ds(pl.multiple_of((1 - self.c) * LANE_HALF + k * D, 128), D)
        mine = pl.ds(pl.multiple_of(self.c * LANE_HALF + k * D, 128), D)
        send(
            s.joined.at[:, theirs],
            s.r_packed.at[pl.ds(TOK, TOK), columns],
            s.pair_send.at[6 + k],
            s.pair_recv.at[6 + k],
            device(self.z, self.x, self.y, 1 - self.c),
        )
        own = s.r_packed.at[pl.ds(0, TOK), columns]
        pltpu.make_async_copy(s.joined.at[:, mine], own, s.trade_sems.at[k]).start()

    def traded(self, k):
        block = self.s.r_packed.at[pl.ds(0, TOK), pl.ds(k * D, D)]
        drain(block, self.s.pair_recv.at[6 + k])
        drain(block, self.s.trade_sems.at[k])


    def load_entry(self, k):
        s = self.s
        width = 768 if k < 4 else WIDTH
        self.load(
            (51, k),
            s.packed_all.at[:, :, :, pl.ds(k * 768, width)],
            s.w.at[k % 2, :, :, :, pl.ds(0, width)],
        )

    def entry(self, k):
        s = self.s
        width = 768 if k < 4 else WIDTH
        self.load_entry(k)
        self.wait((51, k))
        if k < 4:
            self.load_entry(k + 1)
        product = mm_nt(s.joined[:, k * 768 : k * 768 + width], flat(s.w[k % 2, :, :, :, 0:width]))
        if k == 0:
            s.acc[...] = product
        else:
            s.acc[...] += product

    def grad_packed(self, f, jj):
        s = self.s
        self.wait((61, jj))
        right = s.right.at[jj % 2]

        @pl.loop(0, 2)
        def _(k):
            rows = pl.ds(pl.multiple_of(k * 576, 64), 576)
            for half in range(2):
                j = 2 * jj + half
                left = s.left if j < 3 else f.left
                total = mm(left[rows, :], right[:, half * WIDTH : (half + 1) * WIDTH])
                s.held[j, pl.ds(2 * k, 2)] = total.astype(BF16).reshape(2, 2, 144, WIDTH)

        self.reduce.produced(2 * jj)
        self.reduce.produced(2 * jj + 1)

    def load_right(self, jj):
        self.load((61, jj), self.s.r_packed.at[:, pl.ds(768 * jj, 768)], self.s.right.at[jj % 2])

    def last(self, f):
        s, reduce = self.s, self.reduce
        self.traded(0)
        self.load_right(0)
        self.load(72, s.o_lhs.at[0], s.left)
        self.load(73, s.o_lhs.at[self.c], f.left)
        self.load(74, s.tokens, f.tokens)
        self.load(76, s.mod_weight, f.mod_w)
        self.load_entry(0)
        reduce.advance()
        self.wait(72, 73)
        for jj in range(3):
            reduce.free(6 + 2 * jj)
            reduce.free(7 + 2 * jj)
            self.grad_packed(f, jj)
            if jj == 0:
                self.traded(1)
                self.load_right(1)
                self.load_right(2)
            self.entry(jj)
            reduce.advance()
        self.entry(3)
        self.entry(4)
        reduce.advance()
        self.wait(74)

        @pl.loop(0, TOK // TILE)
        def _(i):
            rows = rows_of(i, TILE)
            image = i // (SEQ // TILE)
            mod, d_mod = s.mod, s.d_mod
            normed, inverse = norm_rows(f.tokens[rows, :].astype(F32))
            d_entry = s.acc[rows, :]
            d_mod[image, 0:1, :] += jnp.sum(d_entry, axis=0, keepdims=True)
            d_mod[image, 1:2, :] += jnp.sum(d_entry * normed, axis=0, keepdims=True)
            back = norm_back(normed, inverse, d_entry * (1.0 + mod[image, 1:2, :]))
            s.d_residual[rows, :] += back

        self.load(75, s.d_residual, s.g_tokens)
        self.modulation(f)
        reduce.finish()
        self.wait(75)
        for k in range(2):
            drain(s.r_packed.at[pl.ds(0, TOK), pl.ds(k * D, D)], s.pair_send.at[6 + k])

    def modulation(self, f):
        s, reduce = self.s, self.reduce
        z, x, y, c = spot = (self.z, self.x, self.y, self.c)
        s.back_flat[...] = jnp.zeros_like(s.back_flat)
        for image in range(2):
            for k in range(6):
                row = s.gate_b[image, 0:1, :] if k == 5 else s.d_mod[image, k : k + 1, :]
                rounded = row.astype(BF16).astype(F32)
                s.back_flat[image : image + 1, k * D : (k + 1) * D] = rounded
        for m in range(4):
            s.back_parts[m] = s.back_flat[:, m * MOD_PART : (m + 1) * MOD_PART]
        group = Group(
            spot, s.back_parts, s.back_got_c, s.back_got_y, s.back_blocks, s.back_send, s.back_recv
        )
        group.start()
        reduce.advance()
        group.across_y()
        reduce.advance()
        group.finish()
        for m in range(4):
            s.back[2 * m : 2 * m + 2, :] = s.back_blocks[m, 0:2, :]
        x_peer = device(z, 1 - x, y, c)
        send(s.back, s.back_got_x, s.wide_send.at[0], s.wide_recv.at[0], x_peer)
        self.wait(76)
        partial = mm(s.back[...].astype(BF16), f.mod_w[...])
        s.cond_parts[...] = jnp.zeros_like(s.cond_parts)
        for m in range(4):
            s.cond_parts[m, 0:2, :] = partial[2 * m : 2 * m + 2, :]
        cond = Group(
            spot, s.cond_parts, s.cond_got_c, s.cond_got_y, s.cond_blocks, s.cond_send, s.cond_recv
        )
        cond.start()
        drain(s.back, s.wide_recv.at[0])
        own, other = s.back[...], s.back_got_x[...]
        low = jnp.where(x == 0, own, other)
        high = jnp.where(x == 0, other, own)
        s.back_all[z] = jnp.concatenate([low, high], axis=0).astype(BF16)
        block = s.back_all.at[z]
        for step in (1, 3, 2):
            peer = device((z + step) % 4, x, y, c)
            send(block, block, s.wide_send.at[1], s.wide_recv.at[1], peer)
        cond.across_y()
        reduce.advance()
        cond.finish()
        total = s.cond_blocks[0] + s.cond_blocks[1] + s.cond_blocks[2] + s.cond_blocks[3]
        s.o_cond[...] = total
        reduce.advance()
        drain(s.back_all.at[pl.ds(0, 3)], s.wide_recv.at[1])
        self.load(77, s.back_all, s.o_back)
        drain(s.back, s.wide_send.at[0])
        drain(s.back_all.at[pl.ds(0, 3)], s.wide_send.at[1])
        self.wait(77)


class BackwardInputs(NamedTuple):
    packed_all: object
    gate_all: object
    up_all: object
    down_all: object
    o_branch: object
    o_lhs: object
    o_hidden: object
    o_qkv: object
    o_normed: object
    o_scale: object
    o_soft: object
    o_attended: object
    o_residual: object
    o_active: object
    tokens: object
    cot: object
    cos: object
    sin: object
    mod: object
    spread: object
    widen: object
    gate_b: object
    mod_weight: object


BACKWARD_OUTPUTS = dict(
    g_packed=((144, 4 * D), BF16),
    g_gate=((144, 8 * WIDTH), BF16),
    g_up=((144, 8 * WIDTH), BF16),
    g_down=((384, D), BF16),
    g_tokens=((TOK, D), F32),
    r_ff=((4, 2 * TOK, 2 * WIDTH), BF16),
    r_packed=((2 * TOK, LANE_HALF), BF16),
    o_back=((4, 16, MOD_PART), BF16),
    o_cond=((8, D), F32),
)


def vmem(*shape, kind=BF16):
    return pltpu.VMEM(shape, kind)


def backward_scratch():
    return dict(
        held=vmem(8, 4, 2, 144, WIDTH),
        held_big=vmem(3, 4, 2, 192, WIDTH),
        got_y=vmem(14, 4, 2, 48, WIDTH),
        got_y_big=vmem(3, 4, 2, 48, WIDTH),
        got_x=vmem(14, 4, 112, WIDTH),
        got_x_big=vmem(3, 4, 144, WIDTH),
        got_z=vmem(14, 3, 112, WIDTH),
        got_z_big=vmem(3, 3, 144, WIDTH),
        got_f=vmem(14, 112, WIDTH),
        got_f_big=vmem(3, 144, WIDTH),
        w=vmem(2, 4, 2, 144, 2 * WIDTH),
        acc=vmem(TOK, D, kind=F32),
        d_residual=vmem(TOK, D, kind=F32),
        joined=vmem(TOK, 4 * D),
        left=vmem(D, 2 * TOK),
        right=vmem(2, 2 * TOK, 2 * WIDTH),
        d_mod=vmem(2, 8, D, kind=F32),
        back_flat=vmem(8, 4 * MOD_PART, kind=F32),
        back_parts=group_scratch(MOD_PART)[0],
        back_got_c=group_scratch(MOD_PART)[1],
        back_got_y=group_scratch(MOD_PART)[2],
        back_blocks=group_scratch(MOD_PART)[3],
        back_send=group_scratch(MOD_PART)[4],
        back_recv=group_scratch(MOD_PART)[5],
        cond_parts=group_scratch(D)[0],
        cond_got_c=group_scratch(D)[1],
        cond_got_y=group_scratch(D)[2],
        cond_blocks=group_scratch(D)[3],
        cond_send=group_scratch(D)[4],
        cond_recv=group_scratch(D)[5],
        back=vmem(8, MOD_PART, kind=F32),
        back_got_x=vmem(8, MOD_PART, kind=F32),
        back_all=vmem(4, 16, MOD_PART),
        wide_send=pltpu.SemaphoreType.DMA((2,)),
        wide_recv=pltpu.SemaphoreType.DMA((2,)),
        scatter_send=pltpu.SemaphoreType.DMA((5, N_PIECES)),
        scatter_recv=pltpu.SemaphoreType.DMA((5, N_PIECES)),
        store_sems=pltpu.SemaphoreType.DMA((N_PIECES,)),
        load_sems=pltpu.SemaphoreType.DMA((112,)),
        trade_sems=pltpu.SemaphoreType.DMA((2,)),
        pair_send=pltpu.SemaphoreType.DMA((8,)),
        pair_recv=pltpu.SemaphoreType.DMA((8,)),
    )


def backward_kernel(*refs):
    names = BackwardInputs._fields + tuple(BACKWARD_OUTPUTS) + tuple(backward_scratch())
    s = SimpleNamespace(**dict(zip(names, refs, strict=True)))
    spot = place()
    greet(neighbours(*spot))
    reduce = Reduce(s, spot)
    work = Backward(s, spot, reduce)

    def scoped(act, before=None, **shapes):
        def run(*held):
            f = SimpleNamespace(**dict(zip(shapes, held, strict=True)))
            if before is not None:
                before(f)
            act(f)

        pl.run_scoped(run, *shapes.values())

    def first_loads(f):
        work.load(11, s.o_hidden, f.hidden)
        work.load(12, s.o_branch, f.branch)
        work.load_ff(f, 0)

    scoped(
        work.feed_forward,
        first_loads,
        hidden=vmem(8, 192, 2 * TOK),
        branch=vmem(2 * TOK, D),
        w_down=vmem(2, 384, D),
        active=vmem(2, 2, TOK, WIDTH),
        steep=vmem(2, TOK, 2 * WIDTH),
    )
    scoped(work.middle, cot=vmem(TOK, D), attended=vmem(TOK, D))
    reduce.advance()
    scoped(
        work.attention,
        qkv=vmem(3, TOK, D),
        normed=vmem(2, TOK, D),
        soft=vmem(H // ATTN_STEPS, 2, SEQ, SEQ),
        back=vmem(TOK, D),
        cos=vmem(SEQ, D, kind=F32),
        sin=vmem(SEQ, D, kind=F32),
    )
    scoped(work.last, left=vmem(D, 2 * TOK), tokens=vmem(TOK, D), mod_w=vmem(MOD_PART, D))


def backward_pass(f, tokens, cotangent, mod_weight, tables):
    hbm = pl.BlockSpec(memory_space=pl.ANY)
    inside = pl.BlockSpec(memory_space=pltpu.VMEM)
    cosine, sine, spread, widen = tables
    given = BackwardInputs(
        f.packed_all,
        f.gate_all,
        f.up_all,
        f.down_all,
        f.o_branch,
        f.o_lhs,
        f.o_hidden,
        f.o_qkv,
        f.o_normed,
        f.o_scale,
        f.o_soft,
        f.o_attended,
        f.o_residual,
        f.o_active,
        tokens,
        cotangent,
        cosine,
        sine,
        f.o_mod,
        spread,
        widen,
        f.o_gate_b,
        mod_weight,
    )
    out = pl.pallas_call(
        backward_kernel,
        out_shape=[jax.ShapeDtypeStruct(*spec) for spec in BACKWARD_OUTPUTS.values()],
        in_specs=[hbm] * 18 + [inside] * 4 + [hbm],
        out_specs=[hbm] * 8 + [inside],
        scratch_shapes=list(backward_scratch().values()),
        name="backward_pass",
        compiler_params=pltpu.CompilerParams(
            collective_id=1, has_side_effects=True, vmem_limit_bytes=121 << 19
        ),
    )(*given)
    return SimpleNamespace(**dict(zip(BACKWARD_OUTPUTS, out)))


class SettleInputs(NamedTuple):
    packed: object
    gate: object
    up: object
    down: object
    acted: object
    back: object
    cond: object
    total: object


SETTLE_OUTPUTS = dict(
    g_qkv=((144, 3 * D), F32),
    g_proj=((144, D), F32),
    g_gate=((144, 8 * WIDTH), F32),
    g_up=((144, 8 * WIDTH), F32),
    g_down=((384, D), F32),
    g_mod=((144, MOD_PART), F32),
    g_bias=((1, MOD_PART), F32),
    g_cond=((2, D), F32),
)


def settle_scratch():
    return dict(
        v_packed=vmem(144, 4 * D),
        v_gate=vmem(144, 8 * WIDTH),
        v_up=vmem(144, 8 * WIDTH),
        v_down=vmem(384, D),
        w_qkv=vmem(144, 3 * D, kind=F32),
        w_proj=vmem(144, D, kind=F32),
        w_gate=vmem(144, 8 * WIDTH, kind=F32),
        w_up=vmem(144, 8 * WIDTH, kind=F32),
        w_down=vmem(384, D, kind=F32),
        w_mod=vmem(144, MOD_PART, kind=F32),
        load_sems=pltpu.SemaphoreType.DMA((4,)),
        store_sems=pltpu.SemaphoreType.DMA((6,)),
    )


def settle_kernel(*refs):
    names = SettleInputs._fields + tuple(SETTLE_OUTPUTS) + tuple(settle_scratch())
    s = SimpleNamespace(**dict(zip(names, refs, strict=True)))
    pairs = ((s.packed, s.v_packed), (s.gate, s.v_gate), (s.up, s.v_up), (s.down, s.v_down))
    loads = [pltpu.make_async_copy(a, b, s.load_sems.at[k]) for k, (a, b) in enumerate(pairs)]
    for load in loads:
        load.start()
    stores = []

    def store(source, target):
        copy = pltpu.make_async_copy(source, target, s.store_sems.at[len(stores)])
        copy.start()
        stores.append(copy)

    def widen(source, target, offset=0):
        count = target.shape[0] // 16

        @pl.loop(0, count)
        def _(i):
            rows = rows_of(i, 16)
            columns = pl.ds(offset, target.shape[1])
            target[rows, :] = source[rows, columns].astype(F32)

    s.w_mod[...] = mm_tn(s.acted[...], s.back[...])
    store(s.w_mod, s.g_mod)
    loads[0].wait()
    widen(s.v_packed, s.w_qkv)
    store(s.w_qkv, s.g_qkv)
    widen(s.v_packed, s.w_proj, 3 * D)
    store(s.w_proj, s.g_proj)
    for k, (source, target, out) in enumerate(
        ((s.v_gate, s.w_gate, s.g_gate), (s.v_up, s.w_up, s.g_up), (s.v_down, s.w_down, s.g_down))
    ):
        loads[k + 1].wait()
        widen(source, target)
        store(target, out)
    s.g_bias[...] = jnp.sum(s.back[...].astype(F32), axis=0, keepdims=True)
    total = s.total[...]
    sigma = 1.0 / (1.0 + jnp.exp(-total))
    s.g_cond[...] = s.cond[0:2, :] * sigma * (1.0 + total * (1.0 - sigma))
    for copy in stores:
        copy.wait()


def settle(*given):
    hbm = pl.BlockSpec(memory_space=pl.ANY)
    inside = pl.BlockSpec(memory_space=pltpu.VMEM)
    out = pl.pallas_call(
        settle_kernel,
        out_shape=[jax.ShapeDtypeStruct(*spec) for spec in SETTLE_OUTPUTS.values()],
        in_specs=[hbm] * 4 + [inside] * 4,
        out_specs=[hbm] * 6 + [inside] * 2,
        scratch_shapes=list(settle_scratch().values()),
        name="settle",
        compiler_params=pltpu.CompilerParams(vmem_limit_bytes=60 << 20),
    )(*SettleInputs(*given))
    return SimpleNamespace(**dict(zip(SETTLE_OUTPUTS, out)))


def body_general(
    tokens,
    condition,
    timestep,
    qkv_weight,
    out_weight,
    gate_weight,
    up_weight,
    down_weight,
    mod_weight,
    mod_bias,
    cotangent,
):
    gathered = (
        lax.all_gather(qkv_weight, "dp", axis=0, tiled=True),
        lax.all_gather(out_weight, "dp", axis=0, tiled=True),
        lax.all_gather(gate_weight, "dp", axis=0, tiled=True),
        lax.all_gather(up_weight, "dp", axis=0, tiled=True),
        lax.all_gather(down_weight, "dp", axis=0, tiled=True),
    )
    cond_total = condition.astype(jnp.float32) + embed_steps(timestep)
    acted_cond = jax.nn.silu(cond_total).astype(jnp.bfloat16)
    acted_group = lax.all_gather(acted_cond, "mod", axis=0, tiled=True)
    mod_part = (
        jnp.dot(acted_group, mod_weight, preferred_element_type=jnp.float32)
        + mod_bias.astype(jnp.float32)
    ).astype(jnp.bfloat16)
    modulation = lax.all_to_all(mod_part, "mod", split_axis=0, concat_axis=1, tiled=True).astype(
        jnp.float32
    )
    tables = rope_tables()
    per_micro = tokens.shape[0] // MICRO
    outputs = []
    token_grads = []
    mod_grads = []
    kept = []
    for micro_step in range(MICRO):
        start_row = micro_step * per_micro
        output, d_tokens, d_modulation, factors = layer_pass(
            tokens[start_row : start_row + per_micro],
            modulation[start_row : start_row + per_micro],
            cotangent[start_row : start_row + per_micro],
            gathered,
            tables,
        )
        outputs.append(output)
        token_grads.append(d_tokens)
        mod_grads.append(d_modulation)
        kept.append(factors)
    joined = [jnp.concatenate([factors[number] for factors in kept], axis=0) for number in range(9)]
    (
        entry_first,
        d_projected,
        combined,
        d_attended,
        entry_second,
        d_gate_proj,
        d_up_proj,
        hidden,
        d_branch,
    ) = joined
    grad_qkv = jnp.einsum(
        "bsd,bse->de", entry_first, d_projected, preferred_element_type=jnp.float32
    )
    grad_proj = jnp.einsum("bsd,bse->de", combined, d_attended, preferred_element_type=jnp.float32)
    grad_gate = jnp.einsum(
        "bsd,bsf->df", entry_second, d_gate_proj, preferred_element_type=jnp.float32
    )
    grad_up = jnp.einsum("bsd,bsf->df", entry_second, d_up_proj, preferred_element_type=jnp.float32)
    grad_down = jnp.einsum("bsf,bsd->fd", hidden, d_branch, preferred_element_type=jnp.float32)
    totals = (grad_qkv, grad_proj, grad_gate, grad_up, grad_down)
    output_tokens = jnp.concatenate(outputs, axis=0)
    grad_tokens = jnp.concatenate(token_grads, axis=0)
    mod_grad = jnp.concatenate(mod_grads, axis=0)
    mod_back = lax.all_to_all(mod_grad, "mod", split_axis=1, concat_axis=0, tiled=True)
    grad_mod_part = jnp.einsum(
        "id,ic->dc", acted_group, mod_back, preferred_element_type=jnp.float32
    )
    bias_part = jnp.sum(mod_back.astype(jnp.float32), axis=0)
    acted_grad_part = jnp.einsum(
        "ic,dc->id", mod_back, mod_weight, preferred_element_type=jnp.float32
    )
    acted_grad = lax.psum_scatter(
        acted_grad_part.astype(jnp.bfloat16), "mod", scatter_dimension=0, tiled=True
    ).astype(jnp.float32)
    sigma_cond = jax.nn.sigmoid(cond_total)
    grad_condition = acted_grad * sigma_cond * (1.0 + cond_total * (1.0 - sigma_cond))
    grad_bias = lax.psum(bias_part, "dp")
    count = lax.axis_size("dp")
    arrays = totals + (grad_mod_part,)
    shapes = [array.shape for array in arrays]
    flat = lax.psum_scatter(pack_rows(arrays, count), "dp", scatter_dimension=0, tiled=True)
    summed = unpack_rows(flat, shapes, count)
    finished = (
        lax.psum(summed[0].astype(jnp.bfloat16), "mod").astype(jnp.float32),
        lax.psum(summed[1].astype(jnp.bfloat16), "mod").astype(jnp.float32),
        lax.psum(summed[2].astype(jnp.bfloat16), "mod").astype(jnp.float32),
        lax.psum(summed[3].astype(jnp.bfloat16), "mod").astype(jnp.float32),
        lax.psum(summed[4].astype(jnp.bfloat16), "mod").astype(jnp.float32),
    )
    grad_mod = summed[5]
    return (
        output_tokens,
        grad_tokens,
        grad_condition,
        finished[0],
        finished[1],
        finished[2],
        finished[3],
        finished[4],
        grad_mod,
        grad_bias,
    )


def body_fast(
    tokens,
    condition,
    timestep,
    qkv_weight,
    out_weight,
    gate_weight,
    up_weight,
    down_weight,
    mod_weight,
    mod_bias,
    cotangent,
):
    packed = jnp.concatenate([qkv_weight, out_weight], axis=1)
    cond_total = condition.astype(jnp.float32) + embed_steps(timestep)
    acted_cond = jax.nn.silu(cond_total).astype(jnp.bfloat16)
    acted_rows = acted_cond.astype(F32)
    acted_slim = jnp.pad(acted_rows.reshape(-1, 128), ((0, 6), (0, 0)))
    flat_tokens, flat_cotangent = tokens.reshape(TOK, D), cotangent.reshape(TOK, D)
    tables = head_tables()
    f = forward_pass(
        packed,
        gate_weight,
        up_weight,
        down_weight,
        flat_tokens,
        flat_cotangent,
        jnp.pad(acted_rows, ((0, 6), (0, 0))),
        mod_bias.astype(F32).reshape(1, -1),
        mod_weight.T,
        acted_slim,
        *tables,
    )
    b = backward_pass(f, flat_tokens, flat_cotangent, mod_weight.T, tables)
    acted_all = f.acted_all.reshape(32, -1)[:, : 2 * D].reshape(64, D).astype(BF16)
    back_all = b.o_back.reshape(64, -1)
    rows = D // 8
    acted_part = lax.dynamic_slice_in_dim(acted_all, lax.axis_index("dp") * rows, rows, 1)
    g = settle(b.g_packed, b.g_gate, b.g_up, b.g_down, acted_part, back_all, b.o_cond, cond_total)
    return (
        f.o_result.reshape(tokens.shape),
        b.g_tokens.reshape(tokens.shape),
        g.g_cond,
        g.g_qkv,
        g.g_proj,
        g.g_gate,
        g.g_up,
        g.g_down,
        g.g_mod,
        g.g_bias.reshape(-1),
    )


def pick_body(mesh):
    if dict(mesh.shape) == {"dp": 8, "mod": 4}:
        return body_fast
    return body_general


def solution(mesh):
    in_specs = (
        P(("dp", "mod"), None, None),
        P(("dp", "mod"), None),
        P(("dp", "mod")),
        P("dp", None),
        P("dp", None),
        P("dp", None),
        P("dp", None),
        P("dp", None),
        P(None, "mod"),
        P("mod"),
        P(("dp", "mod"), None, None),
    )
    out_specs = (
        P(("dp", "mod"), None, None),
        P(("dp", "mod"), None, None),
        P(("dp", "mod"), None),
        P("dp", None),
        P("dp", None),
        P("dp", None),
        P("dp", None),
        P("dp", None),
        P("dp", "mod"),
        P("mod"),
    )
    return jax.shard_map(pick_body(mesh), mesh=mesh, in_specs=in_specs, out_specs=out_specs, check_vma=False)
```

```python
import math
from types import SimpleNamespace
from typing import NamedTuple

import jax
import jax.numpy as jnp
from jax import lax
import numpy as np
from jax.experimental import pallas as pl
from jax.experimental.pallas import tpu as pltpu
from jax.sharding import PartitionSpec as P

D = 1152
H = 16
HD = 72
GRID = 16
SEQ = 256
MICRO = 2


EPSILON = 1e-06


def norm_rows(field):
    scale_inv = lax.rsqrt(jnp.mean(field * field, axis=-1, keepdims=True) + EPSILON)
    return (field * scale_inv, scale_inv)


def norm_back(normed, scale_inv, gradient):
    return scale_inv * (gradient - normed * jnp.mean(gradient * normed, axis=-1, keepdims=True))


def embed_steps(timestep):
    half_width = D // 2
    frequency = jnp.exp(-math.log(10000.0) * jnp.arange(half_width, dtype=jnp.float32) / half_width)
    angles = timestep.astype(jnp.float32)[:, None] * frequency[None, :]
    return jnp.concatenate([jnp.cos(angles), jnp.sin(angles)], axis=1)


def rope_tables():
    quarter = HD // 4
    frequency = jnp.exp(-math.log(10000.0) * jnp.arange(quarter, dtype=jnp.float32) / quarter)
    position = jnp.arange(SEQ)
    row_index = (position // GRID).astype(jnp.float32)
    col_index = (position % GRID).astype(jnp.float32)
    angles = jnp.stack(
        [row_index[:, None] * frequency[None, :], col_index[:, None] * frequency[None, :]], axis=1
    )
    return (jnp.cos(angles), jnp.sin(angles))


def rotate(field, cosine_table, sine_table):
    leading = field.shape[:-1]
    quarters = field.reshape(leading + (2, 2, HD // 4))
    first_half = quarters[..., 0, :]
    second_half = quarters[..., 1, :]
    cosine_rows = cosine_table[:, None]
    sine_rows = sine_table[:, None]
    turned_first = first_half * cosine_rows - second_half * sine_rows
    turned_second = first_half * sine_rows + second_half * cosine_rows
    return jnp.stack([turned_first, turned_second], axis=-2).reshape(field.shape)


def pack_rows(arrays, count):
    return jnp.concatenate([array.reshape(count, -1) for array in arrays], axis=1).reshape(-1)


def unpack_rows(flat, shapes, count):
    pieces = []
    offset = 0
    for rows_all, columns in shapes:
        rows = rows_all // count
        pieces.append(flat[offset : offset + rows * columns].reshape(rows, columns))
        offset = offset + rows * columns
    return pieces


def layer_pass(block_in, mod_rows, cotangent, weights, tables):
    qkv_full, proj_full, gate_full, up_full, down_full = weights
    cosine_table, sine_table = tables
    images = block_in.shape[0]
    shift_first, scale_first, gate_first, shift_second, scale_second, gate_second = [
        mod_rows[:, None, number * D : (number + 1) * D] for number in range(6)
    ]
    heads_shape = (images, SEQ, H, HD)
    factor = 1.0 / math.sqrt(HD)
    inputs = block_in.astype(jnp.float32)
    normed_first, inv_first = norm_rows(inputs)
    entry_first = (normed_first * (1.0 + scale_first) + shift_first).astype(jnp.bfloat16)
    projected = jnp.einsum("bsd,de->bse", entry_first, qkv_full, preferred_element_type=jnp.float32)
    q_normed, q_inv = norm_rows(projected[..., :D].reshape(heads_shape))
    k_normed, k_inv = norm_rows(projected[..., D : 2 * D].reshape(heads_shape))
    queries = rotate(q_normed, cosine_table, sine_table).astype(jnp.bfloat16)
    keys_rot = rotate(k_normed, cosine_table, sine_table).astype(jnp.bfloat16)
    values = projected[..., 2 * D :].reshape(heads_shape).astype(jnp.bfloat16)
    scores = (
        jnp.einsum("bqhd,bkhd->bhqk", queries, keys_rot, preferred_element_type=jnp.float32)
        * factor
    )
    highest = jnp.max(scores, axis=-1, keepdims=True)
    log_total = highest + jnp.log(jnp.sum(jnp.exp(scores - highest), axis=-1, keepdims=True))
    weights_soft = jnp.exp(scores - log_total).astype(jnp.bfloat16)
    combined = (
        jnp.einsum("bhqk,bkhd->bqhd", weights_soft, values, preferred_element_type=jnp.float32)
        .reshape(images, SEQ, D)
        .astype(jnp.bfloat16)
    )
    attended = jnp.einsum("bsd,de->bse", combined, proj_full, preferred_element_type=jnp.float32)
    residual = inputs + gate_first * attended
    normed_second, inv_second = norm_rows(residual)
    entry_second = (normed_second * (1.0 + scale_second) + shift_second).astype(jnp.bfloat16)
    gate_proj = jnp.einsum(
        "bsd,df->bsf", entry_second, gate_full, preferred_element_type=jnp.float32
    )
    up_proj = jnp.einsum("bsd,df->bsf", entry_second, up_full, preferred_element_type=jnp.float32)
    sigma_gate = jax.nn.sigmoid(gate_proj)
    activated = gate_proj * sigma_gate
    hidden = (activated * up_proj).astype(jnp.bfloat16)
    branch = jnp.einsum("bsf,fd->bsd", hidden, down_full, preferred_element_type=jnp.float32)
    output = (residual + gate_second * branch).astype(jnp.bfloat16)
    grad_out = cotangent.astype(jnp.float32)
    d_gate_second = jnp.sum(grad_out * branch, axis=1)
    d_branch = (gate_second * grad_out).astype(jnp.bfloat16)
    d_hidden = jnp.einsum("bsd,fd->bsf", d_branch, down_full, preferred_element_type=jnp.float32)
    d_gate_proj = (d_hidden * up_proj * sigma_gate * (1.0 + gate_proj * (1.0 - sigma_gate))).astype(
        jnp.bfloat16
    )
    d_up_proj = (d_hidden * activated).astype(jnp.bfloat16)
    d_entry_second = jnp.einsum(
        "bsf,df->bsd", d_gate_proj, gate_full, preferred_element_type=jnp.float32
    )
    d_entry_second = d_entry_second + jnp.einsum(
        "bsf,df->bsd", d_up_proj, up_full, preferred_element_type=jnp.float32
    )
    d_shift_second = jnp.sum(d_entry_second, axis=1)
    d_scale_second = jnp.sum(d_entry_second * normed_second, axis=1)
    d_residual = grad_out + norm_back(
        normed_second, inv_second, d_entry_second * (1.0 + scale_second)
    )
    d_gate_first = jnp.sum(d_residual * attended, axis=1)
    d_attended = (gate_first * d_residual).astype(jnp.bfloat16)
    d_combined = (
        jnp.einsum("bse,de->bsd", d_attended, proj_full, preferred_element_type=jnp.float32)
        .astype(jnp.bfloat16)
        .reshape(heads_shape)
    )
    scores_again = (
        jnp.einsum("bqhd,bkhd->bhqk", queries, keys_rot, preferred_element_type=jnp.float32)
        * factor
    )
    recomputed = jnp.exp(scores_again - log_total)
    d_weights = jnp.einsum(
        "bqhd,bkhd->bhqk", d_combined, values, preferred_element_type=jnp.float32
    )
    d_scores = (
        recomputed * (d_weights - jnp.sum(recomputed * d_weights, axis=-1, keepdims=True))
    ).astype(jnp.bfloat16)
    d_values = jnp.einsum(
        "bhqk,bqhd->bkhd", weights_soft, d_combined, preferred_element_type=jnp.float32
    ).astype(jnp.bfloat16)
    d_queries = (
        (
            jnp.einsum("bhqk,bkhd->bqhd", d_scores, keys_rot, preferred_element_type=jnp.float32)
            * factor
        )
        .astype(jnp.bfloat16)
        .astype(jnp.float32)
    )
    d_keys = (
        (
            jnp.einsum("bhqk,bqhd->bkhd", d_scores, queries, preferred_element_type=jnp.float32)
            * factor
        )
        .astype(jnp.bfloat16)
        .astype(jnp.float32)
    )
    d_q_raw = norm_back(q_normed, q_inv, rotate(d_queries, cosine_table, -sine_table))
    d_k_raw = norm_back(k_normed, k_inv, rotate(d_keys, cosine_table, -sine_table))
    flat_shape = (images, SEQ, D)
    d_projected = jnp.concatenate(
        [
            d_q_raw.reshape(flat_shape),
            d_k_raw.reshape(flat_shape),
            d_values.astype(jnp.float32).reshape(flat_shape),
        ],
        axis=-1,
    ).astype(jnp.bfloat16)
    d_entry_first = jnp.einsum(
        "bse,de->bsd", d_projected, qkv_full, preferred_element_type=jnp.float32
    )
    d_shift_first = jnp.sum(d_entry_first, axis=1)
    d_scale_first = jnp.sum(d_entry_first * normed_first, axis=1)
    d_tokens = d_residual + norm_back(normed_first, inv_first, d_entry_first * (1.0 + scale_first))
    d_modulation = jnp.concatenate(
        [d_shift_first, d_scale_first, d_gate_first, d_shift_second, d_scale_second, d_gate_second],
        axis=1,
    ).astype(jnp.bfloat16)
    factors = (
        entry_first,
        d_projected,
        combined,
        d_attended,
        entry_second,
        d_gate_proj,
        d_up_proj,
        hidden,
        d_branch,
    )
    return (output, d_tokens, d_modulation, factors)


MESH = pl.DeviceIdType.MESH
WIDTH = 384
LANE_HALF = 2304
FF_HALF = 1536
BF16 = jnp.bfloat16
F32 = jnp.float32


def place():
    dp = lax.axis_index("dp")
    mod = lax.axis_index("mod")
    return dp // 2, dp % 2, mod // 2, mod % 2


def device(z, x, y, c):
    return (z * 2 + x, y * 2 + c)


def greet(peers):
    barrier = pltpu.get_barrier_semaphore()
    for peer in peers:
        pl.semaphore_signal(barrier, inc=1, device_id=peer, device_id_type=MESH)
    pl.semaphore_wait(barrier, len(peers))


def neighbours(z, x, y, c):
    around = [device((z + step) % 4, x, y, c) for step in (1, 2, 3)]
    return around + [device(z, 1 - x, y, c), device(z, x, 1 - y, c), device(z, x, y, 1 - c)]


def send(source, target, send_sem, recv_sem, peer):
    pltpu.make_async_remote_copy(
        src_ref=source,
        dst_ref=target,
        send_sem=send_sem,
        recv_sem=recv_sem,
        device_id=peer,
        device_id_type=MESH,
    ).start()


def drain(window, sem):
    pltpu.make_async_copy(window, window, sem).wait()


class Piece:
    def __init__(self, source, target, row, rows, column, edge):
        self.source, self.target = source, target
        self.row, self.rows, self.column, self.edge = row, rows, column, edge


def gather_pieces(refs, c, edge_of):
    packed, gate, up, down, packed_all, gate_all, up_all, down_all = refs
    pieces = []
    for j in range(6):
        pieces.append(Piece(packed, packed_all, 0, 144, c * LANE_HALF + j * WIDTH, edge_of(144, j)))
    for j in range(4):
        pieces.append(Piece(gate, gate_all, 0, 144, c * FF_HALF + j * WIDTH, edge_of(144, j)))
        pieces.append(Piece(up, up_all, 0, 144, c * FF_HALF + j * WIDTH, edge_of(144, j)))
    for j in range(3):
        pieces.append(Piece(down, down_all, c * 192, 192, j * WIDTH, edge_of(192, j)))
    return pieces


class Gather:
    def __init__(self, refs, sems, spot, stages):
        self.z, self.x, self.y, self.c = spot
        self.stages = stages
        self.pieces = gather_pieces(refs, self.c, lambda rows, j: 64 if rows == 144 and j % 3 == 2 else rows // 3)
        self.send_sems, self.recv_sems, self.own_sems = sems
        self.refs = refs

    def columns(self, piece):
        return pl.ds(pl.multiple_of(piece.column, 128), WIDTH)

    def part(self, piece):
        keep = piece.rows - piece.edge
        return pl.ds(pl.multiple_of(piece.row + self.y * piece.edge, 16), keep), keep

    def mine(self, piece):
        return pl.ds(pl.multiple_of(piece.row + self.y * (piece.rows - piece.edge), 16), piece.edge)

    def own_copies(self):
        for k in range(4):
            pltpu.make_async_copy(self.refs[k], self.stages[k], self.own_sems.at[k]).start()

    def own_stores(self):
        for k in range(4):
            drain(self.stages[k], self.own_sems.at[k])
            pltpu.make_async_copy(
                self.stages[k], self.refs[4 + k].at[self.z, self.x], self.own_sems.at[k]
            ).start()

    def own_done(self):
        for k in range(4):
            drain(self.stages[k], self.own_sems.at[k])

    def start_z(self, t):
        p = self.pieces[t]
        rows, _ = self.part(p)
        here = p.source.at[rows, self.columns(p)]
        there = p.target.at[self.z, self.x, rows, self.columns(p)]
        for step in (1, 3, 2):
            peer = device((self.z + step) % 4, self.x, self.y, self.c)
            send(here, there, self.send_sems.at[0, t], self.recv_sems.at[0, t], peer)
        peer = device(self.z, 1 - self.x, self.y, self.c)
        send(here, there, self.send_sems.at[1, t], self.recv_sems.at[1, t], peer)

    def start_x(self, t):
        p = self.pieces[t]
        rows, keep = self.part(p)
        columns = self.columns(p)
        drain(p.target.at[pl.ds(0, 3), 0, pl.ds(0, keep), pl.ds(0, WIDTH)], self.recv_sems.at[0, t])
        x_peer = device(self.z, 1 - self.x, self.y, self.c)
        y_peer = device(self.z, self.x, 1 - self.y, self.c)
        for step in (1, 3, 2):
            other = (self.z + step) % 4
            block = p.target.at[other, self.x, rows, columns]
            send(block, block, self.send_sems.at[1, t], self.recv_sems.at[1, t], x_peer)
        for step in (1, 3, 2):
            other = (self.z + step) % 4
            block = p.target.at[other, self.x, self.mine(p), columns]
            send(block, block, self.send_sems.at[2, t], self.recv_sems.at[2, t], y_peer)

    def start_y(self, t):
        p = self.pieces[t]
        _, keep = self.part(p)
        columns = self.columns(p)
        drain(p.target.at[:, 0, pl.ds(0, keep), pl.ds(0, WIDTH)], self.recv_sems.at[1, t])
        y_peer = device(self.z, self.x, 1 - self.y, self.c)
        block = p.target.at[:, 1 - self.x, self.mine(p), columns]
        send(block, block, self.send_sems.at[2, t], self.recv_sems.at[2, t], y_peer)

    def start_c(self, t):
        p = self.pieces[t]
        columns = self.columns(p)
        half = pl.ds(pl.multiple_of(p.row, 16), p.rows)
        self.drain_seven(p.edge, self.recv_sems.at[2, t])
        peer = device(self.z, self.x, self.y, 1 - self.c)
        block = p.target.at[:, 1 - self.x, half, columns]
        send(block, block, self.send_sems.at[3, t], self.recv_sems.at[3, t], peer)
        for step in (1, 2, 3):
            block = p.target.at[(self.z + step) % 4, self.x, half, columns]
            send(block, block, self.send_sems.at[3, t], self.recv_sems.at[3, t], peer)

    def arrived(self, t):
        self.drain_seven(self.pieces[t].rows, self.recv_sems.at[3, t])

    def drain_seven(self, rows, sem):
        high = 96 if rows > 144 else rows
        drain(self.refs[4].at[pl.ds(0, rows // high), 0, pl.ds(0, high), pl.ds(0, 7 * WIDTH)], sem)

    def sent_z(self, t):
        p = self.pieces[t]
        _, keep = self.part(p)
        drain(p.target.at[pl.ds(0, 3), 0, pl.ds(0, keep), pl.ds(0, WIDTH)], self.send_sems.at[0, t])

    def sent_rest(self, t):
        p = self.pieces[t]
        _, keep = self.part(p)
        drain(p.target.at[:, 0, pl.ds(0, keep), pl.ds(0, WIDTH)], self.send_sems.at[1, t])
        for stage, rows in ((2, p.edge), (3, p.rows)):
            self.drain_seven(rows, self.send_sems.at[stage, t])


N_PIECES = 17


class Group:
    def __init__(self, spot, parts, got_c, got_y, blocks, send_sems, recv_sems):
        _, _, self.y, self.c = spot
        z, x, y, c = spot
        self.sibling, self.across = device(z, x, y, 1 - c), device(z, x, 1 - y, c)
        self.parts, self.got_c, self.got_y, self.blocks = parts, got_c, got_y, blocks
        self.send_sems, self.recv_sems = send_sems, recv_sems

    def sems(self, k):
        return self.send_sems.at[k], self.recv_sems.at[k]

    def start(self):
        for y in range(2):
            source = self.parts.at[2 * y + 1 - self.c]
            send(source, self.got_c.at[y], *self.sems(y), self.sibling)

    def across_y(self):
        for y in range(2):
            drain(self.got_c.at[y], self.recv_sems.at[y])
        own = self.parts.at[2 * (1 - self.y) + self.c]
        send(own, self.got_y.at[self.c], *self.sems(2), self.across)
        send(self.got_c.at[1 - self.y], self.got_y.at[1 - self.c], *self.sems(3), self.across)

    def finish(self):
        for k in (2, 3):
            drain(self.got_y.at[k - 2], self.recv_sems.at[k])
        y, c, blocks = self.y, self.c, self.blocks
        blocks[2 * y + c] = self.parts[2 * y + c]
        blocks[2 * y + 1 - c] = self.got_c[y]
        for k in range(2):
            blocks[2 * (1 - y) + k] = self.got_y[k]
        for k in range(4):
            drain(self.got_y.at[k % 2], self.send_sems.at[k])


def group_scratch(columns):
    return [
        pltpu.VMEM((4, 8, columns), F32),
        pltpu.VMEM((2, 8, columns), F32),
        pltpu.VMEM((2, 8, columns), F32),
        pltpu.VMEM((4, 8, columns), F32),
        pltpu.SemaphoreType.DMA((4,)),
        pltpu.SemaphoreType.DMA((4,)),
    ]


MOD_PART = 1728
SLIM = (24, 128)


class Acted:
    def __init__(self, s, spot):
        self.s = s
        self.z, self.x, self.y, self.c = spot

    def hop(self, k, where, peers):
        block = self.s.acted_all.at[where]
        for peer in peers:
            send(block, block, self.s.acted_send.at[k], self.s.acted_recv.at[k], peer)

    def step(self, k):
        z, x, y, c = self.z, self.x, self.y, self.c
        s = self.s
        if k == 0:
            pltpu.make_async_copy(s.acted_slim, s.acted_all.at[z, x, y, c], s.acted_own).start()
            drain(s.acted_slim, s.acted_own)
            self.hop(0, (z, x, y, c), [device(z, x, y, 1 - c)])
        elif k == 1:
            drain(s.acted_slim, s.acted_recv.at[0])
            self.hop(1, (z, x, y), [device(z, x, 1 - y, c)])
        elif k == 2:
            drain(s.acted_all.at[0, 0, 0], s.acted_recv.at[1])
            self.hop(2, (z, x), [device(z, 1 - x, y, c)])
        elif k == 3:
            drain(s.acted_all.at[0, 0], s.acted_recv.at[2])
            self.hop(3, (z,), [device((z + step) % 4, x, y, c) for step in (1, 3, 2)])
        else:
            drain(s.acted_all.at[pl.ds(0, 3)], s.acted_recv.at[3])
            drain(s.acted_slim, s.acted_send.at[0])
            drain(s.acted_all.at[0, 0, 0], s.acted_send.at[1])
            drain(s.acted_all.at[0, 0], s.acted_send.at[2])
            drain(s.acted_all.at[pl.ds(0, 3)], s.acted_send.at[3])


TOK = 512
TILE = 128
HEAD_TILE = 256
ATTN_STEPS = 4
STEP_BUDGET = 3.0
GATHER_AHEAD = 2


def mm(left, right):
    return lax.dot_general(left, right, (((1,), (0,)), ((), ())), preferred_element_type=F32)


def mm_nt(left, right):
    return lax.dot_general(left, right, (((1,), (1,)), ((), ())), preferred_element_type=F32)


def mm_tn(left, right):
    return lax.dot_general(left, right, (((0,), (0,)), ((), ())), preferred_element_type=F32)


def split(value):
    high = value.astype(BF16)
    return high, (value - high.astype(F32)).astype(BF16)


def mm_split(value, right):
    high, low = split(value)
    return mm(high, right) + mm(low, right)


def partner(value, first):
    width = value.shape[1]
    return jnp.where(first, pltpu.roll(value, width - 18, 1), pltpu.roll(value, 18, 1))


def first_lanes(rows):
    return lax.broadcasted_iota(jnp.int32, (rows, D), 1) % 36 < 18


def rows_of(block, count):
    return pl.ds(pl.multiple_of(block * count, count), count)


def head_window(head):
    base = min(head * HD // 128 * 128, D - 256)
    offset = head * HD - base
    lane = lax.broadcasted_iota(jnp.int32, (SEQ, 256), 1)
    return base, (lane >= offset) & (lane < offset + HD)


def flat(ref_value):
    return ref_value.reshape(-1, ref_value.shape[-1])


class Saves:
    def __init__(self, sems):
        self.sems, self.count, self.open = sems, 0, []

    def local(self, source, target):
        copy = pltpu.make_async_copy(source, target, self.sems.at[self.count])
        self.count += 1
        copy.start()
        self.open.append(copy)
        return copy

    def done(self, copy):
        copy.wait()
        self.open = [other for other in self.open if other is not copy]

    def finish(self):
        for copy in self.open:
            copy.wait()


class Forward:
    def __init__(self, s, spot, gather):
        self.s, self.gather = s, gather
        self.z, self.x, self.y, self.c = spot
        self.saves = Saves(s.save_sems)
        self.pending = {}
        self.remote = []
        self.slots = {}


    def to_sibling(self, source, target):
        k = len(self.remote)
        peer = device(self.z, self.x, self.y, 1 - self.c)
        copy = pltpu.make_async_remote_copy(
            src_ref=source,
            dst_ref=target,
            send_sem=self.s.pair_send.at[k],
            recv_sem=self.s.pair_recv.at[k],
            device_id=peer,
            device_id_type=MESH,
        )
        copy.start()
        self.remote.append(copy)


    def load(self, key, part, source, target):
        if (key, part) not in self.pending:
            copy = pltpu.make_async_copy(source, target, self.s.load_sems.at[len(self.pending)])
            copy.start()
            self.pending[key, part] = copy

    def window(self, ref, column):
        return ref.at[:, :, :, pl.ds(column, WIDTH)]

    def load_qv(self, j):
        packed, target = self.gather.refs[4], self.s.w.at[j % 2, 0]
        self.load(j, 0, self.window(packed, j * WIDTH), self.window(target, 0))
        self.load(j, 1, self.window(packed, LANE_HALF + j * WIDTH), self.window(target, WIDTH))

    def load_ko(self, j):
        packed = self.gather.refs[4]
        self.load(j, 0, self.window(packed, j * WIDTH), self.window(self.s.w.at[j % 2, 0], 0))
        target = self.window(self.s.w_out, (j - 3) * WIDTH)
        self.load(j, 1, self.window(packed, LANE_HALF + j * WIDTH), target)

    def load_ff(self, j):
        for part in range(4):
            which, half = part // 2, part % 2
            target = self.window(self.s.w.at[j % 2, which], half * WIDTH)
            self.load(6 + j, part, self.window(self.gather.refs[5 + which], (j + 4 * half) * WIDTH), target)

    def load_down(self, j):
        self.load(14 + j, 0, self.window(self.gather.refs[7], j * WIDTH), self.s.w_down.at[j % 2])

    def loaded(self, load, j, key):
        load(j)
        for part in range(4):
            if (key, part) in self.pending:
                self.pending[key, part].wait()


    def modulate(self, k):
        s, y, c = self.s, self.y, self.c
        spot = (self.z, self.x, y, c)
        own = s.acted_group.at[2 * y + c]
        pair = s.acted_group.at[pl.ds(2 * y, 2)]
        load = pltpu.make_async_copy(s.mod_weight, s.mod_w, s.acted_own)
        group = Group(
            spot, s.mod_parts, s.mod_got_c, s.mod_got_y, s.mod_blocks, s.mod_send, s.mod_recv
        )
        if k == 0:
            load.start()
            s.acted_group[2 * y + c] = s.acted[...]
            send(own, own, *self.first(0), device(self.z, self.x, y, 1 - c))
        elif k == 1:
            drain(own, s.first_recv.at[0])
            send(pair, pair, *self.first(1), device(self.z, self.x, 1 - y, c))
        elif k == 2:
            load.wait()
            drain(pair, s.first_recv.at[1])
            total = mm_nt(s.acted_group[...].reshape(32, D).astype(BF16), s.mod_w[...]) + s.bias[...].astype(F32)[None, :]
            s.mod_parts[...] = total.astype(BF16).astype(F32).reshape(4, 8, MOD_PART)
            group.start()
        elif k == 3:
            group.across_y()
        else:
            group.finish()
            for m in range(4):
                s.mod_flat[:, m * MOD_PART : (m + 1) * MOD_PART] = s.mod_blocks[m]
            for image in range(2):
                for m in range(6):
                    row = s.mod_flat[image : image + 1, m * D : (m + 1) * D]
                    s.o_mod[image, m : m + 1, :] = row
            drain(own, s.first_send.at[0])
            drain(pair, s.first_send.at[1])

    def first(self, k):
        return self.s.first_send.at[k], self.s.first_recv.at[k]

    def enter(self):
        s = self.s

        @pl.loop(0, TOK // TILE)
        def _(i):
            rows = rows_of(i, TILE)
            image = i // (SEQ // TILE)
            mod = s.o_mod
            normed, _ = norm_rows(s.tokens[rows, :].astype(F32))
            entry = normed * (1.0 + mod[image, 1:2, :]) + mod[image, 0:1, :]
            s.entry_a[rows, :] = entry.astype(BF16)
            branch = mod[image, 5:6, :] * s.cot[rows, :].astype(F32)
            s.d_branch[rows, :] = branch.astype(BF16)

        self.saves.local(s.d_branch, s.o_branch.at[pl.ds(0, TOK)])
        self.to_sibling(s.d_branch, s.o_branch.at[pl.ds(TOK, TOK)])
        self.turn(s.entry_a, s.t_a)
        self.share(s.t_a, s.o_lhs.at[0])

    def turn(self, source, target):
        @pl.loop(0, source.shape[1] // 128)
        def _(i):
            columns = rows_of(i, 128)
            target[columns, :] = source[:, columns].T

    def share(self, source, target):
        self.shared = [self.saves.local(source, target.at[:, pl.ds(0, TOK)])]
        self.to_sibling(source, target.at[:, pl.ds(TOK, TOK)])

    def qv(self, j):
        s = self.s
        self.loaded(self.load_qv, j, j)
        columns = pl.ds(j * WIDTH, WIDTH)
        both = mm(s.entry_a[...], flat(s.w[j % 2, 0]))
        s.proj[:, columns] = both[:, :WIDTH]
        s.v[:, columns] = both[:, WIDTH:].astype(BF16)
        if j == 2:
            self.saves.local(s.v, s.o_qkv.at[2])

    def ko(self, j):
        s = self.s
        self.loaded(self.load_ko, j, j)
        columns = pl.ds((j - 3) * WIDTH, WIDTH)
        s.proj[:, columns] = mm(s.entry_a[...], flat(s.w[j % 2, 0, :, :, :, 0:WIDTH]))

    def head_norm(self, which):
        s = self.s
        target, normed = (s.q, s.q_normed) if which == 0 else (s.k, s.k_normed)
        scale = s.scale_q if which == 0 else s.scale_k

        @pl.loop(0, TOK // HEAD_TILE)
        def _(i):
            rows = rows_of(i, HEAD_TILE)
            spots = rows_of(i % (SEQ // HEAD_TILE), HEAD_TILE)
            field = s.proj[rows, :]
            inverse = lax.rsqrt(mm_split(field * field, s.spread[...]) * (1.0 / HD) + EPSILON)
            scale[rows, :] = inverse
            field = field * mm_split(inverse, s.widen[...])
            normed[rows, :] = field.astype(BF16)
            turned = field * s.cos[spots, :] + partner(field, first_lanes(HEAD_TILE)) * s.sin[spots, :]
            target[rows, :] = turned.astype(BF16)

        self.saves.local(target, s.o_qkv.at[which])
        self.saves.local(normed, s.o_normed.at[which])
        self.saves.local(scale, s.o_scale.at[which])

    def attend(self, k):
        s = self.s
        heads = H // ATTN_STEPS
        if k >= 1:
            self.saves.done(self.slots[k - 1])
        for i in range(heads):
            base, mask = head_window(k * heads + i)
            window = pl.ds(base, 256)
            for image in range(2):
                rows = pl.ds(image * SEQ, SEQ)
                query = jnp.where(mask, s.q[rows, window].astype(F32), 0.0).astype(BF16)
                scores = mm_nt(query, s.k[rows, window]) * (1.0 / math.sqrt(HD))
                powers = jnp.exp(scores - jnp.max(scores, axis=1, keepdims=True))
                total = jnp.sum(powers, axis=1, keepdims=True)
                soft = (powers * (1.0 / total)).astype(BF16)
                s.soft[i, image] = soft
                mixed = mm(soft, s.v[rows, window])
                old = s.combined[rows, window].astype(F32)
                s.combined[rows, window] = jnp.where(mask, mixed, old).astype(BF16)

        self.slots[k] = self.saves.local(s.soft, s.o_soft.at[pl.ds(k * heads, heads)])

    def leave(self):
        s = self.s
        self.saves.done(self.slots[ATTN_STEPS - 1])
        for copy in self.shared:
            self.saves.done(copy)
        self.remote[1].wait_send()
        self.turn(s.combined, s.t_a)
        self.share(s.t_a, s.o_lhs.at[1])
        for j in range(3):
            columns = pl.ds(j * WIDTH, WIDTH)
            s.proj[:, columns] = mm(s.combined[...], flat(s.w_out[:, :, :, columns]))

        @pl.loop(0, TOK // TILE)
        def _(i):
            rows = rows_of(i, TILE)
            image = i // (SEQ // TILE)
            mod = s.o_mod
            attended = s.proj[rows, :]
            s.attended[rows, :] = attended.astype(BF16)
            residual = s.tokens[rows, :].astype(F32) + mod[image, 2:3, :] * attended
            s.residual[rows, :] = residual
            normed, _ = norm_rows(residual)
            entry = normed * (1.0 + mod[image, 4:5, :]) + mod[image, 3:4, :]
            s.entry_b[rows, :] = entry.astype(BF16)

        self.attended = self.saves.local(s.attended, s.o_attended)
        self.saves.local(s.residual, s.o_residual)
        self.turn(s.entry_b, s.t_b)
        self.share(s.t_b, s.o_lhs.at[2])

    def ff(self, j):
        s = self.s
        self.loaded(self.load_ff, j, 6 + j)
        s.wide[0] = mm(s.entry_b[...], flat(s.w[j % 2, 0]))
        s.wide[1] = mm(s.entry_b[...], flat(s.w[j % 2, 1]))
        mine = pl.ds(pl.multiple_of(self.c * 192, 16), 192)
        theirs = pl.ds(pl.multiple_of((1 - self.c) * 192, 16), 192)
        for half in range(2):
            shard = j + 4 * half
            at = shard * WIDTH
            if (6, j - 1, half) in self.slots:
                self.saves.done(self.slots[6, j - 1, half])

            @pl.loop(0, TOK // TILE)
            def _(i, half=half, at=at):
                rows = rows_of(i, TILE)
                gate = s.wide[0, rows, half * WIDTH : (half + 1) * WIDTH]
                up = s.wide[1, rows, half * WIDTH : (half + 1) * WIDTH]
                sigma = 1.0 / (1.0 + jnp.exp(-gate))
                active = gate * sigma
                s.active[half, 0, rows, :] = active.astype(BF16)
                slope = up * sigma * (1.0 + gate * (1.0 - sigma))
                s.active[half, 1, rows, :] = slope.astype(BF16)
                s.hidden[rows, at : at + WIDTH] = (active * up).astype(BF16)

            self.slots[6, j, half] = self.saves.local(s.active.at[half], s.o_active.at[shard])
            for i in range(3):
                turned = s.hidden[:, at + 128 * i : at + 128 * i + 128].T
                s.t_h[shard, 128 * i : 128 * i + 128, :] = turned
            self.saves.local(s.t_h.at[shard, mine], s.o_hidden.at[shard, :, pl.ds(0, TOK)])
            self.to_sibling(s.t_h.at[shard, theirs], s.o_hidden.at[shard, :, pl.ds(TOK, TOK)])

    def down(self, j):
        s = self.s
        self.loaded(self.load_down, j, 14 + j)
        if j == 0:
            self.saves.done(self.attended)
        columns = pl.ds(j * WIDTH, WIDTH)
        s.wide[0, :, 0:WIDTH] = mm(s.hidden[...], flat(s.w_down[j % 2]))
        for image in range(2):
            gate = s.o_mod[image, 5:6, columns]
            total = jnp.zeros((1, WIDTH), F32)
            for i in range(SEQ // TILE):
                rows = pl.ds(image * SEQ + i * TILE, TILE)
                branch = s.wide[0, rows, 0:WIDTH]
                result = s.residual[rows, columns] + gate * branch
                s.attended[rows, columns] = result.astype(BF16)
                total = total + jnp.sum(
                    s.cot[rows, columns].astype(F32) * branch, axis=0, keepdims=True
                )
            s.o_gate_b[image, 0:1, columns] = total
        if j == 2:
            self.saves.local(s.attended, s.o_result)

    def plan(self):
        steps = [(None, self.modulate, k, 0, 7) for k in range(5)] + [(None, self.enter, None, 0, 4)]
        steps += [(self.load_qv, self.qv, j, j + 1, 2.5) for j in range(3)]
        steps += [(None, self.head_norm, 0, 3, 4)]
        steps += [(self.load_ko, self.ko, j, j + 1, 1.5) for j in range(3, 6)]
        steps += [(None, self.head_norm, 1, 6, 4)]
        steps += [(None, self.attend, k, 6, 3) for k in range(ATTN_STEPS)]
        steps += [(None, self.leave, None, 6, 6)]
        steps += [(self.load_ff, self.ff, j, 8 + 2 * j, 5.5) for j in range(4)]
        steps += [(self.load_down, self.down, j, 15 + j, 3) for j in range(3)]
        return steps

    def finish(self):
        self.saves.finish()
        for k, copy in enumerate(self.remote):
            if k != 1:
                copy.wait_send()
            copy.wait_recv()


class ForwardInputs(NamedTuple):
    packed: object
    gate: object
    up: object
    down: object
    tokens: object
    cot: object
    acted: object
    bias: object
    mod_weight: object
    acted_slim: object
    cos: object
    sin: object
    spread: object
    widen: object


FORWARD_OUTPUTS = dict(
    packed_all=((4, 2, 144, 4608), BF16),
    gate_all=((4, 2, 144, 3072), BF16),
    up_all=((4, 2, 144, 3072), BF16),
    down_all=((4, 2, 384, 1152), BF16),
    o_branch=((2 * TOK, D), BF16),
    o_lhs=((3, D, 2 * TOK), BF16),
    o_hidden=((8, 192, 2 * TOK), BF16),
    o_qkv=((3, TOK, D), BF16),
    o_normed=((2, TOK, D), BF16),
    o_scale=((2, TOK, 128), F32),
    o_soft=((H, 2, SEQ, SEQ), BF16),
    o_attended=((TOK, D), BF16),
    o_residual=((TOK, D), F32),
    o_active=((8, 2, TOK, WIDTH), BF16),
    o_result=((TOK, D), BF16),
    acted_all=((4, 2, 2, 2) + SLIM, F32),
    o_mod=((2, 8, D), F32),
    o_gate_b=((2, 8, D), F32),
)


def forward_scratch():
    def vmem(*shape, kind=BF16):
        return pltpu.VMEM(shape, kind)

    return dict(
        entry_a=vmem(TOK, D),
        d_branch=vmem(TOK, D),
        t_a=vmem(D, TOK),
        proj=vmem(TOK, D, kind=F32),
        q=vmem(TOK, D),
        k=vmem(TOK, D),
        v=vmem(TOK, D),
        q_normed=vmem(TOK, D),
        k_normed=vmem(TOK, D),
        scale_q=vmem(TOK, 128, kind=F32),
        scale_k=vmem(TOK, 128, kind=F32),
        soft=vmem(H // ATTN_STEPS, 2, SEQ, SEQ),
        combined=vmem(TOK, D),
        attended=vmem(TOK, D),
        residual=vmem(TOK, D, kind=F32),
        entry_b=vmem(TOK, D),
        t_b=vmem(D, TOK),
        wide=vmem(2, TOK, 2 * WIDTH, kind=F32),
        active=vmem(2, 2, TOK, WIDTH),
        hidden=vmem(TOK, 8 * WIDTH),
        t_h=vmem(8, WIDTH, TOK),
        w=vmem(2, 2, 4, 2, 144, 2 * WIDTH),
        w_out=vmem(4, 2, 144, D),
        w_down=vmem(2, 4, 2, 384, WIDTH),
        gather_send=pltpu.SemaphoreType.DMA((4, N_PIECES)),
        gather_recv=pltpu.SemaphoreType.DMA((4, N_PIECES)),
        mod_w=vmem(MOD_PART, D),
        acted_group=vmem(4, 8, D, kind=F32),
        mod_flat=vmem(8, 4 * MOD_PART, kind=F32),
        mod_parts=group_scratch(MOD_PART)[0],
        mod_got_c=group_scratch(MOD_PART)[1],
        mod_got_y=group_scratch(MOD_PART)[2],
        mod_blocks=group_scratch(MOD_PART)[3],
        mod_send=group_scratch(MOD_PART)[4],
        mod_recv=group_scratch(MOD_PART)[5],
        acted_send=pltpu.SemaphoreType.DMA((4,)),
        acted_recv=pltpu.SemaphoreType.DMA((4,)),
        acted_own=pltpu.SemaphoreType.DMA,
        first_send=pltpu.SemaphoreType.DMA((2,)),
        first_recv=pltpu.SemaphoreType.DMA((2,)),
        own_packed=vmem(144, 4 * D),
        own_down=vmem(384, D),
        own_sems=pltpu.SemaphoreType.DMA((4,)),
        save_sems=pltpu.SemaphoreType.DMA((56,)),
        load_sems=pltpu.SemaphoreType.DMA((48,)),
        pair_send=pltpu.SemaphoreType.DMA((16,)),
        pair_recv=pltpu.SemaphoreType.DMA((16,)),
    )


def run_step(steps, arrived):
    _, act, j, _, cost = steps.pop(0)
    if steps and steps[0][0] is not None and steps[0][3] <= arrived:
        steps[0][0](steps[0][2])
    act() if j is None else act(j)
    return cost


def forward_kernel(*refs):
    names = ForwardInputs._fields + tuple(FORWARD_OUTPUTS) + tuple(forward_scratch())
    s = SimpleNamespace(**dict(zip(names, refs, strict=True)))
    spot = place()
    greet(neighbours(*spot))
    arrays = [s.packed, s.gate, s.up, s.down, s.packed_all, s.gate_all, s.up_all, s.down_all]
    own_gate, own_up = s.hidden.at[pl.ds(0, 144)], s.hidden.at[pl.ds(144, 144)]
    stages = [s.own_packed, own_gate, own_up, s.own_down]
    gather = Gather(arrays, (s.gather_send, s.gather_recv, s.own_sems), spot, stages)
    work = Forward(s, spot, gather)
    steps = work.plan()
    gather.own_copies()
    acted = Acted(s, spot)
    ahead = GATHER_AHEAD
    arrived = 0
    for t in range(N_PIECES + 4 + ahead):
        if t == 1:
            gather.own_stores()
        if t < N_PIECES:
            if t >= ahead:
                gather.sent_z(t - ahead)
            gather.start_z(t)
        if 0 <= t - ahead < N_PIECES:
            gather.start_x(t - ahead)
        if 0 <= t - ahead - 1 < N_PIECES:
            gather.start_y(t - ahead - 1)
        if 0 <= t - ahead - 2 < N_PIECES:
            gather.start_c(t - ahead - 2)
        if 0 <= t - ahead - 3 < N_PIECES:
            if arrived == 0:
                gather.own_done()
            gather.arrived(t - ahead - 3)
            arrived += 1
        if t >= 6 and t % 3 == 0 and t // 3 - 2 < 5:
            acted.step(t // 3 - 2)
        spent = 0.0
        while steps and steps[0][3] <= arrived and spent < STEP_BUDGET:
            spent += run_step(steps, arrived)
    while steps:
        run_step(steps, arrived)
    for t in range(N_PIECES - ahead, N_PIECES):
        gather.sent_z(t)
    for t in range(N_PIECES):
        gather.sent_rest(t)
    work.finish()


def forward_pass(*given):
    hbm = pl.BlockSpec(memory_space=pl.ANY)
    inside = pl.BlockSpec(memory_space=pltpu.VMEM)
    out = pl.pallas_call(
        forward_kernel,
        out_shape=[jax.ShapeDtypeStruct(*spec) for spec in FORWARD_OUTPUTS.values()],
        in_specs=[hbm] * 4 + [inside] * 4 + [hbm] * 2 + [inside] * 4,
        out_specs=[hbm] * 16 + [inside] * 2,
        scratch_shapes=list(forward_scratch().values()),
        name="forward_pass",
        compiler_params=pltpu.CompilerParams(
            collective_id=0, has_side_effects=True, vmem_limit_bytes=121 << 19
        ),
    )(*ForwardInputs(*given))
    return SimpleNamespace(**dict(zip(FORWARD_OUTPUTS, out)))


def head_tables():
    lane = np.arange(D) % HD
    frequency = np.exp(-math.log(10000.0) * (lane % 18) / 18)
    token = np.arange(SEQ)[:, None]
    angle = np.where(lane < 36, token // GRID, token % GRID) * frequency
    sign = np.where(lane % 36 < 18, -1.0, 1.0)
    spread = (np.arange(D)[:, None] // HD == np.arange(128)).astype(np.float32)
    return (
        jnp.asarray(np.cos(angle), F32),
        jnp.asarray(np.sin(angle) * sign, F32),
        jnp.asarray(spread, BF16),
        jnp.asarray(spread.T, BF16),
    )


SCATTER_ROWS = (144,) * 14 + (192,) * 3
SCATTER_EDGE = tuple((32, 48)[j % 2] for j in range(14)) + (48,) * 3
ASKED = 3
ORDER = (14, 15, 16) + tuple(range(6, 14)) + tuple(range(6))


class Reduce:
    def __init__(self, s, spot):
        self.s = s
        self.z, self.x, self.y, self.c = spot
        self.stage = {}
        self.open = []

    def shape(self, t):
        return SCATTER_ROWS[t], SCATTER_EDGE[t]

    def part(self, t):
        rows, edge = self.shape(t)
        return pl.ds(pl.multiple_of(self.y * edge, 16), rows - edge)

    def held(self, t):
        s = self.s
        return s.held_big.at[t - 14] if t >= 14 else s.held.at[t if t < 6 else t - 6]

    def pick(self, small, big, t):
        return big.at[t - 14] if t >= 14 else small.at[t]

    def got_y(self, t):
        return self.pick(self.s.got_y, self.s.got_y_big, t)

    def got_x(self, t):
        return self.pick(self.s.got_x, self.s.got_x_big, t)

    def got_z(self, t):
        return self.pick(self.s.got_z, self.s.got_z_big, t)

    def got_f(self, t):
        return self.pick(self.s.got_f, self.s.got_f_big, t)

    def sems(self, stage, t):
        return self.s.scatter_send.at[stage, t], self.s.scatter_recv.at[stage, t]

    def produced(self, t):
        self.stage[t] = -1
        self.ask()

    def ask(self):
        entered = sum(stage > 0 for stage in self.stage.values())
        for t in ORDER[: entered + ASKED]:
            if self.stage.get(t) == -1:
                self.stage[t] = 0
                self.start_y(t)

    def advance(self):
        stages = (self.start_x, self.start_z, self.start_f, self.start_c)
        under_way = [t for t in ORDER if 0 < self.stage.get(t, 4) < 4]
        waiting = [t for t in ORDER if self.stage.get(t) == 0]
        for t in waiting[:1] + under_way[::-1]:
            stages[self.stage[t]](t)
            self.stage[t] += 1
        self.ask()

    def free(self, t):
        while self.stage[t] < 4:
            self.advance()
        if t in self.open:
            self.sent(t)

    def start_y(self, t):
        rows, edge = self.shape(t)
        theirs = pl.ds(pl.multiple_of((1 - self.y) * (rows - edge), 16), edge)
        send(
            self.held(t).at[:, :, theirs, :],
            self.got_y(t).at[:, :, pl.ds(0, edge), :],
            *self.sems(0, t),
            device(self.z, self.x, 1 - self.y, self.c),
        )

    def start_x(self, t):
        rows, edge = self.shape(t)
        held, got = self.held(t), self.got_y(t)
        drain(got.at[:, :, pl.ds(0, edge), :], self.s.scatter_recv.at[0, t])
        mine = pl.ds(pl.multiple_of(self.y * (rows - edge), 16), edge)

        @pl.loop(0, 4)
        def _(k):
            for x in range(2):
                total = held[k, x, mine, :].astype(F32) + got[k, x, pl.ds(0, edge), :].astype(F32)
                held[k, x, mine, :] = total.astype(BF16)

        send(
            held.at[:, 1 - self.x, self.part(t), :],
            self.got_x(t).at[:, pl.ds(0, rows - edge), :],
            *self.sems(1, t),
            device(self.z, 1 - self.x, self.y, self.c),
        )

    def start_z(self, t):
        rows, edge = self.shape(t)
        held, got = self.held(t), self.got_x(t)
        keep = rows - edge
        drain(got.at[:, pl.ds(0, keep), :], self.s.scatter_recv.at[1, t])
        part = self.part(t)

        @pl.loop(0, 4)
        def _(k):
            total = held[k, self.x, part, :].astype(F32) + got[k, pl.ds(0, keep), :].astype(F32)
            held[k, self.x, part, :] = total.astype(BF16)

        for step in (1, 3, 2):
            other = (self.z + step) % 4
            send(
                held.at[other, self.x, part, :],
                self.got_z(t).at[step - 1, pl.ds(0, keep), :],
                *self.sems(2, t),
                device(other, self.x, self.y, self.c),
            )

    def start_f(self, t):
        rows, edge = self.shape(t)
        held, got = self.held(t), self.got_z(t)
        keep = rows - edge
        drain(got.at[:, pl.ds(0, keep), :], self.s.scatter_recv.at[2, t])
        part = self.part(t)
        total = held[self.z, self.x, part, :].astype(F32)
        for k in range(3):
            total = total + got[k, pl.ds(0, keep), :].astype(F32)
        held[self.z, self.x, part, :] = total.astype(BF16)
        send(
            held.at[self.z, self.x, part, :],
            self.got_f(t).at[pl.ds(0, keep), :],
            *self.sems(3, t),
            device(self.z, self.x, 1 - self.y, self.c),
        )

    def target(self, t):
        s = self.s
        if t < 6:
            columns = pl.ds(pl.multiple_of(self.c * LANE_HALF + t * WIDTH, 128), WIDTH)
            return s.g_packed.at[:, columns]
        if t < 14:
            columns = pl.ds(pl.multiple_of(self.c * FF_HALF + (t - 6) // 2 * WIDTH, 128), WIDTH)
            return (s.g_gate, s.g_up)[(t - 6) % 2].at[:, columns]
        rows = pl.ds(pl.multiple_of(self.c * 192, 16), 192)
        return s.g_down.at[rows, pl.ds((t - 14) * WIDTH, WIDTH)]

    def start_c(self, t):
        rows, edge = self.shape(t)
        held, got = self.held(t), self.got_f(t)
        y, keep, both = self.y, rows - edge, rows - 2 * edge
        drain(got.at[pl.ds(0, keep), :], self.s.scatter_recv.at[3, t])
        drain(self.got_y(t).at[:, :, pl.ds(0, edge), :], self.s.scatter_send.at[0, t])
        drain(self.got_x(t).at[:, pl.ds(0, keep), :], self.s.scatter_send.at[1, t])
        mid, fin = held.at[self.z, self.x], held.at[self.z, 1 - self.x]

        def at(offset, count):
            return pl.ds(pl.multiple_of(offset, 16), count)

        own, other = at(y * keep, edge), at((1 - y) * keep, edge)
        fin[own, :] = mid[own, :]
        fin[other, :] = got[at((1 - y) * both, edge), :]
        total = mid[pl.ds(edge, both), :].astype(F32) + got[at(y * edge, both), :].astype(F32)
        fin[pl.ds(edge, both), :] = total.astype(BF16)
        target = self.target(t)
        send(fin, target, *self.sems(4, t), device(self.z, self.x, y, 1 - self.c))
        pltpu.make_async_copy(fin, target, self.s.store_sems.at[t]).start()
        self.open.append(t)

    def sent(self, t):
        self.open.remove(t)
        rows, edge = self.shape(t)
        sems = self.s.scatter_send
        drain(self.got_z(t).at[:, pl.ds(0, rows - edge), :], sems.at[2, t])
        drain(self.got_f(t).at[pl.ds(0, rows - edge), :], sems.at[3, t])
        drain(self.target(t), sems.at[4, t])
        drain(self.target(t), self.s.store_sems.at[t])

    def finish(self):
        for t in ORDER:
            self.free(t)
        for t in range(N_PIECES):
            drain(self.target(t), self.s.scatter_recv.at[4, t])


class Backward:
    def __init__(self, s, spot, reduce):
        self.s, self.reduce = s, reduce
        self.z, self.x, self.y, self.c = spot
        self.pending = {}
        self.remote = {}
        self.copies = 0

    def load(self, key, source, target):
        if key not in self.pending:
            copy = pltpu.make_async_copy(source, target, self.s.load_sems.at[self.copies])
            self.copies += 1
            copy.start()
            self.pending[key] = copy

    def wait(self, *keys):
        for key in keys:
            self.pending.pop(key).wait()

    def to_sibling(self, key, source, target):
        k = len(self.remote)
        copy = pltpu.make_async_remote_copy(
            src_ref=source,
            dst_ref=target,
            send_sem=self.s.pair_send.at[k],
            recv_sem=self.s.pair_recv.at[k],
            device_id=device(self.z, self.x, self.y, 1 - self.c),
            device_id_type=MESH,
        )
        copy.start()
        self.remote[key] = copy


    def grad_down(self, hidden, branch):
        s, reduce = self.s, self.reduce

        @pl.loop(0, 4)
        def _(k):
            left = hidden[pl.ds(2 * k, 2)].reshape(384, 2 * TOK)
            total = mm(left, branch[...]).astype(BF16)
            for j in range(3):
                block = total[:, j * WIDTH : (j + 1) * WIDTH]
                s.held_big[j, k] = block.reshape(2, 192, WIDTH)

        for t in (14, 15, 16):
            reduce.produced(t)

    def column(self, w):
        half = (1 - self.c) if w % 2 == 0 else self.c
        return half * 4 + w // 2

    def load_ff(self, f, w):
        s = self.s
        window = self.column(w)
        columns = pl.ds(pl.multiple_of(window * WIDTH, 128), WIDTH)
        slot = w % 2
        self.load((1, w), s.down_all.at[window // 2, window % 2], f.w_down.at[slot])
        self.load((2, w), s.gate_all.at[:, :, :, columns], s.w.at[slot, :, :, :, pl.ds(0, WIDTH)])
        self.load((3, w), s.up_all.at[:, :, :, columns], s.w.at[slot, :, :, :, pl.ds(WIDTH, WIDTH)])
        self.load((4, w), s.o_active.at[window], f.active.at[slot])

    def ff(self, f, w):
        s = self.s
        slot = w % 2
        self.load_ff(f, w)
        self.wait((1, w), (2, w), (3, w), (4, w))
        if w < 7:
            self.load_ff(f, w + 1)
        s.d_residual[:, 0:WIDTH] = mm_nt(f.branch[pl.ds(0, TOK), :], f.w_down[slot])
        if w >= 2:
            if slot == 0:
                self.remote[5, w - 2].wait_send()
            else:
                self.wait((5, w - 2))
        steep = f.steep.at[slot]

        @pl.loop(0, TOK // TILE)
        def _(i):
            rows = rows_of(i, TILE)
            back = s.d_residual[rows, 0:WIDTH]
            steep[rows, 0:WIDTH] = (back * f.active[slot, 1, rows, :].astype(F32)).astype(BF16)
            steep[rows, WIDTH : 2 * WIDTH] = (
                back * f.active[slot, 0, rows, :].astype(F32)
            ).astype(BF16)

        j = w // 2
        if slot == 0:
            self.to_sibling((5, w), steep, s.r_ff.at[j, pl.ds(TOK, TOK)])
        else:
            self.load((5, w), steep, s.r_ff.at[j, pl.ds(0, TOK)])
        product = mm_nt(steep[...], flat(s.w[slot]))
        if w == 0:
            s.acc[...] = product
        else:
            s.acc[...] += product

    def load_grad_ff(self, j):
        s = self.s
        self.remote[5, 2 * j].wait_recv()
        if (5, 2 * j + 1) in self.pending:
            self.wait((5, 2 * j + 1))
        self.load((6, j), s.r_ff.at[j], s.right.at[j % 2])

    def grad_ff(self, j):
        s = self.s
        self.wait((6, j))
        right = s.right.at[j % 2]

        @pl.loop(0, 2)
        def _(k):
            left = s.left[pl.ds(pl.multiple_of(k * 576, 64), 576), :]
            total = mm(left, right[...]).astype(BF16)
            for half in range(2):
                block = total[:, half * WIDTH : (half + 1) * WIDTH]
                s.held[2 * j + half, pl.ds(2 * k, 2)] = block.reshape(2, 2, 144, WIDTH)

        self.reduce.produced(6 + 2 * j)
        self.reduce.produced(7 + 2 * j)

    def feed_forward(self, f):
        s, reduce = self.s, self.reduce
        self.wait(11, 12)
        self.load((7, 0), s.o_lhs.at[2], s.left)
        self.grad_down(f.hidden, f.branch)
        for w in range(8):
            self.ff(f, w)
            if w == 0:
                self.wait((7, 0))
            if w % 2 == 1:
                reduce.advance()
                if w >= 3:
                    self.load_grad_ff(w // 2 - 1)
            elif w >= 4:
                self.grad_ff(w // 2 - 2)
        self.load_grad_ff(3)
        self.grad_ff(2)
        self.grad_ff(3)
        self.remote[5, 6].wait_send()


    def middle(self, f):
        s = self.s
        self.load(21, s.cot, f.cot)
        self.load(22, s.o_residual, s.d_residual)
        self.load(23, s.o_attended, f.attended)
        self.wait(21, 22, 23)
        s.d_mod[...] = jnp.zeros_like(s.d_mod)

        @pl.loop(0, TOK // TILE)
        def _(i):
            rows = rows_of(i, TILE)
            image = i // (SEQ // TILE)
            mod, d_mod = s.mod, s.d_mod
            normed, inverse = norm_rows(s.d_residual[rows, :])
            d_entry = s.acc[rows, :]
            d_mod[image, 3:4, :] += jnp.sum(d_entry, axis=0, keepdims=True)
            d_mod[image, 4:5, :] += jnp.sum(d_entry * normed, axis=0, keepdims=True)
            back = norm_back(normed, inverse, d_entry * (1.0 + mod[image, 4:5, :]))
            d_residual = f.cot[rows, :].astype(F32) + back
            s.d_residual[rows, :] = d_residual
            attended = f.attended[rows, :].astype(F32)
            d_mod[image, 2:3, :] += jnp.sum(d_residual * attended, axis=0, keepdims=True)
            s.joined[rows, 3 * D : 4 * D] = (mod[image, 2:3, :] * d_residual).astype(BF16)


    def load_soft(self, f, k):
        heads = H // ATTN_STEPS
        self.load((31, k), self.s.o_soft.at[pl.ds(k * heads, heads)], f.soft)

    def attend(self, f, k):
        s = self.s
        heads = H // ATTN_STEPS
        self.wait((31, k))
        factor = 1.0 / math.sqrt(HD)
        for i in range(heads):
            base, mask = head_window(k * heads + i)
            window = pl.ds(base, 256)
            for image in range(2):
                rows = pl.ds(image * SEQ, SEQ)
                back = jnp.where(mask, f.back[rows, window].astype(F32), 0.0).astype(BF16)
                soft = f.soft[i, image]
                d_soft = mm_nt(back, f.qkv[2, rows, window])
                wide = soft.astype(F32)
                d_scores = (
                    wide * (d_soft - jnp.sum(wide * d_soft, axis=1, keepdims=True))
                ).astype(BF16)
                results = (
                    mm(d_scores, f.qkv[1, rows, window]) * factor,
                    mm_tn(d_scores, f.qkv[0, rows, window]) * factor,
                    mm_tn(soft, back),
                )
                for part, result in enumerate(results):
                    place_at = pl.ds(part * D + base, 256)
                    old = s.joined[rows, place_at].astype(F32)
                    s.joined[rows, place_at] = jnp.where(mask, result, old).astype(BF16)
        if k + 1 < ATTN_STEPS:
            self.load_soft(f, k + 1)

    def head_back(self, f, which):
        s = self.s

        @pl.loop(0, TOK // HEAD_TILE)
        def _(i):
            rows = rows_of(i, HEAD_TILE)
            spots = rows_of(i % (SEQ // HEAD_TILE), HEAD_TILE)
            columns = pl.ds(which * D, D)
            grad = s.joined[rows, columns].astype(F32)
            grad = grad * f.cos[spots, :] - partner(grad, first_lanes(HEAD_TILE)) * f.sin[spots, :]
            normed = f.normed[which, rows, :].astype(F32)
            mean = mm_split(grad * normed, s.spread[...]) * (1.0 / HD)
            scale = mm_split(s.acc[rows, which * 128 : which * 128 + 128], s.widen[...])
            result = scale * (grad - normed * mm(mean.astype(BF16), s.widen[...]))
            s.joined[rows, columns] = result.astype(BF16)

    def attention(self, f):
        s, reduce = self.s, self.reduce
        self.load(24, s.packed_all.at[:, :, :, pl.ds(3 * D, 768)], s.w.at[0])
        self.load(25, s.packed_all.at[:, :, :, pl.ds(3 * D + 768, WIDTH)], s.w.at[1, :, :, :, pl.ds(0, WIDTH)])
        for k in range(3):
            self.load((41, k), s.o_qkv.at[k], f.qkv.at[k])
        self.load_soft(f, 0)
        self.load(42, s.o_normed, f.normed)
        self.load(44, s.cos, f.cos)
        self.load(45, s.sin, f.sin)
        self.wait(24, 25)
        joined = s.joined
        s.acc[...] = mm_nt(joined[:, 3 * D : 3 * D + 768], flat(s.w[0]))
        s.acc[...] += mm_nt(joined[:, 3 * D + 768 :], flat(s.w[1, :, :, :, 0:WIDTH]))
        f.back[...] = s.acc[...].astype(BF16)
        for k in range(2):
            self.load((43, k), s.o_scale.at[k], s.acc.at[:, pl.ds(128 * k, 128)])
        reduce.advance()
        self.wait((41, 0), (41, 1), (41, 2))
        for k in range(ATTN_STEPS):
            self.attend(f, k)
            if k % 2 == 1:
                reduce.advance()
        self.wait(42, (43, 0), (43, 1), 44, 45)
        self.head_back(f, 0)
        self.trade(0)
        reduce.advance()
        self.head_back(f, 1)
        self.trade(1)

    def trade(self, k):
        s = self.s
        columns = pl.ds(k * D, D)
        theirs = pl.ds(pl.multiple_of((1 - self.c) * LANE_HALF + k * D, 128), D)
        mine = pl.ds(pl.multiple_of(self.c * LANE_HALF + k * D, 128), D)
        send(
            s.joined.at[:, theirs],
            s.r_packed.at[pl.ds(TOK, TOK), columns],
            s.pair_send.at[6 + k],
            s.pair_recv.at[6 + k],
            device(self.z, self.x, self.y, 1 - self.c),
        )
        own = s.r_packed.at[pl.ds(0, TOK), columns]
        pltpu.make_async_copy(s.joined.at[:, mine], own, s.trade_sems.at[k]).start()

    def traded(self, k):
        block = self.s.r_packed.at[pl.ds(0, TOK), pl.ds(k * D, D)]
        drain(block, self.s.pair_recv.at[6 + k])
        drain(block, self.s.trade_sems.at[k])


    def load_entry(self, k):
        s = self.s
        width = 768 if k < 4 else WIDTH
        self.load(
            (51, k),
            s.packed_all.at[:, :, :, pl.ds(k * 768, width)],
            s.w.at[k % 2, :, :, :, pl.ds(0, width)],
        )

    def entry(self, k):
        s = self.s
        width = 768 if k < 4 else WIDTH
        self.load_entry(k)
        self.wait((51, k))
        if k < 4:
            self.load_entry(k + 1)
        product = mm_nt(s.joined[:, k * 768 : k * 768 + width], flat(s.w[k % 2, :, :, :, 0:width]))
        if k == 0:
            s.acc[...] = product
        else:
            s.acc[...] += product

    def grad_packed(self, f, jj):
        s = self.s
        self.wait((61, jj))
        right = s.right.at[jj % 2]

        @pl.loop(0, 2)
        def _(k):
            rows = pl.ds(pl.multiple_of(k * 576, 64), 576)
            for half in range(2):
                j = 2 * jj + half
                left = s.left if j < 3 else f.left
                total = mm(left[rows, :], right[:, half * WIDTH : (half + 1) * WIDTH])
                s.held[j, pl.ds(2 * k, 2)] = total.astype(BF16).reshape(2, 2, 144, WIDTH)

        self.reduce.produced(2 * jj)
        self.reduce.produced(2 * jj + 1)

    def load_right(self, jj):
        self.load((61, jj), self.s.r_packed.at[:, pl.ds(768 * jj, 768)], self.s.right.at[jj % 2])

    def last(self, f):
        s, reduce = self.s, self.reduce
        self.traded(0)
        self.load_right(0)
        self.load(72, s.o_lhs.at[0], s.left)
        self.load(73, s.o_lhs.at[self.c], f.left)
        self.load(74, s.tokens, f.tokens)
        self.load(76, s.mod_weight, f.mod_w)
        self.load_entry(0)
        reduce.advance()
        self.wait(72, 73)
        for jj in range(3):
            reduce.free(6 + 2 * jj)
            reduce.free(7 + 2 * jj)
            self.grad_packed(f, jj)
            if jj == 0:
                self.traded(1)
                self.load_right(1)
                self.load_right(2)
            self.entry(jj)
            reduce.advance()
        self.entry(3)
        self.entry(4)
        reduce.advance()
        self.wait(74)

        @pl.loop(0, TOK // TILE)
        def _(i):
            rows = rows_of(i, TILE)
            image = i // (SEQ // TILE)
            mod, d_mod = s.mod, s.d_mod
            normed, inverse = norm_rows(f.tokens[rows, :].astype(F32))
            d_entry = s.acc[rows, :]
            d_mod[image, 0:1, :] += jnp.sum(d_entry, axis=0, keepdims=True)
            d_mod[image, 1:2, :] += jnp.sum(d_entry * normed, axis=0, keepdims=True)
            back = norm_back(normed, inverse, d_entry * (1.0 + mod[image, 1:2, :]))
            s.d_residual[rows, :] += back

        self.load(75, s.d_residual, s.g_tokens)
        self.modulation(f)
        reduce.finish()
        self.wait(75)
        for k in range(2):
            drain(s.r_packed.at[pl.ds(0, TOK), pl.ds(k * D, D)], s.pair_send.at[6 + k])

    def modulation(self, f):
        s, reduce = self.s, self.reduce
        z, x, y, c = spot = (self.z, self.x, self.y, self.c)
        s.back_flat[...] = jnp.zeros_like(s.back_flat)
        for image in range(2):
            for k in range(6):
                row = s.gate_b[image, 0:1, :] if k == 5 else s.d_mod[image, k : k + 1, :]
                rounded = row.astype(BF16).astype(F32)
                s.back_flat[image : image + 1, k * D : (k + 1) * D] = rounded
        for m in range(4):
            s.back_parts[m] = s.back_flat[:, m * MOD_PART : (m + 1) * MOD_PART]
        group = Group(
            spot, s.back_parts, s.back_got_c, s.back_got_y, s.back_blocks, s.back_send, s.back_recv
        )
        group.start()
        reduce.advance()
        group.across_y()
        reduce.advance()
        group.finish()
        for m in range(4):
            s.back[2 * m : 2 * m + 2, :] = s.back_blocks[m, 0:2, :]
        x_peer = device(z, 1 - x, y, c)
        send(s.back, s.back_got_x, s.wide_send.at[0], s.wide_recv.at[0], x_peer)
        self.wait(76)
        partial = mm(s.back[...].astype(BF16), f.mod_w[...])
        s.cond_parts[...] = jnp.zeros_like(s.cond_parts)
        for m in range(4):
            s.cond_parts[m, 0:2, :] = partial[2 * m : 2 * m + 2, :]
        cond = Group(
            spot, s.cond_parts, s.cond_got_c, s.cond_got_y, s.cond_blocks, s.cond_send, s.cond_recv
        )
        cond.start()
        drain(s.back, s.wide_recv.at[0])
        own, other = s.back[...], s.back_got_x[...]
        low = jnp.where(x == 0, own, other)
        high = jnp.where(x == 0, other, own)
        s.back_all[z] = jnp.concatenate([low, high], axis=0).astype(BF16)
        block = s.back_all.at[z]
        for step in (1, 3, 2):
            peer = device((z + step) % 4, x, y, c)
            send(block, block, s.wide_send.at[1], s.wide_recv.at[1], peer)
        cond.across_y()
        reduce.advance()
        cond.finish()
        total = s.cond_blocks[0] + s.cond_blocks[1] + s.cond_blocks[2] + s.cond_blocks[3]
        s.o_cond[...] = total
        reduce.advance()
        drain(s.back_all.at[pl.ds(0, 3)], s.wide_recv.at[1])
        self.load(77, s.back_all, s.o_back)
        drain(s.back, s.wide_send.at[0])
        drain(s.back_all.at[pl.ds(0, 3)], s.wide_send.at[1])
        self.wait(77)


class BackwardInputs(NamedTuple):
    packed_all: object
    gate_all: object
    up_all: object
    down_all: object
    o_branch: object
    o_lhs: object
    o_hidden: object
    o_qkv: object
    o_normed: object
    o_scale: object
    o_soft: object
    o_attended: object
    o_residual: object
    o_active: object
    tokens: object
    cot: object
    cos: object
    sin: object
    mod: object
    spread: object
    widen: object
    gate_b: object
    mod_weight: object


BACKWARD_OUTPUTS = dict(
    g_packed=((144, 4 * D), BF16),
    g_gate=((144, 8 * WIDTH), BF16),
    g_up=((144, 8 * WIDTH), BF16),
    g_down=((384, D), BF16),
    g_tokens=((TOK, D), F32),
    r_ff=((4, 2 * TOK, 2 * WIDTH), BF16),
    r_packed=((2 * TOK, LANE_HALF), BF16),
    o_back=((4, 16, MOD_PART), BF16),
    o_cond=((8, D), F32),
)


def vmem(*shape, kind=BF16):
    return pltpu.VMEM(shape, kind)


def backward_scratch():
    return dict(
        held=vmem(8, 4, 2, 144, WIDTH),
        held_big=vmem(3, 4, 2, 192, WIDTH),
        got_y=vmem(14, 4, 2, 48, WIDTH),
        got_y_big=vmem(3, 4, 2, 48, WIDTH),
        got_x=vmem(14, 4, 112, WIDTH),
        got_x_big=vmem(3, 4, 144, WIDTH),
        got_z=vmem(14, 3, 112, WIDTH),
        got_z_big=vmem(3, 3, 144, WIDTH),
        got_f=vmem(14, 112, WIDTH),
        got_f_big=vmem(3, 144, WIDTH),
        w=vmem(2, 4, 2, 144, 2 * WIDTH),
        acc=vmem(TOK, D, kind=F32),
        d_residual=vmem(TOK, D, kind=F32),
        joined=vmem(TOK, 4 * D),
        left=vmem(D, 2 * TOK),
        right=vmem(2, 2 * TOK, 2 * WIDTH),
        d_mod=vmem(2, 8, D, kind=F32),
        back_flat=vmem(8, 4 * MOD_PART, kind=F32),
        back_parts=group_scratch(MOD_PART)[0],
        back_got_c=group_scratch(MOD_PART)[1],
        back_got_y=group_scratch(MOD_PART)[2],
        back_blocks=group_scratch(MOD_PART)[3],
        back_send=group_scratch(MOD_PART)[4],
        back_recv=group_scratch(MOD_PART)[5],
        cond_parts=group_scratch(D)[0],
        cond_got_c=group_scratch(D)[1],
        cond_got_y=group_scratch(D)[2],
        cond_blocks=group_scratch(D)[3],
        cond_send=group_scratch(D)[4],
        cond_recv=group_scratch(D)[5],
        back=vmem(8, MOD_PART, kind=F32),
        back_got_x=vmem(8, MOD_PART, kind=F32),
        back_all=vmem(4, 16, MOD_PART),
        wide_send=pltpu.SemaphoreType.DMA((2,)),
        wide_recv=pltpu.SemaphoreType.DMA((2,)),
        scatter_send=pltpu.SemaphoreType.DMA((5, N_PIECES)),
        scatter_recv=pltpu.SemaphoreType.DMA((5, N_PIECES)),
        store_sems=pltpu.SemaphoreType.DMA((N_PIECES,)),
        load_sems=pltpu.SemaphoreType.DMA((112,)),
        trade_sems=pltpu.SemaphoreType.DMA((2,)),
        pair_send=pltpu.SemaphoreType.DMA((8,)),
        pair_recv=pltpu.SemaphoreType.DMA((8,)),
    )


def backward_kernel(*refs):
    names = BackwardInputs._fields + tuple(BACKWARD_OUTPUTS) + tuple(backward_scratch())
    s = SimpleNamespace(**dict(zip(names, refs, strict=True)))
    spot = place()
    greet(neighbours(*spot))
    reduce = Reduce(s, spot)
    work = Backward(s, spot, reduce)

    def scoped(act, before=None, **shapes):
        def run(*held):
            f = SimpleNamespace(**dict(zip(shapes, held, strict=True)))
            if before is not None:
                before(f)
            act(f)

        pl.run_scoped(run, *shapes.values())

    def first_loads(f):
        work.load(11, s.o_hidden, f.hidden)
        work.load(12, s.o_branch, f.branch)
        work.load_ff(f, 0)

    scoped(
        work.feed_forward,
        first_loads,
        hidden=vmem(8, 192, 2 * TOK),
        branch=vmem(2 * TOK, D),
        w_down=vmem(2, 384, D),
        active=vmem(2, 2, TOK, WIDTH),
        steep=vmem(2, TOK, 2 * WIDTH),
    )
    scoped(work.middle, cot=vmem(TOK, D), attended=vmem(TOK, D))
    reduce.advance()
    scoped(
        work.attention,
        qkv=vmem(3, TOK, D),
        normed=vmem(2, TOK, D),
        soft=vmem(H // ATTN_STEPS, 2, SEQ, SEQ),
        back=vmem(TOK, D),
        cos=vmem(SEQ, D, kind=F32),
        sin=vmem(SEQ, D, kind=F32),
    )
    scoped(work.last, left=vmem(D, 2 * TOK), tokens=vmem(TOK, D), mod_w=vmem(MOD_PART, D))


def backward_pass(f, tokens, cotangent, mod_weight, tables):
    hbm = pl.BlockSpec(memory_space=pl.ANY)
    inside = pl.BlockSpec(memory_space=pltpu.VMEM)
    cosine, sine, spread, widen = tables
    given = BackwardInputs(
        f.packed_all,
        f.gate_all,
        f.up_all,
        f.down_all,
        f.o_branch,
        f.o_lhs,
        f.o_hidden,
        f.o_qkv,
        f.o_normed,
        f.o_scale,
        f.o_soft,
        f.o_attended,
        f.o_residual,
        f.o_active,
        tokens,
        cotangent,
        cosine,
        sine,
        f.o_mod,
        spread,
        widen,
        f.o_gate_b,
        mod_weight,
    )
    out = pl.pallas_call(
        backward_kernel,
        out_shape=[jax.ShapeDtypeStruct(*spec) for spec in BACKWARD_OUTPUTS.values()],
        in_specs=[hbm] * 18 + [inside] * 4 + [hbm],
        out_specs=[hbm] * 8 + [inside],
        scratch_shapes=list(backward_scratch().values()),
        name="backward_pass",
        compiler_params=pltpu.CompilerParams(
            collective_id=1, has_side_effects=True, vmem_limit_bytes=121 << 19
        ),
    )(*given)
    return SimpleNamespace(**dict(zip(BACKWARD_OUTPUTS, out)))


class SettleInputs(NamedTuple):
    packed: object
    gate: object
    up: object
    down: object
    acted: object
    back: object
    cond: object
    total: object


SETTLE_OUTPUTS = dict(
    g_qkv=((144, 3 * D), F32),
    g_proj=((144, D), F32),
    g_gate=((144, 8 * WIDTH), F32),
    g_up=((144, 8 * WIDTH), F32),
    g_down=((384, D), F32),
    g_mod=((144, MOD_PART), F32),
    g_bias=((MOD_PART,), F32),
    g_cond=((2, D), F32),
)


def settle_scratch():
    return dict(
        v_packed=vmem(144, 4 * D),
        v_gate=vmem(144, 8 * WIDTH),
        v_up=vmem(144, 8 * WIDTH),
        v_down=vmem(384, D),
        w_qkv=vmem(144, 3 * D, kind=F32),
        w_proj=vmem(144, D, kind=F32),
        w_gate=vmem(144, 8 * WIDTH, kind=F32),
        w_up=vmem(144, 8 * WIDTH, kind=F32),
        w_down=vmem(384, D, kind=F32),
        w_mod=vmem(144, MOD_PART, kind=F32),
        load_sems=pltpu.SemaphoreType.DMA((4,)),
        store_sems=pltpu.SemaphoreType.DMA((16,)),
    )


def settle_kernel(*refs):
    names = SettleInputs._fields + tuple(SETTLE_OUTPUTS) + tuple(settle_scratch())
    s = SimpleNamespace(**dict(zip(names, refs, strict=True)))
    pairs = ((s.packed, s.v_packed), (s.gate, s.v_gate), (s.up, s.v_up), (s.down, s.v_down))
    loads = [pltpu.make_async_copy(a, b, s.load_sems.at[k]) for k, (a, b) in enumerate(pairs)]
    for load in loads:
        load.start()
    stores = []

    def store(source, target):
        copy = pltpu.make_async_copy(source, target, s.store_sems.at[len(stores)])
        copy.start()
        stores.append(copy)

    def widen(source, target, out, offset=0):
        count = target.shape[0] // 3
        for k in range(3):
            for at in range(k * count, (k + 1) * count, 16):
                rows = pl.ds(at, 16)
                target[rows, :] = source[rows, offset : offset + target.shape[1]].astype(F32)
            rows = pl.ds(k * count, count)
            store(target.at[rows], out.at[rows])

    loads[0].wait()
    widen(s.v_packed, s.w_qkv, s.g_qkv)
    widen(s.v_packed, s.w_proj, s.g_proj, 3 * D)
    for k, (source, target, out) in enumerate(
        ((s.v_gate, s.w_gate, s.g_gate), (s.v_up, s.w_up, s.g_up), (s.v_down, s.w_down, s.g_down))
    ):
        loads[k + 1].wait()
        widen(source, target, out)
    s.w_mod[...] = mm_tn(s.acted[...], s.back[...])
    store(s.w_mod, s.g_mod)
    s.g_bias[...] = jnp.sum(s.back[...].astype(F32), axis=0)
    total = s.total[...]
    sigma = 1.0 / (1.0 + jnp.exp(-total))
    s.g_cond[...] = s.cond[0:2, :] * sigma * (1.0 + total * (1.0 - sigma))
    for copy in stores:
        copy.wait()


def settle(*given):
    hbm = pl.BlockSpec(memory_space=pl.ANY)
    inside = pl.BlockSpec(memory_space=pltpu.VMEM)
    out = pl.pallas_call(
        settle_kernel,
        out_shape=[jax.ShapeDtypeStruct(*spec) for spec in SETTLE_OUTPUTS.values()],
        in_specs=[hbm] * 4 + [inside] * 4,
        out_specs=[hbm] * 6 + [inside] * 2,
        scratch_shapes=list(settle_scratch().values()),
        name="settle",
        compiler_params=pltpu.CompilerParams(vmem_limit_bytes=60 << 20),
    )(*SettleInputs(*given))
    return SimpleNamespace(**dict(zip(SETTLE_OUTPUTS, out)))


def body_general(
    tokens,
    condition,
    timestep,
    qkv_weight,
    out_weight,
    gate_weight,
    up_weight,
    down_weight,
    mod_weight,
    mod_bias,
    cotangent,
):
    gathered = (
        lax.all_gather(qkv_weight, "dp", axis=0, tiled=True),
        lax.all_gather(out_weight, "dp", axis=0, tiled=True),
        lax.all_gather(gate_weight, "dp", axis=0, tiled=True),
        lax.all_gather(up_weight, "dp", axis=0, tiled=True),
        lax.all_gather(down_weight, "dp", axis=0, tiled=True),
    )
    cond_total = condition.astype(jnp.float32) + embed_steps(timestep)
    acted_cond = jax.nn.silu(cond_total).astype(jnp.bfloat16)
    acted_group = lax.all_gather(acted_cond, "mod", axis=0, tiled=True)
    mod_part = (
        jnp.dot(acted_group, mod_weight, preferred_element_type=jnp.float32)
        + mod_bias.astype(jnp.float32)
    ).astype(jnp.bfloat16)
    modulation = lax.all_to_all(mod_part, "mod", split_axis=0, concat_axis=1, tiled=True).astype(
        jnp.float32
    )
    tables = rope_tables()
    per_micro = tokens.shape[0] // MICRO
    outputs = []
    token_grads = []
    mod_grads = []
    kept = []
    for micro_step in range(MICRO):
        start_row = micro_step * per_micro
        output, d_tokens, d_modulation, factors = layer_pass(
            tokens[start_row : start_row + per_micro],
            modulation[start_row : start_row + per_micro],
            cotangent[start_row : start_row + per_micro],
            gathered,
            tables,
        )
        outputs.append(output)
        token_grads.append(d_tokens)
        mod_grads.append(d_modulation)
        kept.append(factors)
    joined = [jnp.concatenate([factors[number] for factors in kept], axis=0) for number in range(9)]
    (
        entry_first,
        d_projected,
        combined,
        d_attended,
        entry_second,
        d_gate_proj,
        d_up_proj,
        hidden,
        d_branch,
    ) = joined
    grad_qkv = jnp.einsum(
        "bsd,bse->de", entry_first, d_projected, preferred_element_type=jnp.float32
    )
    grad_proj = jnp.einsum("bsd,bse->de", combined, d_attended, preferred_element_type=jnp.float32)
    grad_gate = jnp.einsum(
        "bsd,bsf->df", entry_second, d_gate_proj, preferred_element_type=jnp.float32
    )
    grad_up = jnp.einsum("bsd,bsf->df", entry_second, d_up_proj, preferred_element_type=jnp.float32)
    grad_down = jnp.einsum("bsf,bsd->fd", hidden, d_branch, preferred_element_type=jnp.float32)
    totals = (grad_qkv, grad_proj, grad_gate, grad_up, grad_down)
    output_tokens = jnp.concatenate(outputs, axis=0)
    grad_tokens = jnp.concatenate(token_grads, axis=0)
    mod_grad = jnp.concatenate(mod_grads, axis=0)
    mod_back = lax.all_to_all(mod_grad, "mod", split_axis=1, concat_axis=0, tiled=True)
    grad_mod_part = jnp.einsum(
        "id,ic->dc", acted_group, mod_back, preferred_element_type=jnp.float32
    )
    bias_part = jnp.sum(mod_back.astype(jnp.float32), axis=0)
    acted_grad_part = jnp.einsum(
        "ic,dc->id", mod_back, mod_weight, preferred_element_type=jnp.float32
    )
    acted_grad = lax.psum_scatter(
        acted_grad_part.astype(jnp.bfloat16), "mod", scatter_dimension=0, tiled=True
    ).astype(jnp.float32)
    sigma_cond = jax.nn.sigmoid(cond_total)
    grad_condition = acted_grad * sigma_cond * (1.0 + cond_total * (1.0 - sigma_cond))
    grad_bias = lax.psum(bias_part, "dp")
    count = lax.axis_size("dp")
    arrays = totals + (grad_mod_part,)
    shapes = [array.shape for array in arrays]
    flat = lax.psum_scatter(pack_rows(arrays, count), "dp", scatter_dimension=0, tiled=True)
    summed = unpack_rows(flat, shapes, count)
    finished = (
        lax.psum(summed[0].astype(jnp.bfloat16), "mod").astype(jnp.float32),
        lax.psum(summed[1].astype(jnp.bfloat16), "mod").astype(jnp.float32),
        lax.psum(summed[2].astype(jnp.bfloat16), "mod").astype(jnp.float32),
        lax.psum(summed[3].astype(jnp.bfloat16), "mod").astype(jnp.float32),
        lax.psum(summed[4].astype(jnp.bfloat16), "mod").astype(jnp.float32),
    )
    grad_mod = summed[5]
    return (
        output_tokens,
        grad_tokens,
        grad_condition,
        finished[0],
        finished[1],
        finished[2],
        finished[3],
        finished[4],
        grad_mod,
        grad_bias,
    )


def body_fast(
    tokens,
    condition,
    timestep,
    qkv_weight,
    out_weight,
    gate_weight,
    up_weight,
    down_weight,
    mod_weight,
    mod_bias,
    cotangent,
):
    packed = jnp.concatenate([qkv_weight, out_weight], axis=1)
    cond_total = condition.astype(jnp.float32) + embed_steps(timestep)
    acted_cond = jax.nn.silu(cond_total).astype(jnp.bfloat16)
    acted_rows = acted_cond.astype(F32)
    acted_slim = jnp.pad(acted_rows.reshape(-1, 128), ((0, 6), (0, 0)))
    flat_tokens, flat_cotangent = tokens.reshape(TOK, D), cotangent.reshape(TOK, D)
    tables = head_tables()
    f = forward_pass(
        packed,
        gate_weight,
        up_weight,
        down_weight,
        flat_tokens,
        flat_cotangent,
        jnp.pad(acted_rows, ((0, 6), (0, 0))),
        mod_bias,
        mod_weight.T,
        acted_slim,
        *tables,
    )
    b = backward_pass(f, flat_tokens, flat_cotangent, mod_weight.T, tables)
    acted_all = f.acted_all.reshape(32, -1)[:, : 2 * D].reshape(64, D).astype(BF16)
    back_all = b.o_back.reshape(64, -1)
    rows = D // 8
    acted_part = lax.dynamic_slice_in_dim(acted_all, lax.axis_index("dp") * rows, rows, 1)
    g = settle(b.g_packed, b.g_gate, b.g_up, b.g_down, acted_part, back_all, b.o_cond, cond_total)
    return (
        f.o_result.reshape(tokens.shape),
        b.g_tokens.reshape(tokens.shape),
        g.g_cond,
        g.g_qkv,
        g.g_proj,
        g.g_gate,
        g.g_up,
        g.g_down,
        g.g_mod,
        g.g_bias,
    )


def pick_body(mesh):
    if dict(mesh.shape) == {"dp": 8, "mod": 4}:
        return body_fast
    return body_general


def solution(mesh):
    in_specs = (
        P(("dp", "mod"), None, None),
        P(("dp", "mod"), None),
        P(("dp", "mod")),
        P("dp", None),
        P("dp", None),
        P("dp", None),
        P("dp", None),
        P("dp", None),
        P(None, "mod"),
        P("mod"),
        P(("dp", "mod"), None, None),
    )
    out_specs = (
        P(("dp", "mod"), None, None),
        P(("dp", "mod"), None, None),
        P(("dp", "mod"), None),
        P("dp", None),
        P("dp", None),
        P("dp", None),
        P("dp", None),
        P("dp", None),
        P("dp", "mod"),
        P("mod"),
    )
    return jax.shard_map(pick_body(mesh), mesh=mesh, in_specs=in_specs, out_specs=out_specs, check_vma=False)
```

```python
import math
from types import SimpleNamespace
from typing import NamedTuple

import jax
import jax.numpy as jnp
from jax import lax
import numpy as np
from jax.experimental import pallas as pl
from jax.experimental.pallas import tpu as pltpu
from jax.sharding import PartitionSpec as P

D = 1152
H = 16
HD = 72
GRID = 16
SEQ = 256
MICRO = 2


EPSILON = 1e-06


def norm_rows(field):
    scale_inv = lax.rsqrt(jnp.mean(field * field, axis=-1, keepdims=True) + EPSILON)
    return (field * scale_inv, scale_inv)


def norm_back(normed, scale_inv, gradient):
    return scale_inv * (gradient - normed * jnp.mean(gradient * normed, axis=-1, keepdims=True))


def embed_steps(timestep):
    half_width = D // 2
    frequency = jnp.exp(-math.log(10000.0) * jnp.arange(half_width, dtype=jnp.float32) / half_width)
    angles = timestep.astype(jnp.float32)[:, None] * frequency[None, :]
    return jnp.concatenate([jnp.cos(angles), jnp.sin(angles)], axis=1)


def rope_tables():
    quarter = HD // 4
    frequency = jnp.exp(-math.log(10000.0) * jnp.arange(quarter, dtype=jnp.float32) / quarter)
    position = jnp.arange(SEQ)
    row_index = (position // GRID).astype(jnp.float32)
    col_index = (position % GRID).astype(jnp.float32)
    angles = jnp.stack(
        [row_index[:, None] * frequency[None, :], col_index[:, None] * frequency[None, :]], axis=1
    )
    return (jnp.cos(angles), jnp.sin(angles))


def rotate(field, cosine_table, sine_table):
    leading = field.shape[:-1]
    quarters = field.reshape(leading + (2, 2, HD // 4))
    first_half = quarters[..., 0, :]
    second_half = quarters[..., 1, :]
    cosine_rows = cosine_table[:, None]
    sine_rows = sine_table[:, None]
    turned_first = first_half * cosine_rows - second_half * sine_rows
    turned_second = first_half * sine_rows + second_half * cosine_rows
    return jnp.stack([turned_first, turned_second], axis=-2).reshape(field.shape)


def pack_rows(arrays, count):
    return jnp.concatenate([array.reshape(count, -1) for array in arrays], axis=1).reshape(-1)


def unpack_rows(flat, shapes, count):
    pieces = []
    offset = 0
    for rows_all, columns in shapes:
        rows = rows_all // count
        pieces.append(flat[offset : offset + rows * columns].reshape(rows, columns))
        offset = offset + rows * columns
    return pieces


def layer_pass(block_in, mod_rows, cotangent, weights, tables):
    qkv_full, proj_full, gate_full, up_full, down_full = weights
    cosine_table, sine_table = tables
    images = block_in.shape[0]
    shift_first, scale_first, gate_first, shift_second, scale_second, gate_second = [
        mod_rows[:, None, number * D : (number + 1) * D] for number in range(6)
    ]
    heads_shape = (images, SEQ, H, HD)
    factor = 1.0 / math.sqrt(HD)
    inputs = block_in.astype(jnp.float32)
    normed_first, inv_first = norm_rows(inputs)
    entry_first = (normed_first * (1.0 + scale_first) + shift_first).astype(jnp.bfloat16)
    projected = jnp.einsum("bsd,de->bse", entry_first, qkv_full, preferred_element_type=jnp.float32)
    q_normed, q_inv = norm_rows(projected[..., :D].reshape(heads_shape))
    k_normed, k_inv = norm_rows(projected[..., D : 2 * D].reshape(heads_shape))
    queries = rotate(q_normed, cosine_table, sine_table).astype(jnp.bfloat16)
    keys_rot = rotate(k_normed, cosine_table, sine_table).astype(jnp.bfloat16)
    values = projected[..., 2 * D :].reshape(heads_shape).astype(jnp.bfloat16)
    scores = (
        jnp.einsum("bqhd,bkhd->bhqk", queries, keys_rot, preferred_element_type=jnp.float32)
        * factor
    )
    highest = jnp.max(scores, axis=-1, keepdims=True)
    log_total = highest + jnp.log(jnp.sum(jnp.exp(scores - highest), axis=-1, keepdims=True))
    weights_soft = jnp.exp(scores - log_total).astype(jnp.bfloat16)
    combined = (
        jnp.einsum("bhqk,bkhd->bqhd", weights_soft, values, preferred_element_type=jnp.float32)
        .reshape(images, SEQ, D)
        .astype(jnp.bfloat16)
    )
    attended = jnp.einsum("bsd,de->bse", combined, proj_full, preferred_element_type=jnp.float32)
    residual = inputs + gate_first * attended
    normed_second, inv_second = norm_rows(residual)
    entry_second = (normed_second * (1.0 + scale_second) + shift_second).astype(jnp.bfloat16)
    gate_proj = jnp.einsum(
        "bsd,df->bsf", entry_second, gate_full, preferred_element_type=jnp.float32
    )
    up_proj = jnp.einsum("bsd,df->bsf", entry_second, up_full, preferred_element_type=jnp.float32)
    sigma_gate = jax.nn.sigmoid(gate_proj)
    activated = gate_proj * sigma_gate
    hidden = (activated * up_proj).astype(jnp.bfloat16)
    branch = jnp.einsum("bsf,fd->bsd", hidden, down_full, preferred_element_type=jnp.float32)
    output = (residual + gate_second * branch).astype(jnp.bfloat16)
    grad_out = cotangent.astype(jnp.float32)
    d_gate_second = jnp.sum(grad_out * branch, axis=1)
    d_branch = (gate_second * grad_out).astype(jnp.bfloat16)
    d_hidden = jnp.einsum("bsd,fd->bsf", d_branch, down_full, preferred_element_type=jnp.float32)
    d_gate_proj = (d_hidden * up_proj * sigma_gate * (1.0 + gate_proj * (1.0 - sigma_gate))).astype(
        jnp.bfloat16
    )
    d_up_proj = (d_hidden * activated).astype(jnp.bfloat16)
    d_entry_second = jnp.einsum(
        "bsf,df->bsd", d_gate_proj, gate_full, preferred_element_type=jnp.float32
    )
    d_entry_second = d_entry_second + jnp.einsum(
        "bsf,df->bsd", d_up_proj, up_full, preferred_element_type=jnp.float32
    )
    d_shift_second = jnp.sum(d_entry_second, axis=1)
    d_scale_second = jnp.sum(d_entry_second * normed_second, axis=1)
    d_residual = grad_out + norm_back(
        normed_second, inv_second, d_entry_second * (1.0 + scale_second)
    )
    d_gate_first = jnp.sum(d_residual * attended, axis=1)
    d_attended = (gate_first * d_residual).astype(jnp.bfloat16)
    d_combined = (
        jnp.einsum("bse,de->bsd", d_attended, proj_full, preferred_element_type=jnp.float32)
        .astype(jnp.bfloat16)
        .reshape(heads_shape)
    )
    scores_again = (
        jnp.einsum("bqhd,bkhd->bhqk", queries, keys_rot, preferred_element_type=jnp.float32)
        * factor
    )
    recomputed = jnp.exp(scores_again - log_total)
    d_weights = jnp.einsum(
        "bqhd,bkhd->bhqk", d_combined, values, preferred_element_type=jnp.float32
    )
    d_scores = (
        recomputed * (d_weights - jnp.sum(recomputed * d_weights, axis=-1, keepdims=True))
    ).astype(jnp.bfloat16)
    d_values = jnp.einsum(
        "bhqk,bqhd->bkhd", weights_soft, d_combined, preferred_element_type=jnp.float32
    ).astype(jnp.bfloat16)
    d_queries = (
        (
            jnp.einsum("bhqk,bkhd->bqhd", d_scores, keys_rot, preferred_element_type=jnp.float32)
            * factor
        )
        .astype(jnp.bfloat16)
        .astype(jnp.float32)
    )
    d_keys = (
        (
            jnp.einsum("bhqk,bqhd->bkhd", d_scores, queries, preferred_element_type=jnp.float32)
            * factor
        )
        .astype(jnp.bfloat16)
        .astype(jnp.float32)
    )
    d_q_raw = norm_back(q_normed, q_inv, rotate(d_queries, cosine_table, -sine_table))
    d_k_raw = norm_back(k_normed, k_inv, rotate(d_keys, cosine_table, -sine_table))
    flat_shape = (images, SEQ, D)
    d_projected = jnp.concatenate(
        [
            d_q_raw.reshape(flat_shape),
            d_k_raw.reshape(flat_shape),
            d_values.astype(jnp.float32).reshape(flat_shape),
        ],
        axis=-1,
    ).astype(jnp.bfloat16)
    d_entry_first = jnp.einsum(
        "bse,de->bsd", d_projected, qkv_full, preferred_element_type=jnp.float32
    )
    d_shift_first = jnp.sum(d_entry_first, axis=1)
    d_scale_first = jnp.sum(d_entry_first * normed_first, axis=1)
    d_tokens = d_residual + norm_back(normed_first, inv_first, d_entry_first * (1.0 + scale_first))
    d_modulation = jnp.concatenate(
        [d_shift_first, d_scale_first, d_gate_first, d_shift_second, d_scale_second, d_gate_second],
        axis=1,
    ).astype(jnp.bfloat16)
    factors = (
        entry_first,
        d_projected,
        combined,
        d_attended,
        entry_second,
        d_gate_proj,
        d_up_proj,
        hidden,
        d_branch,
    )
    return (output, d_tokens, d_modulation, factors)


MESH = pl.DeviceIdType.MESH
WIDTH = 384
LANE_HALF = 2304
FF_HALF = 1536
BF16 = jnp.bfloat16
F32 = jnp.float32


def place():
    dp = lax.axis_index("dp")
    mod = lax.axis_index("mod")
    return dp // 2, dp % 2, mod // 2, mod % 2


def device(z, x, y, c):
    return (z * 2 + x, y * 2 + c)


def greet(peers):
    barrier = pltpu.get_barrier_semaphore()
    for peer in peers:
        pl.semaphore_signal(barrier, inc=1, device_id=peer, device_id_type=MESH)
    pl.semaphore_wait(barrier, len(peers))


def neighbours(z, x, y, c):
    around = [device((z + step) % 4, x, y, c) for step in (1, 2, 3)]
    return around + [device(z, 1 - x, y, c), device(z, x, 1 - y, c), device(z, x, y, 1 - c)]


def send(source, target, send_sem, recv_sem, peer):
    pltpu.make_async_remote_copy(
        src_ref=source,
        dst_ref=target,
        send_sem=send_sem,
        recv_sem=recv_sem,
        device_id=peer,
        device_id_type=MESH,
    ).start()


def drain(window, sem):
    pltpu.make_async_copy(window, window, sem).wait()


class Piece:
    def __init__(self, source, target, row, rows, column, edge):
        self.source, self.target = source, target
        self.row, self.rows, self.column, self.edge = row, rows, column, edge


def gather_pieces(refs, c, edge_of):
    packed, gate, up, down, packed_all, gate_all, up_all, down_all = refs
    pieces = []
    for j in range(6):
        pieces.append(Piece(packed, packed_all, 0, 144, c * LANE_HALF + j * WIDTH, edge_of(144, j)))
    for j in range(4):
        pieces.append(Piece(gate, gate_all, 0, 144, c * FF_HALF + j * WIDTH, edge_of(144, j)))
        pieces.append(Piece(up, up_all, 0, 144, c * FF_HALF + j * WIDTH, edge_of(144, j)))
    for j in range(3):
        pieces.append(Piece(down, down_all, c * 192, 192, j * WIDTH, edge_of(192, j)))
    return pieces


class Gather:
    def __init__(self, refs, sems, spot, stages):
        self.z, self.x, self.y, self.c = spot
        self.stages = stages
        self.pieces = gather_pieces([stages[0]] + list(refs[1:]), self.c, lambda rows, j: 64 if rows == 144 and j % 3 == 2 else rows // 3)
        self.send_sems, self.recv_sems, self.own_sems = sems
        self.refs = refs

    def columns(self, piece):
        return pl.ds(pl.multiple_of(piece.column, 128), WIDTH)

    def part(self, piece):
        keep = piece.rows - piece.edge
        return pl.ds(pl.multiple_of(piece.row + self.y * piece.edge, 16), keep), keep

    def mine(self, piece):
        return pl.ds(pl.multiple_of(piece.row + self.y * (piece.rows - piece.edge), 16), piece.edge)

    def own_copies(self):
        qkv, out = self.refs[0]
        width = qkv.shape[1]
        for source, columns in ((qkv, pl.ds(0, width)), (out, pl.ds(width, out.shape[1]))):
            target = self.stages[0].at[:, columns]
            pltpu.make_async_copy(source, target, self.own_sems.at[0]).start()
        for k in range(1, 4):
            pltpu.make_async_copy(self.refs[k], self.stages[k], self.own_sems.at[k]).start()
        drain(self.stages[0], self.own_sems.at[0])

    def own_stores(self):
        for k in range(4):
            if k > 0:
                drain(self.stages[k], self.own_sems.at[k])
            pltpu.make_async_copy(
                self.stages[k], self.refs[4 + k].at[self.z, self.x], self.own_sems.at[k]
            ).start()

    def own_done(self):
        for k in range(4):
            drain(self.stages[k], self.own_sems.at[k])

    def start_z(self, t):
        p = self.pieces[t]
        rows, _ = self.part(p)
        here = p.source.at[rows, self.columns(p)]
        there = p.target.at[self.z, self.x, rows, self.columns(p)]
        for step in (1, 3, 2):
            peer = device((self.z + step) % 4, self.x, self.y, self.c)
            send(here, there, self.send_sems.at[0, t], self.recv_sems.at[0, t], peer)
        peer = device(self.z, 1 - self.x, self.y, self.c)
        send(here, there, self.send_sems.at[1, t], self.recv_sems.at[1, t], peer)

    def start_x(self, t):
        p = self.pieces[t]
        rows, keep = self.part(p)
        columns = self.columns(p)
        drain(p.target.at[pl.ds(0, 3), 0, pl.ds(0, keep), pl.ds(0, WIDTH)], self.recv_sems.at[0, t])
        x_peer = device(self.z, 1 - self.x, self.y, self.c)
        y_peer = device(self.z, self.x, 1 - self.y, self.c)
        for step in (1, 3, 2):
            other = (self.z + step) % 4
            block = p.target.at[other, self.x, rows, columns]
            send(block, block, self.send_sems.at[1, t], self.recv_sems.at[1, t], x_peer)
        for step in (1, 3, 2):
            other = (self.z + step) % 4
            block = p.target.at[other, self.x, self.mine(p), columns]
            send(block, block, self.send_sems.at[2, t], self.recv_sems.at[2, t], y_peer)

    def start_y(self, t):
        p = self.pieces[t]
        _, keep = self.part(p)
        columns = self.columns(p)
        drain(p.target.at[:, 0, pl.ds(0, keep), pl.ds(0, WIDTH)], self.recv_sems.at[1, t])
        y_peer = device(self.z, self.x, 1 - self.y, self.c)
        block = p.target.at[:, 1 - self.x, self.mine(p), columns]
        send(block, block, self.send_sems.at[2, t], self.recv_sems.at[2, t], y_peer)

    def start_c(self, t):
        p = self.pieces[t]
        columns = self.columns(p)
        half = pl.ds(pl.multiple_of(p.row, 16), p.rows)
        self.drain_seven(p.edge, self.recv_sems.at[2, t])
        peer = device(self.z, self.x, self.y, 1 - self.c)
        block = p.target.at[:, 1 - self.x, half, columns]
        send(block, block, self.send_sems.at[3, t], self.recv_sems.at[3, t], peer)
        for step in (1, 2, 3):
            block = p.target.at[(self.z + step) % 4, self.x, half, columns]
            send(block, block, self.send_sems.at[3, t], self.recv_sems.at[3, t], peer)

    def arrived(self, t):
        self.drain_seven(self.pieces[t].rows, self.recv_sems.at[3, t])

    def drain_seven(self, rows, sem):
        high = 96 if rows > 144 else rows
        drain(self.refs[4].at[pl.ds(0, rows // high), 0, pl.ds(0, high), pl.ds(0, 7 * WIDTH)], sem)

    def sent_z(self, t):
        p = self.pieces[t]
        _, keep = self.part(p)
        drain(p.target.at[pl.ds(0, 3), 0, pl.ds(0, keep), pl.ds(0, WIDTH)], self.send_sems.at[0, t])

    def sent_rest(self, t):
        p = self.pieces[t]
        _, keep = self.part(p)
        drain(p.target.at[:, 0, pl.ds(0, keep), pl.ds(0, WIDTH)], self.send_sems.at[1, t])
        for stage, rows in ((2, p.edge), (3, p.rows)):
            self.drain_seven(rows, self.send_sems.at[stage, t])


N_PIECES = 17


class Group:
    def __init__(self, spot, parts, got_c, got_y, blocks, send_sems, recv_sems):
        _, _, self.y, self.c = spot
        z, x, y, c = spot
        self.sibling, self.across = device(z, x, y, 1 - c), device(z, x, 1 - y, c)
        self.parts, self.got_c, self.got_y, self.blocks = parts, got_c, got_y, blocks
        self.send_sems, self.recv_sems = send_sems, recv_sems

    def sems(self, k):
        return self.send_sems.at[k], self.recv_sems.at[k]

    def start(self):
        for y in range(2):
            source = self.parts.at[2 * y + 1 - self.c]
            send(source, self.got_c.at[y], *self.sems(y), self.sibling)

    def across_y(self):
        for y in range(2):
            drain(self.got_c.at[y], self.recv_sems.at[y])
        own = self.parts.at[2 * (1 - self.y) + self.c]
        send(own, self.got_y.at[self.c], *self.sems(2), self.across)
        send(self.got_c.at[1 - self.y], self.got_y.at[1 - self.c], *self.sems(3), self.across)

    def finish(self):
        for k in (2, 3):
            drain(self.got_y.at[k - 2], self.recv_sems.at[k])
        y, c, blocks = self.y, self.c, self.blocks
        blocks[2 * y + c] = self.parts[2 * y + c]
        blocks[2 * y + 1 - c] = self.got_c[y]
        for k in range(2):
            blocks[2 * (1 - y) + k] = self.got_y[k]
        for k in range(4):
            drain(self.got_y.at[k % 2], self.send_sems.at[k])


def group_scratch(columns):
    return [
        pltpu.VMEM((4, 8, columns), F32),
        pltpu.VMEM((2, 8, columns), F32),
        pltpu.VMEM((2, 8, columns), F32),
        pltpu.VMEM((4, 8, columns), F32),
        pltpu.SemaphoreType.DMA((4,)),
        pltpu.SemaphoreType.DMA((4,)),
    ]


MOD_PART = 1728
SLIM = (24, 128)


class Acted:
    def __init__(self, s, spot):
        self.s = s
        self.z, self.x, self.y, self.c = spot

    def hop(self, k, where, peers):
        block = self.s.acted_all.at[where]
        for peer in peers:
            send(block, block, self.s.acted_send.at[k], self.s.acted_recv.at[k], peer)

    def step(self, k):
        z, x, y, c = self.z, self.x, self.y, self.c
        s = self.s
        if k == 0:
            pltpu.make_async_copy(s.acted_slim, s.acted_all.at[z, x, y, c], s.acted_own).start()
            drain(s.acted_slim, s.acted_own)
            self.hop(0, (z, x, y, c), [device(z, x, y, 1 - c)])
        elif k == 1:
            drain(s.acted_slim, s.acted_recv.at[0])
            self.hop(1, (z, x, y), [device(z, x, 1 - y, c)])
        elif k == 2:
            drain(s.acted_all.at[0, 0, 0], s.acted_recv.at[1])
            self.hop(2, (z, x), [device(z, 1 - x, y, c)])
        elif k == 3:
            drain(s.acted_all.at[0, 0], s.acted_recv.at[2])
            self.hop(3, (z,), [device((z + step) % 4, x, y, c) for step in (1, 3, 2)])
        else:
            drain(s.acted_all.at[pl.ds(0, 3)], s.acted_recv.at[3])
            drain(s.acted_slim, s.acted_send.at[0])
            drain(s.acted_all.at[0, 0, 0], s.acted_send.at[1])
            drain(s.acted_all.at[0, 0], s.acted_send.at[2])
            drain(s.acted_all.at[pl.ds(0, 3)], s.acted_send.at[3])


TOK = 512
TILE = 128
HEAD_TILE = 256
ATTN_STEPS = 4
STEP_BUDGET = 3.0
GATHER_AHEAD = 2


def mm(left, right):
    return lax.dot_general(left, right, (((1,), (0,)), ((), ())), preferred_element_type=F32)


def mm_nt(left, right):
    return lax.dot_general(left, right, (((1,), (1,)), ((), ())), preferred_element_type=F32)


def mm_tn(left, right):
    return lax.dot_general(left, right, (((0,), (0,)), ((), ())), preferred_element_type=F32)


def split(value):
    high = value.astype(BF16)
    return high, (value - high.astype(F32)).astype(BF16)


def mm_split(value, right):
    high, low = split(value)
    return mm(high, right) + mm(low, right)


def partner(value, first):
    width = value.shape[1]
    return jnp.where(first, pltpu.roll(value, width - 18, 1), pltpu.roll(value, 18, 1))


def first_lanes(rows):
    return lax.broadcasted_iota(jnp.int32, (rows, D), 1) % 36 < 18


def rows_of(block, count):
    return pl.ds(pl.multiple_of(block * count, count), count)


def head_window(head):
    base = min(head * HD // 128 * 128, D - 256)
    offset = head * HD - base
    lane = lax.broadcasted_iota(jnp.int32, (SEQ, 256), 1)
    return base, (lane >= offset) & (lane < offset + HD)


def flat(ref_value):
    return ref_value.reshape(-1, ref_value.shape[-1])


class Saves:
    def __init__(self, sems):
        self.sems, self.count, self.open = sems, 0, []

    def local(self, source, target):
        copy = pltpu.make_async_copy(source, target, self.sems.at[self.count])
        self.count += 1
        copy.start()
        self.open.append(copy)
        return copy

    def done(self, copy):
        copy.wait()
        self.open = [other for other in self.open if other is not copy]

    def finish(self):
        for copy in self.open:
            copy.wait()


class Forward:
    def __init__(self, s, spot, gather):
        self.s, self.gather = s, gather
        self.z, self.x, self.y, self.c = spot
        self.saves = Saves(s.save_sems)
        self.pending = {}
        self.remote = []
        self.slots = {}


    def to_sibling(self, source, target):
        k = len(self.remote)
        peer = device(self.z, self.x, self.y, 1 - self.c)
        copy = pltpu.make_async_remote_copy(
            src_ref=source,
            dst_ref=target,
            send_sem=self.s.pair_send.at[k],
            recv_sem=self.s.pair_recv.at[k],
            device_id=peer,
            device_id_type=MESH,
        )
        copy.start()
        self.remote.append(copy)


    def load(self, key, part, source, target):
        if (key, part) not in self.pending:
            copy = pltpu.make_async_copy(source, target, self.s.load_sems.at[len(self.pending)])
            copy.start()
            self.pending[key, part] = copy

    def window(self, ref, column):
        return ref.at[:, :, :, pl.ds(column, WIDTH)]

    def load_qv(self, j):
        packed, target = self.gather.refs[4], self.s.w.at[j % 2, 0]
        self.load(j, 0, self.window(packed, j * WIDTH), self.window(target, 0))
        self.load(j, 1, self.window(packed, LANE_HALF + j * WIDTH), self.window(target, WIDTH))

    def load_ko(self, j):
        packed = self.gather.refs[4]
        self.load(j, 0, self.window(packed, j * WIDTH), self.window(self.s.w.at[j % 2, 0], 0))
        target = self.window(self.s.w_out, (j - 3) * WIDTH)
        self.load(j, 1, self.window(packed, LANE_HALF + j * WIDTH), target)

    def load_ff(self, j):
        for part in range(4):
            which, half = part // 2, part % 2
            target = self.window(self.s.w.at[j % 2, which], half * WIDTH)
            self.load(6 + j, part, self.window(self.gather.refs[5 + which], (j + 4 * half) * WIDTH), target)

    def load_down(self, j):
        self.load(14 + j, 0, self.window(self.gather.refs[7], j * WIDTH), self.s.w_down.at[j % 2])

    def loaded(self, load, j, key):
        load(j)
        for part in range(4):
            if (key, part) in self.pending:
                self.pending[key, part].wait()


    def modulate(self, k):
        s, y, c = self.s, self.y, self.c
        spot = (self.z, self.x, y, c)
        own = s.acted_group.at[2 * y + c]
        pair = s.acted_group.at[pl.ds(2 * y, 2)]
        load = pltpu.make_async_copy(s.mod_weight, s.mod_w, s.acted_own)
        group = Group(
            spot, s.mod_parts, s.mod_got_c, s.mod_got_y, s.mod_blocks, s.mod_send, s.mod_recv
        )
        if k == 0:
            load.start()
            s.acted_group[2 * y + c] = s.acted[...]
            send(own, own, *self.first(0), device(self.z, self.x, y, 1 - c))
        elif k == 1:
            drain(own, s.first_recv.at[0])
            send(pair, pair, *self.first(1), device(self.z, self.x, 1 - y, c))
        elif k == 2:
            load.wait()
            drain(pair, s.first_recv.at[1])
            total = mm_nt(s.acted_group[...].reshape(32, D).astype(BF16), s.mod_w[...]) + s.bias[...].astype(F32)[None, :]
            s.mod_parts[...] = total.astype(BF16).astype(F32).reshape(4, 8, MOD_PART)
            group.start()
        elif k == 3:
            group.across_y()
        else:
            group.finish()
            for m in range(4):
                s.mod_flat[:, m * MOD_PART : (m + 1) * MOD_PART] = s.mod_blocks[m]
            for image in range(2):
                for m in range(6):
                    row = s.mod_flat[image : image + 1, m * D : (m + 1) * D]
                    s.o_mod[image, m : m + 1, :] = row
            drain(own, s.first_send.at[0])
            drain(pair, s.first_send.at[1])

    def first(self, k):
        return self.s.first_send.at[k], self.s.first_recv.at[k]

    def enter(self):
        s = self.s

        @pl.loop(0, TOK // TILE)
        def _(i):
            rows = rows_of(i, TILE)
            image = i // (SEQ // TILE)
            mod = s.o_mod
            normed, _ = norm_rows(s.tokens[rows, :].astype(F32))
            entry = normed * (1.0 + mod[image, 1:2, :]) + mod[image, 0:1, :]
            s.entry_a[rows, :] = entry.astype(BF16)
            branch = mod[image, 5:6, :] * s.cot[rows, :].astype(F32)
            s.d_branch[rows, :] = branch.astype(BF16)

        self.saves.local(s.d_branch, s.o_branch.at[pl.ds(0, TOK)])
        self.to_sibling(s.d_branch, s.o_branch.at[pl.ds(TOK, TOK)])
        self.turn(s.entry_a, s.t_a)
        self.share(s.t_a, s.o_lhs.at[0])

    def turn(self, source, target):
        @pl.loop(0, source.shape[1] // 128)
        def _(i):
            columns = rows_of(i, 128)
            target[columns, :] = source[:, columns].T

    def share(self, source, target):
        self.shared = [self.saves.local(source, target.at[:, pl.ds(0, TOK)])]
        self.to_sibling(source, target.at[:, pl.ds(TOK, TOK)])

    def qv(self, j):
        s = self.s
        self.loaded(self.load_qv, j, j)
        columns = pl.ds(j * WIDTH, WIDTH)
        both = mm(s.entry_a[...], flat(s.w[j % 2, 0]))
        s.proj[:, columns] = both[:, :WIDTH]
        s.v[:, columns] = both[:, WIDTH:].astype(BF16)
        if j == 2:
            self.saves.local(s.v, s.o_qkv.at[2])

    def ko(self, j):
        s = self.s
        self.loaded(self.load_ko, j, j)
        columns = pl.ds((j - 3) * WIDTH, WIDTH)
        s.proj[:, columns] = mm(s.entry_a[...], flat(s.w[j % 2, 0, :, :, :, 0:WIDTH]))

    def head_norm(self, which):
        s = self.s
        target, normed = (s.q, s.q_normed) if which == 0 else (s.k, s.k_normed)
        scale = s.scale_q if which == 0 else s.scale_k

        @pl.loop(0, TOK // HEAD_TILE)
        def _(i):
            rows = rows_of(i, HEAD_TILE)
            spots = rows_of(i % (SEQ // HEAD_TILE), HEAD_TILE)
            field = s.proj[rows, :]
            inverse = lax.rsqrt(mm_split(field * field, s.spread[...]) * (1.0 / HD) + EPSILON)
            scale[rows, :] = inverse
            field = field * mm_split(inverse, s.widen[...])
            normed[rows, :] = field.astype(BF16)
            turned = field * s.cos[spots, :] + partner(field, first_lanes(HEAD_TILE)) * s.sin[spots, :]
            target[rows, :] = turned.astype(BF16)

        self.saves.local(target, s.o_qkv.at[which])
        self.saves.local(normed, s.o_normed.at[which])
        self.saves.local(scale, s.o_scale.at[which])

    def attend(self, k):
        s = self.s
        heads = H // ATTN_STEPS
        if k >= 1:
            self.saves.done(self.slots[k - 1])
        for i in range(heads):
            base, mask = head_window(k * heads + i)
            window = pl.ds(base, 256)
            for image in range(2):
                rows = pl.ds(image * SEQ, SEQ)
                query = jnp.where(mask, s.q[rows, window].astype(F32), 0.0).astype(BF16)
                scores = mm_nt(query, s.k[rows, window]) * (1.0 / math.sqrt(HD))
                powers = jnp.exp(scores - jnp.max(scores, axis=1, keepdims=True))
                total = jnp.sum(powers, axis=1, keepdims=True)
                soft = (powers * (1.0 / total)).astype(BF16)
                s.soft[i, image] = soft
                mixed = mm(soft, s.v[rows, window])
                old = s.combined[rows, window].astype(F32)
                s.combined[rows, window] = jnp.where(mask, mixed, old).astype(BF16)

        self.slots[k] = self.saves.local(s.soft, s.o_soft.at[pl.ds(k * heads, heads)])

    def leave(self):
        s = self.s
        self.saves.done(self.slots[ATTN_STEPS - 1])
        for copy in self.shared:
            self.saves.done(copy)
        self.remote[1].wait_send()
        self.turn(s.combined, s.t_a)
        self.share(s.t_a, s.o_lhs.at[1])
        for j in range(3):
            columns = pl.ds(j * WIDTH, WIDTH)
            s.proj[:, columns] = mm(s.combined[...], flat(s.w_out[:, :, :, columns]))

        @pl.loop(0, TOK // TILE)
        def _(i):
            rows = rows_of(i, TILE)
            image = i // (SEQ // TILE)
            mod = s.o_mod
            attended = s.proj[rows, :]
            s.attended[rows, :] = attended.astype(BF16)
            residual = s.tokens[rows, :].astype(F32) + mod[image, 2:3, :] * attended
            s.residual[rows, :] = residual
            normed, _ = norm_rows(residual)
            entry = normed * (1.0 + mod[image, 4:5, :]) + mod[image, 3:4, :]
            s.entry_b[rows, :] = entry.astype(BF16)

        self.attended = self.saves.local(s.attended, s.o_attended)
        self.saves.local(s.residual, s.o_residual)
        self.turn(s.entry_b, s.t_b)
        self.share(s.t_b, s.o_lhs.at[2])

    def ff(self, j):
        s = self.s
        self.loaded(self.load_ff, j, 6 + j)
        s.wide[0] = mm(s.entry_b[...], flat(s.w[j % 2, 0]))
        s.wide[1] = mm(s.entry_b[...], flat(s.w[j % 2, 1]))
        mine = pl.ds(pl.multiple_of(self.c * 192, 16), 192)
        theirs = pl.ds(pl.multiple_of((1 - self.c) * 192, 16), 192)
        for half in range(2):
            shard = j + 4 * half
            at = shard * WIDTH
            if (6, j - 1, half) in self.slots:
                self.saves.done(self.slots[6, j - 1, half])

            @pl.loop(0, TOK // TILE)
            def _(i, half=half, at=at):
                rows = rows_of(i, TILE)
                gate = s.wide[0, rows, half * WIDTH : (half + 1) * WIDTH]
                up = s.wide[1, rows, half * WIDTH : (half + 1) * WIDTH]
                sigma = 1.0 / (1.0 + jnp.exp(-gate))
                active = gate * sigma
                s.active[half, 0, rows, :] = active.astype(BF16)
                slope = up * sigma * (1.0 + gate * (1.0 - sigma))
                s.active[half, 1, rows, :] = slope.astype(BF16)
                s.hidden[rows, at : at + WIDTH] = (active * up).astype(BF16)

            self.slots[6, j, half] = self.saves.local(s.active.at[half], s.o_active.at[shard])
            for i in range(3):
                turned = s.hidden[:, at + 128 * i : at + 128 * i + 128].T
                s.t_h[shard, 128 * i : 128 * i + 128, :] = turned
            self.saves.local(s.t_h.at[shard, mine], s.o_hidden.at[shard, :, pl.ds(0, TOK)])
            self.to_sibling(s.t_h.at[shard, theirs], s.o_hidden.at[shard, :, pl.ds(TOK, TOK)])

    def down(self, j):
        s = self.s
        self.loaded(self.load_down, j, 14 + j)
        if j == 0:
            self.saves.done(self.attended)
        columns = pl.ds(j * WIDTH, WIDTH)
        s.wide[0, :, 0:WIDTH] = mm(s.hidden[...], flat(s.w_down[j % 2]))
        for image in range(2):
            gate = s.o_mod[image, 5:6, columns]
            total = jnp.zeros((1, WIDTH), F32)
            for i in range(SEQ // TILE):
                rows = pl.ds(image * SEQ + i * TILE, TILE)
                branch = s.wide[0, rows, 0:WIDTH]
                result = s.residual[rows, columns] + gate * branch
                s.attended[rows, columns] = result.astype(BF16)
                total = total + jnp.sum(
                    s.cot[rows, columns].astype(F32) * branch, axis=0, keepdims=True
                )
            s.o_gate_b[image, 0:1, columns] = total
        if j == 2:
            self.saves.local(s.attended, s.o_result)

    def plan(self):
        steps = [(None, self.modulate, k, 0, 7) for k in range(5)] + [(None, self.enter, None, 0, 4)]
        steps += [(self.load_qv, self.qv, j, j + 1, 2.5) for j in range(3)]
        steps += [(None, self.head_norm, 0, 3, 4)]
        steps += [(self.load_ko, self.ko, j, j + 1, 1.5) for j in range(3, 6)]
        steps += [(None, self.head_norm, 1, 6, 4)]
        steps += [(None, self.attend, k, 6, 3) for k in range(ATTN_STEPS)]
        steps += [(None, self.leave, None, 6, 6)]
        steps += [(self.load_ff, self.ff, j, 8 + 2 * j, 5.5) for j in range(4)]
        steps += [(self.load_down, self.down, j, 15 + j, 3) for j in range(3)]
        return steps

    def finish(self):
        self.saves.finish()
        for k, copy in enumerate(self.remote):
            if k != 1:
                copy.wait_send()
            copy.wait_recv()


class ForwardInputs(NamedTuple):
    qkv_shard: object
    out_shard: object
    gate: object
    up: object
    down: object
    tokens: object
    cot: object
    acted: object
    bias: object
    mod_weight: object
    acted_slim: object
    cos: object
    sin: object
    spread: object
    widen: object


FORWARD_OUTPUTS = dict(
    packed_all=((4, 2, 144, 4608), BF16),
    gate_all=((4, 2, 144, 3072), BF16),
    up_all=((4, 2, 144, 3072), BF16),
    down_all=((4, 2, 384, 1152), BF16),
    o_branch=((2 * TOK, D), BF16),
    o_lhs=((3, D, 2 * TOK), BF16),
    o_hidden=((8, 192, 2 * TOK), BF16),
    o_qkv=((3, TOK, D), BF16),
    o_normed=((2, TOK, D), BF16),
    o_scale=((2, TOK, 128), F32),
    o_soft=((H, 2, SEQ, SEQ), BF16),
    o_attended=((TOK, D), BF16),
    o_residual=((TOK, D), F32),
    o_active=((8, 2, TOK, WIDTH), BF16),
    o_result=((TOK, D), BF16),
    acted_all=((4, 2, 2, 2) + SLIM, F32),
    o_mod=((2, 8, D), F32),
    o_gate_b=((2, 8, D), F32),
)


def forward_scratch():
    def vmem(*shape, kind=BF16):
        return pltpu.VMEM(shape, kind)

    return dict(
        entry_a=vmem(TOK, D),
        d_branch=vmem(TOK, D),
        t_a=vmem(D, TOK),
        proj=vmem(TOK, D, kind=F32),
        q=vmem(TOK, D),
        k=vmem(TOK, D),
        v=vmem(TOK, D),
        q_normed=vmem(TOK, D),
        k_normed=vmem(TOK, D),
        scale_q=vmem(TOK, 128, kind=F32),
        scale_k=vmem(TOK, 128, kind=F32),
        soft=vmem(H // ATTN_STEPS, 2, SEQ, SEQ),
        combined=vmem(TOK, D),
        attended=vmem(TOK, D),
        residual=vmem(TOK, D, kind=F32),
        entry_b=vmem(TOK, D),
        t_b=vmem(D, TOK),
        wide=vmem(2, TOK, 2 * WIDTH, kind=F32),
        active=vmem(2, 2, TOK, WIDTH),
        hidden=vmem(TOK, 8 * WIDTH),
        t_h=vmem(8, WIDTH, TOK),
        w=vmem(2, 2, 4, 2, 144, 2 * WIDTH),
        w_out=vmem(4, 2, 144, D),
        w_down=vmem(2, 4, 2, 384, WIDTH),
        gather_send=pltpu.SemaphoreType.DMA((4, N_PIECES)),
        gather_recv=pltpu.SemaphoreType.DMA((4, N_PIECES)),
        mod_w=vmem(MOD_PART, D),
        acted_group=vmem(4, 8, D, kind=F32),
        mod_flat=vmem(8, 4 * MOD_PART, kind=F32),
        mod_parts=group_scratch(MOD_PART)[0],
        mod_got_c=group_scratch(MOD_PART)[1],
        mod_got_y=group_scratch(MOD_PART)[2],
        mod_blocks=group_scratch(MOD_PART)[3],
        mod_send=group_scratch(MOD_PART)[4],
        mod_recv=group_scratch(MOD_PART)[5],
        acted_send=pltpu.SemaphoreType.DMA((4,)),
        acted_recv=pltpu.SemaphoreType.DMA((4,)),
        acted_own=pltpu.SemaphoreType.DMA,
        first_send=pltpu.SemaphoreType.DMA((2,)),
        first_recv=pltpu.SemaphoreType.DMA((2,)),
        own_packed=vmem(144, 4 * D),
        own_down=vmem(384, D),
        own_sems=pltpu.SemaphoreType.DMA((4,)),
        save_sems=pltpu.SemaphoreType.DMA((56,)),
        load_sems=pltpu.SemaphoreType.DMA((48,)),
        pair_send=pltpu.SemaphoreType.DMA((16,)),
        pair_recv=pltpu.SemaphoreType.DMA((16,)),
    )


def run_step(steps, arrived):
    _, act, j, _, cost = steps.pop(0)
    if steps and steps[0][0] is not None and steps[0][3] <= arrived:
        steps[0][0](steps[0][2])
    act() if j is None else act(j)
    return cost


def forward_kernel(*refs):
    names = ForwardInputs._fields + tuple(FORWARD_OUTPUTS) + tuple(forward_scratch())
    s = SimpleNamespace(**dict(zip(names, refs, strict=True)))
    spot = place()
    greet(neighbours(*spot))
    arrays = [(s.qkv_shard, s.out_shard), s.gate, s.up, s.down, s.packed_all, s.gate_all, s.up_all, s.down_all]
    own_gate, own_up = s.hidden.at[pl.ds(0, 144)], s.hidden.at[pl.ds(144, 144)]
    stages = [s.own_packed, own_gate, own_up, s.own_down]
    gather = Gather(arrays, (s.gather_send, s.gather_recv, s.own_sems), spot, stages)
    work = Forward(s, spot, gather)
    steps = work.plan()
    gather.own_copies()
    acted = Acted(s, spot)
    ahead = GATHER_AHEAD
    arrived = 0
    for t in range(N_PIECES + 4 + ahead):
        if t == 1:
            gather.own_stores()
        if t < N_PIECES:
            if t >= ahead:
                gather.sent_z(t - ahead)
            gather.start_z(t)
        if 0 <= t - ahead < N_PIECES:
            gather.start_x(t - ahead)
        if 0 <= t - ahead - 1 < N_PIECES:
            gather.start_y(t - ahead - 1)
        if 0 <= t - ahead - 2 < N_PIECES:
            gather.start_c(t - ahead - 2)
        if 0 <= t - ahead - 3 < N_PIECES:
            if arrived == 0:
                gather.own_done()
            gather.arrived(t - ahead - 3)
            arrived += 1
        if t >= 6 and t % 3 == 0 and t // 3 - 2 < 5:
            acted.step(t // 3 - 2)
        spent = 0.0
        while steps and steps[0][3] <= arrived and spent < STEP_BUDGET:
            spent += run_step(steps, arrived)
    while steps:
        run_step(steps, arrived)
    for t in range(N_PIECES - ahead, N_PIECES):
        gather.sent_z(t)
    for t in range(N_PIECES):
        gather.sent_rest(t)
    work.finish()


def forward_pass(*given):
    hbm = pl.BlockSpec(memory_space=pl.ANY)
    inside = pl.BlockSpec(memory_space=pltpu.VMEM)
    out = pl.pallas_call(
        forward_kernel,
        out_shape=[jax.ShapeDtypeStruct(*spec) for spec in FORWARD_OUTPUTS.values()],
        in_specs=[hbm] * 5 + [inside] * 4 + [hbm] * 2 + [inside] * 4,
        out_specs=[hbm] * 16 + [inside] * 2,
        scratch_shapes=list(forward_scratch().values()),
        name="forward_pass",
        compiler_params=pltpu.CompilerParams(
            collective_id=0, has_side_effects=True, vmem_limit_bytes=121 << 19
        ),
    )(*ForwardInputs(*given))
    return SimpleNamespace(**dict(zip(FORWARD_OUTPUTS, out)))


def head_tables():
    lane = np.arange(D) % HD
    frequency = np.exp(-math.log(10000.0) * (lane % 18) / 18)
    token = np.arange(SEQ)[:, None]
    angle = np.where(lane < 36, token // GRID, token % GRID) * frequency
    sign = np.where(lane % 36 < 18, -1.0, 1.0)
    spread = (np.arange(D)[:, None] // HD == np.arange(128)).astype(np.float32)
    return (
        jnp.asarray(np.cos(angle), F32),
        jnp.asarray(np.sin(angle) * sign, F32),
        jnp.asarray(spread, BF16),
        jnp.asarray(spread.T, BF16),
    )


SCATTER_ROWS = (144,) * 14 + (192,) * 3
SCATTER_EDGE = tuple((32, 48)[j % 2] for j in range(14)) + (48,) * 3
ASKED = 3
ORDER = (14, 15, 16) + tuple(range(6, 14)) + tuple(range(6))


class Reduce:
    def __init__(self, s, spot):
        self.s = s
        self.z, self.x, self.y, self.c = spot
        self.stage = {}
        self.open = []

    def shape(self, t):
        return SCATTER_ROWS[t], SCATTER_EDGE[t]

    def part(self, t):
        rows, edge = self.shape(t)
        return pl.ds(pl.multiple_of(self.y * edge, 16), rows - edge)

    def held(self, t):
        s = self.s
        return s.held_big.at[t - 14] if t >= 14 else s.held.at[t if t < 6 else t - 6]

    def pick(self, small, big, t):
        return big.at[t - 14] if t >= 14 else small.at[t]

    def got_y(self, t):
        return self.pick(self.s.got_y, self.s.got_y_big, t)

    def got_x(self, t):
        return self.pick(self.s.got_x, self.s.got_x_big, t)

    def got_z(self, t):
        return self.pick(self.s.got_z, self.s.got_z_big, t)

    def got_f(self, t):
        return self.pick(self.s.got_f, self.s.got_f_big, t)

    def sems(self, stage, t):
        return self.s.scatter_send.at[stage, t], self.s.scatter_recv.at[stage, t]

    def produced(self, t):
        self.stage[t] = -1
        self.ask()

    def ask(self):
        entered = sum(stage > 0 for stage in self.stage.values())
        for t in ORDER[: entered + ASKED]:
            if self.stage.get(t) == -1:
                self.stage[t] = 0
                self.start_y(t)

    def advance(self):
        stages = (self.start_x, self.start_z, self.start_f, self.start_c)
        under_way = [t for t in ORDER if 0 < self.stage.get(t, 4) < 4]
        waiting = [t for t in ORDER if self.stage.get(t) == 0]
        for t in waiting[:1] + under_way[::-1]:
            stages[self.stage[t]](t)
            self.stage[t] += 1
        self.ask()

    def free(self, t):
        while self.stage[t] < 4:
            self.advance()
        if t in self.open:
            self.sent(t)

    def start_y(self, t):
        rows, edge = self.shape(t)
        theirs = pl.ds(pl.multiple_of((1 - self.y) * (rows - edge), 16), edge)
        send(
            self.held(t).at[:, :, theirs, :],
            self.got_y(t).at[:, :, pl.ds(0, edge), :],
            *self.sems(0, t),
            device(self.z, self.x, 1 - self.y, self.c),
        )

    def start_x(self, t):
        rows, edge = self.shape(t)
        held, got = self.held(t), self.got_y(t)
        drain(got.at[:, :, pl.ds(0, edge), :], self.s.scatter_recv.at[0, t])
        mine = pl.ds(pl.multiple_of(self.y * (rows - edge), 16), edge)

        @pl.loop(0, 4)
        def _(k):
            for x in range(2):
                total = held[k, x, mine, :].astype(F32) + got[k, x, pl.ds(0, edge), :].astype(F32)
                held[k, x, mine, :] = total.astype(BF16)

        send(
            held.at[:, 1 - self.x, self.part(t), :],
            self.got_x(t).at[:, pl.ds(0, rows - edge), :],
            *self.sems(1, t),
            device(self.z, 1 - self.x, self.y, self.c),
        )

    def start_z(self, t):
        rows, edge = self.shape(t)
        held, got = self.held(t), self.got_x(t)
        keep = rows - edge
        drain(got.at[:, pl.ds(0, keep), :], self.s.scatter_recv.at[1, t])
        part = self.part(t)

        @pl.loop(0, 4)
        def _(k):
            total = held[k, self.x, part, :].astype(F32) + got[k, pl.ds(0, keep), :].astype(F32)
            held[k, self.x, part, :] = total.astype(BF16)

        for step in (1, 3, 2):
            other = (self.z + step) % 4
            send(
                held.at[other, self.x, part, :],
                self.got_z(t).at[step - 1, pl.ds(0, keep), :],
                *self.sems(2, t),
                device(other, self.x, self.y, self.c),
            )

    def start_f(self, t):
        rows, edge = self.shape(t)
        held, got = self.held(t), self.got_z(t)
        keep = rows - edge
        drain(got.at[:, pl.ds(0, keep), :], self.s.scatter_recv.at[2, t])
        part = self.part(t)
        total = held[self.z, self.x, part, :].astype(F32)
        for k in range(3):
            total = total + got[k, pl.ds(0, keep), :].astype(F32)
        held[self.z, self.x, part, :] = total.astype(BF16)
        send(
            held.at[self.z, self.x, part, :],
            self.got_f(t).at[pl.ds(0, keep), :],
            *self.sems(3, t),
            device(self.z, self.x, 1 - self.y, self.c),
        )

    def target(self, t):
        s = self.s
        if t < 6:
            columns = pl.ds(pl.multiple_of(self.c * LANE_HALF + t * WIDTH, 128), WIDTH)
            return s.g_packed.at[:, columns]
        if t < 14:
            columns = pl.ds(pl.multiple_of(self.c * FF_HALF + (t - 6) // 2 * WIDTH, 128), WIDTH)
            return (s.g_gate, s.g_up)[(t - 6) % 2].at[:, columns]
        rows = pl.ds(pl.multiple_of(self.c * 192, 16), 192)
        return s.g_down.at[rows, pl.ds((t - 14) * WIDTH, WIDTH)]

    def start_c(self, t):
        rows, edge = self.shape(t)
        held, got = self.held(t), self.got_f(t)
        y, keep, both = self.y, rows - edge, rows - 2 * edge
        drain(got.at[pl.ds(0, keep), :], self.s.scatter_recv.at[3, t])
        drain(self.got_y(t).at[:, :, pl.ds(0, edge), :], self.s.scatter_send.at[0, t])
        drain(self.got_x(t).at[:, pl.ds(0, keep), :], self.s.scatter_send.at[1, t])
        mid, fin = held.at[self.z, self.x], held.at[self.z, 1 - self.x]

        def at(offset, count):
            return pl.ds(pl.multiple_of(offset, 16), count)

        own, other = at(y * keep, edge), at((1 - y) * keep, edge)
        fin[own, :] = mid[own, :]
        fin[other, :] = got[at((1 - y) * both, edge), :]
        total = mid[pl.ds(edge, both), :].astype(F32) + got[at(y * edge, both), :].astype(F32)
        fin[pl.ds(edge, both), :] = total.astype(BF16)
        target = self.target(t)
        send(fin, target, *self.sems(4, t), device(self.z, self.x, y, 1 - self.c))
        pltpu.make_async_copy(fin, target, self.s.store_sems.at[t]).start()
        self.open.append(t)

    def sent(self, t):
        self.open.remove(t)
        rows, edge = self.shape(t)
        sems = self.s.scatter_send
        drain(self.got_z(t).at[:, pl.ds(0, rows - edge), :], sems.at[2, t])
        drain(self.got_f(t).at[pl.ds(0, rows - edge), :], sems.at[3, t])
        drain(self.target(t), sems.at[4, t])
        drain(self.target(t), self.s.store_sems.at[t])

    def finish(self):
        for t in ORDER:
            self.free(t)
        for t in range(N_PIECES):
            drain(self.target(t), self.s.scatter_recv.at[4, t])


class Backward:
    def __init__(self, s, spot, reduce):
        self.s, self.reduce = s, reduce
        self.z, self.x, self.y, self.c = spot
        self.pending = {}
        self.remote = {}
        self.copies = 0

    def load(self, key, source, target):
        if key not in self.pending:
            copy = pltpu.make_async_copy(source, target, self.s.load_sems.at[self.copies])
            self.copies += 1
            copy.start()
            self.pending[key] = copy

    def wait(self, *keys):
        for key in keys:
            self.pending.pop(key).wait()

    def to_sibling(self, key, source, target):
        k = len(self.remote)
        copy = pltpu.make_async_remote_copy(
            src_ref=source,
            dst_ref=target,
            send_sem=self.s.pair_send.at[k],
            recv_sem=self.s.pair_recv.at[k],
            device_id=device(self.z, self.x, self.y, 1 - self.c),
            device_id_type=MESH,
        )
        copy.start()
        self.remote[key] = copy


    def grad_down(self, hidden, branch):
        s, reduce = self.s, self.reduce

        @pl.loop(0, 4)
        def _(k):
            left = hidden[pl.ds(2 * k, 2)].reshape(384, 2 * TOK)
            total = mm(left, branch[...]).astype(BF16)
            for j in range(3):
                block = total[:, j * WIDTH : (j + 1) * WIDTH]
                s.held_big[j, k] = block.reshape(2, 192, WIDTH)

        for t in (14, 15, 16):
            reduce.produced(t)

    def column(self, w):
        half = (1 - self.c) if w % 2 == 0 else self.c
        return half * 4 + w // 2

    def load_ff(self, f, w):
        s = self.s
        window = self.column(w)
        columns = pl.ds(pl.multiple_of(window * WIDTH, 128), WIDTH)
        slot = w % 2
        self.load((1, w), s.down_all.at[window // 2, window % 2], f.w_down.at[slot])
        self.load((2, w), s.gate_all.at[:, :, :, columns], s.w.at[slot, :, :, :, pl.ds(0, WIDTH)])
        self.load((3, w), s.up_all.at[:, :, :, columns], s.w.at[slot, :, :, :, pl.ds(WIDTH, WIDTH)])
        self.load((4, w), s.o_active.at[window], f.active.at[slot])

    def ff(self, f, w):
        s = self.s
        slot = w % 2
        self.load_ff(f, w)
        self.wait((1, w), (2, w), (3, w), (4, w))
        if w < 7:
            self.load_ff(f, w + 1)
        s.d_residual[:, 0:WIDTH] = mm_nt(f.branch[pl.ds(0, TOK), :], f.w_down[slot])
        if w >= 2:
            if slot == 0:
                self.remote[5, w - 2].wait_send()
            else:
                self.wait((5, w - 2))
        steep = f.steep.at[slot]

        @pl.loop(0, TOK // TILE)
        def _(i):
            rows = rows_of(i, TILE)
            back = s.d_residual[rows, 0:WIDTH]
            steep[rows, 0:WIDTH] = (back * f.active[slot, 1, rows, :].astype(F32)).astype(BF16)
            steep[rows, WIDTH : 2 * WIDTH] = (
                back * f.active[slot, 0, rows, :].astype(F32)
            ).astype(BF16)

        j = w // 2
        if slot == 0:
            self.to_sibling((5, w), steep, s.r_ff.at[j, pl.ds(TOK, TOK)])
        else:
            self.load((5, w), steep, s.r_ff.at[j, pl.ds(0, TOK)])
        product = mm_nt(steep[...], flat(s.w[slot]))
        if w == 0:
            s.acc[...] = product
        else:
            s.acc[...] += product

    def load_grad_ff(self, j):
        s = self.s
        self.remote[5, 2 * j].wait_recv()
        if (5, 2 * j + 1) in self.pending:
            self.wait((5, 2 * j + 1))
        self.load((6, j), s.r_ff.at[j], s.right.at[j % 2])

    def grad_ff(self, j):
        s = self.s
        self.wait((6, j))
        right = s.right.at[j % 2]

        @pl.loop(0, 2)
        def _(k):
            left = s.left[pl.ds(pl.multiple_of(k * 576, 64), 576), :]
            total = mm(left, right[...]).astype(BF16)
            for half in range(2):
                block = total[:, half * WIDTH : (half + 1) * WIDTH]
                s.held[2 * j + half, pl.ds(2 * k, 2)] = block.reshape(2, 2, 144, WIDTH)

        self.reduce.produced(6 + 2 * j)
        self.reduce.produced(7 + 2 * j)

    def feed_forward(self, f):
        s, reduce = self.s, self.reduce
        self.wait(11, 12)
        self.load((7, 0), s.o_lhs.at[2], s.left)
        self.grad_down(f.hidden, f.branch)
        for w in range(8):
            self.ff(f, w)
            if w == 0:
                self.wait((7, 0))
            if w % 2 == 1:
                reduce.advance()
                if w >= 3:
                    self.load_grad_ff(w // 2 - 1)
            elif w >= 4:
                self.grad_ff(w // 2 - 2)
        self.load_grad_ff(3)
        self.grad_ff(2)
        self.grad_ff(3)
        self.remote[5, 6].wait_send()


    def middle(self, f):
        s = self.s
        self.load(21, s.cot, f.cot)
        self.load(22, s.o_residual, s.d_residual)
        self.load(23, s.o_attended, f.attended)
        self.wait(21, 22, 23)
        s.d_mod[...] = jnp.zeros_like(s.d_mod)

        @pl.loop(0, TOK // TILE)
        def _(i):
            rows = rows_of(i, TILE)
            image = i // (SEQ // TILE)
            mod, d_mod = s.mod, s.d_mod
            normed, inverse = norm_rows(s.d_residual[rows, :])
            d_entry = s.acc[rows, :]
            d_mod[image, 3:4, :] += jnp.sum(d_entry, axis=0, keepdims=True)
            d_mod[image, 4:5, :] += jnp.sum(d_entry * normed, axis=0, keepdims=True)
            back = norm_back(normed, inverse, d_entry * (1.0 + mod[image, 4:5, :]))
            d_residual = f.cot[rows, :].astype(F32) + back
            s.d_residual[rows, :] = d_residual
            attended = f.attended[rows, :].astype(F32)
            d_mod[image, 2:3, :] += jnp.sum(d_residual * attended, axis=0, keepdims=True)
            s.joined[rows, 3 * D : 4 * D] = (mod[image, 2:3, :] * d_residual).astype(BF16)


    def load_soft(self, f, k):
        heads = H // ATTN_STEPS
        self.load((31, k), self.s.o_soft.at[pl.ds(k * heads, heads)], f.soft)

    def attend(self, f, k):
        s = self.s
        heads = H // ATTN_STEPS
        self.wait((31, k))
        factor = 1.0 / math.sqrt(HD)
        for i in range(heads):
            base, mask = head_window(k * heads + i)
            window = pl.ds(base, 256)
            for image in range(2):
                rows = pl.ds(image * SEQ, SEQ)
                back = jnp.where(mask, f.back[rows, window].astype(F32), 0.0).astype(BF16)
                soft = f.soft[i, image]
                d_soft = mm_nt(back, f.qkv[2, rows, window])
                wide = soft.astype(F32)
                d_scores = (
                    wide * (d_soft - jnp.sum(wide * d_soft, axis=1, keepdims=True))
                ).astype(BF16)
                results = (
                    mm(d_scores, f.qkv[1, rows, window]) * factor,
                    mm_tn(d_scores, f.qkv[0, rows, window]) * factor,
                    mm_tn(soft, back),
                )
                for part, result in enumerate(results):
                    place_at = pl.ds(part * D + base, 256)
                    old = s.joined[rows, place_at].astype(F32)
                    s.joined[rows, place_at] = jnp.where(mask, result, old).astype(BF16)
        if k + 1 < ATTN_STEPS:
            self.load_soft(f, k + 1)

    def head_back(self, f, which):
        s = self.s

        @pl.loop(0, TOK // HEAD_TILE)
        def _(i):
            rows = rows_of(i, HEAD_TILE)
            spots = rows_of(i % (SEQ // HEAD_TILE), HEAD_TILE)
            columns = pl.ds(which * D, D)
            grad = s.joined[rows, columns].astype(F32)
            grad = grad * f.cos[spots, :] - partner(grad, first_lanes(HEAD_TILE)) * f.sin[spots, :]
            normed = f.normed[which, rows, :].astype(F32)
            mean = mm_split(grad * normed, s.spread[...]) * (1.0 / HD)
            scale = mm_split(s.acc[rows, which * 128 : which * 128 + 128], s.widen[...])
            result = scale * (grad - normed * mm(mean.astype(BF16), s.widen[...]))
            s.joined[rows, columns] = result.astype(BF16)

    def attention(self, f):
        s, reduce = self.s, self.reduce
        self.load(24, s.packed_all.at[:, :, :, pl.ds(3 * D, 768)], s.w.at[0])
        self.load(25, s.packed_all.at[:, :, :, pl.ds(3 * D + 768, WIDTH)], s.w.at[1, :, :, :, pl.ds(0, WIDTH)])
        for k in range(3):
            self.load((41, k), s.o_qkv.at[k], f.qkv.at[k])
        self.load_soft(f, 0)
        self.load(42, s.o_normed, f.normed)
        self.load(44, s.cos, f.cos)
        self.load(45, s.sin, f.sin)
        self.wait(24, 25)
        joined = s.joined
        s.acc[...] = mm_nt(joined[:, 3 * D : 3 * D + 768], flat(s.w[0]))
        s.acc[...] += mm_nt(joined[:, 3 * D + 768 :], flat(s.w[1, :, :, :, 0:WIDTH]))
        f.back[...] = s.acc[...].astype(BF16)
        for k in range(2):
            self.load((43, k), s.o_scale.at[k], s.acc.at[:, pl.ds(128 * k, 128)])
        reduce.advance()
        self.wait((41, 0), (41, 1), (41, 2))
        for k in range(ATTN_STEPS):
            self.attend(f, k)
            if k % 2 == 1:
                reduce.advance()
        self.wait(42, (43, 0), (43, 1), 44, 45)
        self.head_back(f, 0)
        self.trade(0)
        reduce.advance()
        self.head_back(f, 1)
        self.trade(1)

    def trade(self, k):
        s = self.s
        columns = pl.ds(k * D, D)
        theirs = pl.ds(pl.multiple_of((1 - self.c) * LANE_HALF + k * D, 128), D)
        mine = pl.ds(pl.multiple_of(self.c * LANE_HALF + k * D, 128), D)
        send(
            s.joined.at[:, theirs],
            s.r_packed.at[pl.ds(TOK, TOK), columns],
            s.pair_send.at[6 + k],
            s.pair_recv.at[6 + k],
            device(self.z, self.x, self.y, 1 - self.c),
        )
        own = s.r_packed.at[pl.ds(0, TOK), columns]
        pltpu.make_async_copy(s.joined.at[:, mine], own, s.trade_sems.at[k]).start()

    def traded(self, k):
        block = self.s.r_packed.at[pl.ds(0, TOK), pl.ds(k * D, D)]
        drain(block, self.s.pair_recv.at[6 + k])
        drain(block, self.s.trade_sems.at[k])


    def load_entry(self, k):
        s = self.s
        width = 768 if k < 4 else WIDTH
        self.load(
            (51, k),
            s.packed_all.at[:, :, :, pl.ds(k * 768, width)],
            s.w.at[k % 2, :, :, :, pl.ds(0, width)],
        )

    def entry(self, k):
        s = self.s
        width = 768 if k < 4 else WIDTH
        self.load_entry(k)
        self.wait((51, k))
        if k < 4:
            self.load_entry(k + 1)
        product = mm_nt(s.joined[:, k * 768 : k * 768 + width], flat(s.w[k % 2, :, :, :, 0:width]))
        if k == 0:
            s.acc[...] = product
        else:
            s.acc[...] += product

    def grad_packed(self, f, jj):
        s = self.s
        self.wait((61, jj))
        right = s.right.at[jj % 2]

        @pl.loop(0, 2)
        def _(k):
            rows = pl.ds(pl.multiple_of(k * 576, 64), 576)
            for half in range(2):
                j = 2 * jj + half
                left = s.left if j < 3 else f.left
                total = mm(left[rows, :], right[:, half * WIDTH : (half + 1) * WIDTH])
                s.held[j, pl.ds(2 * k, 2)] = total.astype(BF16).reshape(2, 2, 144, WIDTH)

        self.reduce.produced(2 * jj)
        self.reduce.produced(2 * jj + 1)

    def load_right(self, jj):
        self.load((61, jj), self.s.r_packed.at[:, pl.ds(768 * jj, 768)], self.s.right.at[jj % 2])

    def last(self, f):
        s, reduce = self.s, self.reduce
        self.traded(0)
        self.load_right(0)
        self.load(72, s.o_lhs.at[0], s.left)
        self.load(73, s.o_lhs.at[self.c], f.left)
        self.load(74, s.tokens, f.tokens)
        self.load(76, s.mod_weight, f.mod_w)
        self.load_entry(0)
        reduce.advance()
        self.wait(72, 73)
        for jj in range(3):
            reduce.free(6 + 2 * jj)
            reduce.free(7 + 2 * jj)
            self.grad_packed(f, jj)
            if jj == 0:
                self.traded(1)
                self.load_right(1)
                self.load_right(2)
            self.entry(jj)
            reduce.advance()
        self.entry(3)
        self.entry(4)
        reduce.advance()
        self.wait(74)

        @pl.loop(0, TOK // TILE)
        def _(i):
            rows = rows_of(i, TILE)
            image = i // (SEQ // TILE)
            mod, d_mod = s.mod, s.d_mod
            normed, inverse = norm_rows(f.tokens[rows, :].astype(F32))
            d_entry = s.acc[rows, :]
            d_mod[image, 0:1, :] += jnp.sum(d_entry, axis=0, keepdims=True)
            d_mod[image, 1:2, :] += jnp.sum(d_entry * normed, axis=0, keepdims=True)
            back = norm_back(normed, inverse, d_entry * (1.0 + mod[image, 1:2, :]))
            s.d_residual[rows, :] += back

        self.load(75, s.d_residual, s.g_tokens)
        self.modulation(f)
        reduce.finish()
        self.wait(75)
        for k in range(2):
            drain(s.r_packed.at[pl.ds(0, TOK), pl.ds(k * D, D)], s.pair_send.at[6 + k])

    def modulation(self, f):
        s, reduce = self.s, self.reduce
        z, x, y, c = spot = (self.z, self.x, self.y, self.c)
        s.back_flat[...] = jnp.zeros_like(s.back_flat)
        for image in range(2):
            for k in range(6):
                row = s.gate_b[image, 0:1, :] if k == 5 else s.d_mod[image, k : k + 1, :]
                rounded = row.astype(BF16).astype(F32)
                s.back_flat[image : image + 1, k * D : (k + 1) * D] = rounded
        for m in range(4):
            s.back_parts[m] = s.back_flat[:, m * MOD_PART : (m + 1) * MOD_PART]
        group = Group(
            spot, s.back_parts, s.back_got_c, s.back_got_y, s.back_blocks, s.back_send, s.back_recv
        )
        group.start()
        reduce.advance()
        group.across_y()
        reduce.advance()
        group.finish()
        for m in range(4):
            s.back[2 * m : 2 * m + 2, :] = s.back_blocks[m, 0:2, :]
        x_peer = device(z, 1 - x, y, c)
        send(s.back, s.back_got_x, s.wide_send.at[0], s.wide_recv.at[0], x_peer)
        self.wait(76)
        partial = mm(s.back[...].astype(BF16), f.mod_w[...])
        s.cond_parts[...] = jnp.zeros_like(s.cond_parts)
        for m in range(4):
            s.cond_parts[m, 0:2, :] = partial[2 * m : 2 * m + 2, :]
        cond = Group(
            spot, s.cond_parts, s.cond_got_c, s.cond_got_y, s.cond_blocks, s.cond_send, s.cond_recv
        )
        cond.start()
        drain(s.back, s.wide_recv.at[0])
        own, other = s.back[...], s.back_got_x[...]
        low = jnp.where(x == 0, own, other)
        high = jnp.where(x == 0, other, own)
        s.back_all[z] = jnp.concatenate([low, high], axis=0).astype(BF16)
        block = s.back_all.at[z]
        for step in (1, 3, 2):
            peer = device((z + step) % 4, x, y, c)
            send(block, block, s.wide_send.at[1], s.wide_recv.at[1], peer)
        cond.across_y()
        reduce.advance()
        cond.finish()
        total = s.cond_blocks[0] + s.cond_blocks[1] + s.cond_blocks[2] + s.cond_blocks[3]
        s.o_cond[...] = total
        reduce.advance()
        drain(s.back_all.at[pl.ds(0, 3)], s.wide_recv.at[1])
        self.load(77, s.back_all, s.o_back)
        drain(s.back, s.wide_send.at[0])
        drain(s.back_all.at[pl.ds(0, 3)], s.wide_send.at[1])
        self.wait(77)


class BackwardInputs(NamedTuple):
    packed_all: object
    gate_all: object
    up_all: object
    down_all: object
    o_branch: object
    o_lhs: object
    o_hidden: object
    o_qkv: object
    o_normed: object
    o_scale: object
    o_soft: object
    o_attended: object
    o_residual: object
    o_active: object
    tokens: object
    cot: object
    cos: object
    sin: object
    mod: object
    spread: object
    widen: object
    gate_b: object
    mod_weight: object


BACKWARD_OUTPUTS = dict(
    g_packed=((144, 4 * D), BF16),
    g_gate=((144, 8 * WIDTH), BF16),
    g_up=((144, 8 * WIDTH), BF16),
    g_down=((384, D), BF16),
    g_tokens=((TOK, D), F32),
    r_ff=((4, 2 * TOK, 2 * WIDTH), BF16),
    r_packed=((2 * TOK, LANE_HALF), BF16),
    o_back=((4, 16, MOD_PART), BF16),
    o_cond=((8, D), F32),
)


def vmem(*shape, kind=BF16):
    return pltpu.VMEM(shape, kind)


def backward_scratch():
    return dict(
        held=vmem(8, 4, 2, 144, WIDTH),
        held_big=vmem(3, 4, 2, 192, WIDTH),
        got_y=vmem(14, 4, 2, 48, WIDTH),
        got_y_big=vmem(3, 4, 2, 48, WIDTH),
        got_x=vmem(14, 4, 112, WIDTH),
        got_x_big=vmem(3, 4, 144, WIDTH),
        got_z=vmem(14, 3, 112, WIDTH),
        got_z_big=vmem(3, 3, 144, WIDTH),
        got_f=vmem(14, 112, WIDTH),
        got_f_big=vmem(3, 144, WIDTH),
        w=vmem(2, 4, 2, 144, 2 * WIDTH),
        acc=vmem(TOK, D, kind=F32),
        d_residual=vmem(TOK, D, kind=F32),
        joined=vmem(TOK, 4 * D),
        left=vmem(D, 2 * TOK),
        right=vmem(2, 2 * TOK, 2 * WIDTH),
        d_mod=vmem(2, 8, D, kind=F32),
        back_flat=vmem(8, 4 * MOD_PART, kind=F32),
        back_parts=group_scratch(MOD_PART)[0],
        back_got_c=group_scratch(MOD_PART)[1],
        back_got_y=group_scratch(MOD_PART)[2],
        back_blocks=group_scratch(MOD_PART)[3],
        back_send=group_scratch(MOD_PART)[4],
        back_recv=group_scratch(MOD_PART)[5],
        cond_parts=group_scratch(D)[0],
        cond_got_c=group_scratch(D)[1],
        cond_got_y=group_scratch(D)[2],
        cond_blocks=group_scratch(D)[3],
        cond_send=group_scratch(D)[4],
        cond_recv=group_scratch(D)[5],
        back=vmem(8, MOD_PART, kind=F32),
        back_got_x=vmem(8, MOD_PART, kind=F32),
        back_all=vmem(4, 16, MOD_PART),
        wide_send=pltpu.SemaphoreType.DMA((2,)),
        wide_recv=pltpu.SemaphoreType.DMA((2,)),
        scatter_send=pltpu.SemaphoreType.DMA((5, N_PIECES)),
        scatter_recv=pltpu.SemaphoreType.DMA((5, N_PIECES)),
        store_sems=pltpu.SemaphoreType.DMA((N_PIECES,)),
        load_sems=pltpu.SemaphoreType.DMA((112,)),
        trade_sems=pltpu.SemaphoreType.DMA((2,)),
        pair_send=pltpu.SemaphoreType.DMA((8,)),
        pair_recv=pltpu.SemaphoreType.DMA((8,)),
    )


def backward_kernel(*refs):
    names = BackwardInputs._fields + tuple(BACKWARD_OUTPUTS) + tuple(backward_scratch())
    s = SimpleNamespace(**dict(zip(names, refs, strict=True)))
    spot = place()
    greet(neighbours(*spot))
    reduce = Reduce(s, spot)
    work = Backward(s, spot, reduce)

    def scoped(act, before=None, **shapes):
        def run(*held):
            f = SimpleNamespace(**dict(zip(shapes, held, strict=True)))
            if before is not None:
                before(f)
            act(f)

        pl.run_scoped(run, *shapes.values())

    def first_loads(f):
        work.load(11, s.o_hidden, f.hidden)
        work.load(12, s.o_branch, f.branch)
        work.load_ff(f, 0)

    scoped(
        work.feed_forward,
        first_loads,
        hidden=vmem(8, 192, 2 * TOK),
        branch=vmem(2 * TOK, D),
        w_down=vmem(2, 384, D),
        active=vmem(2, 2, TOK, WIDTH),
        steep=vmem(2, TOK, 2 * WIDTH),
    )
    scoped(work.middle, cot=vmem(TOK, D), attended=vmem(TOK, D))
    reduce.advance()
    scoped(
        work.attention,
        qkv=vmem(3, TOK, D),
        normed=vmem(2, TOK, D),
        soft=vmem(H // ATTN_STEPS, 2, SEQ, SEQ),
        back=vmem(TOK, D),
        cos=vmem(SEQ, D, kind=F32),
        sin=vmem(SEQ, D, kind=F32),
    )
    scoped(work.last, left=vmem(D, 2 * TOK), tokens=vmem(TOK, D), mod_w=vmem(MOD_PART, D))


def backward_pass(f, tokens, cotangent, mod_weight, tables):
    hbm = pl.BlockSpec(memory_space=pl.ANY)
    inside = pl.BlockSpec(memory_space=pltpu.VMEM)
    cosine, sine, spread, widen = tables
    given = BackwardInputs(
        f.packed_all,
        f.gate_all,
        f.up_all,
        f.down_all,
        f.o_branch,
        f.o_lhs,
        f.o_hidden,
        f.o_qkv,
        f.o_normed,
        f.o_scale,
        f.o_soft,
        f.o_attended,
        f.o_residual,
        f.o_active,
        tokens,
        cotangent,
        cosine,
        sine,
        f.o_mod,
        spread,
        widen,
        f.o_gate_b,
        mod_weight,
    )
    out = pl.pallas_call(
        backward_kernel,
        out_shape=[jax.ShapeDtypeStruct(*spec) for spec in BACKWARD_OUTPUTS.values()],
        in_specs=[hbm] * 18 + [inside] * 4 + [hbm],
        out_specs=[hbm] * 8 + [inside],
        scratch_shapes=list(backward_scratch().values()),
        name="backward_pass",
        compiler_params=pltpu.CompilerParams(
            collective_id=1, has_side_effects=True, vmem_limit_bytes=121 << 19
        ),
    )(*given)
    return SimpleNamespace(**dict(zip(BACKWARD_OUTPUTS, out)))


class SettleInputs(NamedTuple):
    packed: object
    gate: object
    up: object
    down: object
    acted: object
    back: object
    cond: object
    total: object


SETTLE_OUTPUTS = dict(
    g_qkv=((144, 3 * D), F32),
    g_proj=((144, D), F32),
    g_gate=((144, 8 * WIDTH), F32),
    g_up=((144, 8 * WIDTH), F32),
    g_down=((384, D), F32),
    g_mod=((144, MOD_PART), F32),
    g_bias=((MOD_PART,), F32),
    g_cond=((2, D), F32),
)


def settle_scratch():
    return dict(
        v_packed=vmem(144, 4 * D),
        v_gate=vmem(144, 8 * WIDTH),
        v_up=vmem(144, 8 * WIDTH),
        v_down=vmem(384, D),
        w_qkv=vmem(144, 3 * D, kind=F32),
        w_proj=vmem(144, D, kind=F32),
        w_gate=vmem(144, 8 * WIDTH, kind=F32),
        w_up=vmem(144, 8 * WIDTH, kind=F32),
        w_down=vmem(384, D, kind=F32),
        w_mod=vmem(144, MOD_PART, kind=F32),
        load_sems=pltpu.SemaphoreType.DMA((4,)),
        store_sems=pltpu.SemaphoreType.DMA((16,)),
    )


def settle_kernel(*refs):
    names = SettleInputs._fields + tuple(SETTLE_OUTPUTS) + tuple(settle_scratch())
    s = SimpleNamespace(**dict(zip(names, refs, strict=True)))
    pairs = ((s.packed, s.v_packed), (s.gate, s.v_gate), (s.up, s.v_up), (s.down, s.v_down))
    loads = [pltpu.make_async_copy(a, b, s.load_sems.at[k]) for k, (a, b) in enumerate(pairs)]
    for load in loads:
        load.start()
    stores = []

    def store(source, target):
        copy = pltpu.make_async_copy(source, target, s.store_sems.at[len(stores)])
        copy.start()
        stores.append(copy)

    def widen(source, target, out, offset=0):
        count = target.shape[0] // 3
        for k in range(3):
            for at in range(k * count, (k + 1) * count, 16):
                rows = pl.ds(at, 16)
                target[rows, :] = source[rows, offset : offset + target.shape[1]].astype(F32)
            rows = pl.ds(k * count, count)
            store(target.at[rows], out.at[rows])

    loads[0].wait()
    widen(s.v_packed, s.w_qkv, s.g_qkv)
    widen(s.v_packed, s.w_proj, s.g_proj, 3 * D)
    for k, (source, target, out) in enumerate(
        ((s.v_gate, s.w_gate, s.g_gate), (s.v_up, s.w_up, s.g_up), (s.v_down, s.w_down, s.g_down))
    ):
        loads[k + 1].wait()
        widen(source, target, out)
    s.w_mod[...] = mm_tn(s.acted[...], s.back[...])
    store(s.w_mod, s.g_mod)
    s.g_bias[...] = jnp.sum(s.back[...].astype(F32), axis=0)
    total = s.total[...]
    sigma = 1.0 / (1.0 + jnp.exp(-total))
    s.g_cond[...] = s.cond[0:2, :] * sigma * (1.0 + total * (1.0 - sigma))
    for copy in stores:
        copy.wait()


def settle(*given):
    hbm = pl.BlockSpec(memory_space=pl.ANY)
    inside = pl.BlockSpec(memory_space=pltpu.VMEM)
    out = pl.pallas_call(
        settle_kernel,
        out_shape=[jax.ShapeDtypeStruct(*spec) for spec in SETTLE_OUTPUTS.values()],
        in_specs=[hbm] * 4 + [inside] * 4,
        out_specs=[hbm] * 6 + [inside] * 2,
        scratch_shapes=list(settle_scratch().values()),
        name="settle",
        compiler_params=pltpu.CompilerParams(vmem_limit_bytes=60 << 20),
    )(*SettleInputs(*given))
    return SimpleNamespace(**dict(zip(SETTLE_OUTPUTS, out)))


def body_general(
    tokens,
    condition,
    timestep,
    qkv_weight,
    out_weight,
    gate_weight,
    up_weight,
    down_weight,
    mod_weight,
    mod_bias,
    cotangent,
):
    gathered = (
        lax.all_gather(qkv_weight, "dp", axis=0, tiled=True),
        lax.all_gather(out_weight, "dp", axis=0, tiled=True),
        lax.all_gather(gate_weight, "dp", axis=0, tiled=True),
        lax.all_gather(up_weight, "dp", axis=0, tiled=True),
        lax.all_gather(down_weight, "dp", axis=0, tiled=True),
    )
    cond_total = condition.astype(jnp.float32) + embed_steps(timestep)
    acted_cond = jax.nn.silu(cond_total).astype(jnp.bfloat16)
    acted_group = lax.all_gather(acted_cond, "mod", axis=0, tiled=True)
    mod_part = (
        jnp.dot(acted_group, mod_weight, preferred_element_type=jnp.float32)
        + mod_bias.astype(jnp.float32)
    ).astype(jnp.bfloat16)
    modulation = lax.all_to_all(mod_part, "mod", split_axis=0, concat_axis=1, tiled=True).astype(
        jnp.float32
    )
    tables = rope_tables()
    per_micro = tokens.shape[0] // MICRO
    outputs = []
    token_grads = []
    mod_grads = []
    kept = []
    for micro_step in range(MICRO):
        start_row = micro_step * per_micro
        output, d_tokens, d_modulation, factors = layer_pass(
            tokens[start_row : start_row + per_micro],
            modulation[start_row : start_row + per_micro],
            cotangent[start_row : start_row + per_micro],
            gathered,
            tables,
        )
        outputs.append(output)
        token_grads.append(d_tokens)
        mod_grads.append(d_modulation)
        kept.append(factors)
    joined = [jnp.concatenate([factors[number] for factors in kept], axis=0) for number in range(9)]
    (
        entry_first,
        d_projected,
        combined,
        d_attended,
        entry_second,
        d_gate_proj,
        d_up_proj,
        hidden,
        d_branch,
    ) = joined
    grad_qkv = jnp.einsum(
        "bsd,bse->de", entry_first, d_projected, preferred_element_type=jnp.float32
    )
    grad_proj = jnp.einsum("bsd,bse->de", combined, d_attended, preferred_element_type=jnp.float32)
    grad_gate = jnp.einsum(
        "bsd,bsf->df", entry_second, d_gate_proj, preferred_element_type=jnp.float32
    )
    grad_up = jnp.einsum("bsd,bsf->df", entry_second, d_up_proj, preferred_element_type=jnp.float32)
    grad_down = jnp.einsum("bsf,bsd->fd", hidden, d_branch, preferred_element_type=jnp.float32)
    totals = (grad_qkv, grad_proj, grad_gate, grad_up, grad_down)
    output_tokens = jnp.concatenate(outputs, axis=0)
    grad_tokens = jnp.concatenate(token_grads, axis=0)
    mod_grad = jnp.concatenate(mod_grads, axis=0)
    mod_back = lax.all_to_all(mod_grad, "mod", split_axis=1, concat_axis=0, tiled=True)
    grad_mod_part = jnp.einsum(
        "id,ic->dc", acted_group, mod_back, preferred_element_type=jnp.float32
    )
    bias_part = jnp.sum(mod_back.astype(jnp.float32), axis=0)
    acted_grad_part = jnp.einsum(
        "ic,dc->id", mod_back, mod_weight, preferred_element_type=jnp.float32
    )
    acted_grad = lax.psum_scatter(
        acted_grad_part.astype(jnp.bfloat16), "mod", scatter_dimension=0, tiled=True
    ).astype(jnp.float32)
    sigma_cond = jax.nn.sigmoid(cond_total)
    grad_condition = acted_grad * sigma_cond * (1.0 + cond_total * (1.0 - sigma_cond))
    grad_bias = lax.psum(bias_part, "dp")
    count = lax.axis_size("dp")
    arrays = totals + (grad_mod_part,)
    shapes = [array.shape for array in arrays]
    flat = lax.psum_scatter(pack_rows(arrays, count), "dp", scatter_dimension=0, tiled=True)
    summed = unpack_rows(flat, shapes, count)
    finished = (
        lax.psum(summed[0].astype(jnp.bfloat16), "mod").astype(jnp.float32),
        lax.psum(summed[1].astype(jnp.bfloat16), "mod").astype(jnp.float32),
        lax.psum(summed[2].astype(jnp.bfloat16), "mod").astype(jnp.float32),
        lax.psum(summed[3].astype(jnp.bfloat16), "mod").astype(jnp.float32),
        lax.psum(summed[4].astype(jnp.bfloat16), "mod").astype(jnp.float32),
    )
    grad_mod = summed[5]
    return (
        output_tokens,
        grad_tokens,
        grad_condition,
        finished[0],
        finished[1],
        finished[2],
        finished[3],
        finished[4],
        grad_mod,
        grad_bias,
    )


def body_fast(
    tokens,
    condition,
    timestep,
    qkv_weight,
    out_weight,
    gate_weight,
    up_weight,
    down_weight,
    mod_weight,
    mod_bias,
    cotangent,
):
    cond_total = condition.astype(jnp.float32) + embed_steps(timestep)
    acted_cond = jax.nn.silu(cond_total).astype(jnp.bfloat16)
    acted_rows = acted_cond.astype(F32)
    acted_slim = jnp.pad(acted_rows.reshape(-1, 128), ((0, 6), (0, 0)))
    flat_tokens, flat_cotangent = tokens.reshape(TOK, D), cotangent.reshape(TOK, D)
    tables = head_tables()
    f = forward_pass(
        qkv_weight,
        out_weight,
        gate_weight,
        up_weight,
        down_weight,
        flat_tokens,
        flat_cotangent,
        jnp.pad(acted_rows, ((0, 6), (0, 0))),
        mod_bias,
        mod_weight.T,
        acted_slim,
        *tables,
    )
    b = backward_pass(f, flat_tokens, flat_cotangent, mod_weight.T, tables)
    acted_all = f.acted_all.reshape(32, -1)[:, : 2 * D].reshape(64, D).astype(BF16)
    back_all = b.o_back.reshape(64, -1)
    rows = D // 8
    acted_part = lax.dynamic_slice_in_dim(acted_all, lax.axis_index("dp") * rows, rows, 1)
    g = settle(b.g_packed, b.g_gate, b.g_up, b.g_down, acted_part, back_all, b.o_cond, cond_total)
    return (
        f.o_result.reshape(tokens.shape),
        b.g_tokens.reshape(tokens.shape),
        g.g_cond,
        g.g_qkv,
        g.g_proj,
        g.g_gate,
        g.g_up,
        g.g_down,
        g.g_mod,
        g.g_bias,
    )


def pick_body(mesh):
    if dict(mesh.shape) == {"dp": 8, "mod": 4}:
        return body_fast
    return body_general


def solution(mesh):
    in_specs = (
        P(("dp", "mod"), None, None),
        P(("dp", "mod"), None),
        P(("dp", "mod")),
        P("dp", None),
        P("dp", None),
        P("dp", None),
        P("dp", None),
        P("dp", None),
        P(None, "mod"),
        P("mod"),
        P(("dp", "mod"), None, None),
    )
    out_specs = (
        P(("dp", "mod"), None, None),
        P(("dp", "mod"), None, None),
        P(("dp", "mod"), None),
        P("dp", None),
        P("dp", None),
        P("dp", None),
        P("dp", None),
        P("dp", None),
        P("dp", "mod"),
        P("mod"),
    )
    return jax.shard_map(pick_body(mesh), mesh=mesh, in_specs=in_specs, out_specs=out_specs, check_vma=False)
```
